32 devices in a mesh: tile: 4 (over y, x), cuts: 8 (over z, core).
Axes of the slice: x: 2, y: 2, z: 4, core: 2. Of those that a mesh axis runs over, the one named last changes fastest.
Arguments:
- density: bfloat16 [128, 512, 1024], P('cuts', 'tile'), may hold values from -8 to 8
- valid: int32 [512, 1024], P('tile'), may hold values from 0 to 1, as said below
- row_taps: bfloat16 [4, 128, 17], P(None, 'cuts'), may hold values from -1.5 to 1.5
- col_taps: bfloat16 [4, 128, 17], P(None, 'cuts'), may hold values from -1.5 to 1.5
- amp_matrix: bfloat16 [128, 128], replicated, may hold values from -0.5 to 0.5
- like_matrix: bfloat16 [128, 128], replicated, may hold values from -0.5 to 0.5
Outputs:
- amplitude: bfloat16 [128, 524288], P(None, ('tile', 'cuts'))
- likelihood: bfloat16 [128, 524288], P(None, ('tile', 'cuts'))
The draws below stay inside these ranges and needn't reach their ends.
Inputs may be any that keep to these rules, and one draw needn't show every extreme that they name: Every pixel row holds at least one valid pixel; the share of valid pixels rises from about 0.3 in the first row to about 0.9 in the last.
All inputs are finite; a program needn't handle non-finite values.
Results may differ from the reference program's by a relative error of at most 0.0082.
Values may be sent and summed in bfloat16 or wider, within the bound.
No kernel may reach another device: no remote copies, remote signals or barrier semaphores. Data moves between devices by JAX's collectives and lax.ppermute only.
A program may use at most 128 MiB of HBM per device.

```python
import jax
import jax.numpy as jnp
from jax import lax

SLICES = 128
ZBINS = 128
TERMS = 4
REACH = 8
COLS = 1024
NROWS = 512


def draw_valid(key, part):
    row_index = lax.broadcasted_iota(jnp.int32, (NROWS, COLS), 0)
    col_index = lax.broadcasted_iota(jnp.int32, (NROWS, COLS), 1)
    limit = 300 + 600 * row_index // max(NROWS - 1, 1)
    picks = jax.random.randint(key, (NROWS, COLS), 0, 1000)
    keeps = (picks < limit) | (col_index == row_index % COLS)
    return keeps.astype(jnp.int32)


def draw_density(key, part):
    own_key = jax.random.fold_in(key, 11)
    key_offset, key_offsign, key_noise = jax.random.split(own_key, 3)
    magnitude = jax.random.uniform(key_offset, (SLICES, 1, 1), jnp.float32, 0.5, 2.0)
    offset_sign = jnp.where(jax.random.bernoulli(key_offsign, 0.5, (SLICES, 1, 1)), 1.0, -1.0)
    offsets = offset_sign * magnitude
    values = offsets + jax.random.normal(key_noise, (SLICES, NROWS, COLS), jnp.float32)
    return jnp.clip(values, -8.0, 8.0).astype(jnp.bfloat16)


def shard_levels(stream_key, dims, cuts, least, largest):
    def one(axis_at, parts):
        draws = jax.random.uniform(jax.random.fold_in(jax.random.fold_in(stream_key, 6), axis_at), (parts,), jnp.float32, least / len(cuts), largest / len(cuts))
        return jnp.repeat(jnp.exp(draws), dims[axis_at] // parts).reshape((-1,) + (1,) * (len(dims) - axis_at - 1))

    gain = one(*cuts[0])
    for cut in cuts[1:]:
        gain = gain * one(*cut)
    return gain


def scatter_about(key, extent, width, bound, shards=(), dtype=jnp.bfloat16):
    loudness = shard_levels(key, extent, shards, -0.22, 0.18) if shards else 1.0
    array = jax.random.normal(key, extent, jnp.float32) * width * loudness
    return jnp.minimum(jnp.maximum(array, -bound), bound).astype(dtype)


def setup_inputs(seed: int = 0) -> dict:
    streams_of = jax.random.split(jax.random.key(seed), 7)
    density = draw_density(jax.random.fold_in(streams_of[6], 71), 0)
    valid = draw_valid(jax.random.fold_in(streams_of[6], 71), 0)
    row_taps = scatter_about(streams_of[2], (TERMS, SLICES, 2 * REACH + 1), (2 * REACH + 1) ** -0.5, 1.5, ((1, 8),))
    col_taps = scatter_about(streams_of[3], (TERMS, SLICES, 2 * REACH + 1), (2 * REACH + 1) ** -0.5, 1.5, ((1, 8),))
    amp_matrix = scatter_about(streams_of[4], (SLICES, ZBINS), SLICES ** -0.5, 0.5)
    like_matrix = scatter_about(streams_of[5], (SLICES, ZBINS), SLICES ** -0.5, 0.5)
    return {"density": density, "valid": valid, "row_taps": row_taps, "col_taps": col_taps, "amp_matrix": amp_matrix, "like_matrix": like_matrix}


def smooth_axis(plane, taps, axis):
    length = plane.shape[axis]
    widths = [(0, 0), (0, 0)]
    widths[axis] = (REACH, REACH)
    padded = jnp.pad(plane, widths)
    total = jnp.zeros(plane.shape, jnp.float32)
    for offset in range(2 * REACH + 1):
        shifted = lax.slice_in_dim(padded, offset, offset + length, axis=axis)
        total = total + taps[offset].astype(jnp.float32) * shifted
    return total


def filter_slice(packed):
    plane, row_set, col_set = packed
    plane_float = plane.astype(jnp.float32)
    total = jnp.zeros(plane.shape, jnp.float32)
    for term in range(TERMS):
        rowed = smooth_axis(plane_float, row_set[term], 0).astype(jnp.bfloat16)
        total = total + smooth_axis(rowed.astype(jnp.float32), col_set[term], 1)
    return total.astype(jnp.bfloat16)


def project_block(block, amp_matrix, like_matrix):
    amp_float = jnp.dot(amp_matrix.T, block, preferred_element_type=jnp.float32)
    like_float = amp_float * jnp.dot(like_matrix.T, block, preferred_element_type=jnp.float32)
    return amp_float.astype(jnp.bfloat16), like_float.astype(jnp.bfloat16)


def reference(density, valid, row_taps, col_taps, amp_matrix, like_matrix):
    mask_float = valid.astype(jnp.float32)
    sums = jnp.sum(density.astype(jnp.float32) * mask_float[None], axis=(1, 2))
    background = sums / jnp.sum(mask_float)
    masked_field = (mask_float[None] * (density.astype(jnp.float32) - background[:, None, None])).astype(jnp.bfloat16)
    filtered = lax.map(filter_slice, (masked_field, jnp.moveaxis(row_taps, 1, 0), jnp.moveaxis(col_taps, 1, 0)))
    flat = filtered.reshape(SLICES, NROWS * COLS)
    blocks = flat.reshape(SLICES, NROWS, COLS).transpose(1, 0, 2)
    amp_blocks, like_blocks = lax.map(lambda block: project_block(block, amp_matrix, like_matrix), blocks)
    amplitude = amp_blocks.transpose(1, 0, 2).reshape(ZBINS, NROWS * COLS)
    likelihood = like_blocks.transpose(1, 0, 2).reshape(ZBINS, NROWS * COLS)
    return amplitude, likelihood
```

```python
import functools

import jax
import jax.numpy as jnp
from jax import lax
from jax.experimental import pallas as pl
from jax.experimental.pallas import tpu as pltpu
from jax.sharding import PartitionSpec as P

REACH = 8
TAPS = 2 * REACH + 1
LANES = 128
GROUP = 8
VMEM_BYTES = 48 * 1024 * 1024
HALO = 2 * REACH


def params():
    return pltpu.CompilerParams(vmem_limit_bytes=VMEM_BYTES)


def cost(flops, moved):
    return pl.CostEstimate(flops=int(flops), bytes_accessed=int(moved), transcendentals=0)


def matrices_kernel(row_taps, col_taps, col_out, row_out):
    terms, slices, _ = row_taps.shape
    wide = 2 * LANES
    window = LANES + HALO
    tap = lax.broadcasted_iota(jnp.int32, (TAPS, wide), 0)
    lane = lax.broadcasted_iota(jnp.int32, (TAPS, wide), 1)
    flip = (lax.rem(tap + lane, wide) == 0).astype(jnp.bfloat16)
    for k in range(terms):
        base = jnp.dot(col_taps[k], flip, preferred_element_type=jnp.float32)
        for s in range(slices):
            rows = jnp.broadcast_to(base[s : s + 1], (window, wide))
            band = pltpu.roll(rows, 0, 1, stride=1, stride_axis=0)
            col_out[s, :window, k * LANES : (k + 1) * LANES] = band[:, :LANES].astype(jnp.bfloat16)
    for s in range(slices):
        col_out[s, window:, :] = jnp.zeros((wide - window, terms * LANES), jnp.bfloat16)
    high = LANES // terms
    block = high - HALO
    tap = lax.broadcasted_iota(jnp.int32, (TAPS, LANES), 0)
    lane = lax.broadcasted_iota(jnp.int32, (TAPS, LANES), 1)
    base = jnp.zeros((slices, LANES), jnp.float32)
    for k in range(terms):
        place = (lane == tap + k * high).astype(jnp.bfloat16)
        base = base + jnp.dot(row_taps[k], place, preferred_element_type=jnp.float32)
    sub = lax.broadcasted_iota(jnp.int32, (GROUP, LANES), 0)
    for g in range(slices // GROUP):
        own = base[g * GROUP : (g + 1) * GROUP]
        for pair in range(block // 2):
            shifted = [pltpu.roll(own, 2 * pair + h, 1) for h in range(2)]
            for s in range(GROUP):
                both = jnp.concatenate([jnp.where(sub == s, x, 0.0) for x in shifted], axis=0)
                row_out[
                    g, pair * 2 * GROUP : (pair + 1) * 2 * GROUP, s * LANES : (s + 1) * LANES
                ] = both.astype(jnp.bfloat16)


def filter_matrices(row_taps, col_taps):
    terms, slices, _ = row_taps.shape
    block = LANES // terms - HALO
    return pl.pallas_call(
        matrices_kernel,
        name="matrices",
        out_shape=(
            jax.ShapeDtypeStruct((slices, 2 * LANES, terms * LANES), jnp.bfloat16),
            jax.ShapeDtypeStruct((slices // GROUP, block * GROUP, GROUP * LANES), jnp.bfloat16),
        ),
        compiler_params=params(),
        cost_estimate=cost(1e6, 5e6),
    )(row_taps, col_taps)


def sums_kernel(density, valid, out):
    slices, rows, cols = density.shape

    @pl.when(pl.program_id(0) == 0)
    def _():
        out[...] = jnp.zeros_like(out)

    mask = valid[...] != 0
    for s in range(slices + 1):
        if s < slices:
            x = jnp.where(mask, density[s].astype(jnp.float32), 0.0)
        else:
            x = jnp.where(mask, 1.0, 0.0)
        x = x.reshape(rows // 8, 8, cols).sum(axis=0)
        x = sum(x[:, c : c + LANES] for c in range(0, cols, LANES))
        out[s : s + 1, :] += jnp.sum(x, axis=0, keepdims=True)


def masked_sums(density, valid):
    slices, rows, cols = density.shape
    step = 32
    return pl.pallas_call(
        sums_kernel,
        name="sums",
        grid=(rows // step,),
        in_specs=[
            pl.BlockSpec((slices, step, cols), lambda i: (0, i, 0)),
            pl.BlockSpec((step, cols), lambda i: (i, 0)),
        ],
        out_specs=pl.BlockSpec((slices + 8, LANES), lambda i: (0, 0)),
        out_shape=jax.ShapeDtypeStruct((slices + 8, LANES), jnp.float32),
        compiler_params=params(),
        cost_estimate=cost(2 * density.size, 2 * density.size),
    )(density, valid)


def filter_kernel(pieces, ids, *refs):
    (before, now, after, mask_before, mask_now, mask_after, above, below, col, row), refs = refs[:10], refs[10:]
    sums, refs = refs[:4], refs[4:]
    outs, (tall,) = refs[:-1], refs[-1:]
    slices, block, cols = now.shape
    terms = col.shape[2] // LANES
    step = pl.program_id(0)
    blocks = pl.num_programs(0)
    me = ids[step]
    first = me == 0
    last = me == ids[blocks]
    total = sums[0][...] + sums[1][...] + sums[2][...] + sums[3][...]
    total = jnp.sum(total, axis=1, keepdims=True)
    mean = total[:slices] / total[slices : slices + 1]
    halo = block + HALO
    f32 = jnp.float32
    top = jnp.where(first, above[slices].astype(f32), mask_before[REACH:, :].astype(f32))
    bottom = jnp.where(last, below[slices].astype(f32), mask_after[:REACH, :].astype(f32))
    mask = jnp.concatenate([top, mask_now[...].astype(f32), bottom], axis=0)
    parts = []
    for g in range(slices // GROUP):
        for j in range(GROUP):
            s = g * GROUP + j
            top = jnp.where(first, above[s].astype(f32), before[s].astype(f32)[REACH:])
            bottom = jnp.where(last, below[s].astype(f32), after[s].astype(f32)[:REACH])
            x = jnp.concatenate([top, now[s].astype(f32), bottom], axis=0)
            x = mask * (x - mean[s : s + 1, :])
            x = jnp.concatenate([x, jnp.zeros((halo, LANES), f32)], axis=1)
            x = pltpu.roll(x, REACH, 1).astype(jnp.bfloat16)
            x = jnp.concatenate([x[:, c : c + 2 * LANES] for c in range(0, cols, LANES)], axis=0)
            y = jnp.dot(x, col[s], preferred_element_type=f32).astype(jnp.bfloat16)
            for c in range(cols // LANES):
                for k in range(terms):
                    tall[(j * terms + k) * halo : (j * terms + k + 1) * halo, c * LANES : (c + 1) * LANES] = y[
                        c * halo : (c + 1) * halo, k * LANES : (k + 1) * LANES
                    ]
        z = jnp.dot(row[g], tall[...], preferred_element_type=f32)
        parts.append(z.reshape(block, GROUP, cols))
    field = jnp.concatenate(parts, axis=1).astype(jnp.bfloat16)
    count = len(pieces)
    for b in range(len(outs) // count):

        @pl.when(step == b)
        def _():
            for p, (start, stop) in enumerate(pieces):
                outs[b * count + p][...] = field[start:stop]


def filter_blocks(ids, pieces, density, valid, above, below, col, row, sums):
    slices, rows, cols = density.shape
    block = row.shape[1] // GROUP
    last = rows // block - 1
    count = ids.shape[0]
    terms = col.shape[2] // LANES

    def rows_at(shift):
        return lambda i, at: (0, jnp.clip(at[i] + shift, 0, last), 0)

    def mask_at(shift):
        return lambda i, at: (jnp.clip(at[i] + shift, 0, last), 0)

    def whole(x):
        return pl.BlockSpec(x.shape, lambda i, at: (0,) * x.ndim, pipeline_mode=pl.Buffered(1))

    shapes = [(stop - start, slices, cols) for start, stop in pieces] * count
    out = pl.pallas_call(
        functools.partial(filter_kernel, pieces),
        name="filter",
        grid_spec=pltpu.PrefetchScalarGridSpec(
            num_scalar_prefetch=1,
            grid=(count,),
            in_specs=[pl.BlockSpec((slices, block, cols), rows_at(d)) for d in (-1, 0, 1)]
            + [pl.BlockSpec((block, cols), mask_at(d)) for d in (-1, 0, 1)]
            + [whole(x) for x in (above, below, col, row, *sums)],
            out_specs=[pl.BlockSpec(shape, lambda i, at: (0, 0, 0)) for shape in shapes],
            scratch_shapes=[pltpu.VMEM((GROUP * terms * (block + HALO), cols), jnp.bfloat16)],
        ),
        out_shape=[jax.ShapeDtypeStruct(shape, jnp.bfloat16) for shape in shapes],
        compiler_params=params(),
        cost_estimate=cost(count * 2 * slices * 805e6 / 16, count * 3e6),
    )(jnp.concatenate([ids, jnp.full((1,), last, ids.dtype)]), *([density] * 3), *([valid] * 3), above, below, col, row, *sums)
    n = len(pieces)
    return [out[b * n : (b + 1) * n] for b in range(count)]


def project_kernel(count, weights, *refs):
    parts, (amp_out, like_out) = refs[:count], refs[-2:]
    zbins = weights.shape[0] // 2
    pencil = jnp.concatenate([x[0] for x in parts], axis=0)
    both = jnp.dot(weights[...], pencil, preferred_element_type=jnp.float32)
    amp = both[:zbins]
    amp_out[...] = amp.astype(jnp.bfloat16)
    like_out[...] = (amp * both[zbins:]).astype(jnp.bfloat16)


def project(weights, parts, start, total, earlier):
    rows, slices, cols = parts[0].shape
    zbins = weights.shape[0] // 2
    count = len(parts)
    shape = jax.ShapeDtypeStruct((zbins, total * cols), jnp.bfloat16)
    return pl.pallas_call(
        functools.partial(project_kernel, count),
        name="project",
        grid=(rows,),
        in_specs=[pl.BlockSpec(weights.shape, lambda i: (0, 0))]
        + [pl.BlockSpec((1, slices, cols), lambda i: (i, 0, 0))] * count
        + [pl.BlockSpec(memory_space=pl.ANY)] * len(earlier),
        out_specs=[pl.BlockSpec((zbins, cols), lambda i: (0, i + start))] * 2,
        out_shape=[shape, shape],
        input_output_aliases={1 + count + i: i for i in range(len(earlier))},
        compiler_params=params(),
        cost_estimate=cost(4 * zbins * rows * cols * slices * count, 2 * rows * cols * (slices * count + 2 * zbins)),
    )(weights, *parts, *earlier)


def fast(density, valid, row_taps, col_taps, amp_matrix, like_matrix):
    slices, rows, cols = density.shape
    peers = lax.axis_size("cuts")
    tiles = lax.axis_size("tile")
    block = rows // peers
    me = lax.axis_index("cuts")
    mask = valid.astype(jnp.bfloat16)[None]
    first = jnp.concatenate([density[:, :REACH], mask[:, :REACH]], axis=0)
    last = jnp.concatenate([density[:, rows - REACH :], mask[:, rows - REACH :]], axis=0)
    above = lax.ppermute(last, "tile", [(i, i + 1) for i in range(tiles - 1)])
    below = lax.ppermute(first, "tile", [(i + 1, i) for i in range(tiles - 1)])
    own = masked_sums(density, valid)
    sums = [own] + [lax.ppermute(own, "tile", [(i, i ^ k) for i in range(tiles)]) for k in range(1, tiles)]
    col, row = filter_matrices(row_taps, col_taps)

    half = block // 2
    pieces = ((0, half), (half, block))
    early = [4]
    late = [6, 5, 7, 2, 3, 1, 0]
    filtered = {}
    for ks in (early, late):
        ids = jnp.stack([me ^ k for k in ks]).astype(jnp.int32)
        for k, got in zip(ks, filter_blocks(ids, pieces, density, valid, above, below, col, row, sums)):
            filtered[k] = got
    order = [(4, 0), (6, 0), (2, 0), (5, 0), (3, 0), (7, 0), (1, 0), (2, 1), (4, 1), (3, 1), (6, 1), (1, 1), (5, 1), (7, 1)]
    arrived = {(0, p): filtered[0][p] for p in range(len(pieces))}
    for k, p in order:
        arrived[k, p] = lax.ppermute(filtered[k][p], "cuts", [(i, i ^ k) for i in range(peers)])
    weights = jnp.concatenate([amp_matrix, like_matrix], axis=1).T.reshape(-1, peers, slices)
    weights = weights[:, me ^ jnp.arange(peers)].reshape(-1, peers * slices)
    result = []
    for p, (start, _) in enumerate(pieces):
        result = project(weights, [arrived[k, p] for k in range(peers)], start, block, result)
    return tuple(result)


def extended(shard, sides, width):
    for axis, dim in sides:
        size, length = (lax.axis_size(axis), shard.shape[dim])
        up = [(i, (i + 1) % size) for i in range(size - 1)]
        down = [(j, i) for i, j in up]
        last = lax.slice_in_dim(shard, length - width, length, axis=dim)
        initial = lax.slice_in_dim(shard, 0, width, axis=dim)
        before = lax.ppermute(last, axis, up)
        after = lax.ppermute(initial, axis, down)
        shard = jnp.concatenate([before, shard, after], axis=dim)
    return shard


def band_matrix(taps, out_count, in_count):
    offset = lax.broadcasted_iota(jnp.int32, (out_count, in_count), 1) - lax.broadcasted_iota(
        jnp.int32, (out_count, in_count), 0
    )
    positions = lax.broadcasted_iota(jnp.int32, (1, 1, TAPS), 2)
    choose = (offset[:, :, None] == positions).astype(jnp.bfloat16)
    return jnp.einsum("ijt,kst->ksij", choose, taps, preferred_element_type=jnp.float32).astype(jnp.bfloat16)


def filter_field(padded, row_taps, col_taps):
    tall = padded.shape[1]
    cols = padded.shape[2]
    width = 2 * LANES
    row_band = band_matrix(row_taps, tall - HALO, tall)
    rowed = jnp.einsum("ksij,sjc->ksic", row_band, padded, preferred_element_type=jnp.float32).astype(jnp.bfloat16)
    widened = jnp.pad(rowed, ((0, 0), (0, 0), (0, 0), (REACH, REACH)))
    col_band = band_matrix(col_taps, width, width + HALO)
    pieces = []
    for begin in range(0, cols, width):
        segment = widened[:, :, :, begin : begin + width + HALO]
        pieces.append(jnp.einsum("ksrj,ksij->sri", segment, col_band, preferred_element_type=jnp.float32))
    return jnp.concatenate(pieces, axis=2).astype(jnp.bfloat16)


def general(density, valid, row_taps, col_taps, amp_matrix, like_matrix):
    slices, rows, cols = density.shape
    mask = valid.astype(jnp.float32)
    field = density.astype(jnp.float32)
    sums, count = lax.psum((jnp.sum(field * mask[None], axis=(1, 2)), jnp.sum(mask)), "tile")
    masked = (mask[None] * (field - (sums / count)[:, None, None])).astype(jnp.bfloat16)
    filtered = filter_field(extended(masked, (("tile", 1),), REACH), row_taps, col_taps)
    peers = lax.axis_size("cuts")
    share = rows * cols // peers
    pencil = lax.all_to_all(
        filtered.reshape(slices, peers, share), "cuts", split_axis=1, concat_axis=0, tiled=True
    ).reshape(slices * peers, share)
    amp = jnp.dot(amp_matrix.T, pencil, preferred_element_type=jnp.float32)
    like = amp * jnp.dot(like_matrix.T, pencil, preferred_element_type=jnp.float32)
    return amp.astype(jnp.bfloat16), like.astype(jnp.bfloat16)


def per_device(density, valid, row_taps, col_taps, amp_matrix, like_matrix):
    slices, rows, cols = density.shape
    terms = row_taps.shape[0]
    peers = lax.axis_size("cuts")
    fits = (
        peers == 8
        and lax.axis_size("tile") == 4
        and slices == 2 * GROUP
        and terms == 4
        and rows == peers * (LANES // terms - HALO)
        and cols % (2 * LANES) == 0
    )
    run = fast if fits else general
    return run(density, valid, row_taps, col_taps, amp_matrix, like_matrix)


def solution(mesh):
    return jax.shard_map(
        per_device,
        mesh=mesh,
        in_specs=(
            P("cuts", "tile", None),
            P("tile", None),
            P(None, "cuts", None),
            P(None, "cuts", None),
            P(),
            P(),
        ),
        out_specs=(P(None, ("tile", "cuts")), P(None, ("tile", "cuts"))),
        check_vma=False,
    )
```

```python
import functools

import jax
import jax.numpy as jnp
from jax import lax
from jax.experimental import pallas as pl
from jax.experimental.pallas import tpu as pltpu
from jax.sharding import PartitionSpec as P

REACH = 8
TAPS = 2 * REACH + 1
LANES = 128
GROUP = 8
VMEM_BYTES = 48 * 1024 * 1024
HALO = 2 * REACH


def params():
    return pltpu.CompilerParams(vmem_limit_bytes=VMEM_BYTES)


def cost(flops, moved):
    return pl.CostEstimate(flops=int(flops), bytes_accessed=int(moved), transcendentals=0)


def build_matrices(row_taps, col_taps, col_out, row_out):
    terms, slices, _ = row_taps.shape
    wide = 2 * LANES
    window = LANES + HALO
    tap = lax.broadcasted_iota(jnp.int32, (TAPS, wide), 0)
    lane = lax.broadcasted_iota(jnp.int32, (TAPS, wide), 1)
    flip = (lax.rem(tap + lane, wide) == 0).astype(jnp.bfloat16)
    for k in range(terms):
        base = jnp.dot(col_taps[k], flip, preferred_element_type=jnp.float32)
        for s in range(slices):
            rows = jnp.broadcast_to(base[s : s + 1], (window, wide))
            band = pltpu.roll(rows, 0, 1, stride=1, stride_axis=0)
            col_out[s, :window, k * LANES : (k + 1) * LANES] = band[:, :LANES].astype(jnp.bfloat16)
    for s in range(slices):
        col_out[s, window:, :] = jnp.zeros((wide - window, terms * LANES), jnp.bfloat16)
    high = LANES // terms
    tap = lax.broadcasted_iota(jnp.int32, (TAPS, LANES), 0)
    lane = lax.broadcasted_iota(jnp.int32, (TAPS, LANES), 1)
    base = jnp.zeros((slices, LANES), jnp.float32)
    for k in range(terms):
        place = (lane == tap + k * high).astype(jnp.bfloat16)
        base = base + jnp.dot(row_taps[k], place, preferred_element_type=jnp.float32)
    sub = lax.broadcasted_iota(jnp.int32, (GROUP, LANES), 0)
    for g in range(slices // GROUP):
        own = base[g * GROUP : (g + 1) * GROUP]
        for pair in range(row_out.shape[1] // (2 * GROUP)):
            shifted = [pltpu.roll(own, 2 * pair + h, 1) for h in range(2)]
            for s in range(GROUP):
                both = jnp.concatenate([jnp.where(sub == s, x, 0.0) for x in shifted], axis=0)
                row_out[
                    g, pair * 2 * GROUP : (pair + 1) * 2 * GROUP, s * LANES : (s + 1) * LANES
                ] = both.astype(jnp.bfloat16)


def matrix_shapes(terms, slices, rows):
    return (slices, 2 * LANES, terms * LANES), (slices // GROUP, rows * GROUP, GROUP * LANES)


def matrices_kernel(row_taps, col_taps, after, col_out, row_out):
    build_matrices(row_taps, col_taps, col_out, row_out)


def filter_matrices(row_taps, col_taps, after):
    terms, slices, _ = row_taps.shape
    shapes = matrix_shapes(terms, slices, LANES // terms - HALO)
    vmem = pl.BlockSpec(memory_space=pltpu.VMEM)
    return pl.pallas_call(
        matrices_kernel,
        name="matrices",
        in_specs=[vmem, vmem, pl.BlockSpec(memory_space=pl.ANY)],
        out_shape=[jax.ShapeDtypeStruct(shape, jnp.bfloat16) for shape in shapes],
        compiler_params=params(),
        cost_estimate=cost(1e6, 5e6),
    )(row_taps, col_taps, after)


def convolve(field, col, row, tall, rows):
    slices, _, wide = col.shape
    terms = wide // LANES
    high, cols = LANES // terms, tall.shape[1]
    parts = []
    for g in range(slices // GROUP):
        for j in range(GROUP):
            s = g * GROUP + j
            x = jnp.concatenate([field(s), jnp.zeros((high, LANES), jnp.float32)], axis=1)
            x = pltpu.roll(x, REACH, 1).astype(jnp.bfloat16)
            x = jnp.concatenate([x[:, c : c + 2 * LANES] for c in range(0, cols, LANES)], axis=0)
            y = jnp.dot(x, col[s], preferred_element_type=jnp.float32).astype(jnp.bfloat16)
            for c in range(cols // LANES):
                for k in range(terms):
                    tall[(j * terms + k) * high : (j * terms + k + 1) * high, c * LANES : (c + 1) * LANES] = y[
                        c * high : (c + 1) * high, k * LANES : (k + 1) * LANES
                    ]
        z = jnp.dot(row[g, : rows * GROUP], tall[...], preferred_element_type=jnp.float32)
        parts.append(z.reshape(rows, GROUP, cols))
    return jnp.concatenate(parts, axis=1)


def inner_rows(first, second, last):
    both = jnp.concatenate([first.astype(jnp.float32), second.astype(jnp.float32)], axis=0)
    rows = both.shape[0] - REACH
    chosen = jnp.where(last, both[REACH:], both[:rows])
    return jnp.concatenate([chosen, jnp.zeros((REACH, both.shape[1]), jnp.float32)], axis=0)


def early_kernel(ids, one, two, mask_one, mask_two, row_taps, col_taps, after, out, centre, col, row, tall):
    slices = one.shape[0]
    build_matrices(row_taps, col_taps, col, row)
    last = ids[0] == ids[1]
    mask = inner_rows(mask_one[...], mask_two[...], last)

    def folded(x):
        x = x.reshape(x.shape[0] // 8, 8, x.shape[1]).sum(axis=0)
        x = sum(x[:, c : c + LANES] for c in range(0, x.shape[1], LANES))
        return jnp.sum(x, axis=0, keepdims=True)

    sums = jnp.concatenate([folded(mask * inner_rows(one[s], two[s], last)) for s in range(slices)], axis=0)
    mean = jnp.sum(sums, axis=1, keepdims=True) / jnp.sum(folded(mask), axis=1, keepdims=True)
    centre[...] = jnp.broadcast_to(mean, centre.shape)
    field = convolve(
        lambda s: mask * (inner_rows(one[s], two[s], last) - mean[s : s + 1]), col, row, tall, out.shape[0]
    )
    out[...] = field.astype(jnp.bfloat16)


def mend_kernel(ids, mask_one, mask_two, row_taps, col_taps, piece, delta, after, out, col, row, tall):
    build_matrices(row_taps, col_taps, col, row)
    last = ids[0] == ids[1]
    mask = inner_rows(mask_one[...], mask_two[...], last)
    field = convolve(lambda s: mask, col, row, tall, out.shape[0])
    shift = jnp.broadcast_to(delta[:, :1], field.shape[1:])
    out[...] = (piece[...].astype(jnp.float32) + shift[None] * field).astype(jnp.bfloat16)


def early_call(kernel, name, ids, density, valid, row_taps, col_taps, extra, after, out_shape):
    terms, slices, _ = row_taps.shape
    cols = valid.shape[1]
    block = LANES // terms - HALO
    last = valid.shape[0] // block - 1

    def at(shift):
        return lambda i, ids: jnp.minimum(ids[0], last - 1) + shift

    def whole(x):
        return pl.BlockSpec(x.shape, lambda i, ids: (0,) * x.ndim)

    cubes = [] if density is None else [density] * 2
    shapes = matrix_shapes(terms, slices, REACH)
    return pl.pallas_call(
        kernel,
        name=name,
        grid_spec=pltpu.PrefetchScalarGridSpec(
            num_scalar_prefetch=1,
            grid=(1,),
            in_specs=[
                pl.BlockSpec((slices, block, cols), lambda i, ids, f=at(d): (0, f(i, ids), 0)) for d in range(len(cubes))
            ]
            + [pl.BlockSpec((block, cols), lambda i, ids, f=at(d): (f(i, ids), 0)) for d in (0, 1)]
            + [whole(x) for x in (row_taps, col_taps, *extra)]
            + [pl.BlockSpec(memory_space=pl.ANY)],
            out_specs=[whole(x) for x in out_shape],
            scratch_shapes=[pltpu.VMEM(shape, jnp.bfloat16) for shape in shapes]
            + [pltpu.VMEM((GROUP * LANES, cols), jnp.bfloat16)],
        ),
        out_shape=out_shape,
        compiler_params=params(),
        cost_estimate=cost(3e9, 3e6),
    )(jnp.stack([ids, jnp.full_like(ids, last)]).astype(jnp.int32), *cubes, valid, valid, row_taps, col_taps, *extra, after)


def sums_kernel(density, valid, after, out, first, last):
    slices, rows, cols = density.shape
    step = pl.program_id(0)

    @pl.when(step == 0)
    def _():
        out[...] = jnp.zeros_like(out)
        first[:slices] = density[:, :REACH]
        first[slices] = valid[:REACH].astype(jnp.bfloat16)

    @pl.when(step == pl.num_programs(0) - 1)
    def _():
        last[:slices] = density[:, rows - REACH :]
        last[slices] = valid[rows - REACH :].astype(jnp.bfloat16)

    mask = valid[...] != 0
    for s in range(slices + 1):
        if s < slices:
            x = jnp.where(mask, density[s].astype(jnp.float32), 0.0)
        else:
            x = jnp.where(mask, 1.0, 0.0)
        x = x.reshape(rows // 8, 8, cols).sum(axis=0)
        x = sum(x[:, c : c + LANES] for c in range(0, cols, LANES))
        out[s : s + 1, :] += jnp.sum(x, axis=0, keepdims=True)


def masked_sums(density, valid, after):
    slices, rows, cols = density.shape
    step = 32
    edge = jax.ShapeDtypeStruct((slices + 1, REACH, cols), jnp.bfloat16)
    return pl.pallas_call(
        sums_kernel,
        name="sums",
        grid=(rows // step,),
        in_specs=[
            pl.BlockSpec((slices, step, cols), lambda i: (0, i, 0)),
            pl.BlockSpec((step, cols), lambda i: (i, 0)),
            pl.BlockSpec(memory_space=pl.ANY),
        ],
        out_specs=[pl.BlockSpec((slices + 8, LANES), lambda i: (0, 0))]
        + [pl.BlockSpec(edge.shape, lambda i: (0, 0, 0))] * 2,
        out_shape=[jax.ShapeDtypeStruct((slices + 8, LANES), jnp.float32), edge, edge],
        compiler_params=params(),
        cost_estimate=cost(2 * density.size, 2 * density.size),
    )(density, valid, after)


def mean_kernel(*refs):
    sums, centres, out, shifts = refs[:4], refs[4:6], refs[6], refs[7:]
    slices = out.shape[0]
    total = sums[0][...] + sums[1][...] + sums[2][...] + sums[3][...]
    total = jnp.sum(total, axis=1, keepdims=True)
    mean = jnp.broadcast_to(total[:slices] / total[slices : slices + 1], out.shape)
    out[...] = mean
    for centre, shift in zip(centres, shifts):
        shift[...] = centre[...] - mean


def means(sums, centres):
    shape = jax.ShapeDtypeStruct(centres[0].shape, jnp.float32)
    return pl.pallas_call(
        mean_kernel, name="means", out_shape=[shape] * 3, compiler_params=params(), cost_estimate=cost(1e4, 1e5)
    )(*sums, *centres)


def filter_kernel(pieces, ids, before, now, after, mask_before, mask_now, mask_after, *refs):
    (above, below, col, row, mean), outs, (tall, done) = refs[:5], refs[6:-2], refs[-2:]
    slices, block, cols = now.shape
    step = pl.program_id(0)
    first = ids[step] == 0
    last = ids[step] == ids[pl.num_programs(0)]
    f32 = jnp.float32
    top = jnp.where(first, above[slices].astype(f32), mask_before[REACH:, :].astype(f32))
    bottom = jnp.where(last, below[slices].astype(f32), mask_after[:REACH, :].astype(f32))
    mask = jnp.concatenate([top, mask_now[...].astype(f32), bottom], axis=0)

    def field(s):
        top = jnp.where(first, above[s].astype(f32), before[s].astype(f32)[REACH:])
        bottom = jnp.where(last, below[s].astype(f32), after[s].astype(f32)[:REACH])
        x = jnp.concatenate([top, now[s].astype(f32), bottom], axis=0)
        return mask * (x - mean[s : s + 1, :1])

    done[...] = convolve(field, col, row, tall, block).astype(jnp.bfloat16)
    at = 0
    for b, wanted in enumerate(pieces):

        @pl.when(step == b)
        def _():
            for p, (inner, start, stop) in enumerate(wanted):
                here = jnp.where(last != (inner == 1), block - REACH, 0) + start
                outs[at + p][...] = done[pl.ds(here, stop - start)]

        at += len(wanted)


def filter_blocks(ids, pieces, density, valid, above, below, col, row, mean, after):
    slices, rows, cols = density.shape
    block = row.shape[1] // GROUP
    last = rows // block - 1
    count = ids.shape[0]

    def rows_at(shift):
        return lambda i, at: (0, jnp.clip(at[i] + shift, 0, last), 0)

    def mask_at(shift):
        return lambda i, at: (jnp.clip(at[i] + shift, 0, last), 0)

    def whole(x):
        return pl.BlockSpec(x.shape, lambda i, at: (0,) * x.ndim, pipeline_mode=pl.Buffered(1))

    shapes = [(stop - start, slices, cols) for wanted in pieces for _, start, stop in wanted]
    out = pl.pallas_call(
        functools.partial(filter_kernel, pieces),
        name="filter",
        grid_spec=pltpu.PrefetchScalarGridSpec(
            num_scalar_prefetch=1,
            grid=(count,),
            in_specs=[pl.BlockSpec((slices, block, cols), rows_at(d)) for d in (-1, 0, 1)]
            + [pl.BlockSpec((block, cols), mask_at(d)) for d in (-1, 0, 1)]
            + [whole(x) for x in (above, below, col, row, mean)]
            + [pl.BlockSpec(memory_space=pl.ANY)],
            out_specs=[pl.BlockSpec(shape, lambda i, at: (0, 0, 0)) for shape in shapes],
            scratch_shapes=[
                pltpu.VMEM((GROUP * LANES, cols), jnp.bfloat16),
                pltpu.VMEM((block, slices, cols), jnp.bfloat16),
            ],
        ),
        out_shape=[jax.ShapeDtypeStruct(shape, jnp.bfloat16) for shape in shapes],
        compiler_params=params(),
        cost_estimate=cost(count * 2 * 805e6, count * 3e6),
    )(
        jnp.concatenate([ids, jnp.full((1,), last, ids.dtype)]),
        *([density] * 3),
        *([valid] * 3),
        above,
        below,
        col,
        row,
        mean,
        after,
    )
    out = list(out)
    return [[out.pop(0) for _ in wanted] for wanted in pieces]


def project_kernel(count, place, weights, *refs):
    parts, (amp_out, like_out) = refs[:count], refs[-2:]
    zbins = weights.shape[0] // 2
    pencil = jnp.concatenate([x[0] for x in parts], axis=0)
    both = jnp.dot(weights[...], pencil, preferred_element_type=jnp.float32)
    amp = both[:zbins]
    amp_out[...] = amp.astype(jnp.bfloat16)
    like_out[...] = (amp * both[zbins:]).astype(jnp.bfloat16)


def project(place, weights, parts, total, earlier):
    rows, slices, cols = parts[0].shape
    zbins = weights.shape[0] // 2
    count = len(parts)
    shape = jax.ShapeDtypeStruct((zbins, total * cols), jnp.bfloat16)
    return pl.pallas_call(
        functools.partial(project_kernel, count),
        name="project",
        grid_spec=pltpu.PrefetchScalarGridSpec(
            num_scalar_prefetch=1,
            grid=(rows,),
            in_specs=[pl.BlockSpec(weights.shape, lambda i, at: (0, 0))]
            + [pl.BlockSpec((1, slices, cols), lambda i, at: (i, 0, 0))] * count
            + [pl.BlockSpec(memory_space=pl.ANY)] * len(earlier),
            out_specs=[pl.BlockSpec((zbins, cols), lambda i, at: (0, i + at[0]))] * 2,
        ),
        out_shape=[shape, shape],
        input_output_aliases={2 + count + i: i for i in range(len(earlier))},
        compiler_params=params(),
        cost_estimate=cost(4 * zbins * rows * cols * slices * count, 2 * rows * cols * (slices * count + 2 * zbins)),
    )(place.reshape(1), weights, *parts, *earlier)


EARLY = (4, 6)
PIECES = ((1, 0, REACH), (0, 0, 5), (0, 5, REACH))


def fast(density, valid, row_taps, col_taps, amp_matrix, like_matrix):
    slices, rows, cols = density.shape
    terms = row_taps.shape[0]
    peers = lax.axis_size("cuts")
    tiles = lax.axis_size("tile")
    block = rows // peers
    me = lax.axis_index("cuts").astype(jnp.int32)

    def swap(x, k):
        return lax.ppermute(x, "cuts", [(i, i ^ k) for i in range(peers)])

    piece = jax.ShapeDtypeStruct((REACH, slices, cols), jnp.bfloat16)
    centre = jax.ShapeDtypeStruct((slices, LANES), jnp.float32)
    early, centres, after = [], [], row_taps
    for k in EARLY:
        made, about = early_call(
            early_kernel, "early", me ^ k, density, valid, row_taps, col_taps, (), after, [piece, centre]
        )
        early.append(made)
        centres.append(about)
        after = made
    own, first, last = masked_sums(density, valid, after)
    sums = [own] + [lax.ppermute(own, "tile", [(i, i ^ k) for i in range(tiles)]) for k in range(1, tiles)]
    above = lax.ppermute(last, "tile", [(i, i + 1) for i in range(tiles - 1)])
    below = lax.ppermute(first, "tile", [(i + 1, i) for i in range(tiles - 1)])
    col, row = filter_matrices(row_taps, col_taps, own)
    mean, *shifts = means(sums, centres)

    filtered = {}
    after = mean
    for ks in ((5,), (7, 4, 6, 2, 3, 1, 0)):
        ids = jnp.stack([me ^ k for k in ks])
        pieces = [PIECES[1:] if k in EARLY else PIECES for k in ks]
        got = filter_blocks(ids, pieces, density, valid, above, below, col, row, mean, after)
        after = got[0][0]
        for k, made in zip(ks, got):
            for p, x in zip(range(len(PIECES) - len(made), len(PIECES)), made):
                filtered[k, p] = x
    taps = jnp.stack([row_taps, col_taps])
    arrived = {}
    for k, made, shift in zip(EARLY, early, shifts):
        got_taps, got_shift, got = swap(taps, k), swap(shift, k), swap(made, k)
        (arrived[k, 0],) = early_call(
            mend_kernel, "mend", me, None, valid, got_taps[0], got_taps[1], (got, got_shift), after, [piece]
        )
    for p in range(len(PIECES)):
        for k in (5, 7, 4, 6, 2, 3, 1):
            if (k, p) not in arrived:
                arrived[k, p] = swap(filtered[k, p], k)
        arrived[0, p] = filtered[0, p]
    weights = jnp.concatenate([amp_matrix, like_matrix], axis=1).T.reshape(-1, peers, slices)
    weights = weights[:, me ^ jnp.arange(peers)].reshape(-1, peers * slices)
    result = []
    for p, (inner, start, _) in enumerate(PIECES):
        place = jnp.where((me == peers - 1) != (inner == 1), block - REACH, 0) + start
        result = project(place, weights, [arrived[k, p] for k in range(peers)], block, result)
    return tuple(result)


def extended(shard, sides, width):
    for axis, dim in sides:
        size, length = (lax.axis_size(axis), shard.shape[dim])
        up = [(i, (i + 1) % size) for i in range(size - 1)]
        down = [(j, i) for i, j in up]
        last = lax.slice_in_dim(shard, length - width, length, axis=dim)
        initial = lax.slice_in_dim(shard, 0, width, axis=dim)
        before = lax.ppermute(last, axis, up)
        after = lax.ppermute(initial, axis, down)
        shard = jnp.concatenate([before, shard, after], axis=dim)
    return shard


def band_matrix(taps, out_count, in_count):
    offset = lax.broadcasted_iota(jnp.int32, (out_count, in_count), 1) - lax.broadcasted_iota(
        jnp.int32, (out_count, in_count), 0
    )
    positions = lax.broadcasted_iota(jnp.int32, (1, 1, TAPS), 2)
    choose = (offset[:, :, None] == positions).astype(jnp.bfloat16)
    return jnp.einsum("ijt,kst->ksij", choose, taps, preferred_element_type=jnp.float32).astype(jnp.bfloat16)


def filter_field(padded, row_taps, col_taps):
    tall = padded.shape[1]
    cols = padded.shape[2]
    width = 2 * LANES
    row_band = band_matrix(row_taps, tall - HALO, tall)
    rowed = jnp.einsum("ksij,sjc->ksic", row_band, padded, preferred_element_type=jnp.float32).astype(jnp.bfloat16)
    widened = jnp.pad(rowed, ((0, 0), (0, 0), (0, 0), (REACH, REACH)))
    col_band = band_matrix(col_taps, width, width + HALO)
    pieces = []
    for begin in range(0, cols, width):
        segment = widened[:, :, :, begin : begin + width + HALO]
        pieces.append(jnp.einsum("ksrj,ksij->sri", segment, col_band, preferred_element_type=jnp.float32))
    return jnp.concatenate(pieces, axis=2).astype(jnp.bfloat16)


def general(density, valid, row_taps, col_taps, amp_matrix, like_matrix):
    slices, rows, cols = density.shape
    mask = valid.astype(jnp.float32)
    field = density.astype(jnp.float32)
    sums, count = lax.psum((jnp.sum(field * mask[None], axis=(1, 2)), jnp.sum(mask)), "tile")
    masked = (mask[None] * (field - (sums / count)[:, None, None])).astype(jnp.bfloat16)
    filtered = filter_field(extended(masked, (("tile", 1),), REACH), row_taps, col_taps)
    peers = lax.axis_size("cuts")
    share = rows * cols // peers
    pencil = lax.all_to_all(
        filtered.reshape(slices, peers, share), "cuts", split_axis=1, concat_axis=0, tiled=True
    ).reshape(slices * peers, share)
    amp = jnp.dot(amp_matrix.T, pencil, preferred_element_type=jnp.float32)
    like = amp * jnp.dot(like_matrix.T, pencil, preferred_element_type=jnp.float32)
    return amp.astype(jnp.bfloat16), like.astype(jnp.bfloat16)


def per_device(density, valid, row_taps, col_taps, amp_matrix, like_matrix):
    slices, rows, cols = density.shape
    terms = row_taps.shape[0]
    peers = lax.axis_size("cuts")
    fits = (
        peers == 8
        and lax.axis_size("tile") == 4
        and slices == 2 * GROUP
        and terms == 4
        and rows == peers * (LANES // terms - HALO)
        and cols % (2 * LANES) == 0
    )
    run = fast if fits else general
    return run(density, valid, row_taps, col_taps, amp_matrix, like_matrix)


def solution(mesh):
    return jax.shard_map(
        per_device,
        mesh=mesh,
        in_specs=(
            P("cuts", "tile", None),
            P("tile", None),
            P(None, "cuts", None),
            P(None, "cuts", None),
            P(),
            P(),
        ),
        out_specs=(P(None, ("tile", "cuts")), P(None, ("tile", "cuts"))),
        check_vma=False,
    )
```

```python
import functools

import jax
import jax.numpy as jnp
from jax import lax
from jax.experimental import pallas as pl
from jax.experimental.pallas import tpu as pltpu
from jax.sharding import PartitionSpec as P

REACH = 8
TAPS = 2 * REACH + 1
LANES = 128
GROUP = 8
MIB = 1024 * 1024
HALO = 2 * REACH


def params(mib=40):
    return pltpu.CompilerParams(vmem_limit_bytes=mib * MIB)


def cost(flops, moved):
    return pl.CostEstimate(flops=int(flops), bytes_accessed=int(moved), transcendentals=0)


def build_matrices(row_taps, col_taps, col_out, row_out):
    terms, slices = len(row_taps), row_taps[0].shape[0]
    wide = 2 * LANES
    window = LANES + HALO
    tap = lax.broadcasted_iota(jnp.int32, (TAPS, wide), 0)
    lane = lax.broadcasted_iota(jnp.int32, (TAPS, wide), 1)
    flip = (lax.rem(tap + lane, wide) == 0).astype(jnp.bfloat16)
    for k in range(terms):
        base = jnp.dot(col_taps[k], flip, preferred_element_type=jnp.float32)
        for s in range(slices):
            rows = jnp.broadcast_to(base[s : s + 1], (window, wide))
            band = pltpu.roll(rows, 0, 1, stride=1, stride_axis=0)
            col_out[s, :window, k * LANES : (k + 1) * LANES] = band[:, :LANES].astype(jnp.bfloat16)
    for s in range(slices):
        col_out[s, window:, :] = jnp.zeros((wide - window, terms * LANES), jnp.bfloat16)
    high = LANES // terms
    tap = lax.broadcasted_iota(jnp.int32, (TAPS, LANES), 0)
    lane = lax.broadcasted_iota(jnp.int32, (TAPS, LANES), 1)
    base = jnp.zeros((slices, LANES), jnp.float32)
    for k in range(terms):
        place = (lane == tap + k * high).astype(jnp.bfloat16)
        base = base + jnp.dot(row_taps[k], place, preferred_element_type=jnp.float32)
    sub = lax.broadcasted_iota(jnp.int32, (GROUP, LANES), 0)
    for g in range(slices // GROUP):
        own = base[g * GROUP : (g + 1) * GROUP]
        for pair in range(row_out.shape[1] // (2 * GROUP)):
            shifted = [pltpu.roll(own, 2 * pair + h, 1) for h in range(2)]
            for s in range(GROUP):
                both = jnp.concatenate([jnp.where(sub == s, x, 0.0) for x in shifted], axis=0)
                row_out[
                    g, pair * 2 * GROUP : (pair + 1) * 2 * GROUP, s * LANES : (s + 1) * LANES
                ] = both.astype(jnp.bfloat16)


def listed(taps):
    return [taps[k] for k in range(taps.shape[0])]


def matrix_shapes(terms, slices, rows):
    return (slices, 2 * LANES, terms * LANES), (slices // GROUP, rows * GROUP, GROUP * LANES)


def matrices_kernel(row_taps, col_taps, after, col_out, row_out):
    build_matrices(listed(row_taps), listed(col_taps), col_out, row_out)


def filter_matrices(row_taps, col_taps, after):
    terms, slices, _ = row_taps.shape
    shapes = matrix_shapes(terms, slices, LANES // terms - HALO)
    vmem = pl.BlockSpec(memory_space=pltpu.VMEM)
    return pl.pallas_call(
        matrices_kernel,
        name="matrices",
        in_specs=[vmem, vmem, pl.BlockSpec(memory_space=pl.ANY)],
        out_shape=[jax.ShapeDtypeStruct(shape, jnp.bfloat16) for shape in shapes],
        compiler_params=params(),
        cost_estimate=cost(1, 1),
    )(row_taps, col_taps, after)


def convolve(field, col, row, tall, rows):
    slices, _, wide = col.shape
    terms = wide // LANES
    high, cols = LANES // terms, tall.shape[1]
    parts = []
    for g in range(slices // GROUP):
        for j in range(GROUP):
            s = g * GROUP + j
            x = jnp.concatenate([field(s), jnp.zeros((high, LANES), jnp.float32)], axis=1)
            x = pltpu.roll(x, REACH, 1).astype(jnp.bfloat16)
            x = jnp.concatenate([x[:, c : c + 2 * LANES] for c in range(0, cols, LANES)], axis=0)
            y = jnp.dot(x, col[s], preferred_element_type=jnp.float32).astype(jnp.bfloat16)
            for c in range(cols // LANES):
                for k in range(terms):
                    tall[(j * terms + k) * high : (j * terms + k + 1) * high, c * LANES : (c + 1) * LANES] = y[
                        c * high : (c + 1) * high, k * LANES : (k + 1) * LANES
                    ]
        z = jnp.dot(row[g, : rows * GROUP], tall[...], preferred_element_type=jnp.float32)
        parts.append(z.reshape(rows, GROUP, cols))
    return jnp.concatenate(parts, axis=1)


def inner_rows(first, second, last):
    both = jnp.concatenate([first.astype(jnp.float32), second.astype(jnp.float32)], axis=0)
    rows = both.shape[0] - REACH
    chosen = jnp.where(last, both[REACH:], both[:rows])
    return jnp.concatenate([chosen, jnp.zeros((REACH, both.shape[1]), jnp.float32)], axis=0)


def early_kernel(ids, one, two, mask_one, mask_two, row_taps, col_taps, after, out, centre, col, row, tall):
    slices = one.shape[0]
    build_matrices(listed(row_taps), listed(col_taps), col, row)
    last = ids[0] == ids[1]
    mask = inner_rows(mask_one[...], mask_two[...], last)

    def folded(x):
        x = x.reshape(x.shape[0] // 8, 8, x.shape[1]).sum(axis=0)
        x = sum(x[:, c : c + LANES] for c in range(0, x.shape[1], LANES))
        return jnp.sum(x, axis=0, keepdims=True)

    sums = jnp.concatenate([folded(mask * inner_rows(one[s], two[s], last)) for s in range(slices)], axis=0)
    mean = jnp.sum(sums, axis=1, keepdims=True) / jnp.sum(folded(mask), axis=1, keepdims=True)
    centre[...] = jnp.broadcast_to(mean, centre.shape)
    field = convolve(
        lambda s: mask * (inner_rows(one[s], two[s], last) - mean[s : s + 1]), col, row, tall, out.shape[0]
    )
    out[...] = field.astype(jnp.bfloat16)


def mend_kernel(ids, mask_one, mask_two, note, piece, after, out, col, row, tall):
    terms = note.shape[0] // 2
    taps = [note[k, :, :TAPS].astype(jnp.bfloat16) for k in range(2 * terms)]
    build_matrices(taps[:terms], taps[terms:], col, row)
    last = ids[0] == ids[1]
    mask = inner_rows(mask_one[...], mask_two[...], last)
    field = convolve(lambda s: mask, col, row, tall, out.shape[0])
    shift = jnp.broadcast_to(note[2 * terms][:, :1], field.shape[1:])
    out[...] = (piece[...].astype(jnp.float32) + shift[None] * field).astype(jnp.bfloat16)


def early_call(kernel, name, ids, density, valid, terms, extra, after, out_shape):
    slices = out_shape[0].shape[1]
    cols = valid.shape[1]
    block = LANES // terms - HALO
    last = valid.shape[0] // block - 1

    def at(shift):
        return lambda i, ids: jnp.minimum(ids[0], last - 1) + shift

    def whole(x):
        return pl.BlockSpec(x.shape, lambda i, ids: (0,) * x.ndim)

    cubes = [] if density is None else [density] * 2
    shapes = matrix_shapes(terms, slices, REACH)
    return pl.pallas_call(
        kernel,
        name=name,
        grid_spec=pltpu.PrefetchScalarGridSpec(
            num_scalar_prefetch=1,
            grid=(1,),
            in_specs=[
                pl.BlockSpec((slices, block, cols), lambda i, ids, f=at(d): (0, f(i, ids), 0)) for d in range(len(cubes))
            ]
            + [pl.BlockSpec((block, cols), lambda i, ids, f=at(d): (f(i, ids), 0)) for d in (0, 1)]
            + [whole(x) for x in extra]
            + [pl.BlockSpec(memory_space=pl.ANY)],
            out_specs=[whole(x) for x in out_shape],
            scratch_shapes=[pltpu.VMEM(shape, jnp.bfloat16) for shape in shapes]
            + [pltpu.VMEM((GROUP * LANES, cols), jnp.bfloat16)],
        ),
        out_shape=out_shape,
        compiler_params=params(60),
        cost_estimate=cost(1, 1),
    )(jnp.stack([ids, jnp.full_like(ids, last)]).astype(jnp.int32), *cubes, valid, valid, *extra, after)


def sums_kernel(density, valid, after, out, first, last):
    slices, rows, cols = density.shape
    step = pl.program_id(0)

    @pl.when(step == 0)
    def _():
        out[...] = jnp.zeros_like(out)
        first[:slices] = density[:, :REACH]
        first[slices] = valid[:REACH].astype(jnp.bfloat16)

    @pl.when(step == pl.num_programs(0) - 1)
    def _():
        last[:slices] = density[:, rows - REACH :]
        last[slices] = valid[rows - REACH :].astype(jnp.bfloat16)

    mask = valid[...] != 0
    for s in range(slices + 1):
        if s < slices:
            x = jnp.where(mask, density[s].astype(jnp.float32), 0.0)
        else:
            x = jnp.where(mask, 1.0, 0.0)
        x = x.reshape(rows // 8, 8, cols).sum(axis=0)
        x = sum(x[:, c : c + LANES] for c in range(0, cols, LANES))
        out[s : s + 1, :] += jnp.sum(x, axis=0, keepdims=True)


def masked_sums(density, valid, after):
    slices, rows, cols = density.shape
    step = 32
    edge = jax.ShapeDtypeStruct((slices + 1, REACH, cols), jnp.bfloat16)
    return pl.pallas_call(
        sums_kernel,
        name="sums",
        grid=(rows // step,),
        in_specs=[
            pl.BlockSpec((slices, step, cols), lambda i: (0, i, 0)),
            pl.BlockSpec((step, cols), lambda i: (i, 0)),
            pl.BlockSpec(memory_space=pl.ANY),
        ],
        out_specs=[pl.BlockSpec((slices + 8, LANES), lambda i: (0, 0))]
        + [pl.BlockSpec(edge.shape, lambda i: (0, 0, 0))] * 2,
        out_shape=[jax.ShapeDtypeStruct((slices + 8, LANES), jnp.float32), edge, edge],
        compiler_params=params(60),
        cost_estimate=cost(1, 1),
    )(density, valid, after)


def mean_kernel(*refs):
    sums, out = refs[:4], refs[-1]
    slices = out.shape[0]
    total = sums[0][...] + sums[1][...] + sums[2][...] + sums[3][...]
    total = jnp.sum(total, axis=1, keepdims=True)
    out[...] = jnp.broadcast_to(total[:slices] / total[slices : slices + 1], out.shape)


def means(sums, slices, after):
    vmem = pl.BlockSpec(memory_space=pltpu.VMEM)
    return pl.pallas_call(
        mean_kernel,
        name="means",
        in_specs=[vmem] * len(sums) + [pl.BlockSpec(memory_space=pl.ANY)],
        out_specs=vmem,
        out_shape=jax.ShapeDtypeStruct((slices, LANES), jnp.float32),
        compiler_params=params(),
        cost_estimate=cost(1, 1),
    )(*sums, after)


def notes_kernel(mean, row_taps, col_taps, *refs):
    terms, slices, taps = row_taps.shape
    count = len(refs) // 2
    for centre, note in zip(refs[:count], refs[count:]):
        note[...] = jnp.zeros_like(note)
        note[:terms, :, :taps] = row_taps[...].astype(jnp.float32)
        note[terms : 2 * terms, :, :taps] = col_taps[...].astype(jnp.float32)
        note[2 * terms] = centre[...] - mean[...]


def notes_of(mean, row_taps, col_taps, centres):
    terms, slices, _ = row_taps.shape
    note = jax.ShapeDtypeStruct((2 * terms + 1, slices, LANES), jnp.float32)
    return pl.pallas_call(
        notes_kernel,
        name="notes",
        out_shape=[note] * len(centres),
        compiler_params=params(),
        cost_estimate=cost(1, 1),
    )(mean, row_taps, col_taps, *centres)


def filter_kernel(pieces, ids, before, now, after, mask_before, mask_now, mask_after, *refs):
    (above, below, col, row, mean), (tall, done) = refs[:5], refs[-2:]
    count = sum(len(wanted) for wanted in pieces)
    outs = refs[-2 - count : -2]
    slices, block, cols = now.shape
    step = pl.program_id(0)
    first = ids[step] == 0
    last = ids[step] == ids[pl.num_programs(0)]
    f32 = jnp.float32
    top = jnp.where(first, above[slices].astype(f32), mask_before[REACH:, :].astype(f32))
    bottom = jnp.where(last, below[slices].astype(f32), mask_after[:REACH, :].astype(f32))
    mask = jnp.concatenate([top, mask_now[...].astype(f32), bottom], axis=0)

    def field(s):
        top = jnp.where(first, above[s].astype(f32), before[s].astype(f32)[REACH:])
        bottom = jnp.where(last, below[s].astype(f32), after[s].astype(f32)[:REACH])
        x = jnp.concatenate([top, now[s].astype(f32), bottom], axis=0)
        return mask * (x - mean[s : s + 1, :1])

    done[...] = convolve(field, col, row, tall, block).astype(jnp.bfloat16)
    at = 0
    for b, wanted in enumerate(pieces):

        @pl.when(step == b)
        def _():
            for p, (inner, start, stop) in enumerate(wanted):
                here = jnp.where(last != (inner == 1), block - REACH, 0) + start
                outs[at + p][...] = done[pl.ds(here, stop - start)]

        at += len(wanted)


def filter_blocks(ids, pieces, density, valid, above, below, col, row, mean, *after):
    slices, rows, cols = density.shape
    block = row.shape[1] // GROUP
    last = rows // block - 1
    count = ids.shape[0]

    def rows_at(shift):
        return lambda i, at: (0, jnp.clip(at[i] + shift, 0, last), 0)

    def mask_at(shift):
        return lambda i, at: (jnp.clip(at[i] + shift, 0, last), 0)

    def whole(x):
        return pl.BlockSpec(x.shape, lambda i, at: (0,) * x.ndim, pipeline_mode=pl.Buffered(1))

    shapes = [(stop - start, slices, cols) for wanted in pieces for _, start, stop in wanted]
    out = pl.pallas_call(
        functools.partial(filter_kernel, pieces),
        name="filter",
        grid_spec=pltpu.PrefetchScalarGridSpec(
            num_scalar_prefetch=1,
            grid=(count,),
            in_specs=[pl.BlockSpec((slices, block, cols), rows_at(d)) for d in (-1, 0, 1)]
            + [pl.BlockSpec((block, cols), mask_at(d)) for d in (-1, 0, 1)]
            + [whole(x) for x in (above, below, col, row, mean)]
            + [pl.BlockSpec(memory_space=pl.ANY)] * len(after),
            out_specs=[pl.BlockSpec(shape, lambda i, at: (0, 0, 0)) for shape in shapes],
            scratch_shapes=[
                pltpu.VMEM((GROUP * LANES, cols), jnp.bfloat16),
                pltpu.VMEM((block, slices, cols), jnp.bfloat16),
            ],
        ),
        out_shape=[jax.ShapeDtypeStruct(shape, jnp.bfloat16) for shape in shapes],
        compiler_params=params(),
        cost_estimate=cost(1, 1),
    )(
        jnp.concatenate([ids, jnp.full((1,), last, ids.dtype)]),
        *([density] * 3),
        *([valid] * 3),
        above,
        below,
        col,
        row,
        mean,
        *after,
    )
    out = list(out)
    return [[out.pop(0) for _ in wanted] for wanted in pieces]


def project_kernel(count, place, weights, *refs):
    parts, (amp_out, like_out, token) = refs[:count], refs[-3:]
    zbins = weights.shape[0] // 2
    pencil = jnp.concatenate([x[0] for x in parts], axis=0)
    both = jnp.dot(weights[...], pencil, preferred_element_type=jnp.float32)
    amp = both[:zbins]
    amp_out[...] = amp.astype(jnp.bfloat16)
    like_out[...] = (amp * both[zbins:]).astype(jnp.bfloat16)
    token[...] = jnp.zeros_like(token)


def project(place, weights, parts, rows, total, earlier):
    _, slices, cols = parts[0][0].shape
    zbins = weights.shape[0] // 2
    count = len(parts)
    shape = jax.ShapeDtypeStruct((zbins, total * cols), jnp.bfloat16)
    return pl.pallas_call(
        functools.partial(project_kernel, count),
        name="project",
        grid_spec=pltpu.PrefetchScalarGridSpec(
            num_scalar_prefetch=1,
            grid=(rows,),
            in_specs=[pl.BlockSpec(weights.shape, lambda i, at: (0, 0))]
            + [pl.BlockSpec((1, slices, cols), lambda i, at, start=start: (i + start, 0, 0)) for _, start in parts]
            + [pl.BlockSpec(memory_space=pl.ANY)] * len(earlier),
            out_specs=[pl.BlockSpec((zbins, cols), lambda i, at: (0, i + at[0]))] * 2
            + [pl.BlockSpec((8, LANES), lambda i, at: (0, 0))],
        ),
        out_shape=[shape, shape, jax.ShapeDtypeStruct((8, LANES), jnp.float32)],
        input_output_aliases={2 + count + i: i for i in range(len(earlier))},
        compiler_params=params(),
        cost_estimate=cost(1, 1),
    )(place.reshape(1), weights, *[x for x, _ in parts], *earlier)


def gate_kernel(*refs):
    pass


def gate(x, *earlier):
    held = pl.BlockSpec(memory_space=pl.ANY)
    return pl.pallas_call(
        gate_kernel,
        name="gate",
        in_specs=[held] * (1 + len(earlier)),
        out_specs=held,
        out_shape=jax.ShapeDtypeStruct(x.shape, x.dtype),
        input_output_aliases={0: 0},
        cost_estimate=cost(1, 1),
    )(x, *earlier)


INNER, OUTER, HEAD, TAIL = (1, 0, REACH), (0, 0, REACH), (0, 0, 5), (0, 5, REACH)
EARLY = (4, 6, 5)
LATE = (4, 6)
ORDER = (
    ("filter", (7, 5, 2), ((6, 0),)),
    ("send", (7, 0), ((4, 0),)),
    ("send", (2, 0), ((4, 0),)),
    ("send", (5, 1), ((4, 0),)),
    ("filter", (3, 4, 6, 1, 0), ((5, 0),)),
    ("send", (7, 1), ((5, 0),)),
    ("send", (2, 1), ((2, 0),)),
    ("send", (3, 0), ((5, 1), (0, 0))),
    ("send", (4, "note"), ((5, 1), (0, 0))),
    ("send", (6, "note"), ((5, 1), (0, 0))),
    ("send", (5, "note"), ((5, 1), (0, 0))),
    ("send", (4, 1), ((5, 1), (0, 0))),
    ("send", (1, 0), ((5, 1), (2, 1))),
    ("send", (3, 1), ((3, 0),)),
    ("send", (6, 1), ((7, 0), (0, 0))),
    ("send", (1, 1), ((3, 0),)),
    ("project", 0, ()),
    ("send", (4, 2), ((4, 1), "project 0")),
    ("send", (6, 2), ((6, 1),)),
    ("project", 1, ()),
    ("project", 2, ()),
)


def fast(density, valid, row_taps, col_taps, amp_matrix, like_matrix):
    slices, rows, cols = density.shape
    terms = row_taps.shape[0]
    peers = lax.axis_size("cuts")
    tiles = lax.axis_size("tile")
    block = rows // peers
    me = lax.axis_index("cuts").astype(jnp.int32)

    def swap(x, k):
        return lax.ppermute(x, "cuts", [(i, i ^ k) for i in range(peers)])

    piece = jax.ShapeDtypeStruct((REACH, slices, cols), jnp.bfloat16)
    centre = jax.ShapeDtypeStruct((slices, LANES), jnp.float32)

    def early(k, after):
        return early_call(
            early_kernel, "early", me ^ k, density, valid, terms, (row_taps, col_taps), after, [piece, centre]
        )

    made, arrived = {}, {}
    made[4, 0], about_4 = early(4, row_taps)
    arrived[4, 0] = swap(made[4, 0], 4)
    made[6, 0], about_6 = early(6, made[4, 0])
    own, first, last = masked_sums(density, valid, made[6, 0])
    sums = [own] + [lax.ppermute(own, "tile", [(i, i ^ k) for i in range(tiles)]) for k in range(1, tiles)]
    arrived[6, 0] = swap(made[6, 0], 6)
    mean = means(sums, slices, arrived[4, 0])
    above = lax.ppermute(gate(last, mean), "tile", [(i, i + 1) for i in range(tiles - 1)])
    below = lax.ppermute(gate(first, mean), "tile", [(i + 1, i) for i in range(tiles - 1)])
    made[5, 0], about_5 = early(5, mean)
    arrived[5, 0] = swap(made[5, 0], 5)
    col, row = filter_matrices(row_taps, col_taps, made[5, 0])
    for k, note in zip(EARLY, notes_of(mean, row_taps, col_taps, (about_4, about_6, about_5))):
        made[k, "note"] = note

    cuts = {k: (INNER, HEAD, TAIL) if k in LATE else (INNER, OUTER) for k in range(peers)}
    weights = jnp.concatenate([amp_matrix, like_matrix], axis=1).T.reshape(-1, peers, slices)
    weights = weights[:, me ^ jnp.arange(peers)].reshape(-1, peers * slices)
    result = []
    after = made[5, 0]
    for what, how, before in ORDER:
        before = [arrived[x] for x in before]
        if what == "filter":
            ids = jnp.stack([me ^ k for k in how])
            skip = [1 if k in EARLY else 0 for k in how]
            wanted = [cuts[k][n:] for k, n in zip(how, skip)]
            got = filter_blocks(ids, wanted, density, valid, above, below, col, row, mean, after, *before)
            for k, n, parts in zip(how, skip, got):
                for p, x in enumerate(parts, start=n):
                    made[k, p] = x
                    if k == 0:
                        arrived[k, p] = x
            after = got[-1][-1]
        elif what == "send":
            k, p = how
            arrived[how] = swap(gate(made[how], *before), k)
            if p == "note":
                (arrived[k, 0],) = early_call(
                    mend_kernel, "mend", me, None, valid, terms, (arrived[how], arrived[k, 0]), after, [piece]
                )
        else:
            inner, start, stop = (INNER, HEAD, TAIL)[how]
            place = jnp.where((me == peers - 1) != (inner == 1), block - REACH, 0) + start
            parts = [(arrived[k, how], 0) if k in LATE else (arrived[k, min(how, 1)], start) for k in range(peers)]
            *result[:], arrived[f"project {how}"] = project(place, weights, parts, stop - start, block, result)
    return tuple(result)


def extended(shard, sides, width):
    for axis, dim in sides:
        size, length = (lax.axis_size(axis), shard.shape[dim])
        up = [(i, (i + 1) % size) for i in range(size - 1)]
        down = [(j, i) for i, j in up]
        last = lax.slice_in_dim(shard, length - width, length, axis=dim)
        initial = lax.slice_in_dim(shard, 0, width, axis=dim)
        before = lax.ppermute(last, axis, up)
        after = lax.ppermute(initial, axis, down)
        shard = jnp.concatenate([before, shard, after], axis=dim)
    return shard


def band_matrix(taps, out_count, in_count):
    offset = lax.broadcasted_iota(jnp.int32, (out_count, in_count), 1) - lax.broadcasted_iota(
        jnp.int32, (out_count, in_count), 0
    )
    positions = lax.broadcasted_iota(jnp.int32, (1, 1, TAPS), 2)
    choose = (offset[:, :, None] == positions).astype(jnp.bfloat16)
    return jnp.einsum("ijt,kst->ksij", choose, taps, preferred_element_type=jnp.float32).astype(jnp.bfloat16)


def filter_field(padded, row_taps, col_taps):
    tall = padded.shape[1]
    cols = padded.shape[2]
    width = 2 * LANES
    row_band = band_matrix(row_taps, tall - HALO, tall)
    rowed = jnp.einsum("ksij,sjc->ksic", row_band, padded, preferred_element_type=jnp.float32).astype(jnp.bfloat16)
    widened = jnp.pad(rowed, ((0, 0), (0, 0), (0, 0), (REACH, REACH)))
    col_band = band_matrix(col_taps, width, width + HALO)
    pieces = []
    for begin in range(0, cols, width):
        segment = widened[:, :, :, begin : begin + width + HALO]
        pieces.append(jnp.einsum("ksrj,ksij->sri", segment, col_band, preferred_element_type=jnp.float32))
    return jnp.concatenate(pieces, axis=2).astype(jnp.bfloat16)


def general(density, valid, row_taps, col_taps, amp_matrix, like_matrix):
    slices, rows, cols = density.shape
    mask = valid.astype(jnp.float32)
    field = density.astype(jnp.float32)
    sums, count = lax.psum((jnp.sum(field * mask[None], axis=(1, 2)), jnp.sum(mask)), "tile")
    masked = (mask[None] * (field - (sums / count)[:, None, None])).astype(jnp.bfloat16)
    filtered = filter_field(extended(masked, (("tile", 1),), REACH), row_taps, col_taps)
    peers = lax.axis_size("cuts")
    share = rows * cols // peers
    pencil = lax.all_to_all(
        filtered.reshape(slices, peers, share), "cuts", split_axis=1, concat_axis=0, tiled=True
    ).reshape(slices * peers, share)
    amp = jnp.dot(amp_matrix.T, pencil, preferred_element_type=jnp.float32)
    like = amp * jnp.dot(like_matrix.T, pencil, preferred_element_type=jnp.float32)
    return amp.astype(jnp.bfloat16), like.astype(jnp.bfloat16)


def per_device(density, valid, row_taps, col_taps, amp_matrix, like_matrix):
    slices, rows, cols = density.shape
    terms = row_taps.shape[0]
    peers = lax.axis_size("cuts")
    fits = (
        peers == 8
        and lax.axis_size("tile") == 4
        and slices == 2 * GROUP
        and terms == 4
        and rows == peers * (LANES // terms - HALO)
        and cols % (2 * LANES) == 0
    )
    run = fast if fits else general
    return run(density, valid, row_taps, col_taps, amp_matrix, like_matrix)


def solution(mesh):
    return jax.shard_map(
        per_device,
        mesh=mesh,
        in_specs=(
            P("cuts", "tile", None),
            P("tile", None),
            P(None, "cuts", None),
            P(None, "cuts", None),
            P(),
            P(),
        ),
        out_specs=(P(None, ("tile", "cuts")), P(None, ("tile", "cuts"))),
        check_vma=False,
    )
```

```python
import functools

import jax
import jax.numpy as jnp
from jax import lax
from jax.experimental import pallas as pl
from jax.experimental.pallas import tpu as pltpu
from jax.sharding import PartitionSpec as P

REACH = 8
TAPS = 2 * REACH + 1
LANES = 128
GROUP = 8
MIB = 1024 * 1024
HALO = 2 * REACH


def params(mib=28):
    return pltpu.CompilerParams(vmem_limit_bytes=mib * MIB)


def hbm(shape, dtype):
    return pltpu.HBM(shape, dtype)


def held(x):
    return pltpu.with_memory_space_constraint(x, pltpu.HBM)


def anywhere():
    return pl.BlockSpec(memory_space=pl.ANY)


def cost(flops, moved):
    return pl.CostEstimate(flops=int(flops), bytes_accessed=int(moved), transcendentals=0)


def build_matrices(row_taps, col_taps, col_out, row_out):
    terms, slices = len(row_taps), row_taps[0].shape[0]
    wide = 2 * LANES
    window = LANES + HALO
    tap = lax.broadcasted_iota(jnp.int32, (TAPS, wide), 0)
    lane = lax.broadcasted_iota(jnp.int32, (TAPS, wide), 1)
    flip = (lax.rem(tap + lane, wide) == 0).astype(jnp.bfloat16)
    for k in range(terms):
        base = jnp.dot(col_taps[k], flip, preferred_element_type=jnp.float32)
        for s in range(slices):
            rows = jnp.broadcast_to(base[s : s + 1], (window, wide))
            band = pltpu.roll(rows, 0, 1, stride=1, stride_axis=0)
            col_out[s, :window, k * LANES : (k + 1) * LANES] = band[:, :LANES].astype(jnp.bfloat16)
    for s in range(slices):
        col_out[s, window:, :] = jnp.zeros((wide - window, terms * LANES), jnp.bfloat16)
    high = LANES // terms
    tap = lax.broadcasted_iota(jnp.int32, (TAPS, LANES), 0)
    lane = lax.broadcasted_iota(jnp.int32, (TAPS, LANES), 1)
    base = jnp.zeros((slices, LANES), jnp.float32)
    for k in range(terms):
        place = (lane == tap + k * high).astype(jnp.bfloat16)
        base = base + jnp.dot(row_taps[k], place, preferred_element_type=jnp.float32)
    sub = lax.broadcasted_iota(jnp.int32, (GROUP, LANES), 0)
    for g in range(slices // GROUP):
        own = base[g * GROUP : (g + 1) * GROUP]
        for pair in range(row_out.shape[1] // (2 * GROUP)):
            shifted = [pltpu.roll(own, 2 * pair + h, 1) for h in range(2)]
            for s in range(GROUP):
                both = jnp.concatenate([jnp.where(sub == s, x, 0.0) for x in shifted], axis=0)
                row_out[
                    g, pair * 2 * GROUP : (pair + 1) * 2 * GROUP, s * LANES : (s + 1) * LANES
                ] = both.astype(jnp.bfloat16)


def listed(taps):
    return [taps[k] for k in range(taps.shape[0])]


def matrix_shapes(terms, slices, rows):
    return (slices, 2 * LANES, terms * LANES), (slices // GROUP, rows * GROUP, GROUP * LANES)


def convolve(field, col, row, tall, rows):
    slices, _, wide = col.shape
    terms = wide // LANES
    high, cols = LANES // terms, tall.shape[1]
    parts = []
    for g in range(slices // GROUP):
        for j in range(GROUP):
            s = g * GROUP + j
            x = jnp.concatenate([field(s), jnp.zeros((high, LANES), jnp.float32)], axis=1)
            x = pltpu.roll(x, REACH, 1).astype(jnp.bfloat16)
            x = jnp.concatenate([x[:, c : c + 2 * LANES] for c in range(0, cols, LANES)], axis=0)
            y = jnp.dot(x, col[s], preferred_element_type=jnp.float32).astype(jnp.bfloat16)
            for c in range(cols // LANES):
                for k in range(terms):
                    tall[(j * terms + k) * high : (j * terms + k + 1) * high, c * LANES : (c + 1) * LANES] = y[
                        c * high : (c + 1) * high, k * LANES : (k + 1) * LANES
                    ]
        z = jnp.dot(row[g, : rows * GROUP], tall[...], preferred_element_type=jnp.float32)
        parts.append(z.reshape(rows, GROUP, cols))
    return jnp.concatenate(parts, axis=1)


def sums_kernel(density, valid, out, first, last):
    slices, rows, cols = density.shape
    step = pl.program_id(0)

    @pl.when(step == 0)
    def _():
        out[...] = jnp.zeros_like(out)
        first[:slices] = density[:, :REACH]
        first[slices] = valid[:REACH].astype(jnp.bfloat16)

    @pl.when(step == pl.num_programs(0) - 1)
    def _():
        last[:slices] = density[:, rows - REACH :]
        last[slices] = valid[rows - REACH :].astype(jnp.bfloat16)

    mask = valid[...] != 0
    for s in range(slices + 1):
        if s < slices:
            x = jnp.where(mask, density[s].astype(jnp.float32), 0.0)
        else:
            x = jnp.where(mask, 1.0, 0.0)
        x = x.reshape(rows // 8, 8, cols).sum(axis=0)
        x = sum(x[:, c : c + LANES] for c in range(0, cols, LANES))
        out[s : s + 1, :] += jnp.sum(x, axis=0, keepdims=True)


def masked_sums(density, valid):
    slices, rows, cols = density.shape
    step = 32
    edge = hbm((slices + 1, REACH, cols), jnp.bfloat16)
    return pl.pallas_call(
        sums_kernel,
        name="sums",
        grid=(rows // step,),
        in_specs=[
            pl.BlockSpec((slices, step, cols), lambda i: (0, i, 0)),
            pl.BlockSpec((step, cols), lambda i: (i, 0)),
        ],
        out_specs=[pl.BlockSpec((slices + 8, LANES), lambda i: (0, 0))]
        + [pl.BlockSpec((slices + 1, REACH, cols), lambda i: (0, 0, 0))] * 2,
        out_shape=[hbm((slices + 8, LANES), jnp.float32), edge, edge],
        compiler_params=params(),
        cost_estimate=cost(1, 1),
    )(held(density), held(valid))


def mean_kernel(*refs):
    sums, out = refs[:4], refs[-1]
    slices = out.shape[0]
    total = sums[0][...] + sums[1][...] + sums[2][...] + sums[3][...]
    total = jnp.sum(total, axis=1, keepdims=True)
    out[...] = jnp.broadcast_to(total[:slices] / total[slices : slices + 1], out.shape)


def means(sums, slices):
    return pl.pallas_call(
        mean_kernel,
        name="means",
        out_shape=jax.ShapeDtypeStruct((slices, LANES), jnp.float32),
        compiler_params=params(),
        cost_estimate=cost(1, 1),
    )(*sums)


def filter_kernel(pieces, ids, before, now, after, mask_before, mask_now, mask_after, *refs):
    (above, below, row_taps, col_taps, mean), (tall, done, col, row) = refs[:5], refs[-4:]
    count = sum(len(wanted) for wanted in pieces)
    outs = refs[-4 - count : -4]
    slices, block, cols = now.shape
    step = pl.program_id(0)

    @pl.when(step == 0)
    def _():
        build_matrices(listed(row_taps), listed(col_taps), col, row)

    first = ids[step] == 0
    last = ids[step] == ids[pl.num_programs(0)]
    f32 = jnp.float32
    top = jnp.where(first, above[slices].astype(f32), mask_before[REACH:, :].astype(f32))
    bottom = jnp.where(last, below[slices].astype(f32), mask_after[:REACH, :].astype(f32))
    mask = jnp.concatenate([top, mask_now[...].astype(f32), bottom], axis=0)

    def field(s):
        top = jnp.where(first, above[s].astype(f32), before[s].astype(f32)[REACH:])
        bottom = jnp.where(last, below[s].astype(f32), after[s].astype(f32)[:REACH])
        x = jnp.concatenate([top, now[s].astype(f32), bottom], axis=0)
        return mask * (x - mean[s : s + 1, :1])

    done[...] = convolve(field, col, row, tall, block).astype(jnp.bfloat16)
    at = 0
    for b, wanted in enumerate(pieces):

        @pl.when(step == b)
        def _():
            for p, (inner, start, stop) in enumerate(wanted):
                here = jnp.where(last != (inner == 1), block - REACH, 0) + start
                outs[at + p][...] = done[pl.ds(here, stop - start)]

        at += len(wanted)


def filter_blocks(ids, pieces, density, valid, above, below, row_taps, col_taps, mean, *after):
    slices, rows, cols = density.shape
    terms = row_taps.shape[0]
    block = LANES // terms - HALO
    last = rows // block - 1
    count = ids.shape[0]

    def rows_at(shift):
        return lambda i, at: (0, jnp.clip(at[i] + shift, 0, last), 0)

    def mask_at(shift):
        return lambda i, at: (jnp.clip(at[i] + shift, 0, last), 0)

    def whole(x):
        return pl.BlockSpec(x.shape, lambda i, at: (0,) * x.ndim, pipeline_mode=pl.Buffered(1))

    shapes = [(stop - start, slices, cols) for wanted in pieces for _, start, stop in wanted]
    out = pl.pallas_call(
        functools.partial(filter_kernel, pieces),
        name="filter",
        grid_spec=pltpu.PrefetchScalarGridSpec(
            num_scalar_prefetch=1,
            grid=(count,),
            in_specs=[pl.BlockSpec((slices, block, cols), rows_at(d)) for d in (-1, 0, 1)]
            + [pl.BlockSpec((block, cols), mask_at(d)) for d in (-1, 0, 1)]
            + [whole(x) for x in (above, below, row_taps, col_taps, mean)]
            + [anywhere()] * len(after),
            out_specs=[pl.BlockSpec(shape, lambda i, at: (0, 0, 0)) for shape in shapes],
            scratch_shapes=[
                pltpu.VMEM((GROUP * LANES, cols), jnp.bfloat16),
                pltpu.VMEM((block, slices, cols), jnp.bfloat16),
            ]
            + [pltpu.VMEM(shape, jnp.bfloat16) for shape in matrix_shapes(terms, slices, block)],
        ),
        out_shape=[hbm(shape, jnp.bfloat16) for shape in shapes],
        compiler_params=params(),
        cost_estimate=cost(1, 1),
    )(
        jnp.concatenate([ids, jnp.full((1,), last, ids.dtype)]),
        *[held(x) for x in (density, density, density, valid, valid, valid)],
        above,
        below,
        row_taps,
        col_taps,
        mean,
        *after,
    )
    out = list(out)
    return [[out.pop(0) for _ in wanted] for wanted in pieces]


def project_kernel(count, place, weights, *refs):
    parts, (amp_out, like_out, token) = refs[:count], refs[-3:]
    zbins = weights.shape[0] // 2
    pencil = jnp.concatenate([x[0] for x in parts], axis=0)
    both = jnp.dot(weights[...], pencil, preferred_element_type=jnp.float32)
    amp = both[:zbins]
    amp_out[...] = amp.astype(jnp.bfloat16)
    like_out[...] = (amp * both[zbins:]).astype(jnp.bfloat16)
    token[...] = jnp.zeros_like(token)


def project(place, weights, parts, rows, total, earlier):
    _, slices, cols = parts[0][0].shape
    zbins = weights.shape[0] // 2
    count = len(parts)
    shape = hbm((zbins, total * cols), jnp.bfloat16)
    return pl.pallas_call(
        functools.partial(project_kernel, count),
        name="project",
        grid_spec=pltpu.PrefetchScalarGridSpec(
            num_scalar_prefetch=1,
            grid=(rows,),
            in_specs=[pl.BlockSpec(weights.shape, lambda i, at: (0, 0))]
            + [pl.BlockSpec((1, slices, cols), lambda i, at, start=start: (i + start, 0, 0)) for _, start in parts]
            + [anywhere()] * len(earlier),
            out_specs=[pl.BlockSpec((zbins, cols), lambda i, at: (0, i + at[0]))] * 2
            + [pl.BlockSpec((8, LANES), lambda i, at: (0, 0))],
        ),
        out_shape=[shape, shape, hbm((8, LANES), jnp.float32)],
        input_output_aliases={2 + count + i: i for i in range(len(earlier))},
        compiler_params=params(),
        cost_estimate=cost(1, 1),
    )(place.reshape(1), weights, *[x for x, _ in parts], *earlier)


def gate_kernel(*refs):
    pass


def gate(x, *earlier, flops=1):
    return pl.pallas_call(
        gate_kernel,
        name="gate",
        in_specs=[anywhere()] * (1 + len(earlier)),
        out_specs=anywhere(),
        out_shape=hbm(x.shape, x.dtype),
        input_output_aliases={0: 0},
        cost_estimate=cost(flops, 1),
    )(held(x), *earlier)


INNER, OUTER, HEAD, TAIL = (1, 0, REACH), (0, 0, REACH), (0, 0, 5), (0, 5, REACH)
LATE = (4, 6)
FILTERS = ((4, (INNER,)),), ((6, (INNER, HEAD, TAIL)), (5, (INNER, OUTER)), (7, (INNER, OUTER)))
ORDER = (
    ("send", (4, 0), ()),
    ("send", (6, 0), ((4, 0),)),
    ("send", (5, 0), ((4, 0),)),
    ("send", (7, 0), ((4, 0),)),
    ("filter", ((4, (HEAD, TAIL)), (2, (INNER, OUTER)), (3, (INNER, OUTER)), (1, (INNER, OUTER)), (0, (INNER, OUTER))), ((4, 0),)),
    ("send", (2, 0), ((6, 0), (0, 0))),
    ("send", (3, 0), ((6, 0), (0, 0))),
    ("send", (5, 1), ((6, 0),)),
    ("send", (2, 1), ((5, 0), (0, 0))),
    ("send", (7, 1), ((5, 0),)),
    ("send", (4, 1), ((7, 0), (0, 0))),
    ("send", (3, 1), ((7, 0), (0, 0))),
    ("send", (1, 0), ((7, 0), (0, 0))),
    ("send", (6, 1), ((5, 1),)),
    ("send", (1, 1), ((5, 1), (0, 0))),
    ("project", 0, ()),
    ("send", (4, 2), ((7, 1), "project 0")),
    ("send", (6, 2), ((4, 1),)),
    ("project", 1, ()),
    ("project", 2, ()),
)


def fast(density, valid, row_taps, col_taps, amp_matrix, like_matrix):
    slices, rows, cols = density.shape
    peers = lax.axis_size("cuts")
    tiles = lax.axis_size("tile")
    block = rows // peers
    me = lax.axis_index("cuts").astype(jnp.int32)

    def swap(x, k):
        return lax.ppermute(x, "cuts", [(i, i ^ k) for i in range(peers)])

    own, first, last = masked_sums(density, valid)
    sums = [own] + [lax.ppermute(own, "tile", [(i, i ^ k) for i in range(tiles)]) for k in range(1, tiles)]
    above = lax.ppermute(last, "tile", [(i, i + 1) for i in range(tiles - 1)])
    below = lax.ppermute(first, "tile", [(i + 1, i) for i in range(tiles - 1)])
    mean = means(sums, slices)

    made, arrived = {}, {}

    def filter_for(wanted, above, below, *after):
        ids = jnp.stack([me ^ k for k, _ in wanted])
        pieces = [cut for _, cut in wanted]
        got = filter_blocks(ids, pieces, density, valid, above, below, row_taps, col_taps, mean, *after)
        for (k, cut), parts in zip(wanted, got):
            for piece, x in zip(cut, parts):
                p = {INNER: 0, OUTER: 1, HEAD: 1, TAIL: 2}[piece]
                made[k, p] = x
                if k == 0:
                    arrived[k, p] = x

    filter_for(FILTERS[0], last, first)
    filter_for(FILTERS[1], above, below, made[4, 0])
    weights = jnp.concatenate([amp_matrix, like_matrix], axis=1).T.reshape(-1, peers, slices)
    weights = weights[:, me ^ jnp.arange(peers)].reshape(-1, peers * slices)
    result = []
    for what, how, before in ORDER:
        before = [arrived[x] for x in before]
        if what == "filter":
            filter_for(how, above, below, made[7, 0], *before)
        elif what == "send":
            arrived[how] = swap(gate(made[how], *before) if before else made[how], how[0])
        else:
            inner, start, stop = (INNER, HEAD, TAIL)[how]
            place = jnp.where((me == peers - 1) != (inner == 1), block - REACH, 0) + start
            parts = [(arrived[k, how], 0) if k in LATE else (arrived[k, min(how, 1)], start) for k in range(peers)]
            *result[:], arrived[f"project {how}"] = project(place, weights, parts, stop - start, block, result)
    return tuple(result)


def extended(shard, sides, width):
    for axis, dim in sides:
        size, length = (lax.axis_size(axis), shard.shape[dim])
        up = [(i, (i + 1) % size) for i in range(size - 1)]
        down = [(j, i) for i, j in up]
        last = lax.slice_in_dim(shard, length - width, length, axis=dim)
        initial = lax.slice_in_dim(shard, 0, width, axis=dim)
        before = lax.ppermute(last, axis, up)
        after = lax.ppermute(initial, axis, down)
        shard = jnp.concatenate([before, shard, after], axis=dim)
    return shard


def band_matrix(taps, out_count, in_count):
    offset = lax.broadcasted_iota(jnp.int32, (out_count, in_count), 1) - lax.broadcasted_iota(
        jnp.int32, (out_count, in_count), 0
    )
    positions = lax.broadcasted_iota(jnp.int32, (1, 1, TAPS), 2)
    choose = (offset[:, :, None] == positions).astype(jnp.bfloat16)
    return jnp.einsum("ijt,kst->ksij", choose, taps, preferred_element_type=jnp.float32).astype(jnp.bfloat16)


def filter_field(padded, row_taps, col_taps):
    tall = padded.shape[1]
    cols = padded.shape[2]
    width = 2 * LANES
    row_band = band_matrix(row_taps, tall - HALO, tall)
    rowed = jnp.einsum("ksij,sjc->ksic", row_band, padded, preferred_element_type=jnp.float32).astype(jnp.bfloat16)
    widened = jnp.pad(rowed, ((0, 0), (0, 0), (0, 0), (REACH, REACH)))
    col_band = band_matrix(col_taps, width, width + HALO)
    pieces = []
    for begin in range(0, cols, width):
        segment = widened[:, :, :, begin : begin + width + HALO]
        pieces.append(jnp.einsum("ksrj,ksij->sri", segment, col_band, preferred_element_type=jnp.float32))
    return jnp.concatenate(pieces, axis=2).astype(jnp.bfloat16)


def general(density, valid, row_taps, col_taps, amp_matrix, like_matrix):
    slices, rows, cols = density.shape
    mask = valid.astype(jnp.float32)
    field = density.astype(jnp.float32)
    sums, count = lax.psum((jnp.sum(field * mask[None], axis=(1, 2)), jnp.sum(mask)), "tile")
    masked = (mask[None] * (field - (sums / count)[:, None, None])).astype(jnp.bfloat16)
    filtered = filter_field(extended(masked, (("tile", 1),), REACH), row_taps, col_taps)
    peers = lax.axis_size("cuts")
    share = rows * cols // peers
    pencil = lax.all_to_all(
        filtered.reshape(slices, peers, share), "cuts", split_axis=1, concat_axis=0, tiled=True
    ).reshape(slices * peers, share)
    amp = jnp.dot(amp_matrix.T, pencil, preferred_element_type=jnp.float32)
    like = amp * jnp.dot(like_matrix.T, pencil, preferred_element_type=jnp.float32)
    return amp.astype(jnp.bfloat16), like.astype(jnp.bfloat16)


def per_device(density, valid, row_taps, col_taps, amp_matrix, like_matrix):
    slices, rows, cols = density.shape
    terms = row_taps.shape[0]
    peers = lax.axis_size("cuts")
    fits = (
        peers == 8
        and lax.axis_size("tile") == 4
        and slices == 2 * GROUP
        and terms == 4
        and rows == peers * (LANES // terms - HALO)
        and cols % (2 * LANES) == 0
    )
    run = fast if fits else general
    return run(density, valid, row_taps, col_taps, amp_matrix, like_matrix)


def solution(mesh):
    return jax.shard_map(
        per_device,
        mesh=mesh,
        in_specs=(
            P("cuts", "tile", None),
            P("tile", None),
            P(None, "cuts", None),
            P(None, "cuts", None),
            P(),
            P(),
        ),
        out_specs=(P(None, ("tile", "cuts")), P(None, ("tile", "cuts"))),
        check_vma=False,
    )
```

```python
import functools

import jax
import jax.numpy as jnp
from jax import lax
from jax.experimental import pallas as pl
from jax.experimental.pallas import tpu as pltpu
from jax.sharding import PartitionSpec as P

REACH = 8
TAPS = 2 * REACH + 1
LANES = 128
GROUP = 8
MIB = 1024 * 1024
HALO = 2 * REACH


def params(mib=24):
    return pltpu.CompilerParams(vmem_limit_bytes=mib * MIB)


def hbm(shape, dtype):
    return pltpu.HBM(shape, dtype)


def held(x):
    return pltpu.with_memory_space_constraint(x, pltpu.HBM)


def anywhere():
    return pl.BlockSpec(memory_space=pl.ANY)


def cost(flops, moved):
    return pl.CostEstimate(flops=int(flops), bytes_accessed=int(moved), transcendentals=0)


def tap_flip():
    tap = lax.broadcasted_iota(jnp.int32, (TAPS, 2 * LANES), 0)
    lane = lax.broadcasted_iota(jnp.int32, (TAPS, 2 * LANES), 1)
    return (lax.rem(tap + lane, 2 * LANES) == 0).astype(jnp.bfloat16)


def column_band(taps):
    band = pltpu.roll(jnp.broadcast_to(taps, (LANES + HALO, 2 * LANES)), 0, 1, stride=1, stride_axis=0)
    return band[:, :LANES].astype(jnp.bfloat16)


def build_columns(col_taps, col_out):
    terms, slices = len(col_taps), col_taps[0].shape[0]
    for k in range(terms):
        base = jnp.dot(col_taps[k], tap_flip(), preferred_element_type=jnp.float32)
        for s in range(slices):
            col_out[s, : LANES + HALO, k * LANES : (k + 1) * LANES] = column_band(base[s : s + 1])
    for s in range(slices):
        col_out[s, LANES + HALO :, :] = jnp.zeros((LANES - HALO, terms * LANES), jnp.bfloat16)


def build_rows(row_taps, row_out):
    terms, slices = len(row_taps), row_taps[0].shape[0]
    high = LANES // terms
    tap = lax.broadcasted_iota(jnp.int32, (TAPS, LANES), 0)
    lane = lax.broadcasted_iota(jnp.int32, (TAPS, LANES), 1)
    base = jnp.zeros((slices, LANES), jnp.float32)
    for k in range(terms):
        place = (lane == tap + k * high).astype(jnp.bfloat16)
        base = base + jnp.dot(row_taps[k], place, preferred_element_type=jnp.float32)
    sub = lax.broadcasted_iota(jnp.int32, (GROUP, LANES), 0)
    for g in range(slices // GROUP):
        own = base[g * GROUP : (g + 1) * GROUP]
        for pair in range(row_out.shape[1] // (2 * GROUP)):
            shifted = [pltpu.roll(own, 2 * pair + h, 1) for h in range(2)]
            for s in range(GROUP):
                both = jnp.concatenate([jnp.where(sub == s, x, 0.0) for x in shifted], axis=0)
                row_out[
                    g, pair * 2 * GROUP : (pair + 1) * 2 * GROUP, s * LANES : (s + 1) * LANES
                ] = both.astype(jnp.bfloat16)


def listed(taps):
    return [taps[k] for k in range(taps.shape[0])]


def matrix_shapes(terms, slices, rows):
    return (slices, 2 * LANES, terms * LANES), (slices // GROUP, rows * GROUP, GROUP * LANES)


def convolve(field, col, row, tall, rows):
    slices, _, wide = col.shape
    terms = wide // LANES
    high, cols = LANES // terms, tall.shape[1]
    parts = []
    for g in range(slices // GROUP):
        for j in range(GROUP):
            s = g * GROUP + j
            x = jnp.concatenate([field(s), jnp.zeros((high, LANES), jnp.float32)], axis=1)
            x = pltpu.roll(x, REACH, 1).astype(jnp.bfloat16)
            x = jnp.concatenate([x[:, c : c + 2 * LANES] for c in range(0, cols, LANES)], axis=0)
            y = jnp.dot(x, col[s], preferred_element_type=jnp.float32).astype(jnp.bfloat16)
            for c in range(cols // LANES):
                for k in range(terms):
                    tall[(j * terms + k) * high : (j * terms + k + 1) * high, c * LANES : (c + 1) * LANES] = y[
                        c * high : (c + 1) * high, k * LANES : (k + 1) * LANES
                    ]
        z = jnp.dot(row[g, : rows * GROUP], tall[...], preferred_element_type=jnp.float32)
        parts.append(z.reshape(rows, GROUP, cols))
    return jnp.concatenate(parts, axis=1)


def sums_kernel(density, valid, out, first, last):
    slices, rows, cols = density.shape
    step = pl.program_id(0)

    @pl.when(step == 0)
    def _():
        out[...] = jnp.zeros_like(out)
        first[:slices] = density[:, :REACH]
        first[slices] = valid[:REACH].astype(jnp.bfloat16)

    @pl.when(step == pl.num_programs(0) - 1)
    def _():
        last[:slices] = density[:, rows - REACH :]
        last[slices] = valid[rows - REACH :].astype(jnp.bfloat16)

    mask = valid[...] != 0
    for s in range(slices + 1):
        if s < slices:
            x = jnp.where(mask, density[s].astype(jnp.float32), 0.0)
        else:
            x = jnp.where(mask, 1.0, 0.0)
        x = x.reshape(rows // 8, 8, cols).sum(axis=0)
        x = sum(x[:, c : c + LANES] for c in range(0, cols, LANES))
        out[s : s + 1, :] += jnp.sum(x, axis=0, keepdims=True)


def masked_sums(density, valid):
    slices, rows, cols = density.shape
    step = 32
    edge = hbm((slices + 1, REACH, cols), jnp.bfloat16)
    return pl.pallas_call(
        sums_kernel,
        name="sums",
        grid=(rows // step,),
        in_specs=[
            pl.BlockSpec((slices, step, cols), lambda i: (0, i, 0)),
            pl.BlockSpec((step, cols), lambda i: (i, 0)),
        ],
        out_specs=[pl.BlockSpec((slices + 8, LANES), lambda i: (0, 0))]
        + [pl.BlockSpec((slices + 1, REACH, cols), lambda i: (0, 0, 0))] * 2,
        out_shape=[hbm((slices + 8, LANES), jnp.float32), edge, edge],
        compiler_params=params(),
        cost_estimate=cost(1, 1),
    )(held(density), held(valid))


def mean_kernel(*refs):
    sums, out = refs[:4], refs[-1]
    slices = out.shape[0]
    total = sums[0][...] + sums[1][...] + sums[2][...] + sums[3][...]
    total = jnp.sum(total, axis=1, keepdims=True)
    out[...] = jnp.broadcast_to(total[:slices] / total[slices : slices + 1], out.shape)


def means(sums, slices):
    return pl.pallas_call(
        mean_kernel,
        name="means",
        out_shape=jax.ShapeDtypeStruct((slices, LANES), jnp.float32),
        compiler_params=params(),
        cost_estimate=cost(1, 1),
    )(*sums)


def filter_kernel(pieces, ids, before, now, after, mask_before, mask_now, mask_after, *refs):
    (above, below, row_taps, col_taps, mean), (tall, done, col, row) = refs[:5], refs[-4:]
    count = sum(len(wanted) for wanted in pieces)
    outs = refs[-4 - count : -4]
    slices, block, cols = now.shape
    step = pl.program_id(0)

    @pl.when(step == 0)
    def _():
        build_columns(listed(col_taps), col)
        build_rows(listed(row_taps), row)

    first = ids[step] == 0
    last = ids[step] == ids[pl.num_programs(0)]
    f32 = jnp.float32
    top = jnp.where(first, above[slices].astype(f32), mask_before[REACH:, :].astype(f32))
    bottom = jnp.where(last, below[slices].astype(f32), mask_after[:REACH, :].astype(f32))
    mask = jnp.concatenate([top, mask_now[...].astype(f32), bottom], axis=0)

    def field(s):
        top = jnp.where(first, above[s].astype(f32), before[s].astype(f32)[REACH:])
        bottom = jnp.where(last, below[s].astype(f32), after[s].astype(f32)[:REACH])
        x = jnp.concatenate([top, now[s].astype(f32), bottom], axis=0)
        return mask * (x - mean[s : s + 1, :1])

    done[...] = convolve(field, col, row, tall, block).astype(jnp.bfloat16)
    at = 0
    for b, wanted in enumerate(pieces):

        @pl.when(step == b)
        def _():
            for p, (inner, start, stop) in enumerate(wanted):
                here = jnp.where(last != (inner == 1), block - REACH, 0) + start
                outs[at + p][...] = done[pl.ds(here, stop - start)]

        at += len(wanted)


def filter_blocks(ids, pieces, density, valid, above, below, row_taps, col_taps, mean, *after):
    slices, rows, cols = density.shape
    terms = row_taps.shape[0]
    block = LANES // terms - HALO
    last = rows // block - 1
    count = ids.shape[0]

    def rows_at(shift):
        return lambda i, at: (0, jnp.clip(at[i] + shift, 0, last), 0)

    def mask_at(shift):
        return lambda i, at: (jnp.clip(at[i] + shift, 0, last), 0)

    def whole(x):
        return pl.BlockSpec(x.shape, lambda i, at: (0,) * x.ndim, pipeline_mode=pl.Buffered(1))

    shapes = [(stop - start, slices, cols) for wanted in pieces for _, start, stop in wanted]
    out = pl.pallas_call(
        functools.partial(filter_kernel, pieces),
        name="filter",
        grid_spec=pltpu.PrefetchScalarGridSpec(
            num_scalar_prefetch=1,
            grid=(count,),
            in_specs=[pl.BlockSpec((slices, block, cols), rows_at(d)) for d in (-1, 0, 1)]
            + [pl.BlockSpec((block, cols), mask_at(d)) for d in (-1, 0, 1)]
            + [whole(x) for x in (above, below, row_taps, col_taps, mean)]
            + [anywhere()] * len(after),
            out_specs=[pl.BlockSpec(shape, lambda i, at: (0, 0, 0)) for shape in shapes],
            scratch_shapes=[
                pltpu.VMEM((GROUP * LANES, cols), jnp.bfloat16),
                pltpu.VMEM((block, slices, cols), jnp.bfloat16),
            ]
            + [pltpu.VMEM(shape, jnp.bfloat16) for shape in matrix_shapes(terms, slices, block)],
        ),
        out_shape=[hbm(shape, jnp.bfloat16) for shape in shapes],
        compiler_params=params(),
        cost_estimate=cost(1, 1),
    )(
        jnp.concatenate([ids, jnp.full((1,), last, ids.dtype)]),
        *[held(x) for x in (density, density, density, valid, valid, valid)],
        above,
        below,
        row_taps,
        col_taps,
        mean,
        *after,
    )
    out = list(out)
    return [[out.pop(0) for _ in wanted] for wanted in pieces]


def band_kernel(pieces, ids, density, valid, above, below, row_taps, col_taps, mean, *refs):
    (col, row, taps, mask, tall, done, sems) = refs[-7:]
    count = sum(len(wanted) for wanted in pieces)
    outs = refs[-7 - count : -7]
    slices = mean.shape[0]
    rows, cols = valid.shape
    terms = row_taps.shape[0]
    block = done.shape[1]
    high = block + HALO
    step = pl.program_id(0)
    f32 = jnp.float32

    @pl.when(step == 0)
    def _():
        for k in range(terms):
            taps[:, k] = jnp.dot(col_taps[k], tap_flip(), preferred_element_type=f32)
        col[LANES + HALO :, :] = jnp.zeros((LANES - HALO, terms * LANES), jnp.bfloat16)
        build_rows(listed(row_taps), row)
        mask[:REACH] = above[slices].astype(f32)
        mask[REACH : REACH + rows] = valid[...].astype(f32)
        mask[REACH + rows :] = below[slices].astype(f32)

    @pl.when(step < slices)
    def _():
        mine = taps[step]
        for k in range(terms):
            col[: LANES + HALO, k * LANES : (k + 1) * LANES] = column_band(mine[k : k + 1])
        x = jnp.concatenate([above[step].astype(f32), density[0].astype(f32), below[step].astype(f32)], axis=0)
        x = mask[...] * (x - mean[pl.ds(step, 1), :][:, :1])
        x = jnp.concatenate([x, jnp.zeros((rows + HALO, LANES), f32)], axis=1)
        x = pltpu.roll(x, REACH, 1).astype(jnp.bfloat16)
        x = jnp.concatenate([x[:, c : c + 2 * LANES] for c in range(0, cols, LANES)], axis=0)
        y = jnp.dot(x, col[...], preferred_element_type=f32).astype(jnp.bfloat16)
        for c in range(cols // LANES):
            for k in range(terms):
                tall[step * terms + k, :, c * LANES : (c + 1) * LANES] = y[
                    c * (rows + HALO) : (c + 1) * (rows + HALO), k * LANES : (k + 1) * LANES
                ]

    def copies(b):
        at = sum(len(wanted) for wanted in pieces[:b])
        last = ids[b] == ids[len(pieces)]
        for p, (inner, start, stop) in enumerate(pieces[b]):
            here = jnp.where(last != (inner == 1), block - REACH, 0) + start
            yield pltpu.make_async_copy(done.at[b, pl.ds(here, stop - start)], outs[at + p], sems.at[at + p])

    @pl.when(step >= slices)
    def _():
        b = step - slices
        here = pl.ds(pl.multiple_of(ids[b] * block, block), high)
        parts = []
        for g in range(slices // GROUP):
            slab = tall[g * GROUP * terms : (g + 1) * GROUP * terms, here, :].reshape(GROUP * LANES, cols)
            z = jnp.dot(row[g], slab, preferred_element_type=f32)
            parts.append(z.reshape(block, GROUP, cols))
        done[b] = jnp.concatenate(parts, axis=1).astype(jnp.bfloat16)

    for b in range(len(pieces)):

        @pl.when(step == slices + b)
        def _():
            for copy in copies(b):
                copy.start()

    @pl.when(step == slices + len(pieces) - 1)
    def _():
        for b in range(len(pieces)):
            for copy in copies(b):
                copy.wait()


def filter_band(ids, pieces, density, valid, above, below, row_taps, col_taps, mean, *after):
    slices, rows, cols = density.shape
    terms = row_taps.shape[0]
    block = LANES // terms - HALO
    count = len(pieces)

    def whole(x):
        return pl.BlockSpec(x.shape, lambda i, at: (0,) * x.ndim, pipeline_mode=pl.Buffered(1))

    shapes = [(stop - start, slices, cols) for wanted in pieces for _, start, stop in wanted]
    out = pl.pallas_call(
        functools.partial(band_kernel, pieces),
        name="band",
        grid_spec=pltpu.PrefetchScalarGridSpec(
            num_scalar_prefetch=1,
            grid=(slices + count,),
            in_specs=[pl.BlockSpec((1, rows, cols), lambda i, at: (jnp.minimum(i, slices - 1), 0, 0))]
            + [whole(x) for x in (valid, above, below, row_taps, col_taps, mean)]
            + [anywhere()] * len(after),
            out_specs=[anywhere()] * len(shapes),
            scratch_shapes=[
                pltpu.VMEM((2 * LANES, terms * LANES), jnp.bfloat16),
                pltpu.VMEM((slices // GROUP, block * GROUP, GROUP * LANES), jnp.bfloat16),
                pltpu.VMEM((slices, terms, 2 * LANES), jnp.float32),
                pltpu.VMEM((rows + HALO, cols), jnp.float32),
                pltpu.VMEM((slices * terms, rows + HALO, cols), jnp.bfloat16),
                pltpu.VMEM((count, block, slices, cols), jnp.bfloat16),
                pltpu.SemaphoreType.DMA((len(shapes),)),
            ],
        ),
        out_shape=[hbm(shape, jnp.bfloat16) for shape in shapes],
        compiler_params=params(44),
        cost_estimate=cost(1, 1),
    )(
        jnp.concatenate([ids, jnp.full((1,), rows // block - 1, ids.dtype)]),
        held(density),
        held(valid),
        above,
        below,
        row_taps,
        col_taps,
        mean,
        *after,
    )
    out = list(out)
    return [[out.pop(0) for _ in wanted] for wanted in pieces]


def project_kernel(count, place, weights, *refs):
    parts, (amp_out, like_out, token) = refs[:count], refs[-3:]
    zbins = weights.shape[0] // 2
    pencil = jnp.concatenate([x[0] for x in parts], axis=0)
    both = jnp.dot(weights[...], pencil, preferred_element_type=jnp.float32)
    amp = both[:zbins]
    amp_out[...] = amp.astype(jnp.bfloat16)
    like_out[...] = (amp * both[zbins:]).astype(jnp.bfloat16)
    token[...] = jnp.zeros_like(token)


def project(place, weights, parts, rows, total, earlier):
    _, slices, cols = parts[0][0].shape
    zbins = weights.shape[0] // 2
    count = len(parts)
    shape = hbm((zbins, total * cols), jnp.bfloat16)
    return pl.pallas_call(
        functools.partial(project_kernel, count),
        name="project",
        grid_spec=pltpu.PrefetchScalarGridSpec(
            num_scalar_prefetch=1,
            grid=(rows,),
            in_specs=[pl.BlockSpec(weights.shape, lambda i, at: (0, 0))]
            + [pl.BlockSpec((1, slices, cols), lambda i, at, start=start: (i + start, 0, 0)) for _, start in parts]
            + [anywhere()] * len(earlier),
            out_specs=[pl.BlockSpec((zbins, cols), lambda i, at: (0, i + at[0]))] * 2
            + [pl.BlockSpec((8, LANES), lambda i, at: (0, 0))],
        ),
        out_shape=[shape, shape, hbm((8, LANES), jnp.float32)],
        input_output_aliases={2 + count + i: i for i in range(len(earlier))},
        compiler_params=params(),
        cost_estimate=cost(1, 1),
    )(place.reshape(1), weights, *[x for x, _ in parts], *earlier)


def gate_kernel(*refs):
    pass


def gate(x, *earlier, flops=1):
    return pl.pallas_call(
        gate_kernel,
        name="gate",
        in_specs=[anywhere()] * (1 + len(earlier)),
        out_specs=anywhere(),
        out_shape=hbm(x.shape, x.dtype),
        input_output_aliases={0: 0},
        compiler_params=params(1),
        cost_estimate=cost(flops, 1),
    )(held(x), *earlier)


INNER, OUTER, HEAD, TAIL = (1, 0, REACH), (0, 0, REACH), (0, 0, 5), (0, 5, REACH)
LATE = (4, 6, 5, 7)
FIRST = ((4, (INNER,)), (6, (INNER,)))
REST = (
    (5, (INNER, HEAD, TAIL)),
    (7, (INNER, HEAD, TAIL)),
    (2, (INNER, OUTER)),
    (3, (INNER, OUTER)),
    (4, (HEAD, TAIL)),
    (6, (HEAD, TAIL)),
    (1, (INNER, OUTER)),
    (0, (INNER, OUTER)),
)
ORDER = (
    (4, 0), (6, 0), (5, 0), (2, 0), (7, 0), (3, 0), (4, 1), (2, 1), (6, 1), (1, 0), (5, 1), (3, 1), (7, 1), (1, 1),
    (4, 2), (6, 2), (5, 2), (7, 2),
)
IN_FLIGHT = 4


def fast(density, valid, row_taps, col_taps, amp_matrix, like_matrix):
    slices, rows, cols = density.shape
    peers = lax.axis_size("cuts")
    tiles = lax.axis_size("tile")
    block = rows // peers
    me = lax.axis_index("cuts").astype(jnp.int32)

    def swap(x, k):
        return lax.ppermute(x, "cuts", [(i, i ^ k) for i in range(peers)])

    own, first, last = masked_sums(density, valid)
    sums = [own] + [lax.ppermute(own, "tile", [(i, i ^ k) for i in range(tiles)]) for k in range(1, tiles)]
    above = lax.ppermute(last, "tile", [(i, i + 1) for i in range(tiles - 1)])
    below = lax.ppermute(first, "tile", [(i + 1, i) for i in range(tiles - 1)])
    mean = means(sums, slices)

    made, arrived = {}, {}

    def filter_for(kernel, wanted, above, below, *after):
        ids = jnp.stack([me ^ k for k, _ in wanted])
        pieces = [cut for _, cut in wanted]
        got = kernel(ids, pieces, density, valid, above, below, row_taps, col_taps, mean, *after)
        for (k, cut), parts in zip(wanted, got):
            for piece, x in zip(cut, parts):
                p = {INNER: 0, OUTER: 1, HEAD: 1, TAIL: 2}[piece]
                made[k, p] = x
                if k == 0:
                    arrived[k, p] = x

    filter_for(filter_blocks, FIRST, last, first)
    filter_for(filter_band, REST, above, below, made[4, 0])
    weights = jnp.concatenate([amp_matrix, like_matrix], axis=1).T.reshape(-1, peers, slices)
    weights = weights[:, me ^ jnp.arange(peers)].reshape(-1, peers * slices)
    result, tokens = [], []

    def finish(p):
        inner, start, stop = (INNER, HEAD, TAIL)[p]
        place = jnp.where((me == peers - 1) != (inner == 1), block - REACH, 0) + start
        parts = [(arrived[k, p], 0) if k in LATE else (arrived[k, min(p, 1)], start) for k in range(peers)]
        *result[:], token = project(place, weights, parts, stop - start, block, result)
        tokens.append(token)

    for at, (k, p) in enumerate(ORDER):
        before = [arrived[ORDER[at - IN_FLIGHT]]] if at >= IN_FLIGHT else []
        if at == len(ORDER) - 3:
            finish(0)
            before.append(tokens[0])
        arrived[k, p] = swap(gate(made[k, p], *before) if before else made[k, p], k)
    finish(1)
    finish(2)
    return tuple(result)


def extended(shard, sides, width):
    for axis, dim in sides:
        size, length = (lax.axis_size(axis), shard.shape[dim])
        up = [(i, (i + 1) % size) for i in range(size - 1)]
        down = [(j, i) for i, j in up]
        last = lax.slice_in_dim(shard, length - width, length, axis=dim)
        initial = lax.slice_in_dim(shard, 0, width, axis=dim)
        before = lax.ppermute(last, axis, up)
        after = lax.ppermute(initial, axis, down)
        shard = jnp.concatenate([before, shard, after], axis=dim)
    return shard


def band_matrix(taps, out_count, in_count):
    offset = lax.broadcasted_iota(jnp.int32, (out_count, in_count), 1) - lax.broadcasted_iota(
        jnp.int32, (out_count, in_count), 0
    )
    positions = lax.broadcasted_iota(jnp.int32, (1, 1, TAPS), 2)
    choose = (offset[:, :, None] == positions).astype(jnp.bfloat16)
    return jnp.einsum("ijt,kst->ksij", choose, taps, preferred_element_type=jnp.float32).astype(jnp.bfloat16)


def filter_field(padded, row_taps, col_taps):
    tall = padded.shape[1]
    cols = padded.shape[2]
    width = 2 * LANES
    row_band = band_matrix(row_taps, tall - HALO, tall)
    rowed = jnp.einsum("ksij,sjc->ksic", row_band, padded, preferred_element_type=jnp.float32).astype(jnp.bfloat16)
    widened = jnp.pad(rowed, ((0, 0), (0, 0), (0, 0), (REACH, REACH)))
    col_band = band_matrix(col_taps, width, width + HALO)
    pieces = []
    for begin in range(0, cols, width):
        segment = widened[:, :, :, begin : begin + width + HALO]
        pieces.append(jnp.einsum("ksrj,ksij->sri", segment, col_band, preferred_element_type=jnp.float32))
    return jnp.concatenate(pieces, axis=2).astype(jnp.bfloat16)


def general(density, valid, row_taps, col_taps, amp_matrix, like_matrix):
    slices, rows, cols = density.shape
    mask = valid.astype(jnp.float32)
    field = density.astype(jnp.float32)
    sums, count = lax.psum((jnp.sum(field * mask[None], axis=(1, 2)), jnp.sum(mask)), "tile")
    masked = (mask[None] * (field - (sums / count)[:, None, None])).astype(jnp.bfloat16)
    filtered = filter_field(extended(masked, (("tile", 1),), REACH), row_taps, col_taps)
    peers = lax.axis_size("cuts")
    share = rows * cols // peers
    pencil = lax.all_to_all(
        filtered.reshape(slices, peers, share), "cuts", split_axis=1, concat_axis=0, tiled=True
    ).reshape(slices * peers, share)
    amp = jnp.dot(amp_matrix.T, pencil, preferred_element_type=jnp.float32)
    like = amp * jnp.dot(like_matrix.T, pencil, preferred_element_type=jnp.float32)
    return amp.astype(jnp.bfloat16), like.astype(jnp.bfloat16)


def per_device(density, valid, row_taps, col_taps, amp_matrix, like_matrix):
    slices, rows, cols = density.shape
    terms = row_taps.shape[0]
    peers = lax.axis_size("cuts")
    fits = (
        peers == 8
        and lax.axis_size("tile") == 4
        and slices == 2 * GROUP
        and terms == 4
        and rows == peers * (LANES // terms - HALO)
        and cols % (2 * LANES) == 0
    )
    run = fast if fits else general
    return run(density, valid, row_taps, col_taps, amp_matrix, like_matrix)


def solution(mesh):
    return jax.shard_map(
        per_device,
        mesh=mesh,
        in_specs=(
            P("cuts", "tile", None),
            P("tile", None),
            P(None, "cuts", None),
            P(None, "cuts", None),
            P(),
            P(),
        ),
        out_specs=(P(None, ("tile", "cuts")), P(None, ("tile", "cuts"))),
        check_vma=False,
    )
```

```python
import functools

import jax
import jax.numpy as jnp
from jax import lax
from jax.experimental import pallas as pl
from jax.experimental.pallas import tpu as pltpu
from jax.sharding import PartitionSpec as P

REACH = 8
TAPS = 2 * REACH + 1
LANES = 128
GROUP = 8
PER = 4
PAIR = 2
MIB = 1024 * 1024
HALO = 2 * REACH


def params(mib=24):
    return pltpu.CompilerParams(vmem_limit_bytes=mib * MIB)


def hbm(shape, dtype):
    return pltpu.HBM(shape, dtype)


def held(x):
    return pltpu.with_memory_space_constraint(x, pltpu.HBM)


def anywhere():
    return pl.BlockSpec(memory_space=pl.ANY)


def cost(flops, moved):
    return pl.CostEstimate(flops=int(flops), bytes_accessed=int(moved), transcendentals=0)


def tap_flip():
    tap = lax.broadcasted_iota(jnp.int32, (TAPS, 2 * LANES), 0)
    lane = lax.broadcasted_iota(jnp.int32, (TAPS, 2 * LANES), 1)
    return (lax.rem(tap + lane, 2 * LANES) == 0).astype(jnp.bfloat16)


def column_band(taps):
    band = pltpu.roll(jnp.broadcast_to(taps, (LANES + HALO, 2 * LANES)), 0, 1, stride=1, stride_axis=0)
    return band[:, :LANES].astype(jnp.bfloat16)


def build_columns(col_taps, col_out):
    terms, slices = len(col_taps), col_taps[0].shape[0]
    for k in range(terms):
        base = jnp.dot(col_taps[k], tap_flip(), preferred_element_type=jnp.float32)
        for s in range(slices):
            col_out[s, : LANES + HALO, k * LANES : (k + 1) * LANES] = column_band(base[s : s + 1])
    for s in range(slices):
        col_out[s, LANES + HALO :, :] = jnp.zeros((LANES - HALO, terms * LANES), jnp.bfloat16)


def build_rows(row_taps, row_out):
    terms, slices = len(row_taps), row_taps[0].shape[0]
    high = LANES // terms
    tap = lax.broadcasted_iota(jnp.int32, (TAPS, LANES), 0)
    lane = lax.broadcasted_iota(jnp.int32, (TAPS, LANES), 1)
    base = jnp.zeros((slices, LANES), jnp.float32)
    for k in range(terms):
        place = (lane == tap + k * high).astype(jnp.bfloat16)
        base = base + jnp.dot(row_taps[k], place, preferred_element_type=jnp.float32)
    sub = lax.broadcasted_iota(jnp.int32, (GROUP, LANES), 0)
    for g in range(slices // GROUP):
        own = base[g * GROUP : (g + 1) * GROUP]
        for pair in range(row_out.shape[1] // (2 * GROUP)):
            shifted = [pltpu.roll(own, 2 * pair + h, 1) for h in range(2)]
            for s in range(GROUP):
                both = jnp.concatenate([jnp.where(sub == s, x, 0.0) for x in shifted], axis=0)
                row_out[
                    g, pair * 2 * GROUP : (pair + 1) * 2 * GROUP, s * LANES : (s + 1) * LANES
                ] = both.astype(jnp.bfloat16)


def listed(taps):
    return [taps[k] for k in range(taps.shape[0])]


def matrix_shapes(terms, slices, rows):
    return (slices, 2 * LANES, terms * LANES), (slices // GROUP, rows * GROUP, GROUP * LANES)


def convolve(field, col, row, tall, rows):
    slices, _, wide = col.shape
    terms = wide // LANES
    high, cols = LANES // terms, tall.shape[1]
    parts = []
    for g in range(slices // GROUP):
        for j in range(GROUP):
            s = g * GROUP + j
            x = jnp.concatenate([field(s), jnp.zeros((high, LANES), jnp.float32)], axis=1)
            x = pltpu.roll(x, REACH, 1).astype(jnp.bfloat16)
            x = jnp.concatenate([x[:, c : c + 2 * LANES] for c in range(0, cols, LANES)], axis=0)
            y = jnp.dot(x, col[s], preferred_element_type=jnp.float32).astype(jnp.bfloat16)
            for c in range(cols // LANES):
                for k in range(terms):
                    tall[(j * terms + k) * high : (j * terms + k + 1) * high, c * LANES : (c + 1) * LANES] = y[
                        c * high : (c + 1) * high, k * LANES : (k + 1) * LANES
                    ]
        z = jnp.dot(row[g, : rows * GROUP], tall[...], preferred_element_type=jnp.float32)
        parts.append(z.reshape(rows, GROUP, cols))
    return jnp.concatenate(parts, axis=1)


def sums_kernel(density, valid, out, first, last):
    slices, rows, cols = density.shape
    step = pl.program_id(0)

    @pl.when(step == 0)
    def _():
        out[...] = jnp.zeros_like(out)
        first[:slices] = density[:, :REACH]
        first[slices] = valid[:REACH].astype(jnp.bfloat16)

    @pl.when(step == pl.num_programs(0) - 1)
    def _():
        last[:slices] = density[:, rows - REACH :]
        last[slices] = valid[rows - REACH :].astype(jnp.bfloat16)

    mask = valid[...] != 0
    for s in range(slices + 1):
        if s < slices:
            x = jnp.where(mask, density[s].astype(jnp.float32), 0.0)
        else:
            x = jnp.where(mask, 1.0, 0.0)
        x = x.reshape(rows // 8, 8, cols).sum(axis=0)
        x = sum(x[:, c : c + LANES] for c in range(0, cols, LANES))
        out[s : s + 1, :] += jnp.sum(x, axis=0, keepdims=True)


def masked_sums(density, valid):
    slices, rows, cols = density.shape
    step = 32
    edge = jax.ShapeDtypeStruct((slices + 1, REACH, cols), jnp.bfloat16)
    return pl.pallas_call(
        sums_kernel,
        name="sums",
        grid=(rows // step,),
        in_specs=[
            pl.BlockSpec((slices, step, cols), lambda i: (0, i, 0)),
            pl.BlockSpec((step, cols), lambda i: (i, 0)),
        ],
        out_specs=[pl.BlockSpec((slices + 8, LANES), lambda i: (0, 0))]
        + [pl.BlockSpec((slices + 1, REACH, cols), lambda i: (0, 0, 0))] * 2,
        out_shape=[jax.ShapeDtypeStruct((slices + 8, LANES), jnp.float32), edge, edge],
        compiler_params=params(),
        cost_estimate=cost(1, 1),
    )(density, valid)


def mean_kernel(*refs):
    sums, out = refs[:4], refs[-1]
    slices = out.shape[0]
    total = sums[0][...] + sums[1][...] + sums[2][...] + sums[3][...]
    total = jnp.sum(total, axis=1, keepdims=True)
    out[...] = jnp.broadcast_to(total[:slices] / total[slices : slices + 1], out.shape)


def means(sums, slices):
    return pl.pallas_call(
        mean_kernel,
        name="means",
        out_shape=jax.ShapeDtypeStruct((slices, LANES), jnp.float32),
        compiler_params=params(),
        cost_estimate=cost(1, 1),
    )(*sums)


def filter_kernel(pieces, ids, before, now, after, mask_before, mask_now, mask_after, *refs):
    (above, below, row_taps, col_taps, mean), (tall, done, col, row) = refs[:5], refs[-4:]
    count = sum(len(wanted) for wanted in pieces)
    outs = refs[-4 - count : -4]
    slices, block, cols = now.shape
    step = pl.program_id(0)

    @pl.when(step == 0)
    def _():
        build_columns(listed(col_taps), col)
        build_rows(listed(row_taps), row)

    first = ids[step] == 0
    last = ids[step] == ids[pl.num_programs(0)]
    f32 = jnp.float32
    top = jnp.where(first, above[slices].astype(f32), mask_before[REACH:, :].astype(f32))
    bottom = jnp.where(last, below[slices].astype(f32), mask_after[:REACH, :].astype(f32))
    mask = jnp.concatenate([top, mask_now[...].astype(f32), bottom], axis=0)

    def field(s):
        top = jnp.where(first, above[s].astype(f32), before[s].astype(f32)[REACH:])
        bottom = jnp.where(last, below[s].astype(f32), after[s].astype(f32)[:REACH])
        x = jnp.concatenate([top, now[s].astype(f32), bottom], axis=0)
        return mask * (x - mean[s : s + 1, :1])

    done[...] = convolve(field, col, row, tall, block).astype(jnp.bfloat16)
    at = 0
    for b, wanted in enumerate(pieces):

        @pl.when(step == b)
        def _():
            for p, (inner, start, stop) in enumerate(wanted):
                here = jnp.where(last != (inner == 1), block - REACH, 0) + start
                outs[at + p][...] = done[pl.ds(here, stop - start)]

        at += len(wanted)


def filter_blocks(ids, pieces, density, valid, above, below, row_taps, col_taps, mean, *after):
    slices, rows, cols = density.shape
    terms = row_taps.shape[0]
    block = LANES // terms - HALO
    last = rows // block - 1
    count = ids.shape[0]

    def rows_at(shift):
        return lambda i, at: (0, jnp.clip(at[i] + shift, 0, last), 0)

    def mask_at(shift):
        return lambda i, at: (jnp.clip(at[i] + shift, 0, last), 0)

    def whole(x):
        return pl.BlockSpec(x.shape, lambda i, at: (0,) * x.ndim, pipeline_mode=pl.Buffered(1))

    shapes = [(stop - start, slices, cols) for wanted in pieces for _, start, stop in wanted]
    out = pl.pallas_call(
        functools.partial(filter_kernel, pieces),
        name="filter",
        grid_spec=pltpu.PrefetchScalarGridSpec(
            num_scalar_prefetch=1,
            grid=(count,),
            in_specs=[pl.BlockSpec((slices, block, cols), rows_at(d)) for d in (-1, 0, 1)]
            + [pl.BlockSpec((block, cols), mask_at(d)) for d in (-1, 0, 1)]
            + [whole(x) for x in (above, below, row_taps, col_taps, mean)]
            + [anywhere()] * len(after),
            out_specs=[pl.BlockSpec(shape, lambda i, at: (0, 0, 0)) for shape in shapes],
            scratch_shapes=[
                pltpu.VMEM((GROUP * LANES, cols), jnp.bfloat16),
                pltpu.VMEM((block, slices, cols), jnp.bfloat16),
            ]
            + [pltpu.VMEM(shape, jnp.bfloat16) for shape in matrix_shapes(terms, slices, block)],
        ),
        out_shape=[hbm(shape, jnp.bfloat16) for shape in shapes],
        compiler_params=params(),
        cost_estimate=cost(1, 1),
    )(
        jnp.concatenate([ids, jnp.full((1,), last, ids.dtype)]),
        *([density] * 3),
        *([valid] * 3),
        above,
        below,
        row_taps,
        col_taps,
        mean,
        *after,
    )
    out = list(out)
    return [[out.pop(0) for _ in wanted] for wanted in pieces]


def band_kernel(pieces, ids, density, valid, above, below, row_taps, col_taps, mean, *refs):
    (col, row, taps, mask, tall, done, sems) = refs[-7:]
    count = sum(len(wanted) for wanted in pieces)
    outs = refs[-7 - count : -7]
    slices = mean.shape[0]
    rows, cols = valid.shape
    terms = row_taps.shape[0]
    block = done.shape[1]
    high = block + HALO
    step = pl.program_id(0)
    f32 = jnp.float32

    @pl.when(step == 0)
    def _():
        for k in range(terms):
            taps[:, k] = jnp.dot(col_taps[k], tap_flip(), preferred_element_type=f32)
        col[:, LANES + HALO :, :] = jnp.zeros((PER, LANES - HALO, terms * LANES), jnp.bfloat16)
        build_rows(listed(row_taps), row)
        mask[:REACH] = above[slices].astype(f32)
        mask[REACH : REACH + rows] = valid[...].astype(f32)
        mask[REACH + rows :] = below[slices].astype(f32)

    steps = slices // PER

    @pl.when(step < steps)
    def _():
        for j in range(PER):
            s = step * PER + j
            mine = taps[s]
            for k in range(terms):
                col[j, : LANES + HALO, k * LANES : (k + 1) * LANES] = column_band(mine[k : k + 1])
            x = jnp.concatenate([above[s].astype(f32), density[j].astype(f32), below[s].astype(f32)], axis=0)
            x = mask[...] * (x - mean[pl.ds(s, 1), :][:, :1])
            x = jnp.concatenate([x, jnp.zeros((rows + HALO, LANES), f32)], axis=1)
            x = pltpu.roll(x, REACH, 1).astype(jnp.bfloat16)
            x = jnp.concatenate([x[:, c : c + 2 * LANES] for c in range(0, cols, LANES)], axis=0)
            y = jnp.dot(x, col[j], preferred_element_type=f32).astype(jnp.bfloat16)
            for c in range(cols // LANES):
                for k in range(terms):
                    tall[s * terms + k, :, c * LANES : (c + 1) * LANES] = y[
                        c * (rows + HALO) : (c + 1) * (rows + HALO), k * LANES : (k + 1) * LANES
                    ]

    def copies(b):
        at = sum(len(wanted) for wanted in pieces[:b])
        last = ids[b] == ids[len(pieces)]
        for p, (inner, start, stop) in enumerate(pieces[b]):
            here = jnp.where(last != (inner == 1), block - REACH, 0) + start
            yield pltpu.make_async_copy(done.at[b, pl.ds(here, stop - start)], outs[at + p], sems.at[at + p])

    @pl.when(step >= steps)
    def _():
        for j in range(PAIR):
            b = (step - steps) * PAIR + j
            here = pl.ds(pl.multiple_of(ids[b] * block, block), high)
            parts = []
            for g in range(slices // GROUP):
                slab = tall[g * GROUP * terms : (g + 1) * GROUP * terms, here, :].reshape(GROUP * LANES, cols)
                z = jnp.dot(row[g], slab, preferred_element_type=f32)
                parts.append(z.reshape(block, GROUP, cols))
            done[b] = jnp.concatenate(parts, axis=1).astype(jnp.bfloat16)

    for n in range(len(pieces) // PAIR):

        @pl.when(step == steps + n)
        def _():
            for b in range(n * PAIR, (n + 1) * PAIR):
                for copy in copies(b):
                    copy.start()

    @pl.when(step == pl.num_programs(0) - 1)
    def _():
        for b in range(len(pieces)):
            for copy in copies(b):
                copy.wait()


def filter_band(ids, pieces, density, valid, above, below, row_taps, col_taps, mean, *after):
    slices, rows, cols = density.shape
    terms = row_taps.shape[0]
    block = LANES // terms - HALO
    count = len(pieces)

    def whole(x):
        return pl.BlockSpec(x.shape, lambda i, at: (0,) * x.ndim, pipeline_mode=pl.Buffered(1))

    shapes = [(stop - start, slices, cols) for wanted in pieces for _, start, stop in wanted]
    out = pl.pallas_call(
        functools.partial(band_kernel, pieces),
        name="band",
        grid_spec=pltpu.PrefetchScalarGridSpec(
            num_scalar_prefetch=1,
            grid=(slices // PER + count // PAIR,),
            in_specs=[pl.BlockSpec((PER, rows, cols), lambda i, at: (jnp.minimum(i, slices // PER - 1), 0, 0))]
            + [whole(x) for x in (valid, above, below, row_taps, col_taps, mean)]
            + [anywhere()] * len(after),
            out_specs=[anywhere()] * len(shapes),
            scratch_shapes=[
                pltpu.VMEM((PER, 2 * LANES, terms * LANES), jnp.bfloat16),
                pltpu.VMEM((slices // GROUP, block * GROUP, GROUP * LANES), jnp.bfloat16),
                pltpu.VMEM((slices, terms, 2 * LANES), jnp.float32),
                pltpu.VMEM((rows + HALO, cols), jnp.float32),
                pltpu.VMEM((slices * terms, rows + HALO, cols), jnp.bfloat16),
                pltpu.VMEM((count, block, slices, cols), jnp.bfloat16),
                pltpu.SemaphoreType.DMA((len(shapes),)),
            ],
        ),
        out_shape=[hbm(shape, jnp.bfloat16) for shape in shapes],
        compiler_params=params(44),
        cost_estimate=cost(1, 1),
    )(
        jnp.concatenate([ids, jnp.full((1,), rows // block - 1, ids.dtype)]),
        density,
        valid,
        above,
        below,
        row_taps,
        col_taps,
        mean,
        *after,
    )
    out = list(out)
    return [[out.pop(0) for _ in wanted] for wanted in pieces]


def project_kernel(count, place, weights, *refs):
    parts, (amp_out, like_out, token) = refs[:count], refs[-3:]
    zbins = weights.shape[0] // 2
    pencil = jnp.concatenate([x[0] for x in parts], axis=0)
    both = jnp.dot(weights[...], pencil, preferred_element_type=jnp.float32)
    amp = both[:zbins]
    amp_out[...] = amp.astype(jnp.bfloat16)
    like_out[...] = (amp * both[zbins:]).astype(jnp.bfloat16)
    token[...] = jnp.zeros_like(token)


def project(place, weights, parts, rows, total, earlier):
    _, slices, cols = parts[0][0].shape
    zbins = weights.shape[0] // 2
    count = len(parts)
    shape = hbm((zbins, total * cols), jnp.bfloat16)
    return pl.pallas_call(
        functools.partial(project_kernel, count),
        name="project",
        grid_spec=pltpu.PrefetchScalarGridSpec(
            num_scalar_prefetch=1,
            grid=(rows,),
            in_specs=[pl.BlockSpec(weights.shape, lambda i, at: (0, 0))]
            + [pl.BlockSpec((1, slices, cols), lambda i, at, start=start: (i + start, 0, 0)) for _, start in parts]
            + [anywhere()] * len(earlier),
            out_specs=[pl.BlockSpec((zbins, cols), lambda i, at: (0, i + at[0]))] * 2
            + [pl.BlockSpec((8, LANES), lambda i, at: (0, 0))],
        ),
        out_shape=[shape, shape, hbm((8, LANES), jnp.float32)],
        input_output_aliases={2 + count + i: i for i in range(len(earlier))},
        compiler_params=params(),
        cost_estimate=cost(1, 1),
    )(place.reshape(1), weights, *[x for x, _ in parts], *earlier)


def gate_kernel(*refs):
    pass


def gate(x, *earlier, flops=1):
    return pl.pallas_call(
        gate_kernel,
        name="gate",
        in_specs=[anywhere()] * (1 + len(earlier)),
        out_specs=anywhere(),
        out_shape=hbm(x.shape, x.dtype),
        input_output_aliases={0: 0},
        compiler_params=params(1),
        cost_estimate=cost(flops, 1),
    )(held(x), *earlier)


INNER, OUTER, HEAD, TAIL = (1, 0, REACH), (0, 0, REACH), (0, 0, 5), (0, 5, REACH)
LATE = (4, 6, 5, 7)
FIRST = ((4,), (6, 5))
REST = (
    (5, (HEAD, TAIL)),
    (7, (INNER, HEAD, TAIL)),
    (2, (INNER, OUTER)),
    (3, (INNER, OUTER)),
    (4, (HEAD, TAIL)),
    (6, (HEAD, TAIL)),
    (1, (INNER, OUTER)),
    (0, (INNER, OUTER)),
)
ORDER = (
    (4, 0), (6, 0), (5, 0), (7, 0), (2, 0), (4, 1), (3, 0), (6, 1), (2, 1), (5, 1), (1, 0), (7, 1), (3, 1), (1, 1),
    (4, 2), (6, 2), (5, 2), (7, 2),
)
WAITS = {3: 1, 4: 1, 5: 2, 6: 2, **{at: at - 4 for at in range(7, len(ORDER))}}


def fast(density, valid, row_taps, col_taps, amp_matrix, like_matrix):
    slices, rows, cols = density.shape
    peers = lax.axis_size("cuts")
    tiles = lax.axis_size("tile")
    block = rows // peers
    me = lax.axis_index("cuts").astype(jnp.int32)

    def swap(x, k):
        return lax.ppermute(x, "cuts", [(i, i ^ k) for i in range(peers)])

    own, first, last = masked_sums(density, valid)
    sums = [own] + [lax.ppermute(own, "tile", [(i, i ^ k) for i in range(tiles)]) for k in range(1, tiles)]
    mean = means(sums, slices)

    made, arrived = {}, {}

    def filter_for(kernel, wanted, above, below, *after):
        ids = jnp.stack([me ^ k for k, _ in wanted])
        pieces = [cut for _, cut in wanted]
        got = kernel(ids, pieces, density, valid, above, below, row_taps, col_taps, mean, *after)
        for (k, cut), parts in zip(wanted, got):
            for piece, x in zip(cut, parts):
                p = {INNER: 0, OUTER: 1, HEAD: 1, TAIL: 2}[piece]
                made[k, p] = x
                if k == 0:
                    arrived[k, p] = x

    above = lax.ppermute(last, "tile", [(i, i + 1) for i in range(tiles - 1)])
    below = lax.ppermute(first, "tile", [(i + 1, i) for i in range(tiles - 1)])
    after = ()
    for ks in FIRST:
        filter_for(filter_blocks, [(k, (INNER,)) for k in ks], last, first, *after)
        after = (made[ks[0], 0],)
        for k in ks:
            arrived[k, 0] = swap(made[k, 0], k)
    filter_for(filter_band, REST, above, below, *after, gate(mean, arrived[4, 0]))
    weights = jnp.concatenate([amp_matrix, like_matrix], axis=1).T.reshape(-1, peers, slices)
    weights = weights[:, me ^ jnp.arange(peers)].reshape(-1, peers * slices)
    result, tokens = [], []

    def finish(p):
        inner, start, stop = (INNER, HEAD, TAIL)[p]
        place = jnp.where((me == peers - 1) != (inner == 1), block - REACH, 0) + start
        parts = [(arrived[k, p], 0) if k in LATE else (arrived[k, min(p, 1)], start) for k in range(peers)]
        *result[:], token = project(place, weights, parts, stop - start, block, result)
        tokens.append(token)

    for at, (k, p) in enumerate(ORDER):
        if (k, p) in arrived:
            continue
        before = [arrived[ORDER[WAITS[at]]]] if at in WAITS else []
        if at == len(ORDER) - 3:
            finish(0)
            before.append(tokens[0])
        arrived[k, p] = swap(gate(made[k, p], *before) if before else made[k, p], k)
    finish(1)
    finish(2)
    return tuple(result)


def extended(shard, sides, width):
    for axis, dim in sides:
        size, length = (lax.axis_size(axis), shard.shape[dim])
        up = [(i, (i + 1) % size) for i in range(size - 1)]
        down = [(j, i) for i, j in up]
        last = lax.slice_in_dim(shard, length - width, length, axis=dim)
        initial = lax.slice_in_dim(shard, 0, width, axis=dim)
        before = lax.ppermute(last, axis, up)
        after = lax.ppermute(initial, axis, down)
        shard = jnp.concatenate([before, shard, after], axis=dim)
    return shard


def band_matrix(taps, out_count, in_count):
    offset = lax.broadcasted_iota(jnp.int32, (out_count, in_count), 1) - lax.broadcasted_iota(
        jnp.int32, (out_count, in_count), 0
    )
    positions = lax.broadcasted_iota(jnp.int32, (1, 1, TAPS), 2)
    choose = (offset[:, :, None] == positions).astype(jnp.bfloat16)
    return jnp.einsum("ijt,kst->ksij", choose, taps, preferred_element_type=jnp.float32).astype(jnp.bfloat16)


def filter_field(padded, row_taps, col_taps):
    tall = padded.shape[1]
    cols = padded.shape[2]
    width = 2 * LANES
    row_band = band_matrix(row_taps, tall - HALO, tall)
    rowed = jnp.einsum("ksij,sjc->ksic", row_band, padded, preferred_element_type=jnp.float32).astype(jnp.bfloat16)
    widened = jnp.pad(rowed, ((0, 0), (0, 0), (0, 0), (REACH, REACH)))
    col_band = band_matrix(col_taps, width, width + HALO)
    pieces = []
    for begin in range(0, cols, width):
        segment = widened[:, :, :, begin : begin + width + HALO]
        pieces.append(jnp.einsum("ksrj,ksij->sri", segment, col_band, preferred_element_type=jnp.float32))
    return jnp.concatenate(pieces, axis=2).astype(jnp.bfloat16)


def general(density, valid, row_taps, col_taps, amp_matrix, like_matrix):
    slices, rows, cols = density.shape
    mask = valid.astype(jnp.float32)
    field = density.astype(jnp.float32)
    sums, count = lax.psum((jnp.sum(field * mask[None], axis=(1, 2)), jnp.sum(mask)), "tile")
    masked = (mask[None] * (field - (sums / count)[:, None, None])).astype(jnp.bfloat16)
    filtered = filter_field(extended(masked, (("tile", 1),), REACH), row_taps, col_taps)
    peers = lax.axis_size("cuts")
    share = rows * cols // peers
    pencil = lax.all_to_all(
        filtered.reshape(slices, peers, share), "cuts", split_axis=1, concat_axis=0, tiled=True
    ).reshape(slices * peers, share)
    amp = jnp.dot(amp_matrix.T, pencil, preferred_element_type=jnp.float32)
    like = amp * jnp.dot(like_matrix.T, pencil, preferred_element_type=jnp.float32)
    return amp.astype(jnp.bfloat16), like.astype(jnp.bfloat16)


def per_device(density, valid, row_taps, col_taps, amp_matrix, like_matrix):
    slices, rows, cols = density.shape
    terms = row_taps.shape[0]
    peers = lax.axis_size("cuts")
    fits = (
        peers == 8
        and lax.axis_size("tile") == 4
        and slices == 2 * GROUP
        and terms == 4
        and rows == peers * (LANES // terms - HALO)
        and cols % (2 * LANES) == 0
    )
    run = fast if fits else general
    return run(density, valid, row_taps, col_taps, amp_matrix, like_matrix)


def solution(mesh):
    return jax.shard_map(
        per_device,
        mesh=mesh,
        in_specs=(
            P("cuts", "tile", None),
            P("tile", None),
            P(None, "cuts", None),
            P(None, "cuts", None),
            P(),
            P(),
        ),
        out_specs=(P(None, ("tile", "cuts")), P(None, ("tile", "cuts"))),
        check_vma=False,
    )
```

```python
import functools

import jax
import jax.numpy as jnp
from jax import lax
from jax.experimental import pallas as pl
from jax.experimental.pallas import tpu as pltpu
from jax.sharding import PartitionSpec as P

REACH = 8
TAPS = 2 * REACH + 1
LANES = 128
GROUP = 8
PER = 4
PAIR = 2
CHUNKS = 8
BEFORE_BAND = 2e9
MIB = 1024 * 1024
HALO = 2 * REACH


def params(mib=24):
    return pltpu.CompilerParams(vmem_limit_bytes=mib * MIB)


def hbm(shape, dtype):
    return pltpu.HBM(shape, dtype)


def held(x):
    return pltpu.with_memory_space_constraint(x, pltpu.HBM)


def anywhere():
    return pl.BlockSpec(memory_space=pl.ANY)


def cost(flops, moved):
    return pl.CostEstimate(flops=int(flops), bytes_accessed=int(moved), transcendentals=0)


def tap_flip():
    tap = lax.broadcasted_iota(jnp.int32, (TAPS, 2 * LANES), 0)
    lane = lax.broadcasted_iota(jnp.int32, (TAPS, 2 * LANES), 1)
    return (lax.rem(tap + lane, 2 * LANES) == 0).astype(jnp.bfloat16)


def column_band(taps):
    band = pltpu.roll(jnp.broadcast_to(taps, (LANES + HALO, 2 * LANES)), 0, 1, stride=1, stride_axis=0)
    return band[:, :LANES].astype(jnp.bfloat16)


def build_columns(col_taps, col_out):
    terms, slices = len(col_taps), col_taps[0].shape[0]
    for k in range(terms):
        base = jnp.dot(col_taps[k], tap_flip(), preferred_element_type=jnp.float32)
        for s in range(slices):
            col_out[s, : LANES + HALO, k * LANES : (k + 1) * LANES] = column_band(base[s : s + 1])
    for s in range(slices):
        col_out[s, LANES + HALO :, :] = jnp.zeros((LANES - HALO, terms * LANES), jnp.bfloat16)


def build_rows(row_taps, row_out):
    terms, slices = len(row_taps), row_taps[0].shape[0]
    high = LANES // terms
    tap = lax.broadcasted_iota(jnp.int32, (TAPS, LANES), 0)
    lane = lax.broadcasted_iota(jnp.int32, (TAPS, LANES), 1)
    base = jnp.zeros((slices, LANES), jnp.float32)
    for k in range(terms):
        place = (lane == tap + k * high).astype(jnp.bfloat16)
        base = base + jnp.dot(row_taps[k], place, preferred_element_type=jnp.float32)
    sub = lax.broadcasted_iota(jnp.int32, (GROUP, LANES), 0)
    for g in range(slices // GROUP):
        own = base[g * GROUP : (g + 1) * GROUP]
        for pair in range(row_out.shape[1] // (2 * GROUP)):
            shifted = [pltpu.roll(own, 2 * pair + h, 1) for h in range(2)]
            for s in range(GROUP):
                both = jnp.concatenate([jnp.where(sub == s, x, 0.0) for x in shifted], axis=0)
                row_out[
                    g, pair * 2 * GROUP : (pair + 1) * 2 * GROUP, s * LANES : (s + 1) * LANES
                ] = both.astype(jnp.bfloat16)


def listed(taps):
    return [taps[k] for k in range(taps.shape[0])]


def matrix_shapes(terms, slices, rows):
    return (slices, 2 * LANES, terms * LANES), (slices // GROUP, rows * GROUP, GROUP * LANES)


def convolve(field, col, row, tall, rows):
    slices, _, wide = col.shape
    terms = wide // LANES
    high, cols = LANES // terms, tall.shape[1]
    parts = []
    for g in range(slices // GROUP):
        for j in range(GROUP):
            s = g * GROUP + j
            x = jnp.concatenate([field(s), jnp.zeros((high, LANES), jnp.float32)], axis=1)
            x = pltpu.roll(x, REACH, 1).astype(jnp.bfloat16)
            x = jnp.concatenate([x[:, c : c + 2 * LANES] for c in range(0, cols, LANES)], axis=0)
            y = jnp.dot(x, col[s], preferred_element_type=jnp.float32).astype(jnp.bfloat16)
            for c in range(cols // LANES):
                for k in range(terms):
                    tall[(j * terms + k) * high : (j * terms + k + 1) * high, c * LANES : (c + 1) * LANES] = y[
                        c * high : (c + 1) * high, k * LANES : (k + 1) * LANES
                    ]
        z = jnp.dot(row[g, : rows * GROUP], tall[...], preferred_element_type=jnp.float32)
        parts.append(z.reshape(rows, GROUP, cols))
    return jnp.concatenate(parts, axis=1)


def sums_kernel(density, valid, out, first, last, cube, plane, sems):
    slices, rows, cols = cube.shape
    step = rows // CHUNKS

    def copies(i):
        at = pl.ds(pl.multiple_of(i * step, step), step)
        yield pltpu.make_async_copy(density.at[:, at], cube.at[:, at], sems.at[i])
        yield pltpu.make_async_copy(valid.at[at], plane.at[at], sems.at[CHUNKS + i])

    for i in range(CHUNKS):
        for copy in copies(i):
            copy.start()
    out[...] = jnp.zeros_like(out)

    def body(i, _):
        for copy in copies(i):
            copy.wait()
        at = pl.ds(pl.multiple_of(i * step, step), step)
        mask = plane[at] != 0
        for s in range(slices + 1):
            x = cube[s, at].astype(jnp.float32) if s < slices else jnp.ones((step, cols), jnp.float32)
            x = jnp.where(mask, x, 0.0).reshape(step // 8, 8, cols).sum(axis=0)
            x = sum(x[:, c : c + LANES] for c in range(0, cols, LANES))
            out[s : s + 1, :] += jnp.sum(x, axis=0, keepdims=True)
        return 0

    lax.fori_loop(0, CHUNKS, body, 0)
    first[:slices] = cube[:, :REACH]
    first[slices] = plane[:REACH].astype(jnp.bfloat16)
    last[:slices] = cube[:, rows - REACH :]
    last[slices] = plane[rows - REACH :].astype(jnp.bfloat16)


def masked_sums(density, valid):
    slices, rows, cols = density.shape
    edge = hbm((slices + 1, REACH, cols), jnp.bfloat16)
    return pl.pallas_call(
        sums_kernel,
        name="sums",
        in_specs=[anywhere()] * 2,
        out_specs=[pl.BlockSpec(memory_space=pltpu.VMEM)] * 3,
        out_shape=[hbm((slices + 8, LANES), jnp.float32), edge, edge],
        scratch_shapes=[
            pltpu.VMEM(density.shape, jnp.bfloat16),
            pltpu.VMEM(valid.shape, jnp.int32),
            pltpu.SemaphoreType.DMA((2 * CHUNKS,)),
        ],
        compiler_params=params(),
        cost_estimate=cost(1, 1),
    )(held(density), held(valid))


def mean_kernel(*refs):
    sums, out = refs[:4], refs[-1]
    slices = out.shape[0]
    total = sums[0][...] + sums[1][...] + sums[2][...] + sums[3][...]
    total = jnp.sum(total, axis=1, keepdims=True)
    out[...] = jnp.broadcast_to(total[:slices] / total[slices : slices + 1], out.shape)


def means(sums, slices):
    return pl.pallas_call(
        mean_kernel,
        name="means",
        out_shape=jax.ShapeDtypeStruct((slices, LANES), jnp.float32),
        compiler_params=params(),
        cost_estimate=cost(1, 1),
    )(*sums)


def inner_rows(both, last):
    both = both.astype(jnp.float32)
    rows = both.shape[0] - REACH
    chosen = jnp.where(last, both[REACH:], both[:rows])
    return jnp.concatenate([chosen, jnp.zeros((REACH, both.shape[1]), jnp.float32)], axis=0)


def inner_kernel(pieces, ids, density, valid, row_taps, col_taps, mean, *refs):
    (col, row, tall, cube, plane, sems) = refs[-6:]
    count, slices, high, _ = cube.shape
    outs = list(refs[-6 - sum(len(wanted) for wanted in pieces) : -6])
    block = high // 2
    copies = []
    for b in range(count):
        here = pl.ds(pl.multiple_of(jnp.minimum(ids[b], ids[count] - 1) * block, block), high)
        copies.append(pltpu.make_async_copy(density.at[:, here], cube.at[b], sems.at[2 * b]))
        copies.append(pltpu.make_async_copy(valid.at[here], plane.at[b], sems.at[2 * b + 1]))
    for copy in copies:
        copy.start()
    build_columns(listed(col_taps), col)
    build_rows(listed(row_taps), row)
    for copy in copies:
        copy.wait()
    for b, wanted in enumerate(pieces):
        last = ids[b] == ids[count]
        mask = inner_rows(plane[b], last)
        field = convolve(
            lambda s, b=b, last=last, mask=mask: mask * (inner_rows(cube[b, s], last) - mean[s : s + 1, :1]),
            col,
            row,
            tall,
            REACH,
        ).astype(jnp.bfloat16)
        for _, start, stop in wanted:
            outs.pop(0)[...] = field[start:stop]


def filter_inner(ids, pieces, density, valid, row_taps, col_taps, mean, *after):
    slices, rows, cols = density.shape
    terms = row_taps.shape[0]
    high = LANES // terms
    count = ids.shape[0]

    def whole(x):
        return pl.BlockSpec(x.shape, lambda i, at: (0,) * x.ndim)

    shapes = [(stop - start, slices, cols) for wanted in pieces for _, start, stop in wanted]
    out = pl.pallas_call(
        functools.partial(inner_kernel, pieces),
        name="inner",
        grid_spec=pltpu.PrefetchScalarGridSpec(
            num_scalar_prefetch=1,
            grid=(1,),
            in_specs=[anywhere()] * 2 + [whole(x) for x in (row_taps, col_taps, mean)] + [anywhere()] * len(after),
            out_specs=[pl.BlockSpec(shape, lambda i, at: (0, 0, 0)) for shape in shapes],
            scratch_shapes=[pltpu.VMEM(x, jnp.bfloat16) for x in matrix_shapes(terms, slices, REACH)]
            + [
                pltpu.VMEM((GROUP * LANES, cols), jnp.bfloat16),
                pltpu.VMEM((count, slices, high, cols), jnp.bfloat16),
                pltpu.VMEM((count, high, cols), jnp.int32),
                pltpu.SemaphoreType.DMA((2 * count,)),
            ],
        ),
        out_shape=[hbm(shape, jnp.bfloat16) for shape in shapes],
        compiler_params=params(),
        cost_estimate=cost(1, 1),
    )(
        jnp.concatenate([ids, jnp.full((1,), rows // (high - HALO) - 1, ids.dtype)]),
        held(density),
        held(valid),
        row_taps,
        col_taps,
        mean,
        *after,
    )
    out = list(out)
    return [[out.pop(0) for _ in wanted] for wanted in pieces]


def band_kernel(pieces, ids, density, valid, above, below, row_taps, col_taps, mean, *refs):
    (col, row, taps, mask, tall, done, sems) = refs[-7:]
    count = sum(len(wanted) for wanted in pieces)
    outs = refs[-7 - count : -7]
    slices = mean.shape[0]
    rows, cols = valid.shape
    terms = row_taps.shape[0]
    block = done.shape[1]
    high = block + HALO
    step = pl.program_id(0)
    f32 = jnp.float32

    @pl.when(step == 0)
    def _():
        for k in range(terms):
            taps[:, k] = jnp.dot(col_taps[k], tap_flip(), preferred_element_type=f32)
        col[:, LANES + HALO :, :] = jnp.zeros((PER, LANES - HALO, terms * LANES), jnp.bfloat16)
        build_rows(listed(row_taps), row)
        mask[:REACH] = above[slices].astype(f32)
        mask[REACH : REACH + rows] = valid[...].astype(f32)
        mask[REACH + rows :] = below[slices].astype(f32)

    steps = slices // PER

    @pl.when(step < steps)
    def _():
        for j in range(PER):
            s = step * PER + j
            mine = taps[s]
            for k in range(terms):
                col[j, : LANES + HALO, k * LANES : (k + 1) * LANES] = column_band(mine[k : k + 1])
            x = jnp.concatenate([above[s].astype(f32), density[j].astype(f32), below[s].astype(f32)], axis=0)
            x = mask[...] * (x - mean[pl.ds(s, 1), :][:, :1])
            x = jnp.concatenate([x, jnp.zeros((rows + HALO, LANES), f32)], axis=1)
            x = pltpu.roll(x, REACH, 1).astype(jnp.bfloat16)
            x = jnp.concatenate([x[:, c : c + 2 * LANES] for c in range(0, cols, LANES)], axis=0)
            y = jnp.dot(x, col[j], preferred_element_type=f32).astype(jnp.bfloat16)
            for c in range(cols // LANES):
                for k in range(terms):
                    tall[s * terms + k, :, c * LANES : (c + 1) * LANES] = y[
                        c * (rows + HALO) : (c + 1) * (rows + HALO), k * LANES : (k + 1) * LANES
                    ]

    def copies(b):
        at = sum(len(wanted) for wanted in pieces[:b])
        last = ids[b] == ids[len(pieces)]
        for p, (inner, start, stop) in enumerate(pieces[b]):
            here = jnp.where(last != (inner == 1), block - REACH, 0) + start
            yield pltpu.make_async_copy(done.at[b, pl.ds(here, stop - start)], outs[at + p], sems.at[at + p])

    @pl.when(step >= steps)
    def _():
        for j in range(PAIR):
            b = (step - steps) * PAIR + j
            here = pl.ds(pl.multiple_of(ids[b] * block, block), high)
            parts = []
            for g in range(slices // GROUP):
                slab = tall[g * GROUP * terms : (g + 1) * GROUP * terms, here, :].reshape(GROUP * LANES, cols)
                z = jnp.dot(row[g], slab, preferred_element_type=f32)
                parts.append(z.reshape(block, GROUP, cols))
            done[b] = jnp.concatenate(parts, axis=1).astype(jnp.bfloat16)

    for n in range(len(pieces) // PAIR):

        @pl.when(step == steps + n)
        def _():
            for b in range(n * PAIR, (n + 1) * PAIR):
                for copy in copies(b):
                    copy.start()

    @pl.when(step == pl.num_programs(0) - 1)
    def _():
        for b in range(len(pieces)):
            for copy in copies(b):
                copy.wait()


def filter_band(ids, pieces, density, valid, above, below, row_taps, col_taps, mean, *after):
    slices, rows, cols = density.shape
    terms = row_taps.shape[0]
    block = LANES // terms - HALO
    count = len(pieces)

    def whole(x):
        return pl.BlockSpec(x.shape, lambda i, at: (0,) * x.ndim, pipeline_mode=pl.Buffered(1))

    shapes = [(stop - start, slices, cols) for wanted in pieces for _, start, stop in wanted]
    out = pl.pallas_call(
        functools.partial(band_kernel, pieces),
        name="band",
        grid_spec=pltpu.PrefetchScalarGridSpec(
            num_scalar_prefetch=1,
            grid=(slices // PER + count // PAIR,),
            in_specs=[pl.BlockSpec((PER, rows, cols), lambda i, at: (jnp.minimum(i, slices // PER - 1), 0, 0))]
            + [whole(x) for x in (valid, above, below, row_taps, col_taps, mean)]
            + [anywhere()] * len(after),
            out_specs=[anywhere()] * len(shapes),
            scratch_shapes=[
                pltpu.VMEM((PER, 2 * LANES, terms * LANES), jnp.bfloat16),
                pltpu.VMEM((slices // GROUP, block * GROUP, GROUP * LANES), jnp.bfloat16),
                pltpu.VMEM((slices, terms, 2 * LANES), jnp.float32),
                pltpu.VMEM((rows + HALO, cols), jnp.float32),
                pltpu.VMEM((slices * terms, rows + HALO, cols), jnp.bfloat16),
                pltpu.VMEM((count, block, slices, cols), jnp.bfloat16),
                pltpu.SemaphoreType.DMA((len(shapes),)),
            ],
        ),
        out_shape=[hbm(shape, jnp.bfloat16) for shape in shapes],
        compiler_params=params(44),
        cost_estimate=cost(1, 1),
    )(
        jnp.concatenate([ids, jnp.full((1,), rows // block - 1, ids.dtype)]),
        held(density),
        held(valid),
        above,
        below,
        row_taps,
        col_taps,
        mean,
        *after,
    )
    out = list(out)
    return [[out.pop(0) for _ in wanted] for wanted in pieces]


def project_kernel(count, place, weights, *refs):
    parts, (amp_out, like_out, token) = refs[:count], refs[-3:]
    zbins = weights.shape[0] // 2
    pencil = jnp.concatenate([x[0] for x in parts], axis=0)
    both = jnp.dot(weights[...], pencil, preferred_element_type=jnp.float32)
    amp = both[:zbins]
    amp_out[...] = amp.astype(jnp.bfloat16)
    like_out[...] = (amp * both[zbins:]).astype(jnp.bfloat16)
    token[...] = jnp.zeros_like(token)


def project(place, weights, parts, rows, total, earlier):
    _, slices, cols = parts[0][0].shape
    zbins = weights.shape[0] // 2
    count = len(parts)
    shape = hbm((zbins, total * cols), jnp.bfloat16)
    return pl.pallas_call(
        functools.partial(project_kernel, count),
        name="project",
        grid_spec=pltpu.PrefetchScalarGridSpec(
            num_scalar_prefetch=1,
            grid=(rows,),
            in_specs=[pl.BlockSpec(weights.shape, lambda i, at: (0, 0))]
            + [pl.BlockSpec((1, slices, cols), lambda i, at, start=start: (i + start, 0, 0)) for _, start in parts]
            + [anywhere()] * len(earlier),
            out_specs=[pl.BlockSpec((zbins, cols), lambda i, at: (0, i + at[0]))] * 2
            + [pl.BlockSpec((8, LANES), lambda i, at: (0, 0))],
        ),
        out_shape=[shape, shape, hbm((8, LANES), jnp.float32)],
        input_output_aliases={2 + count + i: i for i in range(len(earlier))},
        compiler_params=params(),
        cost_estimate=cost(1, 1),
    )(place.reshape(1), weights, *[x for x, _ in parts], *earlier)


def gate_kernel(*refs):
    pass


def gate(x, *earlier, flops=1):
    return pl.pallas_call(
        gate_kernel,
        name="gate",
        in_specs=[anywhere()] * (1 + len(earlier)),
        out_specs=anywhere(),
        out_shape=hbm(x.shape, x.dtype),
        input_output_aliases={0: 0},
        compiler_params=params(1),
        cost_estimate=cost(flops, 1),
    )(held(x), *earlier)


INNER, OUTER = (1, 0, REACH), (0, 0, REACH)
GROUPS = (1, 0, 5), (1, 5, REACH), (0, 0, 5), (0, 5, REACH)
FIRST = (((4, GROUPS[:2]),), ((6, (INNER,)), (5, (INNER,))))
REST = (
    (5, GROUPS[2:]),
    (7, (INNER, *GROUPS[2:])),
    (2, (INNER, OUTER)),
    (3, (INNER, OUTER)),
    (4, GROUPS[2:]),
    (6, GROUPS[2:]),
    (1, (INNER, OUTER)),
    (0, (INNER, OUTER)),
)
ORDER = (
    (4, GROUPS[0], None),
    (6, INNER, None),
    (5, INNER, None),
    (4, GROUPS[1], None),
    (7, INNER, 3),
    (2, INNER, 3),
    (4, GROUPS[2], 1),
    (3, INNER, 1),
    (6, GROUPS[2], 2),
    (2, OUTER, 2),
    (5, GROUPS[2], 6),
    (1, INNER, 7),
    (7, GROUPS[2], 8),
    (3, OUTER, 9),
    (1, OUTER, 10),
    (4, GROUPS[3], 11),
    (6, GROUPS[3], 12),
    (5, GROUPS[3], 13),
    (7, GROUPS[3], 14),
)


def fast(density, valid, row_taps, col_taps, amp_matrix, like_matrix):
    slices, rows, cols = density.shape
    peers = lax.axis_size("cuts")
    tiles = lax.axis_size("tile")
    block = rows // peers
    me = lax.axis_index("cuts").astype(jnp.int32)

    def swap(x, k):
        return lax.ppermute(x, "cuts", [(i, i ^ k) for i in range(peers)])

    own, first, last = masked_sums(density, valid)
    sums = [own] + [lax.ppermute(own, "tile", [(i, i ^ k) for i in range(tiles)]) for k in range(1, tiles)]
    mean = means(sums, slices)

    made, arrived = {}, {}

    above = lax.ppermute(last, "tile", [(i, i + 1) for i in range(tiles - 1)])
    below = lax.ppermute(first, "tile", [(i + 1, i) for i in range(tiles - 1)])
    def ids(wanted):
        return jnp.stack([me ^ k for k, _ in wanted])

    def keep(wanted, got):
        for (k, cut), parts in zip(wanted, got):
            for piece, x in zip(cut, parts):
                made[k, piece] = x

    def send(k, piece, *before):
        x = made[k, piece]
        arrived[k, piece] = swap(gate(x, *before) if before else x, k)

    inputs = row_taps, col_taps, mean
    after = ()
    for wanted in FIRST:
        got = filter_inner(ids(wanted), [cut for _, cut in wanted], density, valid, *inputs, *after)
        keep(wanted, got)
        after = (got[0][0],)
    first_piece = ORDER[0][:2]
    send(*first_piece)
    got = filter_band(
        ids(REST), [cut for _, cut in REST], density, valid, above, below, *inputs, *after, gate(mean, arrived[first_piece], flops=BEFORE_BAND)
    )
    keep(REST, got)
    for piece in (INNER, OUTER):
        arrived[0, piece] = made[0, piece]

    weights = jnp.concatenate([amp_matrix, like_matrix], axis=1).T.reshape(-1, peers, slices)
    weights = weights[:, me ^ jnp.arange(peers)].reshape(-1, peers * slices)
    result, tokens = [], []

    def finish(group):
        inner, start, stop = group
        place = jnp.where((me == peers - 1) != (inner == 1), block - REACH, 0) + start
        parts = []
        for k in range(peers):
            for piece in (group, INNER, OUTER):
                if (k, piece) in arrived and piece[0] == inner:
                    parts.append((arrived[k, piece], start - piece[1]))
                    break
        *result[:], token = project(place, weights, parts, stop - start, block, result)
        tokens.append(token)

    for at, (k, piece, wait) in enumerate(ORDER):
        if (k, piece) in arrived:
            continue
        before = [] if wait is None else [arrived[ORDER[wait][:2]]]
        if at == len(ORDER) - 3:
            finish(GROUPS[0])
            finish(GROUPS[1])
            before.append(tokens[1])
        send(k, piece, *before)
    finish(GROUPS[2])
    finish(GROUPS[3])
    return tuple(result)


def extended(shard, sides, width):
    for axis, dim in sides:
        size, length = (lax.axis_size(axis), shard.shape[dim])
        up = [(i, (i + 1) % size) for i in range(size - 1)]
        down = [(j, i) for i, j in up]
        last = lax.slice_in_dim(shard, length - width, length, axis=dim)
        initial = lax.slice_in_dim(shard, 0, width, axis=dim)
        before = lax.ppermute(last, axis, up)
        after = lax.ppermute(initial, axis, down)
        shard = jnp.concatenate([before, shard, after], axis=dim)
    return shard


def band_matrix(taps, out_count, in_count):
    offset = lax.broadcasted_iota(jnp.int32, (out_count, in_count), 1) - lax.broadcasted_iota(
        jnp.int32, (out_count, in_count), 0
    )
    positions = lax.broadcasted_iota(jnp.int32, (1, 1, TAPS), 2)
    choose = (offset[:, :, None] == positions).astype(jnp.bfloat16)
    return jnp.einsum("ijt,kst->ksij", choose, taps, preferred_element_type=jnp.float32).astype(jnp.bfloat16)


def filter_field(padded, row_taps, col_taps):
    tall = padded.shape[1]
    cols = padded.shape[2]
    width = 2 * LANES
    row_band = band_matrix(row_taps, tall - HALO, tall)
    rowed = jnp.einsum("ksij,sjc->ksic", row_band, padded, preferred_element_type=jnp.float32).astype(jnp.bfloat16)
    widened = jnp.pad(rowed, ((0, 0), (0, 0), (0, 0), (REACH, REACH)))
    col_band = band_matrix(col_taps, width, width + HALO)
    pieces = []
    for begin in range(0, cols, width):
        segment = widened[:, :, :, begin : begin + width + HALO]
        pieces.append(jnp.einsum("ksrj,ksij->sri", segment, col_band, preferred_element_type=jnp.float32))
    return jnp.concatenate(pieces, axis=2).astype(jnp.bfloat16)


def general(density, valid, row_taps, col_taps, amp_matrix, like_matrix):
    slices, rows, cols = density.shape
    mask = valid.astype(jnp.float32)
    field = density.astype(jnp.float32)
    sums, count = lax.psum((jnp.sum(field * mask[None], axis=(1, 2)), jnp.sum(mask)), "tile")
    masked = (mask[None] * (field - (sums / count)[:, None, None])).astype(jnp.bfloat16)
    filtered = filter_field(extended(masked, (("tile", 1),), REACH), row_taps, col_taps)
    peers = lax.axis_size("cuts")
    share = rows * cols // peers
    pencil = lax.all_to_all(
        filtered.reshape(slices, peers, share), "cuts", split_axis=1, concat_axis=0, tiled=True
    ).reshape(slices * peers, share)
    amp = jnp.dot(amp_matrix.T, pencil, preferred_element_type=jnp.float32)
    like = amp * jnp.dot(like_matrix.T, pencil, preferred_element_type=jnp.float32)
    return amp.astype(jnp.bfloat16), like.astype(jnp.bfloat16)


def per_device(density, valid, row_taps, col_taps, amp_matrix, like_matrix):
    slices, rows, cols = density.shape
    terms = row_taps.shape[0]
    peers = lax.axis_size("cuts")
    fits = (
        peers == 8
        and lax.axis_size("tile") == 4
        and slices == 2 * GROUP
        and terms == 4
        and rows == peers * (LANES // terms - HALO)
        and cols % (2 * LANES) == 0
    )
    run = fast if fits else general
    return run(density, valid, row_taps, col_taps, amp_matrix, like_matrix)


def solution(mesh):
    return jax.shard_map(
        per_device,
        mesh=mesh,
        in_specs=(
            P("cuts", "tile", None),
            P("tile", None),
            P(None, "cuts", None),
            P(None, "cuts", None),
            P(),
            P(),
        ),
        out_specs=(P(None, ("tile", "cuts")), P(None, ("tile", "cuts"))),
        check_vma=False,
    )
```

```python
import functools

import jax
import jax.numpy as jnp
from jax import lax
from jax.experimental import pallas as pl
from jax.experimental.pallas import tpu as pltpu
from jax.sharding import PartitionSpec as P

REACH = 8
TAPS = 2 * REACH + 1
LANES = 128
GROUP = 8
PER = 4
PAIR = 2
CHUNKS = 8
BEFORE_BAND = 2e9
MIB = 1024 * 1024
HALO = 2 * REACH


def params(mib=24):
    return pltpu.CompilerParams(vmem_limit_bytes=mib * MIB)


def hbm(shape, dtype):
    return pltpu.HBM(shape, dtype)


def held(x):
    return pltpu.with_memory_space_constraint(x, pltpu.HBM)


def anywhere():
    return pl.BlockSpec(memory_space=pl.ANY)


def cost(flops, moved):
    return pl.CostEstimate(flops=int(flops), bytes_accessed=int(moved), transcendentals=0)


def tap_flip():
    tap = lax.broadcasted_iota(jnp.int32, (TAPS, 2 * LANES), 0)
    lane = lax.broadcasted_iota(jnp.int32, (TAPS, 2 * LANES), 1)
    return (lax.rem(tap + lane, 2 * LANES) == 0).astype(jnp.bfloat16)


def column_band(taps):
    band = pltpu.roll(jnp.broadcast_to(taps, (LANES + HALO, 2 * LANES)), 0, 1, stride=1, stride_axis=0)
    return band[:, :LANES].astype(jnp.bfloat16)


def build_columns(col_taps, col_out):
    terms, slices = len(col_taps), col_taps[0].shape[0]
    for k in range(terms):
        base = jnp.dot(col_taps[k], tap_flip(), preferred_element_type=jnp.float32)
        for s in range(slices):
            col_out[s, : LANES + HALO, k * LANES : (k + 1) * LANES] = column_band(base[s : s + 1])
    for s in range(slices):
        col_out[s, LANES + HALO :, :] = jnp.zeros((LANES - HALO, terms * LANES), jnp.bfloat16)


def build_rows(row_taps, row_out):
    terms, slices = len(row_taps), row_taps[0].shape[0]
    high = LANES // terms
    tap = lax.broadcasted_iota(jnp.int32, (TAPS, LANES), 0)
    lane = lax.broadcasted_iota(jnp.int32, (TAPS, LANES), 1)
    base = jnp.zeros((slices, LANES), jnp.float32)
    for k in range(terms):
        place = (lane == tap + k * high).astype(jnp.bfloat16)
        base = base + jnp.dot(row_taps[k], place, preferred_element_type=jnp.float32)
    sub = lax.broadcasted_iota(jnp.int32, (GROUP, LANES), 0)
    for g in range(slices // GROUP):
        own = base[g * GROUP : (g + 1) * GROUP]
        for pair in range(row_out.shape[1] // (2 * GROUP)):
            shifted = [pltpu.roll(own, 2 * pair + h, 1) for h in range(2)]
            for s in range(GROUP):
                both = jnp.concatenate([jnp.where(sub == s, x, 0.0) for x in shifted], axis=0)
                row_out[
                    g, pair * 2 * GROUP : (pair + 1) * 2 * GROUP, s * LANES : (s + 1) * LANES
                ] = both.astype(jnp.bfloat16)


def listed(taps):
    return [taps[k] for k in range(taps.shape[0])]


def matrix_shapes(terms, slices, rows):
    return (slices, 2 * LANES, terms * LANES), (slices // GROUP, rows * GROUP, GROUP * LANES)


def convolve(field, col, row, tall, rows):
    slices, _, wide = col.shape
    terms = wide // LANES
    high, cols = LANES // terms, tall.shape[1]
    parts = []
    for g in range(slices // GROUP):
        for j in range(GROUP):
            s = g * GROUP + j
            x = jnp.concatenate([field(s), jnp.zeros((high, LANES), jnp.float32)], axis=1)
            x = pltpu.roll(x, REACH, 1).astype(jnp.bfloat16)
            x = jnp.concatenate([x[:, c : c + 2 * LANES] for c in range(0, cols, LANES)], axis=0)
            y = jnp.dot(x, col[s], preferred_element_type=jnp.float32).astype(jnp.bfloat16)
            for c in range(cols // LANES):
                for k in range(terms):
                    tall[(j * terms + k) * high : (j * terms + k + 1) * high, c * LANES : (c + 1) * LANES] = y[
                        c * high : (c + 1) * high, k * LANES : (k + 1) * LANES
                    ]
        z = jnp.dot(row[g, : rows * GROUP], tall[...], preferred_element_type=jnp.float32)
        parts.append(z.reshape(rows, GROUP, cols))
    return jnp.concatenate(parts, axis=1)


def sums_kernel(density, valid, out, first, last, cube, plane, sems):
    slices, rows, cols = cube.shape
    step = rows // CHUNKS

    def copies(i):
        at = pl.ds(pl.multiple_of(i * step, step), step)
        yield pltpu.make_async_copy(density.at[:, at], cube.at[:, at], sems.at[i])
        yield pltpu.make_async_copy(valid.at[at], plane.at[at], sems.at[CHUNKS + i])

    for i in range(CHUNKS):
        for copy in copies(i):
            copy.start()
    out[...] = jnp.zeros_like(out)

    def body(i, _):
        for copy in copies(i):
            copy.wait()
        at = pl.ds(pl.multiple_of(i * step, step), step)
        mask = plane[at] != 0
        for s in range(slices + 1):
            x = cube[s, at].astype(jnp.float32) if s < slices else jnp.ones((step, cols), jnp.float32)
            x = jnp.where(mask, x, 0.0).reshape(step // 8, 8, cols).sum(axis=0)
            x = sum(x[:, c : c + LANES] for c in range(0, cols, LANES))
            out[s : s + 1, :] += jnp.sum(x, axis=0, keepdims=True)
        return 0

    lax.fori_loop(0, CHUNKS, body, 0)
    first[:slices] = cube[:, :REACH]
    first[slices] = plane[:REACH].astype(jnp.bfloat16)
    last[:slices] = cube[:, rows - REACH :]
    last[slices] = plane[rows - REACH :].astype(jnp.bfloat16)


def masked_sums(density, valid):
    slices, rows, cols = density.shape
    edge = hbm((slices + 1, REACH, cols), jnp.bfloat16)
    return pl.pallas_call(
        sums_kernel,
        name="sums",
        in_specs=[anywhere()] * 2,
        out_specs=[pl.BlockSpec(memory_space=pltpu.VMEM)] * 3,
        out_shape=[hbm((slices + 8, LANES), jnp.float32), edge, edge],
        scratch_shapes=[
            pltpu.VMEM(density.shape, jnp.bfloat16),
            pltpu.VMEM(valid.shape, jnp.int32),
            pltpu.SemaphoreType.DMA((2 * CHUNKS,)),
        ],
        compiler_params=params(),
        cost_estimate=cost(1, 1),
    )(held(density), held(valid))


def mean_kernel(*refs):
    sums, out = refs[:4], refs[-1]
    slices = out.shape[0]
    total = sums[0][...] + sums[1][...] + sums[2][...] + sums[3][...]
    total = jnp.sum(total, axis=1, keepdims=True)
    out[...] = jnp.broadcast_to(total[:slices] / total[slices : slices + 1], out.shape)


def means(sums, slices):
    return pl.pallas_call(
        mean_kernel,
        name="means",
        out_shape=jax.ShapeDtypeStruct((slices, LANES), jnp.float32),
        compiler_params=params(),
        cost_estimate=cost(1, 1),
    )(*sums)


def inner_rows(both, last):
    both = both.astype(jnp.float32)
    rows = both.shape[0] - REACH
    chosen = jnp.where(last, both[REACH:], both[:rows])
    return jnp.concatenate([chosen, jnp.zeros((REACH, both.shape[1]), jnp.float32)], axis=0)


def inner_kernel(pieces, ids, density, valid, row_taps, col_taps, mean, *refs):
    (col, row, tall, cube, plane, sems) = refs[-6:]
    count, slices, high, _ = cube.shape
    outs = list(refs[-6 - sum(len(wanted) for wanted in pieces) : -6])
    block = high // 2
    copies = []
    for b in range(count):
        here = pl.ds(pl.multiple_of(jnp.minimum(ids[b], ids[count] - 1) * block, block), high)
        copies.append(pltpu.make_async_copy(density.at[:, here], cube.at[b], sems.at[2 * b]))
        copies.append(pltpu.make_async_copy(valid.at[here], plane.at[b], sems.at[2 * b + 1]))
    for copy in copies:
        copy.start()
    build_columns(listed(col_taps), col)
    build_rows(listed(row_taps), row)
    for copy in copies:
        copy.wait()
    for b, wanted in enumerate(pieces):
        last = ids[b] == ids[count]
        mask = inner_rows(plane[b], last)
        field = convolve(
            lambda s, b=b, last=last, mask=mask: mask * (inner_rows(cube[b, s], last) - mean[s : s + 1, :1]),
            col,
            row,
            tall,
            REACH,
        ).astype(jnp.bfloat16)
        for _, start, stop in wanted:
            outs.pop(0)[...] = field[start:stop]


def filter_inner(ids, pieces, density, valid, row_taps, col_taps, mean, *after):
    slices, rows, cols = density.shape
    terms = row_taps.shape[0]
    high = LANES // terms
    count = ids.shape[0]

    def whole(x):
        return pl.BlockSpec(x.shape, lambda i, at: (0,) * x.ndim)

    shapes = [(stop - start, slices, cols) for wanted in pieces for _, start, stop in wanted]
    out = pl.pallas_call(
        functools.partial(inner_kernel, pieces),
        name="inner",
        grid_spec=pltpu.PrefetchScalarGridSpec(
            num_scalar_prefetch=1,
            grid=(1,),
            in_specs=[anywhere()] * 2 + [whole(x) for x in (row_taps, col_taps, mean)] + [anywhere()] * len(after),
            out_specs=[pl.BlockSpec(shape, lambda i, at: (0, 0, 0)) for shape in shapes],
            scratch_shapes=[pltpu.VMEM(x, jnp.bfloat16) for x in matrix_shapes(terms, slices, REACH)]
            + [
                pltpu.VMEM((GROUP * LANES, cols), jnp.bfloat16),
                pltpu.VMEM((count, slices, high, cols), jnp.bfloat16),
                pltpu.VMEM((count, high, cols), jnp.int32),
                pltpu.SemaphoreType.DMA((2 * count,)),
            ],
        ),
        out_shape=[hbm(shape, jnp.bfloat16) for shape in shapes],
        compiler_params=params(),
        cost_estimate=cost(1, 1),
    )(
        jnp.concatenate([ids, jnp.full((1,), rows // (high - HALO) - 1, ids.dtype)]),
        held(density),
        held(valid),
        row_taps,
        col_taps,
        mean,
        *after,
    )
    out = list(out)
    return [[out.pop(0) for _ in wanted] for wanted in pieces]


def band_kernel(pieces, ids, density, valid, above, below, row_taps, col_taps, mean, *refs):
    (col, row, taps, mask, tall, done, sems) = refs[-7:]
    count = sum(len(wanted) for wanted in pieces)
    outs = refs[-7 - count : -7]
    slices = mean.shape[0]
    rows, cols = valid.shape
    terms = row_taps.shape[0]
    block = done.shape[1]
    high = block + HALO
    step = pl.program_id(0)
    f32 = jnp.float32

    @pl.when(step == 0)
    def _():
        for k in range(terms):
            taps[:, k] = jnp.dot(col_taps[k], tap_flip(), preferred_element_type=f32)
        col[:, LANES + HALO :, :] = jnp.zeros((PER, LANES - HALO, terms * LANES), jnp.bfloat16)
        build_rows(listed(row_taps), row)
        mask[:REACH] = above[slices].astype(f32)
        mask[REACH : REACH + rows] = valid[...].astype(f32)
        mask[REACH + rows :] = below[slices].astype(f32)

    steps = slices // PER

    @pl.when(step < steps)
    def _():
        for j in range(PER):
            s = step * PER + j
            mine = taps[s]
            for k in range(terms):
                col[j, : LANES + HALO, k * LANES : (k + 1) * LANES] = column_band(mine[k : k + 1])
            x = jnp.concatenate([above[s].astype(f32), density[j].astype(f32), below[s].astype(f32)], axis=0)
            x = mask[...] * (x - mean[pl.ds(s, 1), :][:, :1])
            x = jnp.concatenate([x, jnp.zeros((rows + HALO, LANES), f32)], axis=1)
            x = pltpu.roll(x, REACH, 1).astype(jnp.bfloat16)
            x = jnp.concatenate([x[:, c : c + 2 * LANES] for c in range(0, cols, LANES)], axis=0)
            y = jnp.dot(x, col[j], preferred_element_type=f32).astype(jnp.bfloat16)
            for c in range(cols // LANES):
                for k in range(terms):
                    tall[s * terms + k, :, c * LANES : (c + 1) * LANES] = y[
                        c * (rows + HALO) : (c + 1) * (rows + HALO), k * LANES : (k + 1) * LANES
                    ]

    def copies(b):
        at = sum(len(wanted) for wanted in pieces[:b])
        last = ids[b] == ids[len(pieces)]
        for p, (inner, start, stop) in enumerate(pieces[b]):
            here = jnp.where(last != (inner == 1), block - REACH, 0) + start
            yield pltpu.make_async_copy(done.at[b, pl.ds(here, stop - start)], outs[at + p], sems.at[at + p])

    @pl.when(step >= steps)
    def _():
        for j in range(PAIR):
            b = (step - steps) * PAIR + j
            here = pl.ds(pl.multiple_of(ids[b] * block, block), high)
            parts = []
            for g in range(slices // GROUP):
                slab = tall[g * GROUP * terms : (g + 1) * GROUP * terms, here, :].reshape(GROUP * LANES, cols)
                z = jnp.dot(row[g], slab, preferred_element_type=f32)
                parts.append(z.reshape(block, GROUP, cols))
            done[b] = jnp.concatenate(parts, axis=1).astype(jnp.bfloat16)

    for n in range(len(pieces) // PAIR):

        @pl.when(step == steps + n)
        def _():
            for b in range(n * PAIR, (n + 1) * PAIR):
                for copy in copies(b):
                    copy.start()

    @pl.when(step == pl.num_programs(0) - 1)
    def _():
        for b in range(len(pieces)):
            for copy in copies(b):
                copy.wait()


def filter_band(ids, pieces, density, valid, above, below, row_taps, col_taps, mean, *after):
    slices, rows, cols = density.shape
    terms = row_taps.shape[0]
    block = LANES // terms - HALO
    count = len(pieces)

    def whole(x):
        return pl.BlockSpec(x.shape, lambda i, at: (0,) * x.ndim, pipeline_mode=pl.Buffered(1))

    shapes = [(stop - start, slices, cols) for wanted in pieces for _, start, stop in wanted]
    out = pl.pallas_call(
        functools.partial(band_kernel, pieces),
        name="band",
        grid_spec=pltpu.PrefetchScalarGridSpec(
            num_scalar_prefetch=1,
            grid=(slices // PER + count // PAIR,),
            in_specs=[pl.BlockSpec((PER, rows, cols), lambda i, at: (jnp.minimum(i, slices // PER - 1), 0, 0))]
            + [whole(x) for x in (valid, above, below, row_taps, col_taps, mean)]
            + [anywhere()] * len(after),
            out_specs=[anywhere()] * len(shapes),
            scratch_shapes=[
                pltpu.VMEM((PER, 2 * LANES, terms * LANES), jnp.bfloat16),
                pltpu.VMEM((slices // GROUP, block * GROUP, GROUP * LANES), jnp.bfloat16),
                pltpu.VMEM((slices, terms, 2 * LANES), jnp.float32),
                pltpu.VMEM((rows + HALO, cols), jnp.float32),
                pltpu.VMEM((slices * terms, rows + HALO, cols), jnp.bfloat16),
                pltpu.VMEM((count, block, slices, cols), jnp.bfloat16),
                pltpu.SemaphoreType.DMA((len(shapes),)),
            ],
        ),
        out_shape=[hbm(shape, jnp.bfloat16) for shape in shapes],
        compiler_params=params(44),
        cost_estimate=cost(1, 1),
    )(
        jnp.concatenate([ids, jnp.full((1,), rows // block - 1, ids.dtype)]),
        held(density),
        held(valid),
        above,
        below,
        row_taps,
        col_taps,
        mean,
        *after,
    )
    out = list(out)
    return [[out.pop(0) for _ in wanted] for wanted in pieces]


def project_kernel(count, place, weights, *refs):
    parts, (amp_out, like_out, token) = refs[:count], refs[-3:]
    zbins = weights.shape[0] // 2
    rows, _, cols = parts[0].shape
    for r in range(rows):
        pencil = jnp.concatenate([x[r] for x in parts], axis=0)
        both = jnp.dot(weights[...], pencil, preferred_element_type=jnp.float32)
        amp = both[:zbins]
        amp_out[:, r * cols : (r + 1) * cols] = amp.astype(jnp.bfloat16)
        like_out[:, r * cols : (r + 1) * cols] = (amp * both[zbins:]).astype(jnp.bfloat16)
    token[...] = jnp.zeros_like(token)


def project(place, weights, parts, rows, total, earlier):
    _, slices, cols = parts[0][0].shape
    zbins = weights.shape[0] // 2
    count = len(parts)
    shape = hbm((zbins, total * cols), jnp.bfloat16)
    return pl.pallas_call(
        functools.partial(project_kernel, count),
        name="project",
        grid_spec=pltpu.PrefetchScalarGridSpec(
            num_scalar_prefetch=1,
            grid=(rows // PAIR,),
            in_specs=[pl.BlockSpec(weights.shape, lambda i, at: (0, 0))]
            + [
                pl.BlockSpec((PAIR, slices, cols), lambda i, at, start=start: (i + start // PAIR, 0, 0))
                for _, start in parts
            ]
            + [anywhere()] * len(earlier),
            out_specs=[pl.BlockSpec((zbins, PAIR * cols), lambda i, at: (0, i + at[0] // PAIR))] * 2
            + [pl.BlockSpec((8, LANES), lambda i, at: (0, 0))],
        ),
        out_shape=[shape, shape, hbm((8, LANES), jnp.float32)],
        input_output_aliases={2 + count + i: i for i in range(len(earlier))},
        compiler_params=params(),
        cost_estimate=cost(1, 1),
    )(place.reshape(1), weights, *[x for x, _ in parts], *earlier)


def gate_kernel(*refs):
    pass


def gate(x, *earlier, flops=1):
    return pl.pallas_call(
        gate_kernel,
        name="gate",
        in_specs=[anywhere()] * (1 + len(earlier)),
        out_specs=anywhere(),
        out_shape=hbm(x.shape, x.dtype),
        input_output_aliases={0: 0},
        compiler_params=params(1),
        cost_estimate=cost(flops, 1),
    )(held(x), *earlier)


INNER, OUTER = (1, 0, REACH), (0, 0, REACH)
HEAD, TAIL = (0, 0, 6), (0, 6, REACH)
FIRST = (((4, (INNER,)),), ((6, (INNER,)), (5, (INNER,))))
REST = (
    (5, (HEAD, TAIL)),
    (7, (INNER, HEAD, TAIL)),
    (2, (INNER, OUTER)),
    (3, (INNER, OUTER)),
    (4, (HEAD, TAIL)),
    (6, (HEAD, TAIL)),
    (1, (INNER, OUTER)),
    (0, (INNER, OUTER)),
)
ORDER = (
    (4, INNER, None),
    (6, INNER, None),
    (5, INNER, None),
    (7, INNER, 0),
    (2, INNER, 0),
    (4, HEAD, 1),
    (3, INNER, 1),
    (6, HEAD, 2),
    (2, OUTER, 2),
    (5, HEAD, 5),
    (1, INNER, 6),
    (7, HEAD, 7),
    (3, OUTER, 8),
    (1, OUTER, 9),
    (4, TAIL, 10),
    (6, TAIL, 11),
    (5, TAIL, 12),
    (7, TAIL, 13),
)


def fast(density, valid, row_taps, col_taps, amp_matrix, like_matrix):
    slices, rows, cols = density.shape
    peers = lax.axis_size("cuts")
    tiles = lax.axis_size("tile")
    block = rows // peers
    me = lax.axis_index("cuts").astype(jnp.int32)

    def swap(x, k):
        return lax.ppermute(x, "cuts", [(i, i ^ k) for i in range(peers)])

    own, first, last = masked_sums(density, valid)
    sums = [held(own)] + [lax.ppermute(own, "tile", [(i, i ^ k) for i in range(tiles)]) for k in range(1, tiles)]
    mean = means(sums, slices)

    made, arrived = {}, {}

    above = lax.ppermute(last, "tile", [(i, i + 1) for i in range(tiles - 1)])
    below = lax.ppermute(first, "tile", [(i + 1, i) for i in range(tiles - 1)])
    def ids(wanted):
        return jnp.stack([me ^ k for k, _ in wanted])

    def keep(wanted, got):
        for (k, cut), parts in zip(wanted, got):
            for piece, x in zip(cut, parts):
                made[k, piece] = x

    def send(k, piece, *before):
        x = made[k, piece]
        arrived[k, piece] = swap(gate(x, *before) if before else x, k)

    inputs = row_taps, col_taps, mean
    after = ()
    for wanted in FIRST:
        got = filter_inner(ids(wanted), [cut for _, cut in wanted], density, valid, *inputs, *after)
        keep(wanted, got)
        after = (held(got[0][0]),)
    first_piece = ORDER[0][:2]
    send(*first_piece)
    got = filter_band(
        ids(REST), [cut for _, cut in REST], density, valid, above, below, *inputs, *after, gate(mean, arrived[first_piece], flops=BEFORE_BAND)
    )
    keep(REST, got)
    for piece in (INNER, OUTER):
        arrived[0, piece] = made[0, piece]

    weights = jnp.concatenate([amp_matrix, like_matrix], axis=1).T.reshape(-1, peers, slices)
    weights = weights[:, me ^ jnp.arange(peers)].reshape(-1, peers * slices)
    result, tokens = [], []

    def finish(group):
        inner, start, stop = group
        place = jnp.where((me == peers - 1) != (inner == 1), block - REACH, 0) + start
        parts = []
        for k in range(peers):
            for piece in (group, INNER, OUTER):
                if (k, piece) in arrived and piece[0] == inner:
                    parts.append((arrived[k, piece], start - piece[1]))
                    break
        *result[:], token = project(place, weights, parts, stop - start, block, result)
        tokens.append(token)

    for at, (k, piece, wait) in enumerate(ORDER):
        if (k, piece) in arrived:
            continue
        before = [] if wait is None else [arrived[ORDER[wait][:2]]]
        if at == len(ORDER) - 3:
            finish(INNER)
            before.append(tokens[0])
        send(k, piece, *before)
    finish(HEAD)
    finish(TAIL)
    return tuple(result)


def extended(shard, sides, width):
    for axis, dim in sides:
        size, length = (lax.axis_size(axis), shard.shape[dim])
        up = [(i, (i + 1) % size) for i in range(size - 1)]
        down = [(j, i) for i, j in up]
        last = lax.slice_in_dim(shard, length - width, length, axis=dim)
        initial = lax.slice_in_dim(shard, 0, width, axis=dim)
        before = lax.ppermute(last, axis, up)
        after = lax.ppermute(initial, axis, down)
        shard = jnp.concatenate([before, shard, after], axis=dim)
    return shard


def band_matrix(taps, out_count, in_count):
    offset = lax.broadcasted_iota(jnp.int32, (out_count, in_count), 1) - lax.broadcasted_iota(
        jnp.int32, (out_count, in_count), 0
    )
    positions = lax.broadcasted_iota(jnp.int32, (1, 1, TAPS), 2)
    choose = (offset[:, :, None] == positions).astype(jnp.bfloat16)
    return jnp.einsum("ijt,kst->ksij", choose, taps, preferred_element_type=jnp.float32).astype(jnp.bfloat16)


def filter_field(padded, row_taps, col_taps):
    tall = padded.shape[1]
    cols = padded.shape[2]
    width = 2 * LANES
    row_band = band_matrix(row_taps, tall - HALO, tall)
    rowed = jnp.einsum("ksij,sjc->ksic", row_band, padded, preferred_element_type=jnp.float32).astype(jnp.bfloat16)
    widened = jnp.pad(rowed, ((0, 0), (0, 0), (0, 0), (REACH, REACH)))
    col_band = band_matrix(col_taps, width, width + HALO)
    pieces = []
    for begin in range(0, cols, width):
        segment = widened[:, :, :, begin : begin + width + HALO]
        pieces.append(jnp.einsum("ksrj,ksij->sri", segment, col_band, preferred_element_type=jnp.float32))
    return jnp.concatenate(pieces, axis=2).astype(jnp.bfloat16)


def general(density, valid, row_taps, col_taps, amp_matrix, like_matrix):
    slices, rows, cols = density.shape
    mask = valid.astype(jnp.float32)
    field = density.astype(jnp.float32)
    sums, count = lax.psum((jnp.sum(field * mask[None], axis=(1, 2)), jnp.sum(mask)), "tile")
    masked = (mask[None] * (field - (sums / count)[:, None, None])).astype(jnp.bfloat16)
    filtered = filter_field(extended(masked, (("tile", 1),), REACH), row_taps, col_taps)
    peers = lax.axis_size("cuts")
    share = rows * cols // peers
    pencil = lax.all_to_all(
        filtered.reshape(slices, peers, share), "cuts", split_axis=1, concat_axis=0, tiled=True
    ).reshape(slices * peers, share)
    amp = jnp.dot(amp_matrix.T, pencil, preferred_element_type=jnp.float32)
    like = amp * jnp.dot(like_matrix.T, pencil, preferred_element_type=jnp.float32)
    return amp.astype(jnp.bfloat16), like.astype(jnp.bfloat16)


def per_device(density, valid, row_taps, col_taps, amp_matrix, like_matrix):
    slices, rows, cols = density.shape
    terms = row_taps.shape[0]
    peers = lax.axis_size("cuts")
    fits = (
        peers == 8
        and lax.axis_size("tile") == 4
        and slices == 2 * GROUP
        and terms == 4
        and rows == peers * (LANES // terms - HALO)
        and cols % (2 * LANES) == 0
    )
    run = fast if fits else general
    return run(density, valid, row_taps, col_taps, amp_matrix, like_matrix)


def solution(mesh):
    return jax.shard_map(
        per_device,
        mesh=mesh,
        in_specs=(
            P("cuts", "tile", None),
            P("tile", None),
            P(None, "cuts", None),
            P(None, "cuts", None),
            P(),
            P(),
        ),
        out_specs=(P(None, ("tile", "cuts")), P(None, ("tile", "cuts"))),
        check_vma=False,
    )
```

```python
import functools

import jax
import jax.numpy as jnp
from jax import lax
from jax.experimental import pallas as pl
from jax.experimental.pallas import tpu as pltpu
from jax.sharding import PartitionSpec as P

REACH = 8
TAPS = 2 * REACH + 1
LANES = 128
GROUP = 8
PER = 4
PAIR = 2
CHUNKS = 8
BEFORE_BAND = 2e9
MIB = 1024 * 1024
HALO = 2 * REACH


def params(mib=24):
    return pltpu.CompilerParams(vmem_limit_bytes=mib * MIB)


def hbm(shape, dtype):
    return pltpu.HBM(shape, dtype)


def held(x):
    return pltpu.with_memory_space_constraint(x, pltpu.HBM)


def resident(x):
    return pltpu.with_memory_space_constraint(x, pltpu.VMEM)


def anywhere():
    return pl.BlockSpec(memory_space=pl.ANY)


def cost(flops, moved):
    return pl.CostEstimate(flops=int(flops), bytes_accessed=int(moved), transcendentals=0)


def tap_flip():
    tap = lax.broadcasted_iota(jnp.int32, (TAPS, 2 * LANES), 0)
    lane = lax.broadcasted_iota(jnp.int32, (TAPS, 2 * LANES), 1)
    return (lax.rem(tap + lane, 2 * LANES) == 0).astype(jnp.bfloat16)


def column_band(taps):
    band = pltpu.roll(jnp.broadcast_to(taps, (LANES + HALO, 2 * LANES)), 0, 1, stride=1, stride_axis=0)
    return band[:, :LANES].astype(jnp.bfloat16)


def build_columns(col_taps, col_out):
    terms, slices = len(col_taps), col_taps[0].shape[0]
    for k in range(terms):
        base = jnp.dot(col_taps[k], tap_flip(), preferred_element_type=jnp.float32)
        for s in range(slices):
            col_out[s, : LANES + HALO, k * LANES : (k + 1) * LANES] = column_band(base[s : s + 1])
    for s in range(slices):
        col_out[s, LANES + HALO :, :] = jnp.zeros((LANES - HALO, terms * LANES), jnp.bfloat16)


def build_rows(row_taps, row_out):
    terms, slices = len(row_taps), row_taps[0].shape[0]
    high = LANES // terms
    tap = lax.broadcasted_iota(jnp.int32, (TAPS, LANES), 0)
    lane = lax.broadcasted_iota(jnp.int32, (TAPS, LANES), 1)
    base = jnp.zeros((slices, LANES), jnp.float32)
    for k in range(terms):
        place = (lane == tap + k * high).astype(jnp.bfloat16)
        base = base + jnp.dot(row_taps[k], place, preferred_element_type=jnp.float32)
    sub = lax.broadcasted_iota(jnp.int32, (GROUP, LANES), 0)
    for g in range(slices // GROUP):
        own = base[g * GROUP : (g + 1) * GROUP]
        for pair in range(row_out.shape[1] // (2 * GROUP)):
            shifted = [pltpu.roll(own, 2 * pair + h, 1) for h in range(2)]
            for s in range(GROUP):
                both = jnp.concatenate([jnp.where(sub == s, x, 0.0) for x in shifted], axis=0)
                row_out[
                    g, pair * 2 * GROUP : (pair + 1) * 2 * GROUP, s * LANES : (s + 1) * LANES
                ] = both.astype(jnp.bfloat16)


def listed(taps):
    return [taps[k] for k in range(taps.shape[0])]


def matrix_shapes(terms, slices, rows):
    return (slices, 2 * LANES, terms * LANES), (slices // GROUP, rows * GROUP, GROUP * LANES)


def convolve(field, col, row, tall, rows):
    slices, _, wide = col.shape
    terms = wide // LANES
    high, cols = LANES // terms, tall.shape[1]
    parts = []
    for g in range(slices // GROUP):
        for j in range(GROUP):
            s = g * GROUP + j
            x = jnp.concatenate([field(s), jnp.zeros((high, LANES), jnp.float32)], axis=1)
            x = pltpu.roll(x, REACH, 1).astype(jnp.bfloat16)
            x = jnp.concatenate([x[:, c : c + 2 * LANES] for c in range(0, cols, LANES)], axis=0)
            y = jnp.dot(x, col[s], preferred_element_type=jnp.float32).astype(jnp.bfloat16)
            for c in range(cols // LANES):
                for k in range(terms):
                    tall[(j * terms + k) * high : (j * terms + k + 1) * high, c * LANES : (c + 1) * LANES] = y[
                        c * high : (c + 1) * high, k * LANES : (k + 1) * LANES
                    ]
        z = jnp.dot(row[g, : rows * GROUP], tall[...], preferred_element_type=jnp.float32)
        parts.append(z.reshape(rows, GROUP, cols))
    return jnp.concatenate(parts, axis=1)


def sums_kernel(density, valid, out, first, last, cube, plane, sems):
    slices, rows, cols = cube.shape
    step = rows // CHUNKS

    def copies(i):
        at = pl.ds(pl.multiple_of(i * step, step), step)
        yield pltpu.make_async_copy(density.at[:, at], cube.at[:, at], sems.at[i])
        yield pltpu.make_async_copy(valid.at[at], plane.at[at], sems.at[CHUNKS + i])

    for i in range(CHUNKS):
        for copy in copies(i):
            copy.start()
    out[...] = jnp.zeros_like(out)

    def body(i, _):
        for copy in copies(i):
            copy.wait()
        at = pl.ds(pl.multiple_of(i * step, step), step)
        mask = plane[at] != 0
        for s in range(slices + 1):
            x = cube[s, at].astype(jnp.float32) if s < slices else jnp.ones((step, cols), jnp.float32)
            x = jnp.where(mask, x, 0.0).reshape(step // 8, 8, cols).sum(axis=0)
            x = sum(x[:, c : c + LANES] for c in range(0, cols, LANES))
            out[s : s + 1, :] += jnp.sum(x, axis=0, keepdims=True)
        return 0

    lax.fori_loop(0, CHUNKS, body, 0)
    first[:slices] = cube[:, :REACH]
    first[slices] = plane[:REACH].astype(jnp.bfloat16)
    last[:slices] = cube[:, rows - REACH :]
    last[slices] = plane[rows - REACH :].astype(jnp.bfloat16)


def masked_sums(density, valid):
    slices, rows, cols = density.shape
    edge = hbm((slices + 1, REACH, cols), jnp.bfloat16)
    return pl.pallas_call(
        sums_kernel,
        name="sums",
        in_specs=[anywhere()] * 2,
        out_specs=[pl.BlockSpec(memory_space=pltpu.VMEM)] * 3,
        out_shape=[jax.ShapeDtypeStruct((slices + 8, LANES), jnp.float32), edge, edge],
        scratch_shapes=[
            pltpu.VMEM(density.shape, jnp.bfloat16),
            pltpu.VMEM(valid.shape, jnp.int32),
            pltpu.SemaphoreType.DMA((2 * CHUNKS,)),
        ],
        compiler_params=params(),
        cost_estimate=cost(1, 1),
    )(held(density), held(valid))


def mean_kernel(*refs):
    sums, out = refs[:4], refs[-1]
    slices = out.shape[0]
    total = sums[0][...] + sums[1][...] + sums[2][...] + sums[3][...]
    total = jnp.sum(total, axis=1, keepdims=True)
    out[...] = jnp.broadcast_to(total[:slices] / total[slices : slices + 1], out.shape)


def means(sums, slices, after):
    vmem = pl.BlockSpec(memory_space=pltpu.VMEM)
    return pl.pallas_call(
        mean_kernel,
        name="means",
        in_specs=[vmem] * len(sums) + [anywhere()],
        out_specs=vmem,
        out_shape=jax.ShapeDtypeStruct((slices, LANES), jnp.float32),
        compiler_params=params(1),
        cost_estimate=cost(1, 1),
    )(*sums, resident(after))


def inner_rows(both, last):
    both = both.astype(jnp.float32)
    rows = both.shape[0] - REACH
    chosen = jnp.where(last, both[REACH:], both[:rows])
    return jnp.concatenate([chosen, jnp.zeros((REACH, both.shape[1]), jnp.float32)], axis=0)


def window_copies(ids, b, last, density, valid, cube, plane, sems):
    high = plane.shape[1]
    here = pl.ds(pl.multiple_of(jnp.minimum(ids[b], last - 1) * (high // 2), high // 2), high)
    return [
        pltpu.make_async_copy(density.at[:, here], cube.at[b], sems.at[2 * b]),
        pltpu.make_async_copy(valid.at[here], plane.at[b], sems.at[2 * b + 1]),
    ]


def ready_kernel(ids, density, valid, row_taps, col_taps, after, col, row, cube, plane, sems):
    copies = window_copies(ids, 0, ids[1], density, valid, cube, plane, sems)
    for copy in copies:
        copy.start()
    build_columns(listed(col_taps), col)
    build_rows(listed(row_taps), row)
    for copy in copies:
        copy.wait()


def make_ready(ids, density, valid, row_taps, col_taps, after):
    slices, rows, cols = density.shape
    terms = row_taps.shape[0]
    high = LANES // terms
    vmem = pl.BlockSpec(memory_space=pltpu.VMEM)
    shapes = *matrix_shapes(terms, slices, high - HALO), (1, slices, high, cols)
    return pl.pallas_call(
        ready_kernel,
        name="ready",
        in_specs=[pl.BlockSpec(memory_space=pltpu.SMEM)] + [anywhere()] * 2 + [vmem] * 2 + [anywhere()],
        out_specs=[vmem] * 4,
        out_shape=[pltpu.VMEM(shape, jnp.bfloat16) for shape in shapes] + [pltpu.VMEM((1, high, cols), jnp.int32)],
        scratch_shapes=[pltpu.SemaphoreType.DMA((2,))],
        compiler_params=params(),
        cost_estimate=cost(1, 1),
    )(jnp.stack([ids, jnp.full_like(ids, rows // (high - HALO) - 1)]), held(density), held(valid), row_taps, col_taps, after)


def inner_kernel(pieces, loaded, ids, *refs):
    count = len(pieces)
    outs = sum(len(wanted) for wanted in pieces)
    if loaded:
        (cube, plane, col, row, mean), tall = refs[:5], refs[-1]
        outs = list(refs[-1 - outs : -1])
    else:
        (density, valid, col, row, mean), (tall, cube, plane, sems) = refs[:5], refs[-4:]
        outs = list(refs[-4 - outs : -4])
        copies = [window_copies(ids, b, ids[count], density, valid, cube, plane, sems) for b in range(count)]
        for copy in sum(copies, []):
            copy.start()
    for b, wanted in enumerate(pieces):
        if not loaded:
            for copy in copies[b]:
                copy.wait()
        last = ids[b] == ids[count]
        mask = inner_rows(plane[b], last)
        field = convolve(
            lambda s, b=b, last=last, mask=mask: mask * (inner_rows(cube[b, s], last) - mean[s : s + 1, :1]),
            col,
            row,
            tall,
            REACH,
        ).astype(jnp.bfloat16)
        for _, start, stop in wanted:
            outs.pop(0)[...] = field[start:stop]


def filter_inner(ids, pieces, density, valid, ready, mean, *after):
    slices, rows, cols = density.shape
    col, row, cube, plane = ready
    high = plane.shape[1]
    count = ids.shape[0]
    loaded = not after
    vmem = pl.BlockSpec(memory_space=pltpu.VMEM)
    shapes = [(stop - start, slices, cols) for wanted in pieces for _, start, stop in wanted]
    field = [resident(cube), resident(plane)] if loaded else [held(density), held(valid)]
    scratch = [pltpu.VMEM((GROUP * LANES, cols), jnp.bfloat16)]
    if not loaded:
        scratch += [
            pltpu.VMEM((count, slices, high, cols), jnp.bfloat16),
            pltpu.VMEM((count, high, cols), jnp.int32),
            pltpu.SemaphoreType.DMA((2 * count,)),
        ]
    out = pl.pallas_call(
        functools.partial(inner_kernel, pieces, loaded),
        name="inner",
        in_specs=[pl.BlockSpec(memory_space=pltpu.SMEM)]
        + [vmem if loaded else anywhere()] * 2
        + [vmem] * 3
        + [anywhere()] * len(after),
        out_specs=[vmem] * len(shapes),
        out_shape=[hbm(shape, jnp.bfloat16) for shape in shapes],
        scratch_shapes=scratch,
        compiler_params=params(),
        cost_estimate=cost(1, 1),
    )(
        jnp.concatenate([ids, jnp.full((1,), rows // (high - HALO) - 1, ids.dtype)]),
        *field,
        resident(col),
        resident(row),
        mean,
        *after,
    )
    out = list(out)
    return [[out.pop(0) for _ in wanted] for wanted in pieces]


def band_kernel(pieces, ids, density, valid, above, below, col, row, mean, *refs):
    (mask, tall, done, sems) = refs[-4:]
    count = sum(len(wanted) for wanted in pieces)
    outs = refs[-4 - count : -4]
    slices = mean.shape[0]
    rows, cols = valid.shape
    terms = col.shape[2] // LANES
    block = done.shape[1]
    high = block + HALO
    step = pl.program_id(0)
    f32 = jnp.float32

    @pl.when(step == 0)
    def _():
        mask[:REACH] = above[slices].astype(f32)
        mask[REACH : REACH + rows] = valid[...].astype(f32)
        mask[REACH + rows :] = below[slices].astype(f32)

    steps = slices // PER

    @pl.when(step < steps)
    def _():
        for j in range(PER):
            s = step * PER + j
            x = jnp.concatenate([above[s].astype(f32), density[j].astype(f32), below[s].astype(f32)], axis=0)
            x = mask[...] * (x - mean[pl.ds(s, 1), :][:, :1])
            x = jnp.concatenate([x, jnp.zeros((rows + HALO, LANES), f32)], axis=1)
            x = pltpu.roll(x, REACH, 1).astype(jnp.bfloat16)
            x = jnp.concatenate([x[:, c : c + 2 * LANES] for c in range(0, cols, LANES)], axis=0)
            y = jnp.dot(x, col[s], preferred_element_type=f32).astype(jnp.bfloat16)
            for c in range(cols // LANES):
                for k in range(terms):
                    tall[s * terms + k, :, c * LANES : (c + 1) * LANES] = y[
                        c * (rows + HALO) : (c + 1) * (rows + HALO), k * LANES : (k + 1) * LANES
                    ]

    def copies(b):
        at = sum(len(wanted) for wanted in pieces[:b])
        last = ids[b] == ids[len(pieces)]
        for p, (inner, start, stop) in enumerate(pieces[b]):
            here = jnp.where(last != (inner == 1), block - REACH, 0) + start
            yield pltpu.make_async_copy(done.at[b, pl.ds(here, stop - start)], outs[at + p], sems.at[at + p])

    @pl.when(step >= steps)
    def _():
        for j in range(PAIR):
            b = (step - steps) * PAIR + j
            here = pl.ds(pl.multiple_of(ids[b] * block, block), high)
            parts = []
            for g in range(slices // GROUP):
                slab = tall[g * GROUP * terms : (g + 1) * GROUP * terms, here, :].reshape(GROUP * LANES, cols)
                z = jnp.dot(row[g], slab, preferred_element_type=f32)
                parts.append(z.reshape(block, GROUP, cols))
            done[b] = jnp.concatenate(parts, axis=1).astype(jnp.bfloat16)

    for n in range(len(pieces) // PAIR):

        @pl.when(step == steps + n)
        def _():
            for b in range(n * PAIR, (n + 1) * PAIR):
                for copy in copies(b):
                    copy.start()

    @pl.when(step == pl.num_programs(0) - 1)
    def _():
        for b in range(len(pieces)):
            for copy in copies(b):
                copy.wait()


def filter_band(ids, pieces, density, valid, above, below, ready, mean, *after):
    slices, rows, cols = density.shape
    col, row = ready[:2]
    terms = col.shape[2] // LANES
    block = LANES // terms - HALO
    count = len(pieces)

    def whole(x):
        return pl.BlockSpec(x.shape, lambda i, at: (0,) * x.ndim, pipeline_mode=pl.Buffered(1))

    shapes = [(stop - start, slices, cols) for wanted in pieces for _, start, stop in wanted]
    out = pl.pallas_call(
        functools.partial(band_kernel, pieces),
        name="band",
        grid_spec=pltpu.PrefetchScalarGridSpec(
            num_scalar_prefetch=1,
            grid=(slices // PER + count // PAIR,),
            in_specs=[pl.BlockSpec((PER, rows, cols), lambda i, at: (jnp.minimum(i, slices // PER - 1), 0, 0))]
            + [whole(x) for x in (valid, above, below)]
            + [pl.BlockSpec(memory_space=pltpu.VMEM)] * 2
            + [whole(mean)]
            + [anywhere()] * len(after),
            out_specs=[anywhere()] * len(shapes),
            scratch_shapes=[
                pltpu.VMEM((rows + HALO, cols), jnp.float32),
                pltpu.VMEM((slices * terms, rows + HALO, cols), jnp.bfloat16),
                pltpu.VMEM((count, block, slices, cols), jnp.bfloat16),
                pltpu.SemaphoreType.DMA((len(shapes),)),
            ],
        ),
        out_shape=[hbm(shape, jnp.bfloat16) for shape in shapes],
        compiler_params=params(44),
        cost_estimate=cost(1, 1),
    )(
        jnp.concatenate([ids, jnp.full((1,), rows // block - 1, ids.dtype)]),
        held(density),
        held(valid),
        above,
        below,
        resident(col),
        resident(row),
        mean,
        *after,
    )
    out = list(out)
    return [[out.pop(0) for _ in wanted] for wanted in pieces]


def project_kernel(count, place, weights, *refs):
    parts, (amp_out, like_out, token) = refs[:count], refs[-3:]
    zbins = weights.shape[0] // 2
    rows, _, cols = parts[0].shape
    for r in range(rows):
        pencil = jnp.concatenate([x[r] for x in parts], axis=0)
        both = jnp.dot(weights[...], pencil, preferred_element_type=jnp.float32)
        amp = both[:zbins]
        amp_out[:, r * cols : (r + 1) * cols] = amp.astype(jnp.bfloat16)
        like_out[:, r * cols : (r + 1) * cols] = (amp * both[zbins:]).astype(jnp.bfloat16)
    token[...] = jnp.zeros_like(token)


def project(place, weights, parts, rows, total, earlier):
    _, slices, cols = parts[0][0].shape
    zbins = weights.shape[0] // 2
    count = len(parts)
    shape = hbm((zbins, total * cols), jnp.bfloat16)
    return pl.pallas_call(
        functools.partial(project_kernel, count),
        name="project",
        grid_spec=pltpu.PrefetchScalarGridSpec(
            num_scalar_prefetch=1,
            grid=(rows // PAIR,),
            in_specs=[pl.BlockSpec(weights.shape, lambda i, at: (0, 0))]
            + [
                pl.BlockSpec((PAIR, slices, cols), lambda i, at, start=start: (i + start // PAIR, 0, 0))
                for _, start in parts
            ]
            + [anywhere()] * len(earlier),
            out_specs=[pl.BlockSpec((zbins, PAIR * cols), lambda i, at: (0, i + at[0] // PAIR))] * 2
            + [pl.BlockSpec((8, LANES), lambda i, at: (0, 0))],
        ),
        out_shape=[shape, shape, hbm((8, LANES), jnp.float32)],
        input_output_aliases={2 + count + i: i for i in range(len(earlier))},
        compiler_params=params(),
        cost_estimate=cost(1, 1),
    )(place.reshape(1), weights, *[x for x, _ in parts], *earlier)


def gate_kernel(*refs):
    pass


def gate(x, *earlier, flops=1):
    return pl.pallas_call(
        gate_kernel,
        name="gate",
        in_specs=[anywhere()] * (1 + len(earlier)),
        out_specs=anywhere(),
        out_shape=hbm(x.shape, x.dtype),
        input_output_aliases={0: 0},
        compiler_params=params(1),
        cost_estimate=cost(flops, 1),
    )(held(x), *earlier)


INNER, OUTER = (1, 0, REACH), (0, 0, REACH)
HEAD, TAIL = (0, 0, 6), (0, 6, REACH)
FIRST = (((4, (INNER,)),), ((6, (INNER,)), (5, (INNER,))))
REST = (
    (5, (HEAD, TAIL)),
    (7, (INNER, HEAD, TAIL)),
    (2, (INNER, OUTER)),
    (3, (INNER, OUTER)),
    (4, (HEAD, TAIL)),
    (6, (HEAD, TAIL)),
    (1, (INNER, OUTER)),
    (0, (INNER, OUTER)),
)
ORDER = (
    (4, INNER, None),
    (6, INNER, None),
    (5, INNER, None),
    (7, INNER, 0),
    (2, INNER, 1),
    (4, HEAD, 1),
    (3, INNER, 2),
    (6, HEAD, 2),
    (2, OUTER, 4),
    (5, HEAD, 3),
    (1, INNER, 6),
    (7, HEAD, 5),
    (3, OUTER, 6),
    (1, OUTER, 10),
    (4, TAIL, 7),
    (6, TAIL, 9),
    (5, TAIL, 11),
    (7, TAIL, 14),
)


def fast(density, valid, row_taps, col_taps, amp_matrix, like_matrix):
    slices, rows, cols = density.shape
    peers = lax.axis_size("cuts")
    tiles = lax.axis_size("tile")
    block = rows // peers
    me = lax.axis_index("cuts").astype(jnp.int32)

    def swap(x, k):
        return lax.ppermute(x, "cuts", [(i, i ^ k) for i in range(peers)])

    own, first, last = masked_sums(density, valid)
    sums = [own] + [lax.ppermute(own, "tile", [(i, i ^ k) for i in range(tiles)]) for k in range(1, tiles)]
    ready = make_ready(me ^ ORDER[0][0], density, valid, row_taps, col_taps, own)
    mean = means(sums, slices, ready[0])

    made, arrived = {}, {}

    above = lax.ppermute(last, "tile", [(i, i + 1) for i in range(tiles - 1)])
    below = lax.ppermute(first, "tile", [(i + 1, i) for i in range(tiles - 1)])
    def ids(wanted):
        return jnp.stack([me ^ k for k, _ in wanted])

    def keep(wanted, got):
        for (k, cut), parts in zip(wanted, got):
            for piece, x in zip(cut, parts):
                made[k, piece] = x

    def send(k, piece, *before):
        x = made[k, piece]
        arrived[k, piece] = swap(gate(x, *before) if before else x, k)

    after = ()
    for wanted in FIRST:
        got = filter_inner(ids(wanted), [cut for _, cut in wanted], density, valid, ready, mean, *after)
        keep(wanted, got)
        after = (held(got[0][0]),)
    first_piece = ORDER[0][:2]
    send(*first_piece)
    got = filter_band(
        ids(REST), [cut for _, cut in REST], density, valid, above, below, ready, mean, *after, gate(mean, arrived[first_piece], flops=BEFORE_BAND)
    )
    keep(REST, got)
    for piece in (INNER, OUTER):
        arrived[0, piece] = made[0, piece]

    weights = jnp.concatenate([amp_matrix, like_matrix], axis=1).T.reshape(-1, peers, slices)
    weights = weights[:, me ^ jnp.arange(peers)].reshape(-1, peers * slices)
    result, tokens = [], []

    def finish(group):
        inner, start, stop = group
        place = jnp.where((me == peers - 1) != (inner == 1), block - REACH, 0) + start
        parts = []
        for k in range(peers):
            for piece in (group, INNER, OUTER):
                if (k, piece) in arrived and piece[0] == inner:
                    parts.append((arrived[k, piece], start - piece[1]))
                    break
        *result[:], token = project(place, weights, parts, stop - start, block, result)
        tokens.append(token)

    for at, (k, piece, wait) in enumerate(ORDER):
        if (k, piece) in arrived:
            continue
        before = [] if wait is None else [arrived[ORDER[wait][:2]]]
        if at == len(ORDER) - 3:
            finish(INNER)
            before.append(tokens[0])
        send(k, piece, *before)
    finish(HEAD)
    finish(TAIL)
    return tuple(result)


def extended(shard, sides, width):
    for axis, dim in sides:
        size, length = (lax.axis_size(axis), shard.shape[dim])
        up = [(i, (i + 1) % size) for i in range(size - 1)]
        down = [(j, i) for i, j in up]
        last = lax.slice_in_dim(shard, length - width, length, axis=dim)
        initial = lax.slice_in_dim(shard, 0, width, axis=dim)
        before = lax.ppermute(last, axis, up)
        after = lax.ppermute(initial, axis, down)
        shard = jnp.concatenate([before, shard, after], axis=dim)
    return shard


def band_matrix(taps, out_count, in_count):
    offset = lax.broadcasted_iota(jnp.int32, (out_count, in_count), 1) - lax.broadcasted_iota(
        jnp.int32, (out_count, in_count), 0
    )
    positions = lax.broadcasted_iota(jnp.int32, (1, 1, TAPS), 2)
    choose = (offset[:, :, None] == positions).astype(jnp.bfloat16)
    return jnp.einsum("ijt,kst->ksij", choose, taps, preferred_element_type=jnp.float32).astype(jnp.bfloat16)


def filter_field(padded, row_taps, col_taps):
    tall = padded.shape[1]
    cols = padded.shape[2]
    width = 2 * LANES
    row_band = band_matrix(row_taps, tall - HALO, tall)
    rowed = jnp.einsum("ksij,sjc->ksic", row_band, padded, preferred_element_type=jnp.float32).astype(jnp.bfloat16)
    widened = jnp.pad(rowed, ((0, 0), (0, 0), (0, 0), (REACH, REACH)))
    col_band = band_matrix(col_taps, width, width + HALO)
    pieces = []
    for begin in range(0, cols, width):
        segment = widened[:, :, :, begin : begin + width + HALO]
        pieces.append(jnp.einsum("ksrj,ksij->sri", segment, col_band, preferred_element_type=jnp.float32))
    return jnp.concatenate(pieces, axis=2).astype(jnp.bfloat16)


def general(density, valid, row_taps, col_taps, amp_matrix, like_matrix):
    slices, rows, cols = density.shape
    mask = valid.astype(jnp.float32)
    field = density.astype(jnp.float32)
    sums, count = lax.psum((jnp.sum(field * mask[None], axis=(1, 2)), jnp.sum(mask)), "tile")
    masked = (mask[None] * (field - (sums / count)[:, None, None])).astype(jnp.bfloat16)
    filtered = filter_field(extended(masked, (("tile", 1),), REACH), row_taps, col_taps)
    peers = lax.axis_size("cuts")
    share = rows * cols // peers
    pencil = lax.all_to_all(
        filtered.reshape(slices, peers, share), "cuts", split_axis=1, concat_axis=0, tiled=True
    ).reshape(slices * peers, share)
    amp = jnp.dot(amp_matrix.T, pencil, preferred_element_type=jnp.float32)
    like = amp * jnp.dot(like_matrix.T, pencil, preferred_element_type=jnp.float32)
    return amp.astype(jnp.bfloat16), like.astype(jnp.bfloat16)


def per_device(density, valid, row_taps, col_taps, amp_matrix, like_matrix):
    slices, rows, cols = density.shape
    terms = row_taps.shape[0]
    peers = lax.axis_size("cuts")
    fits = (
        peers == 8
        and lax.axis_size("tile") == 4
        and slices == 2 * GROUP
        and terms == 4
        and rows == peers * (LANES // terms - HALO)
        and cols % (2 * LANES) == 0
    )
    run = fast if fits else general
    return run(density, valid, row_taps, col_taps, amp_matrix, like_matrix)


def solution(mesh):
    return jax.shard_map(
        per_device,
        mesh=mesh,
        in_specs=(
            P("cuts", "tile", None),
            P("tile", None),
            P(None, "cuts", None),
            P(None, "cuts", None),
            P(),
            P(),
        ),
        out_specs=(P(None, ("tile", "cuts")), P(None, ("tile", "cuts"))),
        check_vma=False,
    )
```

```python
import functools

import jax
import jax.numpy as jnp
from jax import lax
from jax.experimental import pallas as pl
from jax.experimental.pallas import tpu as pltpu
from jax.sharding import PartitionSpec as P

REACH = 8
TAPS = 2 * REACH + 1
LANES = 128
GROUP = 8
PER = 4
PAIR = 2
CHUNKS = 8
BEFORE_BAND = 2e9
MIB = 1024 * 1024
HALO = 2 * REACH


def params(mib=44):
    return pltpu.CompilerParams(vmem_limit_bytes=mib * MIB)


def hbm(shape, dtype):
    return pltpu.HBM(shape, dtype)


def held(x):
    return pltpu.with_memory_space_constraint(x, pltpu.HBM)


def resident(x):
    return pltpu.with_memory_space_constraint(x, pltpu.VMEM)


def anywhere():
    return pl.BlockSpec(memory_space=pl.ANY)


def cost(flops, moved):
    return pl.CostEstimate(flops=int(flops), bytes_accessed=int(moved), transcendentals=0)


def tap_flip():
    tap = lax.broadcasted_iota(jnp.int32, (TAPS, 2 * LANES), 0)
    lane = lax.broadcasted_iota(jnp.int32, (TAPS, 2 * LANES), 1)
    return (lax.rem(tap + lane, 2 * LANES) == 0).astype(jnp.bfloat16)


def column_band(taps):
    band = pltpu.roll(jnp.broadcast_to(taps, (LANES + HALO, 2 * LANES)), 0, 1, stride=1, stride_axis=0)
    return band[:, :LANES].astype(jnp.bfloat16)


def build_columns(col_taps, col_out):
    terms, slices = len(col_taps), col_taps[0].shape[0]
    for k in range(terms):
        base = jnp.dot(col_taps[k], tap_flip(), preferred_element_type=jnp.float32)
        for s in range(slices):
            col_out[s, : LANES + HALO, k * LANES : (k + 1) * LANES] = column_band(base[s : s + 1])
    for s in range(slices):
        col_out[s, LANES + HALO :, :] = jnp.zeros((LANES - HALO, terms * LANES), jnp.bfloat16)


def build_rows(row_taps, row_out):
    terms, slices = len(row_taps), row_taps[0].shape[0]
    high = LANES // terms
    tap = lax.broadcasted_iota(jnp.int32, (TAPS, LANES), 0)
    lane = lax.broadcasted_iota(jnp.int32, (TAPS, LANES), 1)
    base = jnp.zeros((slices, LANES), jnp.float32)
    for k in range(terms):
        place = (lane == tap + k * high).astype(jnp.bfloat16)
        base = base + jnp.dot(row_taps[k], place, preferred_element_type=jnp.float32)
    sub = lax.broadcasted_iota(jnp.int32, (GROUP, LANES), 0)
    for g in range(slices // GROUP):
        own = base[g * GROUP : (g + 1) * GROUP]
        for pair in range(row_out.shape[1] // (2 * GROUP)):
            shifted = [pltpu.roll(own, 2 * pair + h, 1) for h in range(2)]
            for s in range(GROUP):
                both = jnp.concatenate([jnp.where(sub == s, x, 0.0) for x in shifted], axis=0)
                row_out[
                    g, pair * 2 * GROUP : (pair + 1) * 2 * GROUP, s * LANES : (s + 1) * LANES
                ] = both.astype(jnp.bfloat16)


def listed(taps):
    return [taps[k] for k in range(taps.shape[0])]


def matrix_shapes(terms, slices, rows):
    return (slices, 2 * LANES, terms * LANES), (slices // GROUP, rows * GROUP, GROUP * LANES)


def convolve(field, col, row, tall, rows):
    slices, _, wide = col.shape
    terms = wide // LANES
    high, cols = LANES // terms, tall.shape[1]
    parts = []
    for g in range(slices // GROUP):
        for j in range(GROUP):
            s = g * GROUP + j
            x = jnp.concatenate([field(s), jnp.zeros((high, LANES), jnp.float32)], axis=1)
            x = pltpu.roll(x, REACH, 1).astype(jnp.bfloat16)
            x = jnp.concatenate([x[:, c : c + 2 * LANES] for c in range(0, cols, LANES)], axis=0)
            y = jnp.dot(x, col[s], preferred_element_type=jnp.float32).astype(jnp.bfloat16)
            for c in range(cols // LANES):
                for k in range(terms):
                    tall[(j * terms + k) * high : (j * terms + k + 1) * high, c * LANES : (c + 1) * LANES] = y[
                        c * high : (c + 1) * high, k * LANES : (k + 1) * LANES
                    ]
        z = jnp.dot(row[g, : rows * GROUP], tall[...], preferred_element_type=jnp.float32)
        parts.append(z.reshape(rows, GROUP, cols))
    return jnp.concatenate(parts, axis=1)


def sums_kernel(density, valid, out, first, last, cube, plane, sems):
    slices, rows, cols = cube.shape
    step = rows // CHUNKS

    def copies(i):
        at = pl.ds(pl.multiple_of(i * step, step), step)
        yield pltpu.make_async_copy(density.at[:, at], cube.at[:, at], sems.at[i])
        yield pltpu.make_async_copy(valid.at[at], plane.at[at], sems.at[CHUNKS + i])

    for i in range(CHUNKS):
        for copy in copies(i):
            copy.start()
    out[...] = jnp.zeros_like(out)

    def body(i, _):
        for copy in copies(i):
            copy.wait()
        at = pl.ds(pl.multiple_of(i * step, step), step)
        mask = plane[at] != 0
        for s in range(slices + 1):
            x = cube[s, at].astype(jnp.float32) if s < slices else jnp.ones((step, cols), jnp.float32)
            x = jnp.where(mask, x, 0.0).reshape(step // 8, 8, cols).sum(axis=0)
            x = sum(x[:, c : c + LANES] for c in range(0, cols, LANES))
            out[s : s + 1, :] += jnp.sum(x, axis=0, keepdims=True)
        return 0

    lax.fori_loop(0, CHUNKS, body, 0)
    first[:slices] = cube[:, :REACH]
    first[slices] = plane[:REACH].astype(jnp.bfloat16)
    last[:slices] = cube[:, rows - REACH :]
    last[slices] = plane[rows - REACH :].astype(jnp.bfloat16)


def masked_sums(density, valid):
    slices, rows, cols = density.shape
    edge = pltpu.VMEM((slices + 1, REACH, cols), jnp.bfloat16)
    return pl.pallas_call(
        sums_kernel,
        name="sums",
        in_specs=[anywhere()] * 2,
        out_specs=[pl.BlockSpec(memory_space=pltpu.VMEM)] * 3,
        out_shape=[pltpu.VMEM((slices + 8, LANES), jnp.float32), edge, edge],
        scratch_shapes=[
            pltpu.VMEM(density.shape, jnp.bfloat16),
            pltpu.VMEM(valid.shape, jnp.int32),
            pltpu.SemaphoreType.DMA((2 * CHUNKS,)),
        ],
        compiler_params=params(),
        cost_estimate=cost(1, 1),
    )(held(density), held(valid))


def mean_kernel(*refs):
    sums, (out, token) = refs[:4], refs[-2:]
    slices = out.shape[0]
    token[...] = jnp.zeros_like(token)
    total = sums[0][...] + sums[1][...] + sums[2][...] + sums[3][...]
    total = jnp.sum(total, axis=1, keepdims=True)
    out[...] = jnp.broadcast_to(total[:slices] / total[slices : slices + 1], out.shape)


def means(sums, slices, after):
    vmem = pl.BlockSpec(memory_space=pltpu.VMEM)
    return pl.pallas_call(
        mean_kernel,
        name="means",
        in_specs=[vmem] * len(sums) + [anywhere()],
        out_specs=[vmem] * 2,
        out_shape=[pltpu.VMEM((slices, LANES), jnp.float32), hbm((8, LANES), jnp.float32)],
        compiler_params=params(),
        cost_estimate=cost(1, 1),
    )(*sums, resident(after))


def inner_rows(both, last):
    both = both.astype(jnp.float32)
    rows = both.shape[0] - REACH
    chosen = jnp.where(last, both[REACH:], both[:rows])
    return jnp.concatenate([chosen, jnp.zeros((REACH, both.shape[1]), jnp.float32)], axis=0)


def window_copies(ids, b, last, density, valid, cube, plane, sems):
    high = plane.shape[1]
    here = pl.ds(pl.multiple_of(jnp.minimum(ids[b], last - 1) * (high // 2), high // 2), high)
    return [
        pltpu.make_async_copy(density.at[:, here], cube.at[b], sems.at[2 * b]),
        pltpu.make_async_copy(valid.at[here], plane.at[b], sems.at[2 * b + 1]),
    ]


def ready_kernel(ids, density, valid, row_taps, col_taps, after, col, row, cube, plane, sems):
    copies = window_copies(ids, 0, ids[1], density, valid, cube, plane, sems)
    for copy in copies:
        copy.start()
    build_columns(listed(col_taps), col)
    build_rows(listed(row_taps), row)
    for copy in copies:
        copy.wait()


def make_ready(ids, density, valid, row_taps, col_taps, after):
    slices, rows, cols = density.shape
    terms = row_taps.shape[0]
    high = LANES // terms
    vmem = pl.BlockSpec(memory_space=pltpu.VMEM)
    shapes = *matrix_shapes(terms, slices, high - HALO), (1, slices, high, cols)
    return pl.pallas_call(
        ready_kernel,
        name="ready",
        in_specs=[pl.BlockSpec(memory_space=pltpu.SMEM)] + [anywhere()] * 2 + [vmem] * 2 + [anywhere()],
        out_specs=[vmem] * 4,
        out_shape=[pltpu.VMEM(shape, jnp.bfloat16) for shape in shapes] + [pltpu.VMEM((1, high, cols), jnp.int32)],
        scratch_shapes=[pltpu.SemaphoreType.DMA((2,))],
        compiler_params=params(),
        cost_estimate=cost(1, 1),
    )(jnp.stack([ids, jnp.full_like(ids, rows // (high - HALO) - 1)]), held(density), held(valid), row_taps, col_taps, after)


def inner_kernel(pieces, loaded, ids, *refs):
    count = len(pieces)
    outs = sum(len(wanted) for wanted in pieces)
    if loaded:
        (cube, plane, col, row, mean), tall = refs[:5], refs[-1]
        outs = list(refs[-1 - outs : -1])
    else:
        (density, valid, col, row, mean), (tall, cube, plane, sems) = refs[:5], refs[-4:]
        outs = list(refs[-4 - outs : -4])
        copies = [window_copies(ids, b, ids[count], density, valid, cube, plane, sems) for b in range(count)]
        for copy in sum(copies, []):
            copy.start()
    for b, wanted in enumerate(pieces):
        if not loaded:
            for copy in copies[b]:
                copy.wait()
        last = ids[b] == ids[count]
        mask = inner_rows(plane[b], last)
        field = convolve(
            lambda s, b=b, last=last, mask=mask: mask * (inner_rows(cube[b, s], last) - mean[s : s + 1, :1]),
            col,
            row,
            tall,
            REACH,
        ).astype(jnp.bfloat16)
        for _, start, stop in wanted:
            outs.pop(0)[...] = field[start:stop]


def filter_inner(ids, pieces, density, valid, ready, mean, *after):
    slices, rows, cols = density.shape
    col, row, cube, plane = ready
    high = plane.shape[1]
    count = ids.shape[0]
    loaded = not after
    vmem = pl.BlockSpec(memory_space=pltpu.VMEM)
    shapes = [(stop - start, slices, cols) for wanted in pieces for _, start, stop in wanted]
    field = [resident(cube), resident(plane)] if loaded else [held(density), held(valid)]
    scratch = [pltpu.VMEM((GROUP * LANES, cols), jnp.bfloat16)]
    if not loaded:
        scratch += [
            pltpu.VMEM((count, slices, high, cols), jnp.bfloat16),
            pltpu.VMEM((count, high, cols), jnp.int32),
            pltpu.SemaphoreType.DMA((2 * count,)),
        ]
    out = pl.pallas_call(
        functools.partial(inner_kernel, pieces, loaded),
        name="inner",
        in_specs=[pl.BlockSpec(memory_space=pltpu.SMEM)]
        + [vmem if loaded else anywhere()] * 2
        + [vmem] * 3
        + [anywhere()] * len(after),
        out_specs=[vmem] * len(shapes),
        out_shape=[pltpu.VMEM(shape, jnp.bfloat16) for shape in shapes],
        scratch_shapes=scratch,
        compiler_params=params(),
        cost_estimate=cost(1, 1),
    )(
        jnp.concatenate([ids, jnp.full((1,), rows // (high - HALO) - 1, ids.dtype)]),
        *field,
        resident(col),
        resident(row),
        mean,
        *after,
    )
    out = list(out)
    return [[out.pop(0) for _ in wanted] for wanted in pieces]


def band_kernel(pieces, ids, density, valid, above, below, col, row, mean, *refs):
    (mask, tall, done, sems) = refs[-4:]
    count = sum(len(wanted) for wanted in pieces)
    outs = refs[-4 - count : -4]
    slices = mean.shape[0]
    rows, cols = valid.shape
    terms = col.shape[2] // LANES
    block = done.shape[1]
    high = block + HALO
    step = pl.program_id(0)
    f32 = jnp.float32

    @pl.when(step == 0)
    def _():
        mask[:REACH] = above[slices].astype(f32)
        mask[REACH : REACH + rows] = valid[...].astype(f32)
        mask[REACH + rows :] = below[slices].astype(f32)

    steps = slices // PER

    @pl.when(step < steps)
    def _():
        for j in range(PER):
            s = step * PER + j
            x = jnp.concatenate([above[s].astype(f32), density[j].astype(f32), below[s].astype(f32)], axis=0)
            x = mask[...] * (x - mean[pl.ds(s, 1), :][:, :1])
            x = jnp.concatenate([x, jnp.zeros((rows + HALO, LANES), f32)], axis=1)
            x = pltpu.roll(x, REACH, 1).astype(jnp.bfloat16)
            x = jnp.concatenate([x[:, c : c + 2 * LANES] for c in range(0, cols, LANES)], axis=0)
            y = jnp.dot(x, col[s], preferred_element_type=f32).astype(jnp.bfloat16)
            for c in range(cols // LANES):
                for k in range(terms):
                    tall[s * terms + k, :, c * LANES : (c + 1) * LANES] = y[
                        c * (rows + HALO) : (c + 1) * (rows + HALO), k * LANES : (k + 1) * LANES
                    ]

    def copies(b):
        at = sum(len(wanted) for wanted in pieces[:b])
        last = ids[b] == ids[len(pieces)]
        for p, (inner, start, stop) in enumerate(pieces[b]):
            here = jnp.where(last != (inner == 1), block - REACH, 0) + start
            yield pltpu.make_async_copy(done.at[b, pl.ds(here, stop - start)], outs[at + p], sems.at[at + p])

    @pl.when(step >= steps)
    def _():
        for j in range(PAIR):
            b = (step - steps) * PAIR + j
            here = pl.ds(pl.multiple_of(ids[b] * block, block), high)
            parts = []
            for g in range(slices // GROUP):
                slab = tall[g * GROUP * terms : (g + 1) * GROUP * terms, here, :].reshape(GROUP * LANES, cols)
                z = jnp.dot(row[g], slab, preferred_element_type=f32)
                parts.append(z.reshape(block, GROUP, cols))
            done[b] = jnp.concatenate(parts, axis=1).astype(jnp.bfloat16)

    for n in range(len(pieces) // PAIR):

        @pl.when(step == steps + n)
        def _():
            for b in range(n * PAIR, (n + 1) * PAIR):
                for copy in copies(b):
                    copy.start()

    @pl.when(step == pl.num_programs(0) - 1)
    def _():
        for b in range(len(pieces)):
            for copy in copies(b):
                copy.wait()


def filter_band(ids, pieces, density, valid, above, below, ready, mean, *after):
    slices, rows, cols = density.shape
    col, row = ready[:2]
    terms = col.shape[2] // LANES
    block = LANES // terms - HALO
    count = len(pieces)

    def whole(x):
        return pl.BlockSpec(x.shape, lambda i, at: (0,) * x.ndim, pipeline_mode=pl.Buffered(1))

    shapes = [(stop - start, slices, cols) for wanted in pieces for _, start, stop in wanted]
    out = pl.pallas_call(
        functools.partial(band_kernel, pieces),
        name="band",
        grid_spec=pltpu.PrefetchScalarGridSpec(
            num_scalar_prefetch=1,
            grid=(slices // PER + count // PAIR,),
            in_specs=[pl.BlockSpec((PER, rows, cols), lambda i, at: (jnp.minimum(i, slices // PER - 1), 0, 0))]
            + [whole(x) for x in (valid, above, below)]
            + [pl.BlockSpec(memory_space=pltpu.VMEM)] * 2
            + [whole(mean)]
            + [anywhere()] * len(after),
            out_specs=[anywhere()] * len(shapes),
            scratch_shapes=[
                pltpu.VMEM((rows + HALO, cols), jnp.float32),
                pltpu.VMEM((slices * terms, rows + HALO, cols), jnp.bfloat16),
                pltpu.VMEM((count, block, slices, cols), jnp.bfloat16),
                pltpu.SemaphoreType.DMA((len(shapes),)),
            ],
        ),
        out_shape=[hbm(shape, jnp.bfloat16) for shape in shapes],
        compiler_params=params(),
        cost_estimate=cost(1, 1),
    )(
        jnp.concatenate([ids, jnp.full((1,), rows // block - 1, ids.dtype)]),
        held(density),
        held(valid),
        above,
        below,
        resident(col),
        resident(row),
        mean,
        *after,
    )
    out = list(out)
    return [[out.pop(0) for _ in wanted] for wanted in pieces]


def project_kernel(count, place, weights, *refs):
    parts, (amp_out, like_out, token) = refs[:count], refs[-3:]
    zbins = weights.shape[0] // 2
    rows, _, cols = parts[0].shape
    for r in range(rows):
        pencil = jnp.concatenate([x[r] for x in parts], axis=0)
        both = jnp.dot(weights[...], pencil, preferred_element_type=jnp.float32)
        amp = both[:zbins]
        amp_out[:, r * cols : (r + 1) * cols] = amp.astype(jnp.bfloat16)
        like_out[:, r * cols : (r + 1) * cols] = (amp * both[zbins:]).astype(jnp.bfloat16)
    token[...] = jnp.zeros_like(token)


def project(place, weights, parts, rows, total, earlier):
    _, slices, cols = parts[0][0].shape
    zbins = weights.shape[0] // 2
    count = len(parts)
    shape = hbm((zbins, total * cols), jnp.bfloat16)
    return pl.pallas_call(
        functools.partial(project_kernel, count),
        name="project",
        grid_spec=pltpu.PrefetchScalarGridSpec(
            num_scalar_prefetch=1,
            grid=(rows // PAIR,),
            in_specs=[pl.BlockSpec(weights.shape, lambda i, at: (0, 0))]
            + [
                pl.BlockSpec((PAIR, slices, cols), lambda i, at, start=start: (i + start // PAIR, 0, 0))
                for _, start in parts
            ]
            + [anywhere()] * len(earlier),
            out_specs=[pl.BlockSpec((zbins, PAIR * cols), lambda i, at: (0, i + at[0] // PAIR))] * 2
            + [pl.BlockSpec((8, LANES), lambda i, at: (0, 0))],
        ),
        out_shape=[shape, shape, hbm((8, LANES), jnp.float32)],
        input_output_aliases={2 + count + i: i for i in range(len(earlier))},
        compiler_params=params(),
        cost_estimate=cost(1, 1),
    )(place.reshape(1), weights, *[x for x, _ in parts], *earlier)


def gate_kernel(*refs):
    pass


def gate(x, *earlier, flops=1):
    return pl.pallas_call(
        gate_kernel,
        name="gate",
        in_specs=[anywhere()] * (1 + len(earlier)),
        out_specs=anywhere(),
        out_shape=hbm(x.shape, x.dtype),
        input_output_aliases={0: 0},
        compiler_params=params(),
        cost_estimate=cost(flops, 1),
    )(held(x), *earlier)


INNER, OUTER = (1, 0, REACH), (0, 0, REACH)
HEAD, TAIL = (0, 0, 6), (0, 6, REACH)
FIRST = (((4, (INNER,)),), ((6, (INNER,)), (5, (INNER,))))
REST = (
    (5, (HEAD, TAIL)),
    (7, (INNER, HEAD, TAIL)),
    (2, (INNER, OUTER)),
    (3, (INNER, OUTER)),
    (4, (HEAD, TAIL)),
    (6, (HEAD, TAIL)),
    (1, (INNER, OUTER)),
    (0, (INNER, OUTER)),
)
ORDER = (
    (4, INNER, None),
    (6, INNER, None),
    (5, INNER, None),
    (7, INNER, 0),
    (2, INNER, 1),
    (4, HEAD, 1),
    (3, INNER, 2),
    (6, HEAD, 2),
    (2, OUTER, 4),
    (5, HEAD, 3),
    (1, INNER, 6),
    (7, HEAD, 5),
    (3, OUTER, 6),
    (1, OUTER, 10),
    (4, TAIL, 7),
    (6, TAIL, 9),
    (5, TAIL, 11),
    (7, TAIL, 14),
)


def fast(density, valid, row_taps, col_taps, amp_matrix, like_matrix):
    slices, rows, cols = density.shape
    peers = lax.axis_size("cuts")
    tiles = lax.axis_size("tile")
    block = rows // peers
    me = lax.axis_index("cuts").astype(jnp.int32)

    def swap(x, k):
        return lax.ppermute(x, "cuts", [(i, i ^ k) for i in range(peers)])

    own, first, last = masked_sums(density, valid)
    sums = [own] + [lax.ppermute(own, "tile", [(i, i ^ k) for i in range(tiles)]) for k in range(1, tiles)]
    ready = make_ready(me ^ ORDER[0][0], density, valid, row_taps, col_taps, own)
    mean, token = means(sums, slices, ready[0])

    made, arrived = {}, {}

    above = lax.ppermute(last, "tile", [(i, i + 1) for i in range(tiles - 1)])
    below = lax.ppermute(first, "tile", [(i + 1, i) for i in range(tiles - 1)])
    def ids(wanted):
        return jnp.stack([me ^ k for k, _ in wanted])

    def keep(wanted, got):
        for (k, cut), parts in zip(wanted, got):
            for piece, x in zip(cut, parts):
                made[k, piece] = x

    def send(k, piece, *before):
        x = made[k, piece]
        arrived[k, piece] = swap(gate(x, *before) if before else x, k)

    after = ()
    for wanted in FIRST:
        got = filter_inner(ids(wanted), [cut for _, cut in wanted], density, valid, ready, mean, *after)
        keep(wanted, got)
        after = (resident(got[0][0]),)
    first_piece = ORDER[0][:2]
    send(*first_piece)
    got = filter_band(
        ids(REST), [cut for _, cut in REST], density, valid, above, below, ready, mean, *after, held(gate(token, arrived[first_piece], flops=BEFORE_BAND))
    )
    keep(REST, got)
    for piece in (INNER, OUTER):
        arrived[0, piece] = made[0, piece]

    weights = jnp.concatenate([amp_matrix, like_matrix], axis=1).T.reshape(-1, peers, slices)
    weights = weights[:, me ^ jnp.arange(peers)].reshape(-1, peers * slices)
    result, tokens = [], []

    def finish(group):
        inner, start, stop = group
        place = jnp.where((me == peers - 1) != (inner == 1), block - REACH, 0) + start
        parts = []
        for k in range(peers):
            for piece in (group, INNER, OUTER):
                if (k, piece) in arrived and piece[0] == inner:
                    parts.append((arrived[k, piece], start - piece[1]))
                    break
        *result[:], token = project(place, weights, parts, stop - start, block, result)
        tokens.append(token)

    for at, (k, piece, wait) in enumerate(ORDER):
        if (k, piece) in arrived:
            continue
        before = [] if wait is None else [arrived[ORDER[wait][:2]]]
        if at == len(ORDER) - 3:
            finish(INNER)
            before.append(tokens[0])
        send(k, piece, *before)
    finish(HEAD)
    finish(TAIL)
    return tuple(result)


def extended(shard, sides, width):
    for axis, dim in sides:
        size, length = (lax.axis_size(axis), shard.shape[dim])
        up = [(i, (i + 1) % size) for i in range(size - 1)]
        down = [(j, i) for i, j in up]
        last = lax.slice_in_dim(shard, length - width, length, axis=dim)
        initial = lax.slice_in_dim(shard, 0, width, axis=dim)
        before = lax.ppermute(last, axis, up)
        after = lax.ppermute(initial, axis, down)
        shard = jnp.concatenate([before, shard, after], axis=dim)
    return shard


def band_matrix(taps, out_count, in_count):
    offset = lax.broadcasted_iota(jnp.int32, (out_count, in_count), 1) - lax.broadcasted_iota(
        jnp.int32, (out_count, in_count), 0
    )
    positions = lax.broadcasted_iota(jnp.int32, (1, 1, TAPS), 2)
    choose = (offset[:, :, None] == positions).astype(jnp.bfloat16)
    return jnp.einsum("ijt,kst->ksij", choose, taps, preferred_element_type=jnp.float32).astype(jnp.bfloat16)


def filter_field(padded, row_taps, col_taps):
    tall = padded.shape[1]
    cols = padded.shape[2]
    width = 2 * LANES
    row_band = band_matrix(row_taps, tall - HALO, tall)
    rowed = jnp.einsum("ksij,sjc->ksic", row_band, padded, preferred_element_type=jnp.float32).astype(jnp.bfloat16)
    widened = jnp.pad(rowed, ((0, 0), (0, 0), (0, 0), (REACH, REACH)))
    col_band = band_matrix(col_taps, width, width + HALO)
    pieces = []
    for begin in range(0, cols, width):
        segment = widened[:, :, :, begin : begin + width + HALO]
        pieces.append(jnp.einsum("ksrj,ksij->sri", segment, col_band, preferred_element_type=jnp.float32))
    return jnp.concatenate(pieces, axis=2).astype(jnp.bfloat16)


def general(density, valid, row_taps, col_taps, amp_matrix, like_matrix):
    slices, rows, cols = density.shape
    mask = valid.astype(jnp.float32)
    field = density.astype(jnp.float32)
    sums, count = lax.psum((jnp.sum(field * mask[None], axis=(1, 2)), jnp.sum(mask)), "tile")
    masked = (mask[None] * (field - (sums / count)[:, None, None])).astype(jnp.bfloat16)
    filtered = filter_field(extended(masked, (("tile", 1),), REACH), row_taps, col_taps)
    peers = lax.axis_size("cuts")
    share = rows * cols // peers
    pencil = lax.all_to_all(
        filtered.reshape(slices, peers, share), "cuts", split_axis=1, concat_axis=0, tiled=True
    ).reshape(slices * peers, share)
    amp = jnp.dot(amp_matrix.T, pencil, preferred_element_type=jnp.float32)
    like = amp * jnp.dot(like_matrix.T, pencil, preferred_element_type=jnp.float32)
    return amp.astype(jnp.bfloat16), like.astype(jnp.bfloat16)


def per_device(density, valid, row_taps, col_taps, amp_matrix, like_matrix):
    slices, rows, cols = density.shape
    terms = row_taps.shape[0]
    peers = lax.axis_size("cuts")
    fits = (
        peers == 8
        and lax.axis_size("tile") == 4
        and slices == 2 * GROUP
        and terms == 4
        and rows == peers * (LANES // terms - HALO)
        and cols % (2 * LANES) == 0
    )
    run = fast if fits else general
    return run(density, valid, row_taps, col_taps, amp_matrix, like_matrix)


def solution(mesh):
    return jax.shard_map(
        per_device,
        mesh=mesh,
        in_specs=(
            P("cuts", "tile", None),
            P("tile", None),
            P(None, "cuts", None),
            P(None, "cuts", None),
            P(),
            P(),
        ),
        out_specs=(P(None, ("tile", "cuts")), P(None, ("tile", "cuts"))),
        check_vma=False,
    )
```

```python
import functools

import jax
import jax.numpy as jnp
from jax import lax
from jax.experimental import pallas as pl
from jax.experimental.pallas import tpu as pltpu
from jax.sharding import PartitionSpec as P

REACH = 8
TAPS = 2 * REACH + 1
LANES = 128
GROUP = 8
PER = 4
PAIR = 2
CHUNKS = 8
BEFORE_BAND = 2e9
MIB = 1024 * 1024
HALO = 2 * REACH


def params(mib=33):
    return pltpu.CompilerParams(vmem_limit_bytes=mib * MIB)


def hbm(shape, dtype):
    return pltpu.HBM(shape, dtype)


def held(x):
    return pltpu.with_memory_space_constraint(x, pltpu.HBM)


def resident(x):
    return pltpu.with_memory_space_constraint(x, pltpu.VMEM)


def anywhere():
    return pl.BlockSpec(memory_space=pl.ANY)


def cost(flops, moved):
    return pl.CostEstimate(flops=int(flops), bytes_accessed=int(moved), transcendentals=0)


def tap_flip():
    tap = lax.broadcasted_iota(jnp.int32, (TAPS, 2 * LANES), 0)
    lane = lax.broadcasted_iota(jnp.int32, (TAPS, 2 * LANES), 1)
    return (lax.rem(tap + lane, 2 * LANES) == 0).astype(jnp.bfloat16)


def column_band(taps):
    band = pltpu.roll(jnp.broadcast_to(taps, (LANES + HALO, 2 * LANES)), 0, 1, stride=1, stride_axis=0)
    return band[:, :LANES].astype(jnp.bfloat16)


def build_columns(col_taps, col_out):
    terms, slices = len(col_taps), col_taps[0].shape[0]
    for k in range(terms):
        base = jnp.dot(col_taps[k], tap_flip(), preferred_element_type=jnp.float32)
        for s in range(slices):
            col_out[s, : LANES + HALO, k * LANES : (k + 1) * LANES] = column_band(base[s : s + 1])
    for s in range(slices):
        col_out[s, LANES + HALO :, :] = jnp.zeros((LANES - HALO, terms * LANES), jnp.bfloat16)


def build_rows(row_taps, row_out):
    terms, slices = len(row_taps), row_taps[0].shape[0]
    high = LANES // terms
    tap = lax.broadcasted_iota(jnp.int32, (TAPS, LANES), 0)
    lane = lax.broadcasted_iota(jnp.int32, (TAPS, LANES), 1)
    base = jnp.zeros((slices, LANES), jnp.float32)
    for k in range(terms):
        place = (lane == tap + k * high).astype(jnp.bfloat16)
        base = base + jnp.dot(row_taps[k], place, preferred_element_type=jnp.float32)
    sub = lax.broadcasted_iota(jnp.int32, (GROUP, LANES), 0)
    for g in range(slices // GROUP):
        own = base[g * GROUP : (g + 1) * GROUP]
        for pair in range(row_out.shape[1] // (2 * GROUP)):
            shifted = [pltpu.roll(own, 2 * pair + h, 1) for h in range(2)]
            for s in range(GROUP):
                both = jnp.concatenate([jnp.where(sub == s, x, 0.0) for x in shifted], axis=0)
                row_out[
                    g, pair * 2 * GROUP : (pair + 1) * 2 * GROUP, s * LANES : (s + 1) * LANES
                ] = both.astype(jnp.bfloat16)


def listed(taps):
    return [taps[k] for k in range(taps.shape[0])]


def matrix_shapes(terms, slices, rows):
    return (slices, 2 * LANES, terms * LANES), (slices // GROUP, rows * GROUP, GROUP * LANES)


def convolve(field, col, row, tall, rows):
    slices, _, wide = col.shape
    terms = wide // LANES
    high, cols = LANES // terms, tall.shape[1]
    parts = []
    for g in range(slices // GROUP):
        for j in range(GROUP):
            s = g * GROUP + j
            x = jnp.concatenate([field(s), jnp.zeros((high, LANES), jnp.float32)], axis=1)
            x = pltpu.roll(x, REACH, 1).astype(jnp.bfloat16)
            x = jnp.concatenate([x[:, c : c + 2 * LANES] for c in range(0, cols, LANES)], axis=0)
            y = jnp.dot(x, col[s], preferred_element_type=jnp.float32).astype(jnp.bfloat16)
            for c in range(cols // LANES):
                for k in range(terms):
                    tall[(j * terms + k) * high : (j * terms + k + 1) * high, c * LANES : (c + 1) * LANES] = y[
                        c * high : (c + 1) * high, k * LANES : (k + 1) * LANES
                    ]
        z = jnp.dot(row[g, : rows * GROUP], tall[...], preferred_element_type=jnp.float32)
        parts.append(z.reshape(rows, GROUP, cols))
    return jnp.concatenate(parts, axis=1)


def sums_kernel(density, valid, out, first, last, cube, plane, sems):
    slices, rows, cols = cube.shape
    step = rows // CHUNKS

    def copies(i):
        at = pl.ds(pl.multiple_of(i * step, step), step)
        yield pltpu.make_async_copy(density.at[:, at], cube.at[:, at], sems.at[i])
        yield pltpu.make_async_copy(valid.at[at], plane.at[at], sems.at[CHUNKS + i])

    for i in range(CHUNKS):
        for copy in copies(i):
            copy.start()
    out[...] = jnp.zeros_like(out)

    def body(i, _):
        for copy in copies(i):
            copy.wait()
        at = pl.ds(pl.multiple_of(i * step, step), step)
        mask = plane[at] != 0
        for s in range(slices + 1):
            x = cube[s, at].astype(jnp.float32) if s < slices else jnp.ones((step, cols), jnp.float32)
            x = jnp.where(mask, x, 0.0).reshape(step // 8, 8, cols).sum(axis=0)
            x = sum(x[:, c : c + LANES] for c in range(0, cols, LANES))
            out[s : s + 1, :] += jnp.sum(x, axis=0, keepdims=True)
        return 0

    lax.fori_loop(0, CHUNKS, body, 0)
    first[:slices] = cube[:, :REACH]
    first[slices] = plane[:REACH].astype(jnp.bfloat16)
    last[:slices] = cube[:, rows - REACH :]
    last[slices] = plane[rows - REACH :].astype(jnp.bfloat16)


def masked_sums(density, valid):
    slices, rows, cols = density.shape
    edge = pltpu.VMEM((slices + 1, REACH, cols), jnp.bfloat16)
    return pl.pallas_call(
        sums_kernel,
        name="sums",
        in_specs=[anywhere()] * 2,
        out_specs=[pl.BlockSpec(memory_space=pltpu.VMEM)] * 3,
        out_shape=[pltpu.VMEM((slices + 8, LANES), jnp.float32), edge, edge],
        scratch_shapes=[
            pltpu.VMEM(density.shape, jnp.bfloat16),
            pltpu.VMEM(valid.shape, jnp.int32),
            pltpu.SemaphoreType.DMA((2 * CHUNKS,)),
        ],
        compiler_params=params(),
        cost_estimate=cost(1, 1),
    )(held(density), held(valid))


def mean_kernel(*refs):
    sums, (out, token) = refs[:4], refs[-2:]
    slices = out.shape[0]
    token[...] = jnp.zeros_like(token)
    total = sums[0][...] + sums[1][...] + sums[2][...] + sums[3][...]
    total = jnp.sum(total, axis=1, keepdims=True)
    out[...] = jnp.broadcast_to(total[:slices] / total[slices : slices + 1], out.shape)


def means(sums, slices, after):
    vmem = pl.BlockSpec(memory_space=pltpu.VMEM)
    return pl.pallas_call(
        mean_kernel,
        name="means",
        in_specs=[vmem] * len(sums) + [anywhere()],
        out_specs=[vmem] * 2,
        out_shape=[pltpu.VMEM((slices, LANES), jnp.float32), pltpu.VMEM((8, LANES), jnp.float32)],
        compiler_params=params(),
        cost_estimate=cost(1, 1),
    )(*sums, resident(after))


def inner_rows(both, last):
    both = both.astype(jnp.float32)
    rows = both.shape[0] - REACH
    chosen = jnp.where(last, both[REACH:], both[:rows])
    return jnp.concatenate([chosen, jnp.zeros((REACH, both.shape[1]), jnp.float32)], axis=0)


def window_copies(ids, b, last, density, valid, cube, plane, sems):
    high = plane.shape[1]
    here = pl.ds(pl.multiple_of(jnp.minimum(ids[b], last - 1) * (high // 2), high // 2), high)
    return [
        pltpu.make_async_copy(density.at[:, here], cube.at[b], sems.at[2 * b]),
        pltpu.make_async_copy(valid.at[here], plane.at[b], sems.at[2 * b + 1]),
    ]


def ready_kernel(ids, density, valid, row_taps, col_taps, after, col, row, cube, plane, sems):
    copies = window_copies(ids, 0, ids[1], density, valid, cube, plane, sems)
    for copy in copies:
        copy.start()
    build_columns(listed(col_taps), col)
    build_rows(listed(row_taps), row)
    for copy in copies:
        copy.wait()


def make_ready(ids, density, valid, row_taps, col_taps, after):
    slices, rows, cols = density.shape
    terms = row_taps.shape[0]
    high = LANES // terms
    vmem = pl.BlockSpec(memory_space=pltpu.VMEM)
    shapes = *matrix_shapes(terms, slices, high - HALO), (1, slices, high, cols)
    return pl.pallas_call(
        ready_kernel,
        name="ready",
        in_specs=[pl.BlockSpec(memory_space=pltpu.SMEM)] + [anywhere()] * 2 + [vmem] * 2 + [anywhere()],
        out_specs=[vmem] * 4,
        out_shape=[pltpu.VMEM(shape, jnp.bfloat16) for shape in shapes] + [pltpu.VMEM((1, high, cols), jnp.int32)],
        scratch_shapes=[pltpu.SemaphoreType.DMA((2,))],
        compiler_params=params(),
        cost_estimate=cost(1, 1),
    )(jnp.stack([ids, jnp.full_like(ids, rows // (high - HALO) - 1)]), held(density), held(valid), row_taps, col_taps, after)


def inner_kernel(pieces, loaded, ids, *refs):
    count = len(pieces)
    outs = sum(len(wanted) for wanted in pieces)
    if loaded:
        (cube, plane, col, row, mean), tall = refs[:5], refs[-1]
        outs = list(refs[-1 - outs : -1])
    else:
        (density, valid, col, row, mean), (tall, cube, plane, sems) = refs[:5], refs[-4:]
        outs = list(refs[-4 - outs : -4])
        copies = [window_copies(ids, b, ids[count], density, valid, cube, plane, sems) for b in range(count)]
        for copy in sum(copies, []):
            copy.start()
    for b, wanted in enumerate(pieces):
        if not loaded:
            for copy in copies[b]:
                copy.wait()
        last = ids[b] == ids[count]
        mask = inner_rows(plane[b], last)
        field = convolve(
            lambda s, b=b, last=last, mask=mask: mask * (inner_rows(cube[b, s], last) - mean[s : s + 1, :1]),
            col,
            row,
            tall,
            REACH,
        ).astype(jnp.bfloat16)
        for _, start, stop in wanted:
            outs.pop(0)[...] = field[start:stop]


def filter_inner(ids, pieces, density, valid, ready, mean, *after):
    slices, rows, cols = density.shape
    col, row, cube, plane = ready
    high = plane.shape[1]
    count = ids.shape[0]
    loaded = not after
    vmem = pl.BlockSpec(memory_space=pltpu.VMEM)
    shapes = [(stop - start, slices, cols) for wanted in pieces for _, start, stop in wanted]
    field = [resident(cube), resident(plane)] if loaded else [held(density), held(valid)]
    scratch = [pltpu.VMEM((GROUP * LANES, cols), jnp.bfloat16)]
    if not loaded:
        scratch += [
            pltpu.VMEM((count, slices, high, cols), jnp.bfloat16),
            pltpu.VMEM((count, high, cols), jnp.int32),
            pltpu.SemaphoreType.DMA((2 * count,)),
        ]
    out = pl.pallas_call(
        functools.partial(inner_kernel, pieces, loaded),
        name="inner",
        in_specs=[pl.BlockSpec(memory_space=pltpu.SMEM)]
        + [vmem if loaded else anywhere()] * 2
        + [vmem] * 3
        + [anywhere()] * len(after),
        out_specs=[vmem] * len(shapes),
        out_shape=[pltpu.VMEM(shape, jnp.bfloat16) for shape in shapes],
        scratch_shapes=scratch,
        compiler_params=params(),
        cost_estimate=cost(1, 1),
    )(
        jnp.concatenate([ids, jnp.full((1,), rows // (high - HALO) - 1, ids.dtype)]),
        *field,
        resident(col),
        resident(row),
        mean,
        *after,
    )
    out = list(out)
    return [[out.pop(0) for _ in wanted] for wanted in pieces]


def band_kernel(pieces, ids, density, valid, above, below, col, row, mean, *refs):
    (mask, tall, done, sems) = refs[-4:]
    count = sum(len(wanted) for wanted in pieces)
    outs = refs[-4 - count : -4]
    slices = mean.shape[0]
    rows, cols = valid.shape
    terms = col.shape[2] // LANES
    block = done.shape[1]
    high = block + HALO
    step = pl.program_id(0)
    f32 = jnp.float32

    @pl.when(step == 0)
    def _():
        mask[:REACH] = above[slices].astype(f32)
        mask[REACH : REACH + rows] = valid[...].astype(f32)
        mask[REACH + rows :] = below[slices].astype(f32)

    steps = slices // PER

    @pl.when(step < steps)
    def _():
        for j in range(PER):
            s = step * PER + j
            x = jnp.concatenate([above[s].astype(f32), density[j].astype(f32), below[s].astype(f32)], axis=0)
            x = mask[...] * (x - mean[pl.ds(s, 1), :][:, :1])
            x = jnp.concatenate([x, jnp.zeros((rows + HALO, LANES), f32)], axis=1)
            x = pltpu.roll(x, REACH, 1).astype(jnp.bfloat16)
            x = jnp.concatenate([x[:, c : c + 2 * LANES] for c in range(0, cols, LANES)], axis=0)
            y = jnp.dot(x, col[s], preferred_element_type=f32).astype(jnp.bfloat16)
            for c in range(cols // LANES):
                for k in range(terms):
                    tall[s * terms + k, :, c * LANES : (c + 1) * LANES] = y[
                        c * (rows + HALO) : (c + 1) * (rows + HALO), k * LANES : (k + 1) * LANES
                    ]

    def copies(b):
        at = sum(len(wanted) for wanted in pieces[:b])
        last = ids[b] == ids[len(pieces)]
        for p, (inner, start, stop) in enumerate(pieces[b]):
            here = jnp.where(last != (inner == 1), block - REACH, 0) + start
            yield pltpu.make_async_copy(done.at[b, pl.ds(here, stop - start)], outs[at + p], sems.at[at + p])

    @pl.when(step >= steps)
    def _():
        for j in range(PAIR):
            b = (step - steps) * PAIR + j
            here = pl.ds(pl.multiple_of(ids[b] * block, block), high)
            parts = []
            for g in range(slices // GROUP):
                slab = tall[g * GROUP * terms : (g + 1) * GROUP * terms, here, :].reshape(GROUP * LANES, cols)
                z = jnp.dot(row[g], slab, preferred_element_type=f32)
                parts.append(z.reshape(block, GROUP, cols))
            done[b] = jnp.concatenate(parts, axis=1).astype(jnp.bfloat16)

    for n in range(len(pieces) // PAIR):

        @pl.when(step == steps + n)
        def _():
            for b in range(n * PAIR, (n + 1) * PAIR):
                for copy in copies(b):
                    copy.start()

    @pl.when(step == pl.num_programs(0) - 1)
    def _():
        for b in range(len(pieces)):
            for copy in copies(b):
                copy.wait()


def filter_band(ids, pieces, density, valid, above, below, ready, mean, *after):
    slices, rows, cols = density.shape
    col, row = ready[:2]
    terms = col.shape[2] // LANES
    block = LANES // terms - HALO
    count = len(pieces)

    def whole(x):
        return pl.BlockSpec(x.shape, lambda i, at: (0,) * x.ndim, pipeline_mode=pl.Buffered(1))

    shapes = [(stop - start, slices, cols) for wanted in pieces for _, start, stop in wanted]
    out = pl.pallas_call(
        functools.partial(band_kernel, pieces),
        name="band",
        grid_spec=pltpu.PrefetchScalarGridSpec(
            num_scalar_prefetch=1,
            grid=(slices // PER + count // PAIR,),
            in_specs=[pl.BlockSpec((PER, rows, cols), lambda i, at: (jnp.minimum(i, slices // PER - 1), 0, 0))]
            + [whole(x) for x in (valid, above, below)]
            + [pl.BlockSpec(memory_space=pltpu.VMEM)] * 2
            + [whole(mean)]
            + [anywhere()] * len(after),
            out_specs=[anywhere()] * len(shapes),
            scratch_shapes=[
                pltpu.VMEM((rows + HALO, cols), jnp.float32),
                pltpu.VMEM((slices * terms, rows + HALO, cols), jnp.bfloat16),
                pltpu.VMEM((count, block, slices, cols), jnp.bfloat16),
                pltpu.SemaphoreType.DMA((len(shapes),)),
            ],
        ),
        out_shape=[hbm(shape, jnp.bfloat16) for shape in shapes],
        compiler_params=params(),
        cost_estimate=cost(1, 1),
    )(
        jnp.concatenate([ids, jnp.full((1,), rows // block - 1, ids.dtype)]),
        held(density),
        held(valid),
        above,
        below,
        resident(col),
        resident(row),
        mean,
        *after,
    )
    out = list(out)
    return [[out.pop(0) for _ in wanted] for wanted in pieces]


def project_kernel(count, place, weights, *refs):
    parts, (amp_out, like_out, token) = refs[:count], refs[-3:]
    zbins = weights.shape[0] // 2
    rows, _, cols = parts[0].shape
    for r in range(rows):
        pencil = jnp.concatenate([x[r] for x in parts], axis=0)
        both = jnp.dot(weights[...], pencil, preferred_element_type=jnp.float32)
        amp = both[:zbins]
        amp_out[:, r * cols : (r + 1) * cols] = amp.astype(jnp.bfloat16)
        like_out[:, r * cols : (r + 1) * cols] = (amp * both[zbins:]).astype(jnp.bfloat16)
    token[...] = jnp.zeros_like(token)


def project(place, weights, parts, rows, total, earlier):
    _, slices, cols = parts[0][0].shape
    zbins = weights.shape[0] // 2
    count = len(parts)
    shape = hbm((zbins, total * cols), jnp.bfloat16)
    return pl.pallas_call(
        functools.partial(project_kernel, count),
        name="project",
        grid_spec=pltpu.PrefetchScalarGridSpec(
            num_scalar_prefetch=1,
            grid=(rows // PAIR,),
            in_specs=[pl.BlockSpec(weights.shape, lambda i, at: (0, 0))]
            + [
                pl.BlockSpec((PAIR, slices, cols), lambda i, at, start=start: (i + start // PAIR, 0, 0))
                for _, start in parts
            ]
            + [anywhere()] * len(earlier),
            out_specs=[pl.BlockSpec((zbins, PAIR * cols), lambda i, at: (0, i + at[0] // PAIR))] * 2
            + [pl.BlockSpec((8, LANES), lambda i, at: (0, 0))],
        ),
        out_shape=[shape, shape, hbm((8, LANES), jnp.float32)],
        input_output_aliases={2 + count + i: i for i in range(len(earlier))},
        compiler_params=params(),
        cost_estimate=cost(1, 1),
    )(place.reshape(1), weights, *[x for x, _ in parts], *earlier)


def gate_kernel(*refs):
    pass


def gate(x, *earlier, flops=1, space=pltpu.HBM):
    return pl.pallas_call(
        gate_kernel,
        name="gate",
        in_specs=[anywhere()] * (1 + len(earlier)),
        out_specs=anywhere(),
        out_shape=space(x.shape, x.dtype),
        input_output_aliases={0: 0},
        compiler_params=params(),
        cost_estimate=cost(flops, 1),
    )(pltpu.with_memory_space_constraint(x, space), *earlier)


INNER, OUTER = (1, 0, REACH), (0, 0, REACH)
HEAD, TAIL = (0, 0, 6), (0, 6, REACH)
FIRST = (((4, (INNER,)),), ((6, (INNER,)), (5, (INNER,))))
REST = (
    (5, (HEAD, TAIL)),
    (7, (INNER, HEAD, TAIL)),
    (2, (INNER, OUTER)),
    (3, (INNER, OUTER)),
    (4, (HEAD, TAIL)),
    (6, (HEAD, TAIL)),
    (1, (INNER, OUTER)),
    (0, (INNER, OUTER)),
)
ORDER = (
    (4, INNER, None),
    (6, INNER, None),
    (5, INNER, None),
    (7, INNER, 0),
    (2, INNER, 1),
    (4, HEAD, 1),
    (3, INNER, 2),
    (6, HEAD, 2),
    (2, OUTER, 4),
    (5, HEAD, 3),
    (1, INNER, 6),
    (7, HEAD, 5),
    (3, OUTER, 6),
    (1, OUTER, 10),
    (4, TAIL, 7),
    (6, TAIL, 9),
    (5, TAIL, 11),
    (7, TAIL, 14),
)


def fast(density, valid, row_taps, col_taps, amp_matrix, like_matrix):
    slices, rows, cols = density.shape
    peers = lax.axis_size("cuts")
    tiles = lax.axis_size("tile")
    block = rows // peers
    me = lax.axis_index("cuts").astype(jnp.int32)

    def swap(x, k):
        return lax.ppermute(x, "cuts", [(i, i ^ k) for i in range(peers)])

    own, first, last = masked_sums(density, valid)
    sums = [own] + [lax.ppermute(own, "tile", [(i, i ^ k) for i in range(tiles)]) for k in range(1, tiles)]
    ready = make_ready(me ^ ORDER[0][0], density, valid, row_taps, col_taps, own)
    mean, token = means(sums, slices, ready[0])

    made, arrived = {}, {}

    above = lax.ppermute(last, "tile", [(i, i + 1) for i in range(tiles - 1)])
    below = lax.ppermute(first, "tile", [(i + 1, i) for i in range(tiles - 1)])
    def ids(wanted):
        return jnp.stack([me ^ k for k, _ in wanted])

    def keep(wanted, got):
        for (k, cut), parts in zip(wanted, got):
            for piece, x in zip(cut, parts):
                made[k, piece] = x

    def send(k, piece, *before):
        x = made[k, piece]
        arrived[k, piece] = swap(gate(x, *before) if before else x, k)

    after = ()
    for wanted in FIRST:
        got = filter_inner(ids(wanted), [cut for _, cut in wanted], density, valid, ready, mean, *after)
        keep(wanted, got)
        after = (resident(got[0][0]),)
    first_piece = ORDER[0][:2]
    send(*first_piece)
    got = filter_band(
        ids(REST), [cut for _, cut in REST], density, valid, above, below, ready, mean, *after, resident(gate(token, arrived[first_piece], flops=BEFORE_BAND, space=pltpu.VMEM))
    )
    keep(REST, got)
    for piece in (INNER, OUTER):
        arrived[0, piece] = made[0, piece]

    weights = jnp.concatenate([amp_matrix, like_matrix], axis=1).T.reshape(-1, peers, slices)
    weights = weights[:, me ^ jnp.arange(peers)].reshape(-1, peers * slices)
    result, tokens = [], []

    def finish(group):
        inner, start, stop = group
        place = jnp.where((me == peers - 1) != (inner == 1), block - REACH, 0) + start
        parts = []
        for k in range(peers):
            for piece in (group, INNER, OUTER):
                if (k, piece) in arrived and piece[0] == inner:
                    parts.append((arrived[k, piece], start - piece[1]))
                    break
        *result[:], token = project(place, weights, parts, stop - start, block, result)
        tokens.append(token)

    for at, (k, piece, wait) in enumerate(ORDER):
        if (k, piece) in arrived:
            continue
        before = [] if wait is None else [arrived[ORDER[wait][:2]]]
        if at == len(ORDER) - 3:
            finish(INNER)
            before.append(tokens[0])
        send(k, piece, *before)
    finish(HEAD)
    finish(TAIL)
    return tuple(result)


def extended(shard, sides, width):
    for axis, dim in sides:
        size, length = (lax.axis_size(axis), shard.shape[dim])
        up = [(i, (i + 1) % size) for i in range(size - 1)]
        down = [(j, i) for i, j in up]
        last = lax.slice_in_dim(shard, length - width, length, axis=dim)
        initial = lax.slice_in_dim(shard, 0, width, axis=dim)
        before = lax.ppermute(last, axis, up)
        after = lax.ppermute(initial, axis, down)
        shard = jnp.concatenate([before, shard, after], axis=dim)
    return shard


def band_matrix(taps, out_count, in_count):
    offset = lax.broadcasted_iota(jnp.int32, (out_count, in_count), 1) - lax.broadcasted_iota(
        jnp.int32, (out_count, in_count), 0
    )
    positions = lax.broadcasted_iota(jnp.int32, (1, 1, TAPS), 2)
    choose = (offset[:, :, None] == positions).astype(jnp.bfloat16)
    return jnp.einsum("ijt,kst->ksij", choose, taps, preferred_element_type=jnp.float32).astype(jnp.bfloat16)


def filter_field(padded, row_taps, col_taps):
    tall = padded.shape[1]
    cols = padded.shape[2]
    width = 2 * LANES
    row_band = band_matrix(row_taps, tall - HALO, tall)
    rowed = jnp.einsum("ksij,sjc->ksic", row_band, padded, preferred_element_type=jnp.float32).astype(jnp.bfloat16)
    widened = jnp.pad(rowed, ((0, 0), (0, 0), (0, 0), (REACH, REACH)))
    col_band = band_matrix(col_taps, width, width + HALO)
    pieces = []
    for begin in range(0, cols, width):
        segment = widened[:, :, :, begin : begin + width + HALO]
        pieces.append(jnp.einsum("ksrj,ksij->sri", segment, col_band, preferred_element_type=jnp.float32))
    return jnp.concatenate(pieces, axis=2).astype(jnp.bfloat16)


def general(density, valid, row_taps, col_taps, amp_matrix, like_matrix):
    slices, rows, cols = density.shape
    mask = valid.astype(jnp.float32)
    field = density.astype(jnp.float32)
    sums, count = lax.psum((jnp.sum(field * mask[None], axis=(1, 2)), jnp.sum(mask)), "tile")
    masked = (mask[None] * (field - (sums / count)[:, None, None])).astype(jnp.bfloat16)
    filtered = filter_field(extended(masked, (("tile", 1),), REACH), row_taps, col_taps)
    peers = lax.axis_size("cuts")
    share = rows * cols // peers
    pencil = lax.all_to_all(
        filtered.reshape(slices, peers, share), "cuts", split_axis=1, concat_axis=0, tiled=True
    ).reshape(slices * peers, share)
    amp = jnp.dot(amp_matrix.T, pencil, preferred_element_type=jnp.float32)
    like = amp * jnp.dot(like_matrix.T, pencil, preferred_element_type=jnp.float32)
    return amp.astype(jnp.bfloat16), like.astype(jnp.bfloat16)


def per_device(density, valid, row_taps, col_taps, amp_matrix, like_matrix):
    slices, rows, cols = density.shape
    terms = row_taps.shape[0]
    peers = lax.axis_size("cuts")
    fits = (
        peers == 8
        and lax.axis_size("tile") == 4
        and slices == 2 * GROUP
        and terms == 4
        and rows == peers * (LANES // terms - HALO)
        and cols % (2 * LANES) == 0
    )
    run = fast if fits else general
    return run(density, valid, row_taps, col_taps, amp_matrix, like_matrix)


def solution(mesh):
    return jax.shard_map(
        per_device,
        mesh=mesh,
        in_specs=(
            P("cuts", "tile", None),
            P("tile", None),
            P(None, "cuts", None),
            P(None, "cuts", None),
            P(),
            P(),
        ),
        out_specs=(P(None, ("tile", "cuts")), P(None, ("tile", "cuts"))),
        check_vma=False,
    )
```

```python
import functools

import jax
import jax.numpy as jnp
from jax import lax
from jax.experimental import pallas as pl
from jax.experimental.pallas import tpu as pltpu
from jax.sharding import PartitionSpec as P

REACH = 8
TAPS = 2 * REACH + 1
LANES = 128
GROUP = 8
PER = 4
PAIR = 2
CHUNKS = 8
BEFORE_BAND = 2e9
MIB = 1024 * 1024
HALO = 2 * REACH


def params(mib=33):
    return pltpu.CompilerParams(vmem_limit_bytes=mib * MIB)


def hbm(shape, dtype):
    return pltpu.HBM(shape, dtype)


def held(x):
    return pltpu.with_memory_space_constraint(x, pltpu.HBM)


def resident(x):
    return pltpu.with_memory_space_constraint(x, pltpu.VMEM)


def anywhere():
    return pl.BlockSpec(memory_space=pl.ANY)


def cost(flops, moved):
    return pl.CostEstimate(flops=int(flops), bytes_accessed=int(moved), transcendentals=0)


def tap_flip():
    tap = lax.broadcasted_iota(jnp.int32, (TAPS, 2 * LANES), 0)
    lane = lax.broadcasted_iota(jnp.int32, (TAPS, 2 * LANES), 1)
    return (lax.rem(tap + lane, 2 * LANES) == 0).astype(jnp.bfloat16)


def column_band(taps):
    band = pltpu.roll(jnp.broadcast_to(taps, (LANES + HALO, 2 * LANES)), 0, 1, stride=1, stride_axis=0)
    return band[:, :LANES].astype(jnp.bfloat16)


def build_columns(col_taps, col_out):
    terms, slices = len(col_taps), col_taps[0].shape[0]
    for k in range(terms):
        base = jnp.dot(col_taps[k], tap_flip(), preferred_element_type=jnp.float32)
        for s in range(slices):
            col_out[s, : LANES + HALO, k * LANES : (k + 1) * LANES] = column_band(base[s : s + 1])
    for s in range(slices):
        col_out[s, LANES + HALO :, :] = jnp.zeros((LANES - HALO, terms * LANES), jnp.bfloat16)


def build_rows(row_taps, row_out):
    terms, slices = len(row_taps), row_taps[0].shape[0]
    high = LANES // terms
    tap = lax.broadcasted_iota(jnp.int32, (TAPS, LANES), 0)
    lane = lax.broadcasted_iota(jnp.int32, (TAPS, LANES), 1)
    base = jnp.zeros((slices, LANES), jnp.float32)
    for k in range(terms):
        place = (lane == tap + k * high).astype(jnp.bfloat16)
        base = base + jnp.dot(row_taps[k], place, preferred_element_type=jnp.float32)
    sub = lax.broadcasted_iota(jnp.int32, (GROUP, LANES), 0)
    for g in range(slices // GROUP):
        own = base[g * GROUP : (g + 1) * GROUP]
        for pair in range(row_out.shape[1] // (2 * GROUP)):
            shifted = [pltpu.roll(own, 2 * pair + h, 1) for h in range(2)]
            for s in range(GROUP):
                both = jnp.concatenate([jnp.where(sub == s, x, 0.0) for x in shifted], axis=0)
                row_out[
                    g, pair * 2 * GROUP : (pair + 1) * 2 * GROUP, s * LANES : (s + 1) * LANES
                ] = both.astype(jnp.bfloat16)


def listed(taps):
    return [taps[k] for k in range(taps.shape[0])]


def matrix_shapes(terms, slices, rows):
    return (slices, 2 * LANES, terms * LANES), (slices // GROUP, rows * GROUP, GROUP * LANES)


def convolve(field, col, row, tall, rows):
    slices, _, wide = col.shape
    terms = wide // LANES
    high, cols = LANES // terms, tall.shape[1]
    parts = []
    for g in range(slices // GROUP):
        for j in range(GROUP):
            s = g * GROUP + j
            x = jnp.concatenate([field(s), jnp.zeros((high, LANES), jnp.float32)], axis=1)
            x = pltpu.roll(x, REACH, 1).astype(jnp.bfloat16)
            x = jnp.concatenate([x[:, c : c + 2 * LANES] for c in range(0, cols, LANES)], axis=0)
            y = jnp.dot(x, col[s], preferred_element_type=jnp.float32).astype(jnp.bfloat16)
            for c in range(cols // LANES):
                for k in range(terms):
                    tall[(j * terms + k) * high : (j * terms + k + 1) * high, c * LANES : (c + 1) * LANES] = y[
                        c * high : (c + 1) * high, k * LANES : (k + 1) * LANES
                    ]
        z = jnp.dot(row[g, : rows * GROUP], tall[...], preferred_element_type=jnp.float32)
        parts.append(z.reshape(rows, GROUP, cols))
    return jnp.concatenate(parts, axis=1)


def sums_kernel(density, valid, out, first, last, cube, plane, sems):
    slices, rows, cols = cube.shape
    step = rows // CHUNKS

    def copies(i):
        at = pl.ds(pl.multiple_of(i * step, step), step)
        yield pltpu.make_async_copy(density.at[:, at], cube.at[:, at], sems.at[i])
        yield pltpu.make_async_copy(valid.at[at], plane.at[at], sems.at[CHUNKS + i])

    for i in range(CHUNKS):
        for copy in copies(i):
            copy.start()
    out[...] = jnp.zeros_like(out)

    def body(i, _):
        for copy in copies(i):
            copy.wait()
        at = pl.ds(pl.multiple_of(i * step, step), step)
        mask = plane[at] != 0
        for s in range(slices + 1):
            x = cube[s, at].astype(jnp.float32) if s < slices else jnp.ones((step, cols), jnp.float32)
            x = jnp.where(mask, x, 0.0).reshape(step // 8, 8, cols).sum(axis=0)
            x = sum(x[:, c : c + LANES] for c in range(0, cols, LANES))
            out[s : s + 1, :] += jnp.sum(x, axis=0, keepdims=True)
        return 0

    lax.fori_loop(0, CHUNKS, body, 0)
    first[:slices] = cube[:, :REACH]
    first[slices] = plane[:REACH].astype(jnp.bfloat16)
    last[:slices] = cube[:, rows - REACH :]
    last[slices] = plane[rows - REACH :].astype(jnp.bfloat16)


def masked_sums(density, valid):
    slices, rows, cols = density.shape
    edge = pltpu.VMEM((slices + 1, REACH, cols), jnp.bfloat16)
    return pl.pallas_call(
        sums_kernel,
        name="sums",
        in_specs=[anywhere()] * 2,
        out_specs=[pl.BlockSpec(memory_space=pltpu.VMEM)] * 3,
        out_shape=[pltpu.VMEM((slices + 8, LANES), jnp.float32), edge, edge],
        scratch_shapes=[
            pltpu.VMEM(density.shape, jnp.bfloat16),
            pltpu.VMEM(valid.shape, jnp.int32),
            pltpu.SemaphoreType.DMA((2 * CHUNKS,)),
        ],
        compiler_params=params(),
        cost_estimate=cost(1, 1),
    )(held(density), held(valid))


def mean_kernel(*refs):
    sums, (out, token) = refs[:4], refs[-2:]
    slices = out.shape[0]
    token[...] = jnp.zeros_like(token)
    total = sums[0][...] + sums[1][...] + sums[2][...] + sums[3][...]
    total = jnp.sum(total, axis=1, keepdims=True)
    out[...] = jnp.broadcast_to(total[:slices] / total[slices : slices + 1], out.shape)


def means(sums, slices, after):
    vmem = pl.BlockSpec(memory_space=pltpu.VMEM)
    return pl.pallas_call(
        mean_kernel,
        name="means",
        in_specs=[vmem] * len(sums) + [anywhere()],
        out_specs=[vmem] * 2,
        out_shape=[pltpu.VMEM((slices, LANES), jnp.float32), pltpu.VMEM((8, LANES), jnp.float32)],
        compiler_params=params(),
        cost_estimate=cost(1, 1),
    )(*sums, resident(after))


def inner_rows(both, last):
    both = both.astype(jnp.float32)
    rows = both.shape[0] - REACH
    chosen = jnp.where(last, both[REACH:], both[:rows])
    return jnp.concatenate([chosen, jnp.zeros((REACH, both.shape[1]), jnp.float32)], axis=0)


def window_copies(b, block, last, density, valid, cube, plane, sems):
    high = plane.shape[1]
    here = pl.ds(pl.multiple_of(jnp.minimum(block, last - 1) * (high // 2), high // 2), high)
    return [
        pltpu.make_async_copy(density.at[:, here], cube.at[b], sems.at[2 * b]),
        pltpu.make_async_copy(valid.at[here], plane.at[b], sems.at[2 * b + 1]),
    ]


def ready_kernel(partner, me, density, valid, row_taps, col_taps, after, col, row, cube, plane, sems):
    last = density.shape[1] * 2 // plane.shape[1] - 1
    copies = window_copies(0, me[0] ^ partner, last, density, valid, cube, plane, sems)
    for copy in copies:
        copy.start()
    build_columns(listed(col_taps), col)
    build_rows(listed(row_taps), row)
    for copy in copies:
        copy.wait()


def make_ready(me, partner, density, valid, row_taps, col_taps, after):
    slices, rows, cols = density.shape
    terms = row_taps.shape[0]
    high = LANES // terms
    vmem = pl.BlockSpec(memory_space=pltpu.VMEM)
    shapes = *matrix_shapes(terms, slices, high - HALO), (1, slices, high, cols)
    return pl.pallas_call(
        functools.partial(ready_kernel, partner),
        name="ready",
        in_specs=[pl.BlockSpec(memory_space=pltpu.SMEM)] + [anywhere()] * 2 + [vmem] * 2 + [anywhere()],
        out_specs=[vmem] * 4,
        out_shape=[pltpu.VMEM(shape, jnp.bfloat16) for shape in shapes] + [pltpu.VMEM((1, high, cols), jnp.int32)],
        scratch_shapes=[pltpu.SemaphoreType.DMA((2,))],
        compiler_params=params(),
        cost_estimate=cost(1, 1),
    )(me, held(density), held(valid), row_taps, col_taps, after)


def inner_kernel(wanted, loaded, end, me, *refs):
    count = len(wanted)
    pieces = [cut for _, cut in wanted]
    blocks = [me[0] ^ k for k, _ in wanted]
    outs = sum(len(cut) for cut in pieces)
    if loaded:
        (cube, plane, col, row, mean), tall = refs[:5], refs[-1]
        outs = list(refs[-1 - outs : -1])
    else:
        (density, valid, col, row, mean), (tall, cube, plane, sems) = refs[:5], refs[-4:]
        outs = list(refs[-4 - outs : -4])
        copies = [window_copies(b, blocks[b], end, density, valid, cube, plane, sems) for b in range(count)]
        for copy in sum(copies, []):
            copy.start()
    for b, cut in enumerate(pieces):
        if not loaded:
            for copy in copies[b]:
                copy.wait()
        last = blocks[b] == end
        mask = inner_rows(plane[b], last)
        field = convolve(
            lambda s, b=b, last=last, mask=mask: mask * (inner_rows(cube[b, s], last) - mean[s : s + 1, :1]),
            col,
            row,
            tall,
            REACH,
        ).astype(jnp.bfloat16)
        for _, start, stop in cut:
            outs.pop(0)[...] = field[start:stop]


def filter_inner(me, wanted, density, valid, ready, mean, *after):
    slices, rows, cols = density.shape
    col, row, cube, plane = ready
    high = plane.shape[1]
    count = len(wanted)
    loaded = not after
    vmem = pl.BlockSpec(memory_space=pltpu.VMEM)
    shapes = [(stop - start, slices, cols) for _, cut in wanted for _, start, stop in cut]
    field = [resident(cube), resident(plane)] if loaded else [held(density), held(valid)]
    scratch = [pltpu.VMEM((GROUP * LANES, cols), jnp.bfloat16)]
    if not loaded:
        scratch += [
            pltpu.VMEM((count, slices, high, cols), jnp.bfloat16),
            pltpu.VMEM((count, high, cols), jnp.int32),
            pltpu.SemaphoreType.DMA((2 * count,)),
        ]
    out = pl.pallas_call(
        functools.partial(inner_kernel, wanted, loaded, rows // (high - HALO) - 1),
        name="inner",
        in_specs=[pl.BlockSpec(memory_space=pltpu.SMEM)]
        + [vmem if loaded else anywhere()] * 2
        + [vmem] * 3
        + [anywhere()] * len(after),
        out_specs=[vmem] * len(shapes),
        out_shape=[pltpu.VMEM(shape, jnp.bfloat16) for shape in shapes],
        scratch_shapes=scratch,
        compiler_params=params(),
        cost_estimate=cost(1, 1),
    )(
        me,
        *field,
        resident(col),
        resident(row),
        mean,
        *after,
    )
    out = list(out)
    return [[out.pop(0) for _ in cut] for _, cut in wanted]


def band_kernel(wanted, me, density, valid, above, below, col, row, mean, *refs):
    (mask, tall, done, sems) = refs[-4:]
    pieces = [cut for _, cut in wanted]
    count = sum(len(cut) for cut in pieces)
    outs = refs[-4 - count : -4]
    slices = mean.shape[0]
    rows, cols = valid.shape
    terms = col.shape[2] // LANES
    block = done.shape[1]
    high = block + HALO
    step = pl.program_id(0)
    f32 = jnp.float32

    @pl.when(step == 0)
    def _():
        mask[:REACH] = above[slices].astype(f32)
        mask[REACH : REACH + rows] = valid[...].astype(f32)
        mask[REACH + rows :] = below[slices].astype(f32)

    steps = slices // PER

    @pl.when(step < steps)
    def _():
        for j in range(PER):
            s = step * PER + j
            x = jnp.concatenate([above[s].astype(f32), density[j].astype(f32), below[s].astype(f32)], axis=0)
            x = mask[...] * (x - mean[pl.ds(s, 1), :][:, :1])
            x = jnp.concatenate([x, jnp.zeros((rows + HALO, LANES), f32)], axis=1)
            x = pltpu.roll(x, REACH, 1).astype(jnp.bfloat16)
            x = jnp.concatenate([x[:, c : c + 2 * LANES] for c in range(0, cols, LANES)], axis=0)
            y = jnp.dot(x, col[s], preferred_element_type=f32).astype(jnp.bfloat16)
            for c in range(cols // LANES):
                for k in range(terms):
                    tall[s * terms + k, :, c * LANES : (c + 1) * LANES] = y[
                        c * (rows + HALO) : (c + 1) * (rows + HALO), k * LANES : (k + 1) * LANES
                    ]

    def copies(b):
        at = sum(len(cut) for cut in pieces[:b])
        last = (me[0] ^ wanted[b][0]) == rows // block - 1
        for p, (inner, start, stop) in enumerate(pieces[b]):
            here = jnp.where(last != (inner == 1), block - REACH, 0) + start
            yield pltpu.make_async_copy(done.at[b, pl.ds(here, stop - start)], outs[at + p], sems.at[at + p])

    @pl.when(step >= steps)
    def _():
        for j in range(PAIR):
            b = (step - steps) * PAIR + j
            partner = sum(jnp.where(b == i, k, 0) for i, (k, _) in enumerate(wanted))
            here = pl.ds(pl.multiple_of((me[0] ^ partner) * block, block), high)
            parts = []
            for g in range(slices // GROUP):
                slab = tall[g * GROUP * terms : (g + 1) * GROUP * terms, here, :].reshape(GROUP * LANES, cols)
                z = jnp.dot(row[g], slab, preferred_element_type=f32)
                parts.append(z.reshape(block, GROUP, cols))
            done[b] = jnp.concatenate(parts, axis=1).astype(jnp.bfloat16)

    for n in range(len(pieces) // PAIR):

        @pl.when(step == steps + n)
        def _():
            for b in range(n * PAIR, (n + 1) * PAIR):
                for copy in copies(b):
                    copy.start()

    @pl.when(step == pl.num_programs(0) - 1)
    def _():
        for b in range(len(pieces)):
            for copy in copies(b):
                copy.wait()


def filter_band(me, wanted, density, valid, above, below, ready, mean, *after):
    slices, rows, cols = density.shape
    col, row = ready[:2]
    terms = col.shape[2] // LANES
    block = LANES // terms - HALO
    count = len(wanted)

    def whole(x):
        return pl.BlockSpec(x.shape, lambda i, at: (0,) * x.ndim, pipeline_mode=pl.Buffered(1))

    shapes = [(stop - start, slices, cols) for _, cut in wanted for _, start, stop in cut]
    out = pl.pallas_call(
        functools.partial(band_kernel, wanted),
        name="band",
        grid_spec=pltpu.PrefetchScalarGridSpec(
            num_scalar_prefetch=1,
            grid=(slices // PER + count // PAIR,),
            in_specs=[pl.BlockSpec((PER, rows, cols), lambda i, at: (jnp.minimum(i, slices // PER - 1), 0, 0))]
            + [whole(x) for x in (valid, above, below)]
            + [pl.BlockSpec(memory_space=pltpu.VMEM)] * 2
            + [whole(mean)]
            + [anywhere()] * len(after),
            out_specs=[anywhere()] * len(shapes),
            scratch_shapes=[
                pltpu.VMEM((rows + HALO, cols), jnp.float32),
                pltpu.VMEM((slices * terms, rows + HALO, cols), jnp.bfloat16),
                pltpu.VMEM((count, block, slices, cols), jnp.bfloat16),
                pltpu.SemaphoreType.DMA((len(shapes),)),
            ],
        ),
        out_shape=[hbm(shape, jnp.bfloat16) for shape in shapes],
        compiler_params=params(),
        cost_estimate=cost(1, 1),
    )(
        me,
        held(density),
        held(valid),
        above,
        below,
        resident(col),
        resident(row),
        mean,
        *after,
    )
    out = list(out)
    return [[out.pop(0) for _ in cut] for _, cut in wanted]


def project_kernel(count, me, weights, *refs):
    parts, (amp_out, like_out, token) = refs[:count], refs[-3:]
    zbins = weights.shape[0] // 2
    rows, _, cols = parts[0].shape
    for r in range(rows):
        pencil = jnp.concatenate([x[r] for x in parts], axis=0)
        both = jnp.dot(weights[...], pencil, preferred_element_type=jnp.float32)
        amp = both[:zbins]
        amp_out[:, r * cols : (r + 1) * cols] = amp.astype(jnp.bfloat16)
        like_out[:, r * cols : (r + 1) * cols] = (amp * both[zbins:]).astype(jnp.bfloat16)
    token[...] = jnp.zeros_like(token)


def weights_kernel(peers, me, amp_matrix, like_matrix, out):
    slices = amp_matrix.shape[0] // peers
    for n, matrix in enumerate((amp_matrix, like_matrix)):
        rows = [matrix[pl.ds(pl.multiple_of((me[0] ^ k) * slices, slices), slices)] for k in range(peers)]
        turned = jnp.concatenate(rows, axis=0).astype(jnp.float32).T
        out[n * turned.shape[0] : (n + 1) * turned.shape[0]] = turned.astype(jnp.bfloat16)


def arrange_weights(me, peers, amp_matrix, like_matrix):
    slices, zbins = amp_matrix.shape
    vmem = pl.BlockSpec(memory_space=pltpu.VMEM)
    return pl.pallas_call(
        functools.partial(weights_kernel, peers),
        name="weights",
        in_specs=[pl.BlockSpec(memory_space=pltpu.SMEM), vmem, vmem],
        out_specs=vmem,
        out_shape=pltpu.VMEM((2 * zbins, slices), jnp.bfloat16),
        compiler_params=params(),
        cost_estimate=cost(1, 1),
    )(me, amp_matrix, like_matrix)


def project(me, group, weights, parts, total, earlier):
    inner, start, stop = group
    rows = stop - start
    _, slices, cols = parts[0][0].shape
    peers = len(parts)

    def place(i, me):
        upper = (me[0] == peers - 1) != (inner == 1)
        return 0, i + jnp.where(upper, (total - REACH) // PAIR, 0) + start // PAIR

    zbins = weights.shape[0] // 2
    count = len(parts)
    shape = hbm((zbins, total * cols), jnp.bfloat16)
    return pl.pallas_call(
        functools.partial(project_kernel, count),
        name="project",
        grid_spec=pltpu.PrefetchScalarGridSpec(
            num_scalar_prefetch=1,
            grid=(rows // PAIR,),
            in_specs=[pl.BlockSpec(weights.shape, lambda i, at: (0, 0))]
            + [
                pl.BlockSpec((PAIR, slices, cols), lambda i, at, start=start: (i + start // PAIR, 0, 0))
                for _, start in parts
            ]
            + [anywhere()] * len(earlier),
            out_specs=[pl.BlockSpec((zbins, PAIR * cols), place)] * 2
            + [pl.BlockSpec((8, LANES), lambda i, at: (0, 0))],
        ),
        out_shape=[shape, shape, hbm((8, LANES), jnp.float32)],
        input_output_aliases={2 + count + i: i for i in range(len(earlier))},
        compiler_params=params(),
        cost_estimate=cost(1, 1),
    )(me, weights, *[x for x, _ in parts], *earlier)


def gate_kernel(*refs):
    pass


def gate(x, *earlier, flops=1, space=pltpu.HBM):
    return pl.pallas_call(
        gate_kernel,
        name="gate",
        in_specs=[anywhere()] * (1 + len(earlier)),
        out_specs=anywhere(),
        out_shape=space(x.shape, x.dtype),
        input_output_aliases={0: 0},
        compiler_params=params(),
        cost_estimate=cost(flops, 1),
    )(pltpu.with_memory_space_constraint(x, space), *earlier)


INNER, OUTER = (1, 0, REACH), (0, 0, REACH)
HEAD, TAIL = (0, 0, 6), (0, 6, REACH)
FIRST = (((4, (INNER,)),), ((6, (INNER,)), (5, (INNER,))))
REST = (
    (5, (HEAD, TAIL)),
    (7, (INNER, HEAD, TAIL)),
    (2, (INNER, OUTER)),
    (3, (INNER, OUTER)),
    (4, (HEAD, TAIL)),
    (6, (HEAD, TAIL)),
    (1, (INNER, OUTER)),
    (0, (INNER, OUTER)),
)
ORDER = (
    (4, INNER, None),
    (6, INNER, None),
    (5, INNER, None),
    (7, INNER, 0),
    (2, INNER, 0),
    (4, HEAD, 1),
    (3, INNER, 1),
    (6, HEAD, 2),
    (2, OUTER, 2),
    (5, HEAD, 3),
    (1, INNER, 4),
    (7, HEAD, 5),
    (3, OUTER, 6),
    (1, OUTER, 7),
    (4, TAIL, 9),
    (6, TAIL, 10),
    (5, TAIL, 11),
    (7, TAIL, 12),
)


def fast(density, valid, row_taps, col_taps, amp_matrix, like_matrix):
    slices, rows, cols = density.shape
    peers = lax.axis_size("cuts")
    tiles = lax.axis_size("tile")
    block = rows // peers
    me = lax.axis_index("cuts").astype(jnp.int32).reshape(1)

    def swap(x, k):
        return lax.ppermute(x, "cuts", [(i, i ^ k) for i in range(peers)])

    own, first, last = masked_sums(density, valid)
    sums = [own] + [lax.ppermute(own, "tile", [(i, i ^ k) for i in range(tiles)]) for k in range(1, tiles)]
    ready = make_ready(me, ORDER[0][0], density, valid, row_taps, col_taps, own)
    mean, token = means(sums, slices, ready[0])

    made, arrived = {}, {}

    above = lax.ppermute(last, "tile", [(i, i + 1) for i in range(tiles - 1)])
    below = lax.ppermute(first, "tile", [(i + 1, i) for i in range(tiles - 1)])
    def keep(wanted, got):
        for (k, cut), parts in zip(wanted, got):
            for piece, x in zip(cut, parts):
                made[k, piece] = x

    def send(k, piece, *before):
        x = made[k, piece]
        arrived[k, piece] = swap(gate(x, *before) if before else x, k)

    after = ()
    for wanted in FIRST:
        got = filter_inner(me, wanted, density, valid, ready, mean, *after)
        keep(wanted, got)
        after = (resident(got[0][0]),)
    first_piece = ORDER[0][:2]
    send(*first_piece)
    got = filter_band(
        me, REST, density, valid, above, below, ready, mean, *after, resident(gate(token, arrived[first_piece], flops=BEFORE_BAND, space=pltpu.VMEM))
    )
    keep(REST, got)
    for piece in (INNER, OUTER):
        arrived[0, piece] = made[0, piece]

    weights = arrange_weights(me, peers, amp_matrix, like_matrix)
    result, tokens = [], []

    def finish(group):
        parts = []
        for k in range(peers):
            for piece in (group, INNER, OUTER):
                if (k, piece) in arrived and piece[0] == group[0]:
                    parts.append((arrived[k, piece], group[1] - piece[1]))
                    break
        *result[:], token = project(me, group, weights, parts, block, result)
        tokens.append(token)

    for at, (k, piece, wait) in enumerate(ORDER):
        if (k, piece) in arrived:
            continue
        before = [] if wait is None else [arrived[ORDER[wait][:2]]]
        if at == len(ORDER) - 3:
            finish(INNER)
            before.append(tokens[0])
        send(k, piece, *before)
    finish(HEAD)
    finish(TAIL)
    return tuple(result)


def extended(shard, sides, width):
    for axis, dim in sides:
        size, length = (lax.axis_size(axis), shard.shape[dim])
        up = [(i, (i + 1) % size) for i in range(size - 1)]
        down = [(j, i) for i, j in up]
        last = lax.slice_in_dim(shard, length - width, length, axis=dim)
        initial = lax.slice_in_dim(shard, 0, width, axis=dim)
        before = lax.ppermute(last, axis, up)
        after = lax.ppermute(initial, axis, down)
        shard = jnp.concatenate([before, shard, after], axis=dim)
    return shard


def band_matrix(taps, out_count, in_count):
    offset = lax.broadcasted_iota(jnp.int32, (out_count, in_count), 1) - lax.broadcasted_iota(
        jnp.int32, (out_count, in_count), 0
    )
    positions = lax.broadcasted_iota(jnp.int32, (1, 1, TAPS), 2)
    choose = (offset[:, :, None] == positions).astype(jnp.bfloat16)
    return jnp.einsum("ijt,kst->ksij", choose, taps, preferred_element_type=jnp.float32).astype(jnp.bfloat16)


def filter_field(padded, row_taps, col_taps):
    tall = padded.shape[1]
    cols = padded.shape[2]
    width = 2 * LANES
    row_band = band_matrix(row_taps, tall - HALO, tall)
    rowed = jnp.einsum("ksij,sjc->ksic", row_band, padded, preferred_element_type=jnp.float32).astype(jnp.bfloat16)
    widened = jnp.pad(rowed, ((0, 0), (0, 0), (0, 0), (REACH, REACH)))
    col_band = band_matrix(col_taps, width, width + HALO)
    pieces = []
    for begin in range(0, cols, width):
        segment = widened[:, :, :, begin : begin + width + HALO]
        pieces.append(jnp.einsum("ksrj,ksij->sri", segment, col_band, preferred_element_type=jnp.float32))
    return jnp.concatenate(pieces, axis=2).astype(jnp.bfloat16)


def general(density, valid, row_taps, col_taps, amp_matrix, like_matrix):
    slices, rows, cols = density.shape
    mask = valid.astype(jnp.float32)
    field = density.astype(jnp.float32)
    sums, count = lax.psum((jnp.sum(field * mask[None], axis=(1, 2)), jnp.sum(mask)), "tile")
    masked = (mask[None] * (field - (sums / count)[:, None, None])).astype(jnp.bfloat16)
    filtered = filter_field(extended(masked, (("tile", 1),), REACH), row_taps, col_taps)
    peers = lax.axis_size("cuts")
    share = rows * cols // peers
    pencil = lax.all_to_all(
        filtered.reshape(slices, peers, share), "cuts", split_axis=1, concat_axis=0, tiled=True
    ).reshape(slices * peers, share)
    amp = jnp.dot(amp_matrix.T, pencil, preferred_element_type=jnp.float32)
    like = amp * jnp.dot(like_matrix.T, pencil, preferred_element_type=jnp.float32)
    return amp.astype(jnp.bfloat16), like.astype(jnp.bfloat16)


def per_device(density, valid, row_taps, col_taps, amp_matrix, like_matrix):
    slices, rows, cols = density.shape
    terms = row_taps.shape[0]
    peers = lax.axis_size("cuts")
    fits = (
        peers == 8
        and lax.axis_size("tile") == 4
        and slices == 2 * GROUP
        and terms == 4
        and rows == peers * (LANES // terms - HALO)
        and cols % (2 * LANES) == 0
    )
    run = fast if fits else general
    return run(density, valid, row_taps, col_taps, amp_matrix, like_matrix)


def solution(mesh):
    return jax.shard_map(
        per_device,
        mesh=mesh,
        in_specs=(
            P("cuts", "tile", None),
            P("tile", None),
            P(None, "cuts", None),
            P(None, "cuts", None),
            P(),
            P(),
        ),
        out_specs=(P(None, ("tile", "cuts")), P(None, ("tile", "cuts"))),
        check_vma=False,
    )
```

```python
import functools

import jax
import jax.numpy as jnp
from jax import lax
from jax.experimental import pallas as pl
from jax.experimental.pallas import tpu as pltpu
from jax.sharding import PartitionSpec as P

REACH = 8
TAPS = 2 * REACH + 1
LANES = 128
GROUP = 8
PER = 4
PAIR = 2
CHUNKS = 8
BEFORE_BAND = 2e9
MIB = 1024 * 1024
HALO = 2 * REACH


def params(mib=33):
    return pltpu.CompilerParams(vmem_limit_bytes=mib * MIB)


def hbm(shape, dtype):
    return pltpu.HBM(shape, dtype)


def held(x):
    return pltpu.with_memory_space_constraint(x, pltpu.HBM)


def resident(x):
    return pltpu.with_memory_space_constraint(x, pltpu.VMEM)


def anywhere():
    return pl.BlockSpec(memory_space=pl.ANY)


def cost(flops, moved):
    return pl.CostEstimate(flops=int(flops), bytes_accessed=int(moved), transcendentals=0)


def tap_flip():
    tap = lax.broadcasted_iota(jnp.int32, (TAPS, 2 * LANES), 0)
    lane = lax.broadcasted_iota(jnp.int32, (TAPS, 2 * LANES), 1)
    return (lax.rem(tap + lane, 2 * LANES) == 0).astype(jnp.bfloat16)


def column_band(taps):
    band = pltpu.roll(jnp.broadcast_to(taps, (LANES + HALO, 2 * LANES)), 0, 1, stride=1, stride_axis=0)
    return band[:, :LANES].astype(jnp.bfloat16)


def build_columns(col_taps, col_out):
    terms, slices = len(col_taps), col_taps[0].shape[0]
    for k in range(terms):
        base = jnp.dot(col_taps[k], tap_flip(), preferred_element_type=jnp.float32)
        for s in range(slices):
            col_out[s, : LANES + HALO, k * LANES : (k + 1) * LANES] = column_band(base[s : s + 1])
    for s in range(slices):
        col_out[s, LANES + HALO :, :] = jnp.zeros((LANES - HALO, terms * LANES), jnp.bfloat16)


def build_rows(row_taps, row_out):
    terms, slices = len(row_taps), row_taps[0].shape[0]
    high = LANES // terms
    tap = lax.broadcasted_iota(jnp.int32, (TAPS, LANES), 0)
    lane = lax.broadcasted_iota(jnp.int32, (TAPS, LANES), 1)
    base = jnp.zeros((slices, LANES), jnp.float32)
    for k in range(terms):
        place = (lane == tap + k * high).astype(jnp.bfloat16)
        base = base + jnp.dot(row_taps[k], place, preferred_element_type=jnp.float32)
    sub = lax.broadcasted_iota(jnp.int32, (GROUP, LANES), 0)
    for g in range(slices // GROUP):
        own = base[g * GROUP : (g + 1) * GROUP]
        for pair in range(row_out.shape[1] // (2 * GROUP)):
            shifted = [pltpu.roll(own, 2 * pair + h, 1) for h in range(2)]
            for s in range(GROUP):
                both = jnp.concatenate([jnp.where(sub == s, x, 0.0) for x in shifted], axis=0)
                row_out[
                    g, pair * 2 * GROUP : (pair + 1) * 2 * GROUP, s * LANES : (s + 1) * LANES
                ] = both.astype(jnp.bfloat16)


def listed(taps):
    return [taps[k] for k in range(taps.shape[0])]


def matrix_shapes(terms, slices, rows):
    return (slices, 2 * LANES, terms * LANES), (slices // GROUP, rows * GROUP, GROUP * LANES)


def convolve(field, col, row, tall, rows):
    slices, _, wide = col.shape
    terms = wide // LANES
    high, cols = LANES // terms, tall.shape[1]
    parts = []
    for g in range(slices // GROUP):
        for j in range(GROUP):
            s = g * GROUP + j
            x = jnp.concatenate([field(s), jnp.zeros((high, LANES), jnp.float32)], axis=1)
            x = pltpu.roll(x, REACH, 1).astype(jnp.bfloat16)
            x = jnp.concatenate([x[:, c : c + 2 * LANES] for c in range(0, cols, LANES)], axis=0)
            y = jnp.dot(x, col[s], preferred_element_type=jnp.float32).astype(jnp.bfloat16)
            for c in range(cols // LANES):
                for k in range(terms):
                    tall[(j * terms + k) * high : (j * terms + k + 1) * high, c * LANES : (c + 1) * LANES] = y[
                        c * high : (c + 1) * high, k * LANES : (k + 1) * LANES
                    ]
        z = jnp.dot(row[g, : rows * GROUP], tall[...], preferred_element_type=jnp.float32)
        parts.append(z.reshape(rows, GROUP, cols))
    return jnp.concatenate(parts, axis=1)


def sums_kernel(density, valid, after, out, cube, plane, sems):
    slices, rows, cols = cube.shape
    step = rows // CHUNKS

    def copies(i):
        at = pl.ds(pl.multiple_of(i * step, step), step)
        yield pltpu.make_async_copy(density.at[:, at], cube.at[:, at], sems.at[i])
        yield pltpu.make_async_copy(valid.at[at], plane.at[at], sems.at[CHUNKS + i])

    for i in range(CHUNKS):
        for copy in copies(i):
            copy.start()
    out[...] = jnp.zeros_like(out)

    def body(i, _):
        for copy in copies(i):
            copy.wait()
        at = pl.ds(pl.multiple_of(i * step, step), step)
        mask = plane[at] != 0
        for s in range(slices + 1):
            x = cube[s, at].astype(jnp.float32) if s < slices else jnp.ones((step, cols), jnp.float32)
            x = jnp.where(mask, x, 0.0).reshape(step // 8, 8, cols).sum(axis=0)
            x = sum(x[:, c : c + LANES] for c in range(0, cols, LANES))
            out[s : s + 1, :] += jnp.sum(x, axis=0, keepdims=True)
        return 0

    lax.fori_loop(0, CHUNKS, body, 0)


def masked_sums(density, valid, after):
    slices, rows, cols = density.shape
    return pl.pallas_call(
        sums_kernel,
        name="sums",
        in_specs=[anywhere()] * 3,
        out_specs=pl.BlockSpec(memory_space=pltpu.VMEM),
        out_shape=pltpu.VMEM((slices + 8, LANES), jnp.float32),
        scratch_shapes=[
            pltpu.VMEM(density.shape, jnp.bfloat16),
            pltpu.VMEM(valid.shape, jnp.int32),
            pltpu.SemaphoreType.DMA((2 * CHUNKS,)),
        ],
        compiler_params=params(),
        cost_estimate=cost(1, 1),
    )(held(density), held(valid), resident(after))


def mean_kernel(*refs):
    sums, (out, token) = refs[:2], refs[-2:]
    slices = out.shape[0]
    token[...] = jnp.zeros_like(token)
    total = sums[0][...] + sums[1][...]
    total = jnp.sum(total, axis=1, keepdims=True)
    out[...] = jnp.broadcast_to(total[:slices] / total[slices : slices + 1], out.shape)


def add_kernel(one, two, out):
    out[...] = one[...] + two[...]


def add(one, two):
    vmem = pl.BlockSpec(memory_space=pltpu.VMEM)
    return pl.pallas_call(
        add_kernel,
        name="add",
        in_specs=[vmem] * 2,
        out_specs=vmem,
        out_shape=pltpu.VMEM(one.shape, one.dtype),
        compiler_params=params(),
        cost_estimate=cost(1, 1),
    )(one, two)


def means(sums, slices, after):
    vmem = pl.BlockSpec(memory_space=pltpu.VMEM)
    return pl.pallas_call(
        mean_kernel,
        name="means",
        in_specs=[vmem] * len(sums) + [anywhere()],
        out_specs=[vmem] * 2,
        out_shape=[pltpu.VMEM((slices, LANES), jnp.float32), pltpu.VMEM((8, LANES), jnp.float32)],
        compiler_params=params(),
        cost_estimate=cost(1, 1),
    )(*sums, resident(after))


def inner_rows(both, last):
    both = both.astype(jnp.float32)
    rows = both.shape[0] - REACH
    chosen = jnp.where(last, both[REACH:], both[:rows])
    return jnp.concatenate([chosen, jnp.zeros((REACH, both.shape[1]), jnp.float32)], axis=0)


def window_copies(b, block, last, density, valid, cube, plane, sems):
    high = plane.shape[1]
    here = pl.ds(pl.multiple_of(jnp.minimum(block, last - 1) * (high // 2), high // 2), high)
    return [
        pltpu.make_async_copy(density.at[:, here], cube.at[b], sems.at[2 * b]),
        pltpu.make_async_copy(valid.at[here], plane.at[b], sems.at[2 * b + 1]),
    ]


def ready_kernel(partner, me, density, valid, row_taps, col_taps, col, row, cube, plane, first, last, ends, masks, sems):
    slices, rows, _ = density.shape
    block = ends.shape[2]
    copies = window_copies(0, me[0] ^ partner, rows // block - 1, density, valid, cube, plane, sems)
    for n, start in enumerate((0, rows - block)):
        copies.append(pltpu.make_async_copy(density.at[:, start : start + block], ends.at[n], sems.at[2 + 2 * n]))
        copies.append(pltpu.make_async_copy(valid.at[start : start + block], masks.at[n], sems.at[3 + 2 * n]))
    for copy in copies:
        copy.start()
    build_columns(listed(col_taps), col)
    build_rows(listed(row_taps), row)
    for copy in copies:
        copy.wait()
    first[:slices] = ends[0, :, :REACH]
    first[slices] = masks[0, :REACH].astype(jnp.bfloat16)
    last[:slices] = ends[1, :, block - REACH :]
    last[slices] = masks[1, block - REACH :].astype(jnp.bfloat16)


def make_ready(me, partner, density, valid, row_taps, col_taps):
    slices, rows, cols = density.shape
    terms = row_taps.shape[0]
    high = LANES // terms
    block = high - HALO
    vmem = pl.BlockSpec(memory_space=pltpu.VMEM)
    edge = pltpu.VMEM((slices + 1, REACH, cols), jnp.bfloat16)
    shapes = *matrix_shapes(terms, slices, block), (1, slices, high, cols)
    return pl.pallas_call(
        functools.partial(ready_kernel, partner),
        name="ready",
        in_specs=[pl.BlockSpec(memory_space=pltpu.SMEM)] + [anywhere()] * 2 + [vmem] * 2,
        out_specs=[vmem] * 6,
        out_shape=[pltpu.VMEM(shape, jnp.bfloat16) for shape in shapes]
        + [pltpu.VMEM((1, high, cols), jnp.int32), edge, edge],
        scratch_shapes=[
            pltpu.VMEM((2, slices, block, cols), jnp.bfloat16),
            pltpu.VMEM((2, block, cols), jnp.int32),
            pltpu.SemaphoreType.DMA((6,)),
        ],
        compiler_params=params(),
        cost_estimate=cost(1, 1),
    )(me, held(density), held(valid), row_taps, col_taps)


def inner_kernel(wanted, loaded, own_mean, end, me, *refs):
    count = len(wanted)
    blocks = [me[0] ^ k for k, _ in wanted]
    (first, second, col, row), refs = refs[:4], refs[4:]
    mean = None if own_mean else refs[0]
    results = sum(len(cut) for _, cut in wanted) + (1 if own_mean else 0)
    if loaded:
        cube, plane, tall = first, second, refs[-1]
        outs = list(refs[-1 - results : -1])
    else:
        tall, cube, plane, sems = refs[-4:]
        outs = list(refs[-4 - results : -4])
        copies = [window_copies(b, blocks[b], end, first, second, cube, plane, sems) for b in range(count)]
        for copy in sum(copies, []):
            copy.start()
    for b, (_, cut) in enumerate(wanted):
        if not loaded:
            for copy in copies[b]:
                copy.wait()
        last = blocks[b] == end
        mask = inner_rows(plane[b], last)
        if own_mean:

            def total(x):
                x = x.reshape(x.shape[0] // 8, 8, x.shape[1]).sum(axis=0)
                x = sum(x[:, c : c + LANES] for c in range(0, x.shape[1], LANES))
                return jnp.sum(x, axis=0, keepdims=True)

            sums = [total(mask * inner_rows(cube[b, s], last)) for s in range(cube.shape[1])]
            sums = jnp.sum(jnp.concatenate(sums, axis=0), axis=1, keepdims=True)
            centre = sums / jnp.sum(total(mask), axis=1, keepdims=True)
            outs[-1][...] = jnp.broadcast_to(centre, outs[-1].shape)
        else:
            centre = mean[:, :1]
        field = convolve(
            lambda s, b=b, last=last, mask=mask: mask * (inner_rows(cube[b, s], last) - centre[s : s + 1]),
            col,
            row,
            tall,
            REACH,
        ).astype(jnp.bfloat16)
        for _, start, stop in cut:
            outs.pop(0)[...] = field[start:stop]


def filter_inner(me, wanted, density, valid, ready, loaded, mean, *after):
    slices, rows, cols = density.shape
    col, row, cube, plane = ready[:4]
    high = plane.shape[1]
    count = len(wanted)
    own_mean = mean is None
    vmem = pl.BlockSpec(memory_space=pltpu.VMEM)
    shapes = [(stop - start, slices, cols) for _, cut in wanted for _, start, stop in cut]
    field = [resident(cube), resident(plane)] if loaded else [held(density), held(valid)]
    scratch = [pltpu.VMEM((GROUP * LANES, cols), jnp.bfloat16)]
    if not loaded:
        scratch += [
            pltpu.VMEM((count, slices, high, cols), jnp.bfloat16),
            pltpu.VMEM((count, high, cols), jnp.int32),
            pltpu.SemaphoreType.DMA((2 * count,)),
        ]
    means_in, means_out = ([], [pltpu.VMEM((slices, LANES), jnp.float32)]) if own_mean else ([mean], [])
    out = pl.pallas_call(
        functools.partial(inner_kernel, wanted, loaded, own_mean, rows // (high - HALO) - 1),
        name="inner",
        in_specs=[pl.BlockSpec(memory_space=pltpu.SMEM)]
        + [vmem if loaded else anywhere()] * 2
        + [vmem] * (2 + len(means_in))
        + [anywhere()] * len(after),
        out_specs=[vmem] * (len(shapes) + len(means_out)),
        out_shape=[pltpu.VMEM(shape, jnp.bfloat16) for shape in shapes] + means_out,
        scratch_shapes=scratch,
        compiler_params=params(),
        cost_estimate=cost(1, 1),
    )(me, *field, resident(col), resident(row), *means_in, *after)
    out = list(out)
    return [[out.pop(0) for _ in cut] for _, cut in wanted] + out


def notes_kernel(mean, row_taps, col_taps, *refs):
    terms, _, taps = row_taps.shape
    count = len(refs) // 2
    for centre, note in zip(refs[:count], refs[count:]):
        note[...] = jnp.zeros_like(note)
        note[:terms, :, :taps] = row_taps[...].astype(jnp.float32)
        note[terms : 2 * terms, :, :taps] = col_taps[...].astype(jnp.float32)
        note[2 * terms] = centre[...] - mean[...]


def notes_of(mean, row_taps, col_taps, centres):
    terms, slices, _ = row_taps.shape
    vmem = pl.BlockSpec(memory_space=pltpu.VMEM)
    return pl.pallas_call(
        notes_kernel,
        name="notes",
        in_specs=[vmem] * (3 + len(centres)),
        out_specs=[vmem] * len(centres),
        out_shape=[hbm((2 * terms + 1, slices, LANES), jnp.float32)] * len(centres),
        compiler_params=params(),
        cost_estimate=cost(1, 1),
    )(mean, row_taps, col_taps, *centres)


def mend_kernel(end, me, valid, note, piece, out, col, row, tall, plane, sem):
    terms = note.shape[0] // 2
    high = plane.shape[0]
    here = pl.ds(pl.multiple_of(jnp.minimum(me[0], end - 1) * (high // 2), high // 2), high)
    copy = pltpu.make_async_copy(valid.at[here], plane, sem)
    copy.start()
    taps = [note[k, :, :TAPS].astype(jnp.bfloat16) for k in range(2 * terms)]
    build_columns(taps[terms:], col)
    build_rows(taps[:terms], row)
    copy.wait()
    mask = inner_rows(plane[...], me[0] == end)
    field = convolve(lambda s: mask, col, row, tall, REACH)
    shift = jnp.broadcast_to(note[2 * terms][:, :1], field.shape[1:])
    out[...] = (piece[...].astype(jnp.float32) + shift[None] * field).astype(jnp.bfloat16)


def mend(me, valid, note, piece):
    rows, cols = valid.shape
    terms, slices = note.shape[0] // 2, note.shape[1]
    high = LANES // terms
    vmem = pl.BlockSpec(memory_space=pltpu.VMEM)
    return pl.pallas_call(
        functools.partial(mend_kernel, rows // (high - HALO) - 1),
        name="mend",
        in_specs=[pl.BlockSpec(memory_space=pltpu.SMEM), anywhere(), vmem, vmem],
        out_specs=vmem,
        out_shape=pltpu.VMEM(piece.shape, jnp.bfloat16),
        scratch_shapes=[pltpu.VMEM(shape, jnp.bfloat16) for shape in matrix_shapes(terms, slices, REACH)]
        + [
            pltpu.VMEM((GROUP * LANES, cols), jnp.bfloat16),
            pltpu.VMEM((high, cols), jnp.int32),
            pltpu.SemaphoreType.DMA,
        ],
        compiler_params=params(),
        cost_estimate=cost(1, 1),
    )(me, held(valid), note, piece)


def band_kernel(wanted, me, density, valid, above, below, col, row, mean, *refs):
    (mask, tall, done, sems) = refs[-4:]
    pieces = [cut for _, cut in wanted]
    count = sum(len(cut) for cut in pieces)
    outs = refs[-4 - count : -4]
    slices = mean.shape[0]
    rows, cols = valid.shape
    terms = col.shape[2] // LANES
    block = done.shape[1]
    high = block + HALO
    step = pl.program_id(0)
    f32 = jnp.float32

    @pl.when(step == 0)
    def _():
        mask[:REACH] = above[slices].astype(f32)
        mask[REACH : REACH + rows] = valid[...].astype(f32)
        mask[REACH + rows :] = below[slices].astype(f32)

    steps = slices // PER

    @pl.when(step < steps)
    def _():
        for j in range(PER):
            s = step * PER + j
            x = jnp.concatenate([above[s].astype(f32), density[j].astype(f32), below[s].astype(f32)], axis=0)
            x = mask[...] * (x - mean[pl.ds(s, 1), :][:, :1])
            x = jnp.concatenate([x, jnp.zeros((rows + HALO, LANES), f32)], axis=1)
            x = pltpu.roll(x, REACH, 1).astype(jnp.bfloat16)
            x = jnp.concatenate([x[:, c : c + 2 * LANES] for c in range(0, cols, LANES)], axis=0)
            y = jnp.dot(x, col[s], preferred_element_type=f32).astype(jnp.bfloat16)
            for c in range(cols // LANES):
                for k in range(terms):
                    tall[s * terms + k, :, c * LANES : (c + 1) * LANES] = y[
                        c * (rows + HALO) : (c + 1) * (rows + HALO), k * LANES : (k + 1) * LANES
                    ]

    def copies(b):
        at = sum(len(cut) for cut in pieces[:b])
        last = (me[0] ^ wanted[b][0]) == rows // block - 1
        for p, (inner, start, stop) in enumerate(pieces[b]):
            here = jnp.where(last != (inner == 1), block - REACH, 0) + start
            yield pltpu.make_async_copy(done.at[b, pl.ds(here, stop - start)], outs[at + p], sems.at[at + p])

    @pl.when(step >= steps)
    def _():
        for j in range(PAIR):
            b = (step - steps) * PAIR + j
            partner = sum(jnp.where(b == i, k, 0) for i, (k, _) in enumerate(wanted))
            here = pl.ds(pl.multiple_of((me[0] ^ partner) * block, block), high)
            parts = []
            for g in range(slices // GROUP):
                slab = tall[g * GROUP * terms : (g + 1) * GROUP * terms, here, :].reshape(GROUP * LANES, cols)
                z = jnp.dot(row[g], slab, preferred_element_type=f32)
                parts.append(z.reshape(block, GROUP, cols))
            done[b] = jnp.concatenate(parts, axis=1).astype(jnp.bfloat16)

    for n in range(len(pieces) // PAIR):

        @pl.when(step == steps + n)
        def _():
            for b in range(n * PAIR, (n + 1) * PAIR):
                for copy in copies(b):
                    copy.start()

    @pl.when(step == pl.num_programs(0) - 1)
    def _():
        for b in range(len(pieces)):
            for copy in copies(b):
                copy.wait()


def filter_band(me, wanted, density, valid, above, below, ready, mean, *after):
    slices, rows, cols = density.shape
    col, row = ready[:2]
    terms = col.shape[2] // LANES
    block = LANES // terms - HALO
    count = len(wanted)

    def whole(x):
        return pl.BlockSpec(x.shape, lambda i, at: (0,) * x.ndim, pipeline_mode=pl.Buffered(1))

    shapes = [(stop - start, slices, cols) for _, cut in wanted for _, start, stop in cut]
    out = pl.pallas_call(
        functools.partial(band_kernel, wanted),
        name="band",
        grid_spec=pltpu.PrefetchScalarGridSpec(
            num_scalar_prefetch=1,
            grid=(slices // PER + count // PAIR,),
            in_specs=[pl.BlockSpec((PER, rows, cols), lambda i, at: (jnp.minimum(i, slices // PER - 1), 0, 0))]
            + [whole(x) for x in (valid, above, below)]
            + [pl.BlockSpec(memory_space=pltpu.VMEM)] * 2
            + [whole(mean)]
            + [anywhere()] * len(after),
            out_specs=[anywhere()] * len(shapes),
            scratch_shapes=[
                pltpu.VMEM((rows + HALO, cols), jnp.float32),
                pltpu.VMEM((slices * terms, rows + HALO, cols), jnp.bfloat16),
                pltpu.VMEM((count, block, slices, cols), jnp.bfloat16),
                pltpu.SemaphoreType.DMA((len(shapes),)),
            ],
        ),
        out_shape=[hbm(shape, jnp.bfloat16) for shape in shapes],
        compiler_params=params(),
        cost_estimate=cost(1, 1),
    )(
        me,
        held(density),
        held(valid),
        above,
        below,
        resident(col),
        resident(row),
        mean,
        *after,
    )
    out = list(out)
    return [[out.pop(0) for _ in cut] for _, cut in wanted]


def project_kernel(count, me, weights, *refs):
    parts, (amp_out, like_out, token) = refs[:count], refs[-3:]
    zbins = weights.shape[0] // 2
    rows, _, cols = parts[0].shape
    for r in range(rows):
        pencil = jnp.concatenate([x[r] for x in parts], axis=0)
        both = jnp.dot(weights[...], pencil, preferred_element_type=jnp.float32)
        amp = both[:zbins]
        amp_out[:, r * cols : (r + 1) * cols] = amp.astype(jnp.bfloat16)
        like_out[:, r * cols : (r + 1) * cols] = (amp * both[zbins:]).astype(jnp.bfloat16)
    token[...] = jnp.zeros_like(token)


def weights_kernel(peers, me, amp_matrix, like_matrix, out):
    slices = amp_matrix.shape[0] // peers
    for n, matrix in enumerate((amp_matrix, like_matrix)):
        rows = [matrix[pl.ds(pl.multiple_of((me[0] ^ k) * slices, slices), slices)] for k in range(peers)]
        turned = jnp.concatenate(rows, axis=0).astype(jnp.float32).T
        out[n * turned.shape[0] : (n + 1) * turned.shape[0]] = turned.astype(jnp.bfloat16)


def arrange_weights(me, peers, amp_matrix, like_matrix):
    slices, zbins = amp_matrix.shape
    vmem = pl.BlockSpec(memory_space=pltpu.VMEM)
    return pl.pallas_call(
        functools.partial(weights_kernel, peers),
        name="weights",
        in_specs=[pl.BlockSpec(memory_space=pltpu.SMEM), vmem, vmem],
        out_specs=vmem,
        out_shape=pltpu.VMEM((2 * zbins, slices), jnp.bfloat16),
        compiler_params=params(),
        cost_estimate=cost(1, 1),
    )(me, amp_matrix, like_matrix)


def project(me, group, weights, parts, total, earlier):
    inner, start, stop = group
    rows = stop - start
    _, slices, cols = parts[0][0].shape
    peers = len(parts)

    def place(i, me):
        upper = (me[0] == peers - 1) != (inner == 1)
        return 0, i + jnp.where(upper, (total - REACH) // PAIR, 0) + start // PAIR

    zbins = weights.shape[0] // 2
    count = len(parts)
    shape = hbm((zbins, total * cols), jnp.bfloat16)
    return pl.pallas_call(
        functools.partial(project_kernel, count),
        name="project",
        grid_spec=pltpu.PrefetchScalarGridSpec(
            num_scalar_prefetch=1,
            grid=(rows // PAIR,),
            in_specs=[pl.BlockSpec(weights.shape, lambda i, at: (0, 0))]
            + [
                pl.BlockSpec((PAIR, slices, cols), lambda i, at, start=start: (i + start // PAIR, 0, 0))
                for _, start in parts
            ]
            + [anywhere()] * len(earlier),
            out_specs=[pl.BlockSpec((zbins, PAIR * cols), place)] * 2
            + [pl.BlockSpec((8, LANES), lambda i, at: (0, 0))],
        ),
        out_shape=[shape, shape, hbm((8, LANES), jnp.float32)],
        input_output_aliases={2 + count + i: i for i in range(len(earlier))},
        compiler_params=params(),
        cost_estimate=cost(1, 1),
    )(me, weights, *[x for x, _ in parts], *earlier)


def gate_kernel(*refs):
    pass


def gate(x, *earlier, flops=1, space=pltpu.HBM):
    return pl.pallas_call(
        gate_kernel,
        name="gate",
        in_specs=[anywhere()] * (1 + len(earlier)),
        out_specs=anywhere(),
        out_shape=space(x.shape, x.dtype),
        input_output_aliases={0: 0},
        compiler_params=params(),
        cost_estimate=cost(flops, 1),
    )(pltpu.with_memory_space_constraint(x, space), *earlier)


INNER, OUTER = (1, 0, REACH), (0, 0, REACH)
HEAD, TAIL = (0, 0, 6), (0, 6, REACH)
EARLY = (4, 6)
REST = (
    (5, (HEAD, TAIL)),
    (7, (INNER, HEAD, TAIL)),
    (2, (INNER, OUTER)),
    (3, (INNER, OUTER)),
    (4, (HEAD, TAIL)),
    (6, (HEAD, TAIL)),
    (1, (INNER, OUTER)),
    (0, (INNER, OUTER)),
)
ORDER = (
    (4, INNER, None),
    (6, INNER, None),
    (5, INNER, None),
    (7, INNER, 0),
    (2, INNER, 0),
    (4, HEAD, 1),
    (3, INNER, 1),
    (6, HEAD, 2),
    (2, OUTER, 2),
    (5, HEAD, 3),
    (1, INNER, 4),
    (7, HEAD, 5),
    (3, OUTER, 6),
    (1, OUTER, 7),
    (4, TAIL, 9),
    (6, TAIL, 10),
    (5, TAIL, 11),
    (7, TAIL, 12),
)
NOTES, MENDED = 3, 14
AFTER = 1


def fast(density, valid, row_taps, col_taps, amp_matrix, like_matrix):
    slices, rows, cols = density.shape
    peers = lax.axis_size("cuts")
    tiles = lax.axis_size("tile")
    block = rows // peers
    me = lax.axis_index("cuts").astype(jnp.int32).reshape(1)

    def swap(x, k):
        return lax.ppermute(x, "cuts", [(i, i ^ k) for i in range(peers)])

    made, arrived = {}, {}

    def keep(wanted, got):
        for (k, cut), parts in zip(wanted, got):
            for piece, x in zip(cut, parts):
                made[k, piece] = x

    def send(k, piece, *before):
        x = made[k, piece]
        arrived[k, piece] = swap(gate(x, *before) if before else x, k)

    ready = make_ready(me, EARLY[0], density, valid, row_taps, col_taps)
    centres = []
    for k in EARLY:
        wanted = ((k, (INNER,)),)
        got, centre = filter_inner(
            me, wanted, density, valid, ready, not centres, None, *[resident(x) for x in centres]
        )
        keep(wanted, [got])
        centres.append(centre)
        send(k, INNER)
    first, last = [gate(x, centres[0], space=pltpu.VMEM) for x in ready[4:]]
    above = lax.ppermute(last, "tile", [(i, i + 1) for i in range(tiles - 1)])
    below = lax.ppermute(first, "tile", [(i + 1, i) for i in range(tiles - 1)])
    sums = [masked_sums(density, valid, centres[AFTER])]
    for k in (1, 2):
        if k == 2:
            sums = [add(*sums)]
        sums.append(lax.ppermute(sums[0], "tile", [(i, i ^ k) for i in range(tiles)]))
    mean, token = means(sums, slices, centres[-1])
    wanted = ((5, (INNER,)),)
    got = filter_inner(me, wanted, density, valid, ready, False, mean)
    keep(wanted, got)
    first_piece = ORDER[0][:2]
    got = filter_band(
        me, REST, density, valid, above, below, ready, mean, resident(made[5, INNER]),
        resident(gate(token, arrived[first_piece], flops=BEFORE_BAND, space=pltpu.VMEM)),
    )
    keep(REST, got)
    for piece in (INNER, OUTER):
        arrived[0, piece] = made[0, piece]

    weights = arrange_weights(me, peers, amp_matrix, like_matrix)
    result, tokens = [], []

    def finish(group):
        parts = []
        for k in range(peers):
            for piece in (group, INNER, OUTER):
                if (k, piece) in arrived and piece[0] == group[0]:
                    parts.append((arrived[k, piece], group[1] - piece[1]))
                    break
        *result[:], token = project(me, group, weights, parts, block, result)
        tokens.append(token)

    notes = notes_of(mean, row_taps, col_taps, centres)
    for at, (k, piece, wait) in enumerate(ORDER):
        if at == NOTES:
            notes = [swap(gate(note, arrived[ORDER[0][:2]]), k) for k, note in zip(EARLY, notes)]
        if at == MENDED:
            for k_early, note in zip(EARLY, notes):
                arrived[k_early, INNER] = mend(me, valid, note, arrived[k_early, INNER])
        if (k, piece) in arrived:
            continue
        before = [] if wait is None else [arrived[ORDER[wait][:2]]]
        if at == MENDED:
            before += [arrived[k_early, INNER] for k_early in EARLY]
        if at == len(ORDER) - 3:
            finish(INNER)
            before.append(tokens[0])
        send(k, piece, *before)
    finish(HEAD)
    finish(TAIL)
    return tuple(result)


def extended(shard, sides, width):
    for axis, dim in sides:
        size, length = (lax.axis_size(axis), shard.shape[dim])
        up = [(i, (i + 1) % size) for i in range(size - 1)]
        down = [(j, i) for i, j in up]
        last = lax.slice_in_dim(shard, length - width, length, axis=dim)
        initial = lax.slice_in_dim(shard, 0, width, axis=dim)
        before = lax.ppermute(last, axis, up)
        after = lax.ppermute(initial, axis, down)
        shard = jnp.concatenate([before, shard, after], axis=dim)
    return shard


def band_matrix(taps, out_count, in_count):
    offset = lax.broadcasted_iota(jnp.int32, (out_count, in_count), 1) - lax.broadcasted_iota(
        jnp.int32, (out_count, in_count), 0
    )
    positions = lax.broadcasted_iota(jnp.int32, (1, 1, TAPS), 2)
    choose = (offset[:, :, None] == positions).astype(jnp.bfloat16)
    return jnp.einsum("ijt,kst->ksij", choose, taps, preferred_element_type=jnp.float32).astype(jnp.bfloat16)


def filter_field(padded, row_taps, col_taps):
    tall = padded.shape[1]
    cols = padded.shape[2]
    width = 2 * LANES
    row_band = band_matrix(row_taps, tall - HALO, tall)
    rowed = jnp.einsum("ksij,sjc->ksic", row_band, padded, preferred_element_type=jnp.float32).astype(jnp.bfloat16)
    widened = jnp.pad(rowed, ((0, 0), (0, 0), (0, 0), (REACH, REACH)))
    col_band = band_matrix(col_taps, width, width + HALO)
    pieces = []
    for begin in range(0, cols, width):
        segment = widened[:, :, :, begin : begin + width + HALO]
        pieces.append(jnp.einsum("ksrj,ksij->sri", segment, col_band, preferred_element_type=jnp.float32))
    return jnp.concatenate(pieces, axis=2).astype(jnp.bfloat16)


def general(density, valid, row_taps, col_taps, amp_matrix, like_matrix):
    slices, rows, cols = density.shape
    mask = valid.astype(jnp.float32)
    field = density.astype(jnp.float32)
    sums, count = lax.psum((jnp.sum(field * mask[None], axis=(1, 2)), jnp.sum(mask)), "tile")
    masked = (mask[None] * (field - (sums / count)[:, None, None])).astype(jnp.bfloat16)
    filtered = filter_field(extended(masked, (("tile", 1),), REACH), row_taps, col_taps)
    peers = lax.axis_size("cuts")
    share = rows * cols // peers
    pencil = lax.all_to_all(
        filtered.reshape(slices, peers, share), "cuts", split_axis=1, concat_axis=0, tiled=True
    ).reshape(slices * peers, share)
    amp = jnp.dot(amp_matrix.T, pencil, preferred_element_type=jnp.float32)
    like = amp * jnp.dot(like_matrix.T, pencil, preferred_element_type=jnp.float32)
    return amp.astype(jnp.bfloat16), like.astype(jnp.bfloat16)


def per_device(density, valid, row_taps, col_taps, amp_matrix, like_matrix):
    slices, rows, cols = density.shape
    terms = row_taps.shape[0]
    peers = lax.axis_size("cuts")
    fits = (
        peers == 8
        and lax.axis_size("tile") == 4
        and slices == 2 * GROUP
        and terms == 4
        and rows == peers * (LANES // terms - HALO)
        and cols % (2 * LANES) == 0
    )
    run = fast if fits else general
    return run(density, valid, row_taps, col_taps, amp_matrix, like_matrix)


def solution(mesh):
    return jax.shard_map(
        per_device,
        mesh=mesh,
        in_specs=(
            P("cuts", "tile", None),
            P("tile", None),
            P(None, "cuts", None),
            P(None, "cuts", None),
            P(),
            P(),
        ),
        out_specs=(P(None, ("tile", "cuts")), P(None, ("tile", "cuts"))),
        check_vma=False,
    )
```

```python
import functools

import jax
import jax.numpy as jnp
from jax import lax
from jax.experimental import pallas as pl
from jax.experimental.pallas import tpu as pltpu
from jax.sharding import PartitionSpec as P

REACH = 8
TAPS = 2 * REACH + 1
LANES = 128
GROUP = 8
PER = 4
PAIR = 2
CHUNKS = 8
BEFORE_BAND = 1e9
MIB = 1024 * 1024
HALO = 2 * REACH


def params(mib=33):
    return pltpu.CompilerParams(vmem_limit_bytes=mib * MIB)


def hbm(shape, dtype):
    return pltpu.HBM(shape, dtype)


def held(x):
    return pltpu.with_memory_space_constraint(x, pltpu.HBM)


def resident(x):
    return pltpu.with_memory_space_constraint(x, pltpu.VMEM)


def anywhere():
    return pl.BlockSpec(memory_space=pl.ANY)


def cost(flops, moved):
    return pl.CostEstimate(flops=int(flops), bytes_accessed=int(moved), transcendentals=0)


def tap_flip():
    tap = lax.broadcasted_iota(jnp.int32, (TAPS, 2 * LANES), 0)
    lane = lax.broadcasted_iota(jnp.int32, (TAPS, 2 * LANES), 1)
    return (lax.rem(tap + lane, 2 * LANES) == 0).astype(jnp.bfloat16)


def column_band(taps):
    band = pltpu.roll(jnp.broadcast_to(taps, (LANES + HALO, 2 * LANES)), 0, 1, stride=1, stride_axis=0)
    return band[:, :LANES].astype(jnp.bfloat16)


def build_columns(col_taps, col_out):
    terms, slices = len(col_taps), col_taps[0].shape[0]
    for k in range(terms):
        base = jnp.dot(col_taps[k], tap_flip(), preferred_element_type=jnp.float32)
        for s in range(slices):
            col_out[s, : LANES + HALO, k * LANES : (k + 1) * LANES] = column_band(base[s : s + 1])
    for s in range(slices):
        col_out[s, LANES + HALO :, :] = jnp.zeros((LANES - HALO, terms * LANES), jnp.bfloat16)


def build_rows(row_taps, row_out):
    terms, slices = len(row_taps), row_taps[0].shape[0]
    high = LANES // terms
    tap = lax.broadcasted_iota(jnp.int32, (TAPS, LANES), 0)
    lane = lax.broadcasted_iota(jnp.int32, (TAPS, LANES), 1)
    base = jnp.zeros((slices, LANES), jnp.float32)
    for k in range(terms):
        place = (lane == tap + k * high).astype(jnp.bfloat16)
        base = base + jnp.dot(row_taps[k], place, preferred_element_type=jnp.float32)
    sub = lax.broadcasted_iota(jnp.int32, (GROUP, LANES), 0)
    for g in range(slices // GROUP):
        own = base[g * GROUP : (g + 1) * GROUP]
        for pair in range(row_out.shape[1] // (2 * GROUP)):
            shifted = [pltpu.roll(own, 2 * pair + h, 1) for h in range(2)]
            for s in range(GROUP):
                both = jnp.concatenate([jnp.where(sub == s, x, 0.0) for x in shifted], axis=0)
                row_out[
                    g, pair * 2 * GROUP : (pair + 1) * 2 * GROUP, s * LANES : (s + 1) * LANES
                ] = both.astype(jnp.bfloat16)


def listed(taps):
    return [taps[k] for k in range(taps.shape[0])]


def matrix_shapes(terms, slices, rows):
    return (slices, 2 * LANES, terms * LANES), (slices // GROUP, rows * GROUP, GROUP * LANES)


def convolve(field, col, row, tall, rows):
    slices, _, wide = col.shape
    terms = wide // LANES
    high, cols = LANES // terms, tall.shape[1]
    parts = []
    for g in range(slices // GROUP):
        for j in range(GROUP):
            s = g * GROUP + j
            x = jnp.concatenate([field(s), jnp.zeros((high, LANES), jnp.float32)], axis=1)
            x = pltpu.roll(x, REACH, 1).astype(jnp.bfloat16)
            x = jnp.concatenate([x[:, c : c + 2 * LANES] for c in range(0, cols, LANES)], axis=0)
            y = jnp.dot(x, col[s], preferred_element_type=jnp.float32).astype(jnp.bfloat16)
            for c in range(cols // LANES):
                for k in range(terms):
                    tall[(j * terms + k) * high : (j * terms + k + 1) * high, c * LANES : (c + 1) * LANES] = y[
                        c * high : (c + 1) * high, k * LANES : (k + 1) * LANES
                    ]
        z = jnp.dot(row[g, : rows * GROUP], tall[...], preferred_element_type=jnp.float32)
        parts.append(z.reshape(rows, GROUP, cols))
    return jnp.concatenate(parts, axis=1)


def sums_kernel(density, valid, after, out, cube, plane, sems):
    slices, rows, cols = cube.shape
    step = rows // CHUNKS

    def copies(i):
        at = pl.ds(pl.multiple_of(i * step, step), step)
        yield pltpu.make_async_copy(density.at[:, at], cube.at[:, at], sems.at[i])
        yield pltpu.make_async_copy(valid.at[at], plane.at[at], sems.at[CHUNKS + i])

    for i in range(CHUNKS):
        for copy in copies(i):
            copy.start()
    out[...] = jnp.zeros_like(out)

    def body(i, _):
        for copy in copies(i):
            copy.wait()
        at = pl.ds(pl.multiple_of(i * step, step), step)
        mask = plane[at] != 0
        for s in range(slices + 1):
            x = cube[s, at].astype(jnp.float32) if s < slices else jnp.ones((step, cols), jnp.float32)
            x = jnp.where(mask, x, 0.0).reshape(step // 8, 8, cols).sum(axis=0)
            x = sum(x[:, c : c + LANES] for c in range(0, cols, LANES))
            out[s : s + 1, :] += jnp.sum(x, axis=0, keepdims=True)
        return 0

    lax.fori_loop(0, CHUNKS, body, 0)


def masked_sums(density, valid, after):
    slices, rows, cols = density.shape
    return pl.pallas_call(
        sums_kernel,
        name="sums",
        in_specs=[anywhere()] * 3,
        out_specs=pl.BlockSpec(memory_space=pltpu.VMEM),
        out_shape=pltpu.VMEM((slices + 8, LANES), jnp.float32),
        scratch_shapes=[
            pltpu.VMEM(density.shape, jnp.bfloat16),
            pltpu.VMEM(valid.shape, jnp.int32),
            pltpu.SemaphoreType.DMA((2 * CHUNKS,)),
        ],
        compiler_params=params(),
        cost_estimate=cost(1, 1),
    )(held(density), held(valid), resident(after))


def mean_kernel(*refs):
    sums, (out, token) = refs[:2], refs[-2:]
    slices = out.shape[0]
    token[...] = jnp.zeros_like(token)
    total = sums[0][...] + sums[1][...]
    total = jnp.sum(total, axis=1, keepdims=True)
    out[...] = jnp.broadcast_to(total[:slices] / total[slices : slices + 1], out.shape)


def add_kernel(one, two, out):
    out[...] = one[...] + two[...]


def add(one, two):
    vmem = pl.BlockSpec(memory_space=pltpu.VMEM)
    return pl.pallas_call(
        add_kernel,
        name="add",
        in_specs=[vmem] * 2,
        out_specs=vmem,
        out_shape=pltpu.VMEM(one.shape, one.dtype),
        compiler_params=params(),
        cost_estimate=cost(1, 1),
    )(one, two)


def means(sums, slices, after):
    vmem = pl.BlockSpec(memory_space=pltpu.VMEM)
    return pl.pallas_call(
        mean_kernel,
        name="means",
        in_specs=[vmem] * len(sums) + [anywhere()],
        out_specs=[vmem] * 2,
        out_shape=[pltpu.VMEM((slices, LANES), jnp.float32), pltpu.VMEM((8, LANES), jnp.float32)],
        compiler_params=params(),
        cost_estimate=cost(1, 1),
    )(*sums, resident(after))


def inner_rows(both, last):
    both = both.astype(jnp.float32)
    rows = both.shape[0] - REACH
    chosen = jnp.where(last, both[REACH:], both[:rows])
    return jnp.concatenate([chosen, jnp.zeros((REACH, both.shape[1]), jnp.float32)], axis=0)


def window_copies(b, block, last, density, valid, cube, plane, sems):
    high = plane.shape[1]
    here = pl.ds(pl.multiple_of(jnp.minimum(block, last - 1) * (high // 2), high // 2), high)
    return [
        pltpu.make_async_copy(density.at[:, here], cube.at[b], sems.at[2 * b]),
        pltpu.make_async_copy(valid.at[here], plane.at[b], sems.at[2 * b + 1]),
    ]


def ready_kernel(partner, me, density, valid, row_taps, col_taps, col, row, cube, plane, first, last, ends, masks, sems):
    slices, rows, _ = density.shape
    block = ends.shape[2]
    copies = window_copies(0, me[0] ^ partner, rows // block - 1, density, valid, cube, plane, sems)
    for n, start in enumerate((0, rows - block)):
        copies.append(pltpu.make_async_copy(density.at[:, start : start + block], ends.at[n], sems.at[2 + 2 * n]))
        copies.append(pltpu.make_async_copy(valid.at[start : start + block], masks.at[n], sems.at[3 + 2 * n]))
    for copy in copies:
        copy.start()
    build_columns(listed(col_taps), col)
    build_rows(listed(row_taps), row)
    for copy in copies:
        copy.wait()
    first[:slices] = ends[0, :, :REACH]
    first[slices] = masks[0, :REACH].astype(jnp.bfloat16)
    last[:slices] = ends[1, :, block - REACH :]
    last[slices] = masks[1, block - REACH :].astype(jnp.bfloat16)


def make_ready(me, partner, density, valid, row_taps, col_taps):
    slices, rows, cols = density.shape
    terms = row_taps.shape[0]
    high = LANES // terms
    block = high - HALO
    vmem = pl.BlockSpec(memory_space=pltpu.VMEM)
    edge = pltpu.VMEM((slices + 1, REACH, cols), jnp.bfloat16)
    shapes = *matrix_shapes(terms, slices, block), (1, slices, high, cols)
    return pl.pallas_call(
        functools.partial(ready_kernel, partner),
        name="ready",
        in_specs=[pl.BlockSpec(memory_space=pltpu.SMEM)] + [anywhere()] * 2 + [vmem] * 2,
        out_specs=[vmem] * 6,
        out_shape=[pltpu.VMEM(shape, jnp.bfloat16) for shape in shapes]
        + [pltpu.VMEM((1, high, cols), jnp.int32), edge, edge],
        scratch_shapes=[
            pltpu.VMEM((2, slices, block, cols), jnp.bfloat16),
            pltpu.VMEM((2, block, cols), jnp.int32),
            pltpu.SemaphoreType.DMA((6,)),
        ],
        compiler_params=params(),
        cost_estimate=cost(1, 1),
    )(me, held(density), held(valid), row_taps, col_taps)


def inner_kernel(wanted, loaded, own_mean, end, me, *refs):
    count = len(wanted)
    blocks = [me[0] ^ k for k, _ in wanted]
    (first, second, col, row), refs = refs[:4], refs[4:]
    mean = None if own_mean else refs[0]
    results = sum(len(cut) for _, cut in wanted) + (1 if own_mean else 0)
    if loaded:
        cube, plane, tall = first, second, refs[-1]
        outs = list(refs[-1 - results : -1])
    else:
        tall, cube, plane, sems = refs[-4:]
        outs = list(refs[-4 - results : -4])
        copies = [window_copies(b, blocks[b], end, first, second, cube, plane, sems) for b in range(count)]
        for copy in sum(copies, []):
            copy.start()
    for b, (_, cut) in enumerate(wanted):
        if not loaded:
            for copy in copies[b]:
                copy.wait()
        last = blocks[b] == end
        mask = inner_rows(plane[b], last)
        if own_mean:

            def total(x):
                x = x.reshape(x.shape[0] // 8, 8, x.shape[1]).sum(axis=0)
                x = sum(x[:, c : c + LANES] for c in range(0, x.shape[1], LANES))
                return jnp.sum(x, axis=0, keepdims=True)

            sums = [total(mask * inner_rows(cube[b, s], last)) for s in range(cube.shape[1])]
            sums = jnp.sum(jnp.concatenate(sums, axis=0), axis=1, keepdims=True)
            centre = sums / jnp.sum(total(mask), axis=1, keepdims=True)
            outs[-1][...] = jnp.broadcast_to(centre, outs[-1].shape)
        else:
            centre = mean[:, :1]
        field = convolve(
            lambda s, b=b, last=last, mask=mask: mask * (inner_rows(cube[b, s], last) - centre[s : s + 1]),
            col,
            row,
            tall,
            REACH,
        ).astype(jnp.bfloat16)
        for _, start, stop in cut:
            outs.pop(0)[...] = field[start:stop]


def filter_inner(me, wanted, density, valid, ready, loaded, mean, *after):
    slices, rows, cols = density.shape
    col, row, cube, plane = ready[:4]
    high = plane.shape[1]
    count = len(wanted)
    own_mean = mean is None
    vmem = pl.BlockSpec(memory_space=pltpu.VMEM)
    shapes = [(stop - start, slices, cols) for _, cut in wanted for _, start, stop in cut]
    field = [resident(cube), resident(plane)] if loaded else [held(density), held(valid)]
    scratch = [pltpu.VMEM((GROUP * LANES, cols), jnp.bfloat16)]
    if not loaded:
        scratch += [
            pltpu.VMEM((count, slices, high, cols), jnp.bfloat16),
            pltpu.VMEM((count, high, cols), jnp.int32),
            pltpu.SemaphoreType.DMA((2 * count,)),
        ]
    means_in, means_out = ([], [pltpu.VMEM((slices, LANES), jnp.float32)]) if own_mean else ([mean], [])
    out = pl.pallas_call(
        functools.partial(inner_kernel, wanted, loaded, own_mean, rows // (high - HALO) - 1),
        name="inner",
        in_specs=[pl.BlockSpec(memory_space=pltpu.SMEM)]
        + [vmem if loaded else anywhere()] * 2
        + [vmem] * (2 + len(means_in))
        + [anywhere()] * len(after),
        out_specs=[vmem] * (len(shapes) + len(means_out)),
        out_shape=[pltpu.VMEM(shape, jnp.bfloat16) for shape in shapes] + means_out,
        scratch_shapes=scratch,
        compiler_params=params(),
        cost_estimate=cost(1, 1),
    )(me, *field, resident(col), resident(row), *means_in, *after)
    out = list(out)
    return [[out.pop(0) for _ in cut] for _, cut in wanted] + out


def notes_kernel(mean, row_taps, col_taps, *refs):
    terms, _, taps = row_taps.shape
    count = len(refs) // 2
    for centre, note in zip(refs[:count], refs[count:]):
        note[...] = jnp.zeros_like(note)
        note[:terms, :, :taps] = row_taps[...].astype(jnp.float32)
        note[terms : 2 * terms, :, :taps] = col_taps[...].astype(jnp.float32)
        note[2 * terms] = centre[...] - mean[...]


def notes_of(mean, row_taps, col_taps, centres):
    terms, slices, _ = row_taps.shape
    vmem = pl.BlockSpec(memory_space=pltpu.VMEM)
    return pl.pallas_call(
        notes_kernel,
        name="notes",
        in_specs=[vmem] * (3 + len(centres)),
        out_specs=[vmem] * len(centres),
        out_shape=[hbm((2 * terms + 1, slices, LANES), jnp.float32)] * len(centres),
        compiler_params=params(),
        cost_estimate=cost(1, 1),
    )(mean, row_taps, col_taps, *centres)


def mend_kernel(end, me, valid, note, piece, out, col, row, tall, plane, sem):
    terms = note.shape[0] // 2
    high = plane.shape[0]
    here = pl.ds(pl.multiple_of(jnp.minimum(me[0], end - 1) * (high // 2), high // 2), high)
    copy = pltpu.make_async_copy(valid.at[here], plane, sem)
    copy.start()
    taps = [note[k, :, :TAPS].astype(jnp.bfloat16) for k in range(2 * terms)]
    build_columns(taps[terms:], col)
    build_rows(taps[:terms], row)
    copy.wait()
    mask = inner_rows(plane[...], me[0] == end)
    field = convolve(lambda s: mask, col, row, tall, REACH)
    shift = jnp.broadcast_to(note[2 * terms][:, :1], field.shape[1:])
    out[...] = (piece[...].astype(jnp.float32) + shift[None] * field).astype(jnp.bfloat16)


def mend(me, valid, note, piece):
    rows, cols = valid.shape
    terms, slices = note.shape[0] // 2, note.shape[1]
    high = LANES // terms
    vmem = pl.BlockSpec(memory_space=pltpu.VMEM)
    return pl.pallas_call(
        functools.partial(mend_kernel, rows // (high - HALO) - 1),
        name="mend",
        in_specs=[pl.BlockSpec(memory_space=pltpu.SMEM), anywhere(), vmem, vmem],
        out_specs=vmem,
        out_shape=pltpu.VMEM(piece.shape, jnp.bfloat16),
        scratch_shapes=[pltpu.VMEM(shape, jnp.bfloat16) for shape in matrix_shapes(terms, slices, REACH)]
        + [
            pltpu.VMEM((GROUP * LANES, cols), jnp.bfloat16),
            pltpu.VMEM((high, cols), jnp.int32),
            pltpu.SemaphoreType.DMA,
        ],
        compiler_params=params(),
        cost_estimate=cost(1, 1),
    )(me, held(valid), note, piece)


def band_kernel(wanted, me, density, valid, above, below, col, row, mean, *refs):
    (mask, tall, done, sems) = refs[-4:]
    pieces = [cut for _, cut in wanted]
    count = sum(len(cut) for cut in pieces)
    outs = refs[-4 - count : -4]
    slices = mean.shape[0]
    rows, cols = valid.shape
    terms = col.shape[2] // LANES
    block = done.shape[1]
    high = block + HALO
    step = pl.program_id(0)
    f32 = jnp.float32

    @pl.when(step == 0)
    def _():
        mask[:REACH] = above[slices].astype(f32)
        mask[REACH : REACH + rows] = valid[...].astype(f32)
        mask[REACH + rows :] = below[slices].astype(f32)

    steps = slices // PER

    @pl.when(step < steps)
    def _():
        for j in range(PER):
            s = step * PER + j
            x = jnp.concatenate([above[s].astype(f32), density[j].astype(f32), below[s].astype(f32)], axis=0)
            x = mask[...] * (x - mean[pl.ds(s, 1), :][:, :1])
            x = jnp.concatenate([x, jnp.zeros((rows + HALO, LANES), f32)], axis=1)
            x = pltpu.roll(x, REACH, 1).astype(jnp.bfloat16)
            x = jnp.concatenate([x[:, c : c + 2 * LANES] for c in range(0, cols, LANES)], axis=0)
            y = jnp.dot(x, col[s], preferred_element_type=f32).astype(jnp.bfloat16)
            for c in range(cols // LANES):
                for k in range(terms):
                    tall[s * terms + k, :, c * LANES : (c + 1) * LANES] = y[
                        c * (rows + HALO) : (c + 1) * (rows + HALO), k * LANES : (k + 1) * LANES
                    ]

    def copies(b):
        at = sum(len(cut) for cut in pieces[:b])
        last = (me[0] ^ wanted[b][0]) == rows // block - 1
        for p, (inner, start, stop) in enumerate(pieces[b]):
            here = jnp.where(last != (inner == 1), block - REACH, 0) + start
            yield pltpu.make_async_copy(done.at[b, pl.ds(here, stop - start)], outs[at + p], sems.at[at + p])

    @pl.when(step >= steps)
    def _():
        for j in range(PAIR):
            b = (step - steps) * PAIR + j
            partner = sum(jnp.where(b == i, k, 0) for i, (k, _) in enumerate(wanted))
            here = pl.ds(pl.multiple_of((me[0] ^ partner) * block, block), high)
            parts = []
            for g in range(slices // GROUP):
                slab = tall[g * GROUP * terms : (g + 1) * GROUP * terms, here, :].reshape(GROUP * LANES, cols)
                z = jnp.dot(row[g], slab, preferred_element_type=f32)
                parts.append(z.reshape(block, GROUP, cols))
            done[b] = jnp.concatenate(parts, axis=1).astype(jnp.bfloat16)

    for n in range(len(pieces) // PAIR):

        @pl.when(step == steps + n)
        def _():
            for b in range(n * PAIR, (n + 1) * PAIR):
                for copy in copies(b):
                    copy.start()

    @pl.when(step == pl.num_programs(0) - 1)
    def _():
        for b in range(len(pieces)):
            for copy in copies(b):
                copy.wait()


def filter_band(me, wanted, density, valid, above, below, ready, mean, *after):
    slices, rows, cols = density.shape
    col, row = ready[:2]
    terms = col.shape[2] // LANES
    block = LANES // terms - HALO
    count = len(wanted)

    def whole(x):
        return pl.BlockSpec(x.shape, lambda i, at: (0,) * x.ndim, pipeline_mode=pl.Buffered(1))

    shapes = [(stop - start, slices, cols) for _, cut in wanted for _, start, stop in cut]
    out = pl.pallas_call(
        functools.partial(band_kernel, wanted),
        name="band",
        grid_spec=pltpu.PrefetchScalarGridSpec(
            num_scalar_prefetch=1,
            grid=(slices // PER + count // PAIR,),
            in_specs=[pl.BlockSpec((PER, rows, cols), lambda i, at: (jnp.minimum(i, slices // PER - 1), 0, 0))]
            + [whole(x) for x in (valid, above, below)]
            + [pl.BlockSpec(memory_space=pltpu.VMEM)] * 2
            + [whole(mean)]
            + [anywhere()] * len(after),
            out_specs=[anywhere()] * len(shapes),
            scratch_shapes=[
                pltpu.VMEM((rows + HALO, cols), jnp.float32),
                pltpu.VMEM((slices * terms, rows + HALO, cols), jnp.bfloat16),
                pltpu.VMEM((count, block, slices, cols), jnp.bfloat16),
                pltpu.SemaphoreType.DMA((len(shapes),)),
            ],
        ),
        out_shape=[hbm(shape, jnp.bfloat16) for shape in shapes],
        compiler_params=params(),
        cost_estimate=cost(1, 1),
    )(
        me,
        held(density),
        held(valid),
        above,
        below,
        resident(col),
        resident(row),
        mean,
        *after,
    )
    out = list(out)
    return [[out.pop(0) for _ in cut] for _, cut in wanted]


def project_kernel(count, me, weights, *refs):
    parts, (amp_out, like_out, token) = refs[:count], refs[-3:]
    zbins = weights.shape[0] // 2
    rows, _, cols = parts[0].shape
    for r in range(rows):
        pencil = jnp.concatenate([x[r] for x in parts], axis=0)
        both = jnp.dot(weights[...], pencil, preferred_element_type=jnp.float32)
        amp = both[:zbins]
        amp_out[:, r * cols : (r + 1) * cols] = amp.astype(jnp.bfloat16)
        like_out[:, r * cols : (r + 1) * cols] = (amp * both[zbins:]).astype(jnp.bfloat16)
    token[...] = jnp.zeros_like(token)


def weights_kernel(peers, me, amp_matrix, like_matrix, out):
    slices = amp_matrix.shape[0] // peers
    for n, matrix in enumerate((amp_matrix, like_matrix)):
        rows = [matrix[pl.ds(pl.multiple_of((me[0] ^ k) * slices, slices), slices)] for k in range(peers)]
        turned = jnp.concatenate(rows, axis=0).astype(jnp.float32).T
        out[n * turned.shape[0] : (n + 1) * turned.shape[0]] = turned.astype(jnp.bfloat16)


def arrange_weights(me, peers, amp_matrix, like_matrix):
    slices, zbins = amp_matrix.shape
    vmem = pl.BlockSpec(memory_space=pltpu.VMEM)
    return pl.pallas_call(
        functools.partial(weights_kernel, peers),
        name="weights",
        in_specs=[pl.BlockSpec(memory_space=pltpu.SMEM), vmem, vmem],
        out_specs=vmem,
        out_shape=pltpu.VMEM((2 * zbins, slices), jnp.bfloat16),
        compiler_params=params(),
        cost_estimate=cost(1, 1),
    )(me, amp_matrix, like_matrix)


def project(me, group, weights, parts, total, earlier):
    inner, start, stop = group
    rows = stop - start
    _, slices, cols = parts[0][0].shape
    peers = len(parts)

    def place(i, me):
        upper = (me[0] == peers - 1) != (inner == 1)
        return 0, i + jnp.where(upper, (total - REACH) // PAIR, 0) + start // PAIR

    zbins = weights.shape[0] // 2
    count = len(parts)
    shape = hbm((zbins, total * cols), jnp.bfloat16)
    return pl.pallas_call(
        functools.partial(project_kernel, count),
        name="project",
        grid_spec=pltpu.PrefetchScalarGridSpec(
            num_scalar_prefetch=1,
            grid=(rows // PAIR,),
            in_specs=[pl.BlockSpec(weights.shape, lambda i, at: (0, 0))]
            + [
                pl.BlockSpec((PAIR, slices, cols), lambda i, at, start=start: (i + start // PAIR, 0, 0))
                for _, start in parts
            ]
            + [anywhere()] * len(earlier),
            out_specs=[pl.BlockSpec((zbins, PAIR * cols), place)] * 2
            + [pl.BlockSpec((8, LANES), lambda i, at: (0, 0))],
        ),
        out_shape=[shape, shape, hbm((8, LANES), jnp.float32)],
        input_output_aliases={2 + count + i: i for i in range(len(earlier))},
        compiler_params=params(),
        cost_estimate=cost(1, 1),
    )(me, weights, *[x for x, _ in parts], *earlier)


def gate_kernel(*refs):
    pass


def gate(x, *earlier, flops=1, space=pltpu.HBM):
    return pl.pallas_call(
        gate_kernel,
        name="gate",
        in_specs=[anywhere()] * (1 + len(earlier)),
        out_specs=anywhere(),
        out_shape=space(x.shape, x.dtype),
        input_output_aliases={0: 0},
        compiler_params=params(),
        cost_estimate=cost(flops, 1),
    )(pltpu.with_memory_space_constraint(x, space), *earlier)


INNER, OUTER = (1, 0, REACH), (0, 0, REACH)
HEAD, TAIL = (0, 0, 6), (0, 6, REACH)
EARLY = (4, 6)
REST = (
    (5, (HEAD, TAIL)),
    (7, (HEAD, TAIL)),
    (2, (INNER, OUTER)),
    (3, (INNER, OUTER)),
    (4, (HEAD, TAIL)),
    (6, (HEAD, TAIL)),
    (1, (INNER, OUTER)),
    (0, (INNER, OUTER)),
)
ORDER = (
    (4, INNER, None),
    (6, INNER, None),
    (5, INNER, None),
    (7, INNER, None),
    (2, INNER, 0),
    (4, HEAD, 1),
    (3, INNER, 1),
    (6, HEAD, (2, 3)),
    (2, OUTER, 4),
    (5, HEAD, 5),
    (1, INNER, 6),
    (7, HEAD, 5),
    (3, OUTER, 6),
    (1, OUTER, 7),
    (4, TAIL, 9),
    (6, TAIL, 10),
    (5, TAIL, 11),
    (7, TAIL, 12),
)
MENDED = 11
AFTER = 1


def fast(density, valid, row_taps, col_taps, amp_matrix, like_matrix):
    slices, rows, cols = density.shape
    peers = lax.axis_size("cuts")
    tiles = lax.axis_size("tile")
    block = rows // peers
    me = lax.axis_index("cuts").astype(jnp.int32).reshape(1)

    def swap(x, k):
        return lax.ppermute(x, "cuts", [(i, i ^ k) for i in range(peers)])

    made, arrived = {}, {}

    def keep(wanted, got):
        for (k, cut), parts in zip(wanted, got):
            for piece, x in zip(cut, parts):
                made[k, piece] = x

    def send(k, piece, *before):
        x = made[k, piece]
        arrived[k, piece] = swap(gate(x, *before) if before else x, k)

    ready = make_ready(me, EARLY[0], density, valid, row_taps, col_taps)
    centres = []
    for k in EARLY:
        wanted = ((k, (INNER,)),)
        got, centre = filter_inner(
            me, wanted, density, valid, ready, not centres, None, *[resident(x) for x in centres]
        )
        keep(wanted, [got])
        centres.append(centre)
        send(k, INNER)
    first, last = [gate(x, centres[0], space=pltpu.VMEM) for x in ready[4:]]
    above = lax.ppermute(last, "tile", [(i, i + 1) for i in range(tiles - 1)])
    below = lax.ppermute(first, "tile", [(i + 1, i) for i in range(tiles - 1)])
    sums = [masked_sums(density, valid, centres[AFTER])]
    for k in (1, 2):
        if k == 2:
            sums = [add(*sums)]
        sums.append(lax.ppermute(sums[0], "tile", [(i, i ^ k) for i in range(tiles)]))
    mean, token = means(sums, slices, centres[-1])
    notes = notes_of(mean, row_taps, col_taps, centres)
    notes = [swap(note, k) for k, note in zip(EARLY, notes)]
    wanted = ((5, (INNER,)), (7, (INNER,)))
    token = gate(token, arrived[4, INNER], flops=BEFORE_BAND, space=pltpu.VMEM)
    got = filter_inner(me, wanted, density, valid, ready, False, mean, above, below, resident(token))
    keep(wanted, got)
    token = gate(token, *notes, space=pltpu.VMEM)
    got = filter_band(
        me, REST, density, valid, above, below, ready, mean, resident(made[5, INNER]), resident(token)
    )
    keep(REST, got)
    for piece in (INNER, OUTER):
        arrived[0, piece] = made[0, piece]

    weights = arrange_weights(me, peers, amp_matrix, like_matrix)
    result, tokens = [], []

    def finish(group):
        parts = []
        for k in range(peers):
            for piece in (group, INNER, OUTER):
                if (k, piece) in arrived and piece[0] == group[0]:
                    parts.append((arrived[k, piece], group[1] - piece[1]))
                    break
        *result[:], token = project(me, group, weights, parts, block, result)
        tokens.append(token)

    for at, (k, piece, wait) in enumerate(ORDER):
        if at == MENDED:
            for k_early, note in zip(EARLY, notes):
                arrived[k_early, INNER] = mend(me, valid, note, arrived[k_early, INNER])
        if (k, piece) in arrived:
            continue
        waits = wait if isinstance(wait, tuple) else () if wait is None else (wait,)
        before = [arrived[ORDER[n][:2]] for n in waits]
        if at == MENDED:
            before += [arrived[k_early, INNER] for k_early in EARLY]
        if at == len(ORDER) - 3:
            finish(INNER)
            before.append(tokens[0])
        send(k, piece, *before)
    finish(HEAD)
    finish(TAIL)
    return tuple(result)


def extended(shard, sides, width):
    for axis, dim in sides:
        size, length = (lax.axis_size(axis), shard.shape[dim])
        up = [(i, (i + 1) % size) for i in range(size - 1)]
        down = [(j, i) for i, j in up]
        last = lax.slice_in_dim(shard, length - width, length, axis=dim)
        initial = lax.slice_in_dim(shard, 0, width, axis=dim)
        before = lax.ppermute(last, axis, up)
        after = lax.ppermute(initial, axis, down)
        shard = jnp.concatenate([before, shard, after], axis=dim)
    return shard


def band_matrix(taps, out_count, in_count):
    offset = lax.broadcasted_iota(jnp.int32, (out_count, in_count), 1) - lax.broadcasted_iota(
        jnp.int32, (out_count, in_count), 0
    )
    positions = lax.broadcasted_iota(jnp.int32, (1, 1, TAPS), 2)
    choose = (offset[:, :, None] == positions).astype(jnp.bfloat16)
    return jnp.einsum("ijt,kst->ksij", choose, taps, preferred_element_type=jnp.float32).astype(jnp.bfloat16)


def filter_field(padded, row_taps, col_taps):
    tall = padded.shape[1]
    cols = padded.shape[2]
    width = 2 * LANES
    row_band = band_matrix(row_taps, tall - HALO, tall)
    rowed = jnp.einsum("ksij,sjc->ksic", row_band, padded, preferred_element_type=jnp.float32).astype(jnp.bfloat16)
    widened = jnp.pad(rowed, ((0, 0), (0, 0), (0, 0), (REACH, REACH)))
    col_band = band_matrix(col_taps, width, width + HALO)
    pieces = []
    for begin in range(0, cols, width):
        segment = widened[:, :, :, begin : begin + width + HALO]
        pieces.append(jnp.einsum("ksrj,ksij->sri", segment, col_band, preferred_element_type=jnp.float32))
    return jnp.concatenate(pieces, axis=2).astype(jnp.bfloat16)


def general(density, valid, row_taps, col_taps, amp_matrix, like_matrix):
    slices, rows, cols = density.shape
    mask = valid.astype(jnp.float32)
    field = density.astype(jnp.float32)
    sums, count = lax.psum((jnp.sum(field * mask[None], axis=(1, 2)), jnp.sum(mask)), "tile")
    masked = (mask[None] * (field - (sums / count)[:, None, None])).astype(jnp.bfloat16)
    filtered = filter_field(extended(masked, (("tile", 1),), REACH), row_taps, col_taps)
    peers = lax.axis_size("cuts")
    share = rows * cols // peers
    pencil = lax.all_to_all(
        filtered.reshape(slices, peers, share), "cuts", split_axis=1, concat_axis=0, tiled=True
    ).reshape(slices * peers, share)
    amp = jnp.dot(amp_matrix.T, pencil, preferred_element_type=jnp.float32)
    like = amp * jnp.dot(like_matrix.T, pencil, preferred_element_type=jnp.float32)
    return amp.astype(jnp.bfloat16), like.astype(jnp.bfloat16)


def per_device(density, valid, row_taps, col_taps, amp_matrix, like_matrix):
    slices, rows, cols = density.shape
    terms = row_taps.shape[0]
    peers = lax.axis_size("cuts")
    fits = (
        peers == 8
        and lax.axis_size("tile") == 4
        and slices == 2 * GROUP
        and terms == 4
        and rows == peers * (LANES // terms - HALO)
        and cols % (2 * LANES) == 0
    )
    run = fast if fits else general
    return run(density, valid, row_taps, col_taps, amp_matrix, like_matrix)


def solution(mesh):
    return jax.shard_map(
        per_device,
        mesh=mesh,
        in_specs=(
            P("cuts", "tile", None),
            P("tile", None),
            P(None, "cuts", None),
            P(None, "cuts", None),
            P(),
            P(),
        ),
        out_specs=(P(None, ("tile", "cuts")), P(None, ("tile", "cuts"))),
        check_vma=False,
    )
```

```python
import functools

import jax
import jax.numpy as jnp
from jax import lax
from jax.experimental import pallas as pl
from jax.experimental.pallas import tpu as pltpu
from jax.sharding import PartitionSpec as P

REACH = 8
TAPS = 2 * REACH + 1
LANES = 128
GROUP = 8
PER = 4
PAIR = 2
CHUNKS = 8
BEFORE_BAND = 2e9
MIB = 1024 * 1024
HALO = 2 * REACH


def params(mib=33):
    return pltpu.CompilerParams(vmem_limit_bytes=mib * MIB)


def hbm(shape, dtype):
    return pltpu.HBM(shape, dtype)


def held(x):
    return pltpu.with_memory_space_constraint(x, pltpu.HBM)


def resident(x):
    return pltpu.with_memory_space_constraint(x, pltpu.VMEM)


def anywhere():
    return pl.BlockSpec(memory_space=pl.ANY)


def cost(flops, moved):
    return pl.CostEstimate(flops=int(flops), bytes_accessed=int(moved), transcendentals=0)


def tap_flip():
    tap = lax.broadcasted_iota(jnp.int32, (TAPS, 2 * LANES), 0)
    lane = lax.broadcasted_iota(jnp.int32, (TAPS, 2 * LANES), 1)
    return (lax.rem(tap + lane, 2 * LANES) == 0).astype(jnp.bfloat16)


def column_band(taps):
    band = pltpu.roll(jnp.broadcast_to(taps, (LANES + HALO, 2 * LANES)), 0, 1, stride=1, stride_axis=0)
    return band[:, :LANES].astype(jnp.bfloat16)


def build_columns(col_taps, col_out):
    terms, slices = len(col_taps), col_taps[0].shape[0]
    for k in range(terms):
        base = jnp.dot(col_taps[k], tap_flip(), preferred_element_type=jnp.float32)
        for s in range(slices):
            col_out[s, : LANES + HALO, k * LANES : (k + 1) * LANES] = column_band(base[s : s + 1])
    for s in range(slices):
        col_out[s, LANES + HALO :, :] = jnp.zeros((LANES - HALO, terms * LANES), jnp.bfloat16)


def build_rows(row_taps, row_out):
    terms, slices = len(row_taps), row_taps[0].shape[0]
    high = LANES // terms
    tap = lax.broadcasted_iota(jnp.int32, (TAPS, LANES), 0)
    lane = lax.broadcasted_iota(jnp.int32, (TAPS, LANES), 1)
    base = jnp.zeros((slices, LANES), jnp.float32)
    for k in range(terms):
        place = (lane == tap + k * high).astype(jnp.bfloat16)
        base = base + jnp.dot(row_taps[k], place, preferred_element_type=jnp.float32)
    sub = lax.broadcasted_iota(jnp.int32, (GROUP, LANES), 0)
    for g in range(slices // GROUP):
        own = base[g * GROUP : (g + 1) * GROUP]
        for pair in range(row_out.shape[1] // (2 * GROUP)):
            shifted = [pltpu.roll(own, 2 * pair + h, 1) for h in range(2)]
            for s in range(GROUP):
                both = jnp.concatenate([jnp.where(sub == s, x, 0.0) for x in shifted], axis=0)
                row_out[
                    g, pair * 2 * GROUP : (pair + 1) * 2 * GROUP, s * LANES : (s + 1) * LANES
                ] = both.astype(jnp.bfloat16)


def listed(taps):
    return [taps[k] for k in range(taps.shape[0])]


def matrix_shapes(terms, slices, rows):
    return (slices, 2 * LANES, terms * LANES), (slices // GROUP, rows * GROUP, GROUP * LANES)


def convolve(field, col, row, tall, rows):
    slices, _, wide = col.shape
    terms = wide // LANES
    high, cols = LANES // terms, tall.shape[1]
    parts = []
    for g in range(slices // GROUP):
        for j in range(GROUP):
            s = g * GROUP + j
            x = jnp.concatenate([field(s), jnp.zeros((high, LANES), jnp.float32)], axis=1)
            x = pltpu.roll(x, REACH, 1).astype(jnp.bfloat16)
            x = jnp.concatenate([x[:, c : c + 2 * LANES] for c in range(0, cols, LANES)], axis=0)
            y = jnp.dot(x, col[s], preferred_element_type=jnp.float32).astype(jnp.bfloat16)
            for c in range(cols // LANES):
                for k in range(terms):
                    tall[(j * terms + k) * high : (j * terms + k + 1) * high, c * LANES : (c + 1) * LANES] = y[
                        c * high : (c + 1) * high, k * LANES : (k + 1) * LANES
                    ]
        z = jnp.dot(row[g, : rows * GROUP], tall[...], preferred_element_type=jnp.float32)
        parts.append(z.reshape(rows, GROUP, cols))
    return jnp.concatenate(parts, axis=1)


def sums_kernel(density, valid, out, first, last, cube, plane, sems):
    slices, rows, cols = cube.shape
    step = rows // CHUNKS

    def copies(i):
        at = pl.ds(pl.multiple_of(i * step, step), step)
        yield pltpu.make_async_copy(density.at[:, at], cube.at[:, at], sems.at[i])
        yield pltpu.make_async_copy(valid.at[at], plane.at[at], sems.at[CHUNKS + i])

    for i in range(CHUNKS):
        for copy in copies(i):
            copy.start()
    out[...] = jnp.zeros_like(out)

    def body(i, _):
        for copy in copies(i):
            copy.wait()
        at = pl.ds(pl.multiple_of(i * step, step), step)
        mask = plane[at] != 0
        for s in range(slices + 1):
            x = cube[s, at].astype(jnp.float32) if s < slices else jnp.ones((step, cols), jnp.float32)
            x = jnp.where(mask, x, 0.0).reshape(step // 8, 8, cols).sum(axis=0)
            x = sum(x[:, c : c + LANES] for c in range(0, cols, LANES))
            out[s : s + 1, :] += jnp.sum(x, axis=0, keepdims=True)
        return 0

    lax.fori_loop(0, CHUNKS, body, 0)
    first[:slices] = cube[:, :REACH]
    first[slices] = plane[:REACH].astype(jnp.bfloat16)
    last[:slices] = cube[:, rows - REACH :]
    last[slices] = plane[rows - REACH :].astype(jnp.bfloat16)


def masked_sums(density, valid):
    slices, rows, cols = density.shape
    edge = pltpu.VMEM((slices + 1, REACH, cols), jnp.bfloat16)
    return pl.pallas_call(
        sums_kernel,
        name="sums",
        in_specs=[anywhere()] * 2,
        out_specs=[pl.BlockSpec(memory_space=pltpu.VMEM)] * 3,
        out_shape=[pltpu.VMEM((slices + 8, LANES), jnp.float32), edge, edge],
        scratch_shapes=[
            pltpu.VMEM(density.shape, jnp.bfloat16),
            pltpu.VMEM(valid.shape, jnp.int32),
            pltpu.SemaphoreType.DMA((2 * CHUNKS,)),
        ],
        compiler_params=params(),
        cost_estimate=cost(1, 1),
    )(held(density), held(valid))


def mean_kernel(*refs):
    sums, (out, token) = refs[:4], refs[-2:]
    slices = out.shape[0]
    token[...] = jnp.zeros_like(token)
    total = sums[0][...] + sums[1][...] + sums[2][...] + sums[3][...]
    total = jnp.sum(total, axis=1, keepdims=True)
    out[...] = jnp.broadcast_to(total[:slices] / total[slices : slices + 1], out.shape)


def means(sums, slices, after):
    vmem = pl.BlockSpec(memory_space=pltpu.VMEM)
    return pl.pallas_call(
        mean_kernel,
        name="means",
        in_specs=[vmem] * len(sums) + [anywhere()],
        out_specs=[vmem] * 2,
        out_shape=[pltpu.VMEM((slices, LANES), jnp.float32), pltpu.VMEM((8, LANES), jnp.float32)],
        compiler_params=params(),
        cost_estimate=cost(1, 1),
    )(*sums, resident(after))


def inner_rows(both, last):
    both = both.astype(jnp.float32)
    rows = both.shape[0] - REACH
    chosen = jnp.where(last, both[REACH:], both[:rows])
    return jnp.concatenate([chosen, jnp.zeros((REACH, both.shape[1]), jnp.float32)], axis=0)


def window_copies(b, block, last, density, valid, cube, plane, sems):
    high = plane.shape[1]
    here = pl.ds(pl.multiple_of(jnp.minimum(block, last - 1) * (high // 2), high // 2), high)
    return [
        pltpu.make_async_copy(density.at[:, here], cube.at[b], sems.at[2 * b]),
        pltpu.make_async_copy(valid.at[here], plane.at[b], sems.at[2 * b + 1]),
    ]


def ready_kernel(partner, me, density, valid, row_taps, col_taps, after, col, row, cube, plane, sems):
    last = density.shape[1] * 2 // plane.shape[1] - 1
    copies = window_copies(0, me[0] ^ partner, last, density, valid, cube, plane, sems)
    for copy in copies:
        copy.start()
    build_columns(listed(col_taps), col)
    build_rows(listed(row_taps), row)
    for copy in copies:
        copy.wait()


def make_ready(me, partner, density, valid, row_taps, col_taps, after):
    slices, rows, cols = density.shape
    terms = row_taps.shape[0]
    high = LANES // terms
    vmem = pl.BlockSpec(memory_space=pltpu.VMEM)
    shapes = *matrix_shapes(terms, slices, high - HALO), (1, slices, high, cols)
    return pl.pallas_call(
        functools.partial(ready_kernel, partner),
        name="ready",
        in_specs=[pl.BlockSpec(memory_space=pltpu.SMEM)] + [anywhere()] * 2 + [vmem] * 2 + [anywhere()],
        out_specs=[vmem] * 4,
        out_shape=[pltpu.VMEM(shape, jnp.bfloat16) for shape in shapes] + [pltpu.VMEM((1, high, cols), jnp.int32)],
        scratch_shapes=[pltpu.SemaphoreType.DMA((2,))],
        compiler_params=params(),
        cost_estimate=cost(1, 1),
    )(me, held(density), held(valid), row_taps, col_taps, after)


def inner_kernel(wanted, loaded, end, me, *refs):
    count = len(wanted)
    pieces = [cut for _, cut in wanted]
    blocks = [me[0] ^ k for k, _ in wanted]
    outs = sum(len(cut) for cut in pieces)
    if loaded:
        (cube, plane, col, row, mean), tall = refs[:5], refs[-1]
        outs = list(refs[-1 - outs : -1])
    else:
        (density, valid, col, row, mean), (tall, cube, plane, sems) = refs[:5], refs[-4:]
        outs = list(refs[-4 - outs : -4])
        copies = [window_copies(b, blocks[b], end, density, valid, cube, plane, sems) for b in range(count)]
        for copy in sum(copies, []):
            copy.start()
    for b, cut in enumerate(pieces):
        if not loaded:
            for copy in copies[b]:
                copy.wait()
        last = blocks[b] == end
        mask = inner_rows(plane[b], last)
        field = convolve(
            lambda s, b=b, last=last, mask=mask: mask * (inner_rows(cube[b, s], last) - mean[s : s + 1, :1]),
            col,
            row,
            tall,
            REACH,
        ).astype(jnp.bfloat16)
        for _, start, stop in cut:
            outs.pop(0)[...] = field[start:stop]


def filter_inner(me, wanted, density, valid, ready, mean, *after):
    slices, rows, cols = density.shape
    col, row, cube, plane = ready
    high = plane.shape[1]
    count = len(wanted)
    loaded = not after
    vmem = pl.BlockSpec(memory_space=pltpu.VMEM)
    shapes = [(stop - start, slices, cols) for _, cut in wanted for _, start, stop in cut]
    field = [resident(cube), resident(plane)] if loaded else [held(density), held(valid)]
    scratch = [pltpu.VMEM((GROUP * LANES, cols), jnp.bfloat16)]
    if not loaded:
        scratch += [
            pltpu.VMEM((count, slices, high, cols), jnp.bfloat16),
            pltpu.VMEM((count, high, cols), jnp.int32),
            pltpu.SemaphoreType.DMA((2 * count,)),
        ]
    out = pl.pallas_call(
        functools.partial(inner_kernel, wanted, loaded, rows // (high - HALO) - 1),
        name="inner",
        in_specs=[pl.BlockSpec(memory_space=pltpu.SMEM)]
        + [vmem if loaded else anywhere()] * 2
        + [vmem] * 3
        + [anywhere()] * len(after),
        out_specs=[vmem] * len(shapes),
        out_shape=[pltpu.VMEM(shape, jnp.bfloat16) for shape in shapes],
        scratch_shapes=scratch,
        compiler_params=params(),
        cost_estimate=cost(1, 1),
    )(
        me,
        *field,
        resident(col),
        resident(row),
        mean,
        *after,
    )
    out = list(out)
    return [[out.pop(0) for _ in cut] for _, cut in wanted]


def band_kernel(wanted, me, density, valid, above, below, col, row, mean, *refs):
    (mask, tall, done, sems) = refs[-4:]
    pieces = [cut for _, cut in wanted]
    count = sum(len(cut) for cut in pieces)
    outs = refs[-4 - count : -4]
    slices = mean.shape[0]
    rows, cols = valid.shape
    terms = col.shape[2] // LANES
    block = done.shape[1]
    high = block + HALO
    step = pl.program_id(0)
    f32 = jnp.float32

    @pl.when(step == 0)
    def _():
        mask[:REACH] = above[slices].astype(f32)
        mask[REACH : REACH + rows] = valid[...].astype(f32)
        mask[REACH + rows :] = below[slices].astype(f32)

    steps = slices // PER

    @pl.when(step < steps)
    def _():
        for j in range(PER):
            s = step * PER + j
            x = jnp.concatenate([above[s].astype(f32), density[j].astype(f32), below[s].astype(f32)], axis=0)
            x = mask[...] * (x - mean[pl.ds(s, 1), :][:, :1])
            x = jnp.concatenate([x, jnp.zeros((rows + HALO, LANES), f32)], axis=1)
            x = pltpu.roll(x, REACH, 1).astype(jnp.bfloat16)
            x = jnp.concatenate([x[:, c : c + 2 * LANES] for c in range(0, cols, LANES)], axis=0)
            y = jnp.dot(x, col[s], preferred_element_type=f32).astype(jnp.bfloat16)
            for c in range(cols // LANES):
                for k in range(terms):
                    tall[s * terms + k, :, c * LANES : (c + 1) * LANES] = y[
                        c * (rows + HALO) : (c + 1) * (rows + HALO), k * LANES : (k + 1) * LANES
                    ]

    def copies(b):
        at = sum(len(cut) for cut in pieces[:b])
        last = (me[0] ^ wanted[b][0]) == rows // block - 1
        for p, (inner, start, stop) in enumerate(pieces[b]):
            here = jnp.where(last != (inner == 1), block - REACH, 0) + start
            yield pltpu.make_async_copy(done.at[b, pl.ds(here, stop - start)], outs[at + p], sems.at[at + p])

    @pl.when(step >= steps)
    def _():
        for j in range(PAIR):
            b = (step - steps) * PAIR + j
            partner = sum(jnp.where(b == i, k, 0) for i, (k, _) in enumerate(wanted))
            here = pl.ds(pl.multiple_of((me[0] ^ partner) * block, block), high)
            parts = []
            for g in range(slices // GROUP):
                slab = tall[g * GROUP * terms : (g + 1) * GROUP * terms, here, :].reshape(GROUP * LANES, cols)
                z = jnp.dot(row[g], slab, preferred_element_type=f32)
                parts.append(z.reshape(block, GROUP, cols))
            done[b] = jnp.concatenate(parts, axis=1).astype(jnp.bfloat16)

    for n in range(len(pieces) // PAIR):

        @pl.when(step == steps + n)
        def _():
            for b in range(n * PAIR, (n + 1) * PAIR):
                for copy in copies(b):
                    copy.start()

    @pl.when(step == pl.num_programs(0) - 1)
    def _():
        for b in range(len(pieces)):
            for copy in copies(b):
                copy.wait()


def filter_band(me, wanted, density, valid, above, below, ready, mean, *after):
    slices, rows, cols = density.shape
    col, row = ready[:2]
    terms = col.shape[2] // LANES
    block = LANES // terms - HALO
    count = len(wanted)

    def whole(x):
        return pl.BlockSpec(x.shape, lambda i, at: (0,) * x.ndim, pipeline_mode=pl.Buffered(1))

    shapes = [(stop - start, slices, cols) for _, cut in wanted for _, start, stop in cut]
    out = pl.pallas_call(
        functools.partial(band_kernel, wanted),
        name="band",
        grid_spec=pltpu.PrefetchScalarGridSpec(
            num_scalar_prefetch=1,
            grid=(slices // PER + count // PAIR,),
            in_specs=[pl.BlockSpec((PER, rows, cols), lambda i, at: (jnp.minimum(i, slices // PER - 1), 0, 0))]
            + [whole(x) for x in (valid, above, below)]
            + [pl.BlockSpec(memory_space=pltpu.VMEM)] * 2
            + [whole(mean)]
            + [anywhere()] * len(after),
            out_specs=[anywhere()] * len(shapes),
            scratch_shapes=[
                pltpu.VMEM((rows + HALO, cols), jnp.float32),
                pltpu.VMEM((slices * terms, rows + HALO, cols), jnp.bfloat16),
                pltpu.VMEM((count, block, slices, cols), jnp.bfloat16),
                pltpu.SemaphoreType.DMA((len(shapes),)),
            ],
        ),
        out_shape=[hbm(shape, jnp.bfloat16) for shape in shapes],
        compiler_params=params(),
        cost_estimate=cost(1, 1),
    )(
        me,
        held(density),
        held(valid),
        above,
        below,
        resident(col),
        resident(row),
        mean,
        *after,
    )
    out = list(out)
    return [[out.pop(0) for _ in cut] for _, cut in wanted]


def project_kernel(count, me, weights, *refs):
    parts, (amp_out, like_out, token) = refs[:count], refs[-3:]
    zbins = weights.shape[0] // 2
    rows, _, cols = parts[0].shape
    for r in range(rows):
        pencil = jnp.concatenate([x[r] for x in parts], axis=0)
        both = jnp.dot(weights[...], pencil, preferred_element_type=jnp.float32)
        amp = both[:zbins]
        amp_out[:, r * cols : (r + 1) * cols] = amp.astype(jnp.bfloat16)
        like_out[:, r * cols : (r + 1) * cols] = (amp * both[zbins:]).astype(jnp.bfloat16)
    token[...] = jnp.zeros_like(token)


def weights_kernel(peers, me, amp_matrix, like_matrix, out):
    slices = amp_matrix.shape[0] // peers
    for n, matrix in enumerate((amp_matrix, like_matrix)):
        rows = [matrix[pl.ds(pl.multiple_of((me[0] ^ k) * slices, slices), slices)] for k in range(peers)]
        turned = jnp.concatenate(rows, axis=0).astype(jnp.float32).T
        out[n * turned.shape[0] : (n + 1) * turned.shape[0]] = turned.astype(jnp.bfloat16)


def arrange_weights(me, peers, amp_matrix, like_matrix):
    slices, zbins = amp_matrix.shape
    vmem = pl.BlockSpec(memory_space=pltpu.VMEM)
    return pl.pallas_call(
        functools.partial(weights_kernel, peers),
        name="weights",
        in_specs=[pl.BlockSpec(memory_space=pltpu.SMEM), vmem, vmem],
        out_specs=vmem,
        out_shape=pltpu.VMEM((2 * zbins, slices), jnp.bfloat16),
        compiler_params=params(),
        cost_estimate=cost(1, 1),
    )(me, amp_matrix, like_matrix)


def project(me, group, weights, parts, total, earlier):
    inner, start, stop = group
    rows = stop - start
    _, slices, cols = parts[0][0].shape
    peers = len(parts)

    def place(i, me):
        upper = (me[0] == peers - 1) != (inner == 1)
        return 0, i + jnp.where(upper, (total - REACH) // PAIR, 0) + start // PAIR

    zbins = weights.shape[0] // 2
    count = len(parts)
    shape = hbm((zbins, total * cols), jnp.bfloat16)
    return pl.pallas_call(
        functools.partial(project_kernel, count),
        name="project",
        grid_spec=pltpu.PrefetchScalarGridSpec(
            num_scalar_prefetch=1,
            grid=(rows // PAIR,),
            in_specs=[pl.BlockSpec(weights.shape, lambda i, at: (0, 0))]
            + [
                pl.BlockSpec((PAIR, slices, cols), lambda i, at, start=start: (i + start // PAIR, 0, 0))
                for _, start in parts
            ]
            + [anywhere()] * len(earlier),
            out_specs=[pl.BlockSpec((zbins, PAIR * cols), place)] * 2
            + [pl.BlockSpec((8, LANES), lambda i, at: (0, 0))],
        ),
        out_shape=[shape, shape, hbm((8, LANES), jnp.float32)],
        input_output_aliases={2 + count + i: i for i in range(len(earlier))},
        compiler_params=params(),
        cost_estimate=cost(1, 1),
    )(me, weights, *[x for x, _ in parts], *earlier)


def gate_kernel(*refs):
    pass


def gate(x, *earlier, flops=1, space=pltpu.HBM):
    return pl.pallas_call(
        gate_kernel,
        name="gate",
        in_specs=[anywhere()] * (1 + len(earlier)),
        out_specs=anywhere(),
        out_shape=space(x.shape, x.dtype),
        input_output_aliases={0: 0},
        compiler_params=params(),
        cost_estimate=cost(flops, 1),
    )(pltpu.with_memory_space_constraint(x, space), *earlier)


INNER, OUTER = (1, 0, REACH), (0, 0, REACH)
HEAD, TAIL = (0, 0, 6), (0, 6, REACH)
FIRST = (((4, (INNER,)),), ((6, (INNER,)), (5, (INNER,))))
REST = (
    (5, (HEAD, TAIL)),
    (7, (INNER, HEAD, TAIL)),
    (2, (INNER, OUTER)),
    (3, (INNER, OUTER)),
    (4, (HEAD, TAIL)),
    (6, (HEAD, TAIL)),
    (1, (INNER, OUTER)),
    (0, (INNER, OUTER)),
)
ORDER = (
    (4, INNER, None),
    (6, INNER, None),
    (5, INNER, None),
    (7, INNER, 0),
    (2, INNER, 0),
    (4, HEAD, 1),
    (3, INNER, 1),
    (6, HEAD, 2),
    (2, OUTER, 2),
    (5, HEAD, 3),
    (1, INNER, 4),
    (7, HEAD, 5),
    (3, OUTER, 6),
    (1, OUTER, 7),
    (4, TAIL, 7),
    (6, TAIL, 9),
    (5, TAIL, 10),
    (7, TAIL, 11),
)


def fast(density, valid, row_taps, col_taps, amp_matrix, like_matrix):
    slices, rows, cols = density.shape
    peers = lax.axis_size("cuts")
    tiles = lax.axis_size("tile")
    block = rows // peers
    me = lax.axis_index("cuts").astype(jnp.int32).reshape(1)

    def swap(x, k):
        return lax.ppermute(x, "cuts", [(i, i ^ k) for i in range(peers)])

    own, first, last = masked_sums(density, valid)
    sums = [own] + [lax.ppermute(own, "tile", [(i, i ^ k) for i in range(tiles)]) for k in range(1, tiles)]
    ready = make_ready(me, ORDER[0][0], density, valid, row_taps, col_taps, own)
    mean, token = means(sums, slices, ready[0])

    made, arrived = {}, {}

    above = lax.ppermute(last, "tile", [(i, i + 1) for i in range(tiles - 1)])
    below = lax.ppermute(first, "tile", [(i + 1, i) for i in range(tiles - 1)])
    def keep(wanted, got):
        for (k, cut), parts in zip(wanted, got):
            for piece, x in zip(cut, parts):
                made[k, piece] = x

    def send(k, piece, *before):
        x = made[k, piece]
        arrived[k, piece] = swap(gate(x, *before) if before else x, k)

    after = ()
    for wanted in FIRST:
        got = filter_inner(me, wanted, density, valid, ready, mean, *after)
        keep(wanted, got)
        after = (resident(got[0][0]),)
    first_piece = ORDER[0][:2]
    send(*first_piece)
    got = filter_band(
        me, REST, density, valid, above, below, ready, mean, *after, resident(gate(token, arrived[first_piece], flops=BEFORE_BAND, space=pltpu.VMEM))
    )
    keep(REST, got)
    for piece in (INNER, OUTER):
        arrived[0, piece] = made[0, piece]

    weights = arrange_weights(me, peers, amp_matrix, like_matrix)
    result, tokens = [], []

    def finish(group):
        parts = []
        for k in range(peers):
            for piece in (group, INNER, OUTER):
                if (k, piece) in arrived and piece[0] == group[0]:
                    parts.append((arrived[k, piece], group[1] - piece[1]))
                    break
        *result[:], token = project(me, group, weights, parts, block, result)
        tokens.append(token)

    for at, (k, piece, wait) in enumerate(ORDER):
        if (k, piece) in arrived:
            continue
        before = [] if wait is None else [arrived[ORDER[wait][:2]]]
        send(k, piece, *before)
    finish(INNER)
    finish(HEAD)
    finish(TAIL)
    return tuple(result)


def extended(shard, sides, width):
    for axis, dim in sides:
        size, length = (lax.axis_size(axis), shard.shape[dim])
        up = [(i, (i + 1) % size) for i in range(size - 1)]
        down = [(j, i) for i, j in up]
        last = lax.slice_in_dim(shard, length - width, length, axis=dim)
        initial = lax.slice_in_dim(shard, 0, width, axis=dim)
        before = lax.ppermute(last, axis, up)
        after = lax.ppermute(initial, axis, down)
        shard = jnp.concatenate([before, shard, after], axis=dim)
    return shard


def band_matrix(taps, out_count, in_count):
    offset = lax.broadcasted_iota(jnp.int32, (out_count, in_count), 1) - lax.broadcasted_iota(
        jnp.int32, (out_count, in_count), 0
    )
    positions = lax.broadcasted_iota(jnp.int32, (1, 1, TAPS), 2)
    choose = (offset[:, :, None] == positions).astype(jnp.bfloat16)
    return jnp.einsum("ijt,kst->ksij", choose, taps, preferred_element_type=jnp.float32).astype(jnp.bfloat16)


def filter_field(padded, row_taps, col_taps):
    tall = padded.shape[1]
    cols = padded.shape[2]
    width = 2 * LANES
    row_band = band_matrix(row_taps, tall - HALO, tall)
    rowed = jnp.einsum("ksij,sjc->ksic", row_band, padded, preferred_element_type=jnp.float32).astype(jnp.bfloat16)
    widened = jnp.pad(rowed, ((0, 0), (0, 0), (0, 0), (REACH, REACH)))
    col_band = band_matrix(col_taps, width, width + HALO)
    pieces = []
    for begin in range(0, cols, width):
        segment = widened[:, :, :, begin : begin + width + HALO]
        pieces.append(jnp.einsum("ksrj,ksij->sri", segment, col_band, preferred_element_type=jnp.float32))
    return jnp.concatenate(pieces, axis=2).astype(jnp.bfloat16)


def general(density, valid, row_taps, col_taps, amp_matrix, like_matrix):
    slices, rows, cols = density.shape
    mask = valid.astype(jnp.float32)
    field = density.astype(jnp.float32)
    sums, count = lax.psum((jnp.sum(field * mask[None], axis=(1, 2)), jnp.sum(mask)), "tile")
    masked = (mask[None] * (field - (sums / count)[:, None, None])).astype(jnp.bfloat16)
    filtered = filter_field(extended(masked, (("tile", 1),), REACH), row_taps, col_taps)
    peers = lax.axis_size("cuts")
    share = rows * cols // peers
    pencil = lax.all_to_all(
        filtered.reshape(slices, peers, share), "cuts", split_axis=1, concat_axis=0, tiled=True
    ).reshape(slices * peers, share)
    amp = jnp.dot(amp_matrix.T, pencil, preferred_element_type=jnp.float32)
    like = amp * jnp.dot(like_matrix.T, pencil, preferred_element_type=jnp.float32)
    return amp.astype(jnp.bfloat16), like.astype(jnp.bfloat16)


def per_device(density, valid, row_taps, col_taps, amp_matrix, like_matrix):
    slices, rows, cols = density.shape
    terms = row_taps.shape[0]
    peers = lax.axis_size("cuts")
    fits = (
        peers == 8
        and lax.axis_size("tile") == 4
        and slices == 2 * GROUP
        and terms == 4
        and rows == peers * (LANES // terms - HALO)
        and cols % (2 * LANES) == 0
    )
    run = fast if fits else general
    return run(density, valid, row_taps, col_taps, amp_matrix, like_matrix)


def solution(mesh):
    return jax.shard_map(
        per_device,
        mesh=mesh,
        in_specs=(
            P("cuts", "tile", None),
            P("tile", None),
            P(None, "cuts", None),
            P(None, "cuts", None),
            P(),
            P(),
        ),
        out_specs=(P(None, ("tile", "cuts")), P(None, ("tile", "cuts"))),
        check_vma=False,
    )
```

```python
import functools

import jax
import jax.numpy as jnp
from jax import lax
from jax.experimental import pallas as pl
from jax.experimental.pallas import tpu as pltpu
from jax.sharding import PartitionSpec as P

REACH = 8
TAPS = 2 * REACH + 1
LANES = 128
GROUP = 8
PER = 4
PAIR = 2
CHUNKS = 8
BEFORE_BAND = 2e9
MIB = 1024 * 1024
HALO = 2 * REACH


def params(mib=33):
    return pltpu.CompilerParams(vmem_limit_bytes=mib * MIB)


def hbm(shape, dtype):
    return pltpu.HBM(shape, dtype)


def held(x):
    return pltpu.with_memory_space_constraint(x, pltpu.HBM)


def resident(x):
    return pltpu.with_memory_space_constraint(x, pltpu.VMEM)


def anywhere():
    return pl.BlockSpec(memory_space=pl.ANY)


def cost(flops, moved):
    return pl.CostEstimate(flops=int(flops), bytes_accessed=int(moved), transcendentals=0)


def tap_flip():
    tap = lax.broadcasted_iota(jnp.int32, (TAPS, 2 * LANES), 0)
    lane = lax.broadcasted_iota(jnp.int32, (TAPS, 2 * LANES), 1)
    return (lax.rem(tap + lane, 2 * LANES) == 0).astype(jnp.bfloat16)


def column_band(taps):
    band = pltpu.roll(jnp.broadcast_to(taps, (LANES + HALO, 2 * LANES)), 0, 1, stride=1, stride_axis=0)
    return band[:, :LANES].astype(jnp.bfloat16)


def build_columns(col_taps, col_out):
    terms, slices = len(col_taps), col_taps[0].shape[0]
    for k in range(terms):
        base = jnp.dot(col_taps[k], tap_flip(), preferred_element_type=jnp.float32)
        for s in range(slices):
            col_out[s, : LANES + HALO, k * LANES : (k + 1) * LANES] = column_band(base[s : s + 1])
    for s in range(slices):
        col_out[s, LANES + HALO :, :] = jnp.zeros((LANES - HALO, terms * LANES), jnp.bfloat16)


def build_rows(row_taps, row_out):
    terms, slices = len(row_taps), row_taps[0].shape[0]
    high = LANES // terms
    tap = lax.broadcasted_iota(jnp.int32, (TAPS, LANES), 0)
    lane = lax.broadcasted_iota(jnp.int32, (TAPS, LANES), 1)
    base = jnp.zeros((slices, LANES), jnp.float32)
    for k in range(terms):
        place = (lane == tap + k * high).astype(jnp.bfloat16)
        base = base + jnp.dot(row_taps[k], place, preferred_element_type=jnp.float32)
    sub = lax.broadcasted_iota(jnp.int32, (GROUP, LANES), 0)
    for g in range(slices // GROUP):
        own = base[g * GROUP : (g + 1) * GROUP]
        for pair in range(row_out.shape[1] // (2 * GROUP)):
            shifted = [pltpu.roll(own, 2 * pair + h, 1) for h in range(2)]
            for s in range(GROUP):
                both = jnp.concatenate([jnp.where(sub == s, x, 0.0) for x in shifted], axis=0)
                row_out[
                    g, pair * 2 * GROUP : (pair + 1) * 2 * GROUP, s * LANES : (s + 1) * LANES
                ] = both.astype(jnp.bfloat16)


def listed(taps):
    return [taps[k] for k in range(taps.shape[0])]


def matrix_shapes(terms, slices, rows):
    return (slices, 2 * LANES, terms * LANES), (slices // GROUP, rows * GROUP, GROUP * LANES)


def convolve(field, col, row, tall, rows):
    slices, _, wide = col.shape
    terms = wide // LANES
    high, cols = LANES // terms, tall.shape[1]
    read = rows + HALO
    if read < high:
        for n in range(tall.shape[0] // high):
            tall[n * high + read : (n + 1) * high] = jnp.zeros((high - read, cols), jnp.bfloat16)
    parts = []
    for g in range(slices // GROUP):
        for j in range(GROUP):
            s = g * GROUP + j
            x = jnp.concatenate([field(s), jnp.zeros((read, LANES), jnp.float32)], axis=1)
            x = pltpu.roll(x, REACH, 1)
            x = jnp.concatenate([x[:, c : c + 2 * LANES] for c in range(0, cols, LANES)], axis=0)
            y = jnp.dot(x.astype(jnp.bfloat16), col[s], preferred_element_type=jnp.float32)
            for c in range(cols // LANES):
                for k in range(terms):
                    at = (j * terms + k) * high
                    tall[at : at + read, c * LANES : (c + 1) * LANES] = y[
                        c * read : (c + 1) * read, k * LANES : (k + 1) * LANES
                    ].astype(jnp.bfloat16)
        z = jnp.dot(row[g, : rows * GROUP], tall[...], preferred_element_type=jnp.float32)
        parts.append(z.reshape(rows, GROUP, cols))
    return jnp.concatenate(parts, axis=1)


def sums_kernel(density, valid, out, first, last, cube, plane, sems):
    slices, rows, cols = cube.shape
    step = rows // CHUNKS

    def copies(i):
        at = pl.ds(pl.multiple_of(i * step, step), step)
        yield pltpu.make_async_copy(density.at[:, at], cube.at[:, at], sems.at[i])
        yield pltpu.make_async_copy(valid.at[at], plane.at[at], sems.at[CHUNKS + i])

    for i in range(CHUNKS):
        for copy in copies(i):
            copy.start()
    out[...] = jnp.zeros_like(out)

    def body(i, _):
        for copy in copies(i):
            copy.wait()
        at = pl.ds(pl.multiple_of(i * step, step), step)
        mask = plane[at] != 0
        for s in range(slices + 1):
            x = cube[s, at].astype(jnp.float32) if s < slices else jnp.ones((step, cols), jnp.float32)
            x = jnp.where(mask, x, 0.0).reshape(step // 8, 8, cols).sum(axis=0)
            x = sum(x[:, c : c + LANES] for c in range(0, cols, LANES))
            out[s : s + 1, :] += jnp.sum(x, axis=0, keepdims=True)
        return 0

    lax.fori_loop(0, CHUNKS, body, 0)
    first[:slices] = cube[:, :REACH]
    first[slices] = plane[:REACH].astype(jnp.bfloat16)
    last[:slices] = cube[:, rows - REACH :]
    last[slices] = plane[rows - REACH :].astype(jnp.bfloat16)


def masked_sums(density, valid):
    slices, rows, cols = density.shape
    edge = pltpu.VMEM((slices + 1, REACH, cols), jnp.bfloat16)
    return pl.pallas_call(
        sums_kernel,
        name="sums",
        in_specs=[anywhere()] * 2,
        out_specs=[pl.BlockSpec(memory_space=pltpu.VMEM)] * 3,
        out_shape=[pltpu.VMEM((slices + 8, LANES), jnp.float32), edge, edge],
        scratch_shapes=[
            pltpu.VMEM(density.shape, jnp.bfloat16),
            pltpu.VMEM(valid.shape, jnp.int32),
            pltpu.SemaphoreType.DMA((2 * CHUNKS,)),
        ],
        compiler_params=params(),
        cost_estimate=cost(1, 1),
    )(held(density), held(valid))


def mean_kernel(*refs):
    sums, (out, token) = refs[:4], refs[-2:]
    slices = out.shape[0]
    token[...] = jnp.zeros_like(token)
    total = sums[0][...] + sums[1][...] + sums[2][...] + sums[3][...]
    total = jnp.sum(total, axis=1, keepdims=True)
    out[...] = jnp.broadcast_to(total[:slices] / total[slices : slices + 1], out.shape)


def means(sums, slices, after):
    vmem = pl.BlockSpec(memory_space=pltpu.VMEM)
    return pl.pallas_call(
        mean_kernel,
        name="means",
        in_specs=[vmem] * len(sums) + [anywhere()],
        out_specs=[vmem] * 2,
        out_shape=[pltpu.VMEM((slices, LANES), jnp.float32), pltpu.VMEM((8, LANES), jnp.float32)],
        compiler_params=params(),
        cost_estimate=cost(1, 1),
    )(*sums, resident(after))


def inner_rows(both, last):
    both = both.astype(jnp.float32)
    rows = both.shape[0] - REACH
    return jnp.where(last, both[REACH:], both[:rows])


def window_copies(b, block, last, density, valid, cube, plane, sems):
    high = plane.shape[1]
    here = pl.ds(pl.multiple_of(jnp.minimum(block, last - 1) * (high // 2), high // 2), high)
    return [
        pltpu.make_async_copy(density.at[:, here], cube.at[b], sems.at[2 * b]),
        pltpu.make_async_copy(valid.at[here], plane.at[b], sems.at[2 * b + 1]),
    ]


def ready_kernel(partner, me, density, valid, row_taps, col_taps, after, col, row, cube, plane, sems):
    last = density.shape[1] * 2 // plane.shape[1] - 1
    copies = window_copies(0, me[0] ^ partner, last, density, valid, cube, plane, sems)
    for copy in copies:
        copy.start()
    build_columns(listed(col_taps), col)
    build_rows(listed(row_taps), row)
    for copy in copies:
        copy.wait()


def make_ready(me, partner, density, valid, row_taps, col_taps, after):
    slices, rows, cols = density.shape
    terms = row_taps.shape[0]
    high = LANES // terms
    vmem = pl.BlockSpec(memory_space=pltpu.VMEM)
    shapes = *matrix_shapes(terms, slices, high - HALO), (1, slices, high, cols)
    return pl.pallas_call(
        functools.partial(ready_kernel, partner),
        name="ready",
        in_specs=[pl.BlockSpec(memory_space=pltpu.SMEM)] + [anywhere()] * 2 + [vmem] * 2 + [anywhere()],
        out_specs=[vmem] * 4,
        out_shape=[pltpu.VMEM(shape, jnp.bfloat16) for shape in shapes] + [pltpu.VMEM((1, high, cols), jnp.int32)],
        scratch_shapes=[pltpu.SemaphoreType.DMA((2,))],
        compiler_params=params(),
        cost_estimate=cost(1, 1),
    )(me, held(density), held(valid), row_taps, col_taps, after)


def inner_kernel(wanted, loaded, end, me, *refs):
    count = len(wanted)
    pieces = [cut for _, cut in wanted]
    blocks = [me[0] ^ k for k, _ in wanted]
    outs = sum(len(cut) for cut in pieces)
    if loaded:
        (cube, plane, col, row, mean), tall = refs[:5], refs[-1]
        outs = list(refs[-1 - outs : -1])
    else:
        (density, valid, col, row, mean), (tall, cube, plane, sems) = refs[:5], refs[-4:]
        outs = list(refs[-4 - outs : -4])
        copies = [window_copies(b, blocks[b], end, density, valid, cube, plane, sems) for b in range(count)]
        for copy in sum(copies, []):
            copy.start()
    for b, cut in enumerate(pieces):
        if not loaded:
            for copy in copies[b]:
                copy.wait()
        last = blocks[b] == end
        mask = inner_rows(plane[b], last)
        field = convolve(
            lambda s, b=b, last=last, mask=mask: mask * (inner_rows(cube[b, s], last) - mean[s : s + 1, :1]),
            col,
            row,
            tall,
            REACH,
        ).astype(jnp.bfloat16)
        for _, start, stop in cut:
            outs.pop(0)[...] = field[start:stop]


def filter_inner(me, wanted, density, valid, ready, mean, *after):
    slices, rows, cols = density.shape
    col, row, cube, plane = ready
    high = plane.shape[1]
    count = len(wanted)
    loaded = not after
    vmem = pl.BlockSpec(memory_space=pltpu.VMEM)
    shapes = [(stop - start, slices, cols) for _, cut in wanted for _, start, stop in cut]
    field = [resident(cube), resident(plane)] if loaded else [held(density), held(valid)]
    scratch = [pltpu.VMEM((GROUP * LANES, cols), jnp.bfloat16)]
    if not loaded:
        scratch += [
            pltpu.VMEM((count, slices, high, cols), jnp.bfloat16),
            pltpu.VMEM((count, high, cols), jnp.int32),
            pltpu.SemaphoreType.DMA((2 * count,)),
        ]
    out = pl.pallas_call(
        functools.partial(inner_kernel, wanted, loaded, rows // (high - HALO) - 1),
        name="inner",
        in_specs=[pl.BlockSpec(memory_space=pltpu.SMEM)]
        + [vmem if loaded else anywhere()] * 2
        + [vmem] * 3
        + [anywhere()] * len(after),
        out_specs=[vmem] * len(shapes),
        out_shape=[pltpu.VMEM(shape, jnp.bfloat16) for shape in shapes],
        scratch_shapes=scratch,
        compiler_params=params(),
        cost_estimate=cost(1, 1),
    )(
        me,
        *field,
        resident(col),
        resident(row),
        mean,
        *after,
    )
    out = list(out)
    return [[out.pop(0) for _ in cut] for _, cut in wanted]


def band_kernel(wanted, me, density, valid, above, below, col, row, mean, *refs):
    (mask, tall, done, sems) = refs[-4:]
    pieces = [cut for _, cut in wanted]
    count = sum(len(cut) for cut in pieces)
    outs = refs[-4 - count : -4]
    slices = mean.shape[0]
    rows, cols = valid.shape
    terms = col.shape[2] // LANES
    block = done.shape[1]
    high = block + HALO
    step = pl.program_id(0)
    f32 = jnp.float32

    @pl.when(step == 0)
    def _():
        mask[:REACH] = above[slices].astype(f32)
        mask[REACH : REACH + rows] = valid[...].astype(f32)
        mask[REACH + rows :] = below[slices].astype(f32)

    steps = slices // PER

    @pl.when(step < steps)
    def _():
        for j in range(PER):
            s = step * PER + j
            x = jnp.concatenate([above[s].astype(f32), density[j].astype(f32), below[s].astype(f32)], axis=0)
            x = mask[...] * (x - mean[pl.ds(s, 1), :][:, :1])
            x = jnp.concatenate([x, jnp.zeros((rows + HALO, LANES), f32)], axis=1)
            x = pltpu.roll(x, REACH, 1).astype(jnp.bfloat16)
            x = jnp.concatenate([x[:, c : c + 2 * LANES] for c in range(0, cols, LANES)], axis=0)
            y = jnp.dot(x, col[s], preferred_element_type=f32).astype(jnp.bfloat16)
            for c in range(cols // LANES):
                for k in range(terms):
                    tall[s * terms + k, :, c * LANES : (c + 1) * LANES] = y[
                        c * (rows + HALO) : (c + 1) * (rows + HALO), k * LANES : (k + 1) * LANES
                    ]

    def copies(b):
        at = sum(len(cut) for cut in pieces[:b])
        last = (me[0] ^ wanted[b][0]) == rows // block - 1
        for p, (inner, start, stop) in enumerate(pieces[b]):
            here = jnp.where(last != (inner == 1), block - REACH, 0) + start
            yield pltpu.make_async_copy(done.at[b, pl.ds(here, stop - start)], outs[at + p], sems.at[at + p])

    @pl.when(step >= steps)
    def _():
        for j in range(PAIR):
            b = (step - steps) * PAIR + j
            partner = sum(jnp.where(b == i, k, 0) for i, (k, _) in enumerate(wanted))
            here = pl.ds(pl.multiple_of((me[0] ^ partner) * block, block), high)
            parts = []
            for g in range(slices // GROUP):
                slab = tall[g * GROUP * terms : (g + 1) * GROUP * terms, here, :].reshape(GROUP * LANES, cols)
                z = jnp.dot(row[g], slab, preferred_element_type=f32)
                parts.append(z.reshape(block, GROUP, cols))
            done[b] = jnp.concatenate(parts, axis=1).astype(jnp.bfloat16)

    for n in range(len(pieces) // PAIR):

        @pl.when(step == steps + n)
        def _():
            for b in range(n * PAIR, (n + 1) * PAIR):
                for copy in copies(b):
                    copy.start()

    @pl.when(step == pl.num_programs(0) - 1)
    def _():
        for b in range(len(pieces)):
            for copy in copies(b):
                copy.wait()


def filter_band(me, wanted, density, valid, above, below, ready, mean, *after):
    slices, rows, cols = density.shape
    col, row = ready[:2]
    terms = col.shape[2] // LANES
    block = LANES // terms - HALO
    count = len(wanted)

    def whole(x):
        return pl.BlockSpec(x.shape, lambda i, at: (0,) * x.ndim, pipeline_mode=pl.Buffered(1))

    shapes = [(stop - start, slices, cols) for _, cut in wanted for _, start, stop in cut]
    out = pl.pallas_call(
        functools.partial(band_kernel, wanted),
        name="band",
        grid_spec=pltpu.PrefetchScalarGridSpec(
            num_scalar_prefetch=1,
            grid=(slices // PER + count // PAIR,),
            in_specs=[pl.BlockSpec((PER, rows, cols), lambda i, at: (jnp.minimum(i, slices // PER - 1), 0, 0))]
            + [whole(x) for x in (valid, above, below)]
            + [pl.BlockSpec(memory_space=pltpu.VMEM)] * 2
            + [whole(mean)]
            + [anywhere()] * len(after),
            out_specs=[anywhere()] * len(shapes),
            scratch_shapes=[
                pltpu.VMEM((rows + HALO, cols), jnp.float32),
                pltpu.VMEM((slices * terms, rows + HALO, cols), jnp.bfloat16),
                pltpu.VMEM((count, block, slices, cols), jnp.bfloat16),
                pltpu.SemaphoreType.DMA((len(shapes),)),
            ],
        ),
        out_shape=[hbm(shape, jnp.bfloat16) for shape in shapes],
        compiler_params=params(),
        cost_estimate=cost(1, 1),
    )(
        me,
        held(density),
        held(valid),
        above,
        below,
        resident(col),
        resident(row),
        mean,
        *after,
    )
    out = list(out)
    return [[out.pop(0) for _ in cut] for _, cut in wanted]


def project_kernel(count, me, weights, *refs):
    parts, (amp_out, like_out, token) = refs[:count], refs[-3:]
    zbins = weights.shape[0] // 2
    rows, _, cols = parts[0].shape
    for r in range(rows):
        pencil = jnp.concatenate([x[r] for x in parts], axis=0)
        both = jnp.dot(weights[...], pencil, preferred_element_type=jnp.float32)
        amp = both[:zbins]
        amp_out[:, r * cols : (r + 1) * cols] = amp.astype(jnp.bfloat16)
        like_out[:, r * cols : (r + 1) * cols] = (amp * both[zbins:]).astype(jnp.bfloat16)
    token[...] = jnp.zeros_like(token)


def weights_kernel(peers, me, amp_matrix, like_matrix, out):
    slices = amp_matrix.shape[0] // peers
    for n, matrix in enumerate((amp_matrix, like_matrix)):
        rows = [matrix[pl.ds(pl.multiple_of((me[0] ^ k) * slices, slices), slices)] for k in range(peers)]
        turned = jnp.concatenate(rows, axis=0).astype(jnp.float32).T
        out[n * turned.shape[0] : (n + 1) * turned.shape[0]] = turned.astype(jnp.bfloat16)


def arrange_weights(me, peers, amp_matrix, like_matrix):
    slices, zbins = amp_matrix.shape
    vmem = pl.BlockSpec(memory_space=pltpu.VMEM)
    return pl.pallas_call(
        functools.partial(weights_kernel, peers),
        name="weights",
        in_specs=[pl.BlockSpec(memory_space=pltpu.SMEM), vmem, vmem],
        out_specs=vmem,
        out_shape=pltpu.VMEM((2 * zbins, slices), jnp.bfloat16),
        compiler_params=params(),
        cost_estimate=cost(1, 1),
    )(me, amp_matrix, like_matrix)


def project(me, group, weights, parts, total, earlier):
    inner, start, stop = group
    rows = stop - start
    _, slices, cols = parts[0][0].shape
    peers = len(parts)

    def place(i, me):
        upper = (me[0] == peers - 1) != (inner == 1)
        return 0, i + jnp.where(upper, (total - REACH) // PAIR, 0) + start // PAIR

    zbins = weights.shape[0] // 2
    count = len(parts)
    shape = hbm((zbins, total * cols), jnp.bfloat16)
    return pl.pallas_call(
        functools.partial(project_kernel, count),
        name="project",
        grid_spec=pltpu.PrefetchScalarGridSpec(
            num_scalar_prefetch=1,
            grid=(rows // PAIR,),
            in_specs=[pl.BlockSpec(weights.shape, lambda i, at: (0, 0))]
            + [
                pl.BlockSpec((PAIR, slices, cols), lambda i, at, start=start: (i + start // PAIR, 0, 0))
                for _, start in parts
            ]
            + [anywhere()] * len(earlier),
            out_specs=[pl.BlockSpec((zbins, PAIR * cols), place)] * 2
            + [pl.BlockSpec((8, LANES), lambda i, at: (0, 0))],
        ),
        out_shape=[shape, shape, hbm((8, LANES), jnp.float32)],
        input_output_aliases={2 + count + i: i for i in range(len(earlier))},
        compiler_params=params(),
        cost_estimate=cost(1, 1),
    )(me, weights, *[x for x, _ in parts], *earlier)


def gate_kernel(*refs):
    pass


def gate(x, *earlier, flops=1, space=pltpu.HBM):
    return pl.pallas_call(
        gate_kernel,
        name="gate",
        in_specs=[anywhere()] * (1 + len(earlier)),
        out_specs=anywhere(),
        out_shape=space(x.shape, x.dtype),
        input_output_aliases={0: 0},
        compiler_params=params(),
        cost_estimate=cost(flops, 1),
    )(pltpu.with_memory_space_constraint(x, space), *earlier)


INNER, OUTER = (1, 0, REACH), (0, 0, REACH)
HEAD, TAIL = (0, 0, 6), (0, 6, REACH)
FIRST = (((4, (INNER,)),), ((6, (INNER,)), (5, (INNER,))))
REST = (
    (5, (HEAD, TAIL)),
    (7, (INNER, HEAD, TAIL)),
    (2, (INNER, OUTER)),
    (3, (INNER, OUTER)),
    (4, (HEAD, TAIL)),
    (6, (HEAD, TAIL)),
    (1, (INNER, OUTER)),
    (0, (INNER, OUTER)),
)
ORDER = (
    (4, INNER, None),
    (6, INNER, None),
    (5, INNER, None),
    (7, INNER, 0),
    (2, INNER, 0),
    (4, HEAD, 1),
    (3, INNER, 1),
    (6, HEAD, 2),
    (2, OUTER, 2),
    (5, HEAD, 3),
    (1, INNER, 4),
    (7, HEAD, 5),
    (3, OUTER, 6),
    (1, OUTER, 7),
    (4, TAIL, 9),
    (6, TAIL, 10),
    (5, TAIL, 11),
    (7, TAIL, 12),
)


def fast(density, valid, row_taps, col_taps, amp_matrix, like_matrix):
    slices, rows, cols = density.shape
    peers = lax.axis_size("cuts")
    tiles = lax.axis_size("tile")
    block = rows // peers
    me = lax.axis_index("cuts").astype(jnp.int32).reshape(1)

    def swap(x, k):
        return lax.ppermute(x, "cuts", [(i, i ^ k) for i in range(peers)])

    own, first, last = masked_sums(density, valid)
    sums = [own] + [lax.ppermute(own, "tile", [(i, i ^ k) for i in range(tiles)]) for k in range(1, tiles)]
    ready = make_ready(me, ORDER[0][0], density, valid, row_taps, col_taps, own)
    mean, token = means(sums, slices, ready[0])

    made, arrived = {}, {}

    above = lax.ppermute(last, "tile", [(i, i + 1) for i in range(tiles - 1)])
    below = lax.ppermute(first, "tile", [(i + 1, i) for i in range(tiles - 1)])
    def keep(wanted, got):
        for (k, cut), parts in zip(wanted, got):
            for piece, x in zip(cut, parts):
                made[k, piece] = x

    def send(k, piece, *before):
        x = made[k, piece]
        arrived[k, piece] = swap(gate(x, *before) if before else x, k)

    after = ()
    for wanted in FIRST:
        got = filter_inner(me, wanted, density, valid, ready, mean, *after)
        keep(wanted, got)
        after = (resident(got[0][0]),)
    first_piece = ORDER[0][:2]
    send(*first_piece)
    got = filter_band(
        me, REST, density, valid, above, below, ready, mean, *after, resident(gate(token, arrived[first_piece], flops=BEFORE_BAND, space=pltpu.VMEM))
    )
    keep(REST, got)
    for piece in (INNER, OUTER):
        arrived[0, piece] = made[0, piece]

    weights = arrange_weights(me, peers, amp_matrix, like_matrix)
    result, tokens = [], []

    def finish(group):
        parts = []
        for k in range(peers):
            for piece in (group, INNER, OUTER):
                if (k, piece) in arrived and piece[0] == group[0]:
                    parts.append((arrived[k, piece], group[1] - piece[1]))
                    break
        *result[:], token = project(me, group, weights, parts, block, result)
        tokens.append(token)

    for at, (k, piece, wait) in enumerate(ORDER):
        if (k, piece) in arrived:
            continue
        before = [] if wait is None else [arrived[ORDER[wait][:2]]]
        if at == len(ORDER) - 3:
            finish(INNER)
            before.append(tokens[0])
        send(k, piece, *before)
    finish(HEAD)
    finish(TAIL)
    return tuple(result)


def extended(shard, sides, width):
    for axis, dim in sides:
        size, length = (lax.axis_size(axis), shard.shape[dim])
        up = [(i, (i + 1) % size) for i in range(size - 1)]
        down = [(j, i) for i, j in up]
        last = lax.slice_in_dim(shard, length - width, length, axis=dim)
        initial = lax.slice_in_dim(shard, 0, width, axis=dim)
        before = lax.ppermute(last, axis, up)
        after = lax.ppermute(initial, axis, down)
        shard = jnp.concatenate([before, shard, after], axis=dim)
    return shard


def band_matrix(taps, out_count, in_count):
    offset = lax.broadcasted_iota(jnp.int32, (out_count, in_count), 1) - lax.broadcasted_iota(
        jnp.int32, (out_count, in_count), 0
    )
    positions = lax.broadcasted_iota(jnp.int32, (1, 1, TAPS), 2)
    choose = (offset[:, :, None] == positions).astype(jnp.bfloat16)
    return jnp.einsum("ijt,kst->ksij", choose, taps, preferred_element_type=jnp.float32).astype(jnp.bfloat16)


def filter_field(padded, row_taps, col_taps):
    tall = padded.shape[1]
    cols = padded.shape[2]
    width = 2 * LANES
    row_band = band_matrix(row_taps, tall - HALO, tall)
    rowed = jnp.einsum("ksij,sjc->ksic", row_band, padded, preferred_element_type=jnp.float32).astype(jnp.bfloat16)
    widened = jnp.pad(rowed, ((0, 0), (0, 0), (0, 0), (REACH, REACH)))
    col_band = band_matrix(col_taps, width, width + HALO)
    pieces = []
    for begin in range(0, cols, width):
        segment = widened[:, :, :, begin : begin + width + HALO]
        pieces.append(jnp.einsum("ksrj,ksij->sri", segment, col_band, preferred_element_type=jnp.float32))
    return jnp.concatenate(pieces, axis=2).astype(jnp.bfloat16)


def general(density, valid, row_taps, col_taps, amp_matrix, like_matrix):
    slices, rows, cols = density.shape
    mask = valid.astype(jnp.float32)
    field = density.astype(jnp.float32)
    sums, count = lax.psum((jnp.sum(field * mask[None], axis=(1, 2)), jnp.sum(mask)), "tile")
    masked = (mask[None] * (field - (sums / count)[:, None, None])).astype(jnp.bfloat16)
    filtered = filter_field(extended(masked, (("tile", 1),), REACH), row_taps, col_taps)
    peers = lax.axis_size("cuts")
    share = rows * cols // peers
    pencil = lax.all_to_all(
        filtered.reshape(slices, peers, share), "cuts", split_axis=1, concat_axis=0, tiled=True
    ).reshape(slices * peers, share)
    amp = jnp.dot(amp_matrix.T, pencil, preferred_element_type=jnp.float32)
    like = amp * jnp.dot(like_matrix.T, pencil, preferred_element_type=jnp.float32)
    return amp.astype(jnp.bfloat16), like.astype(jnp.bfloat16)


def per_device(density, valid, row_taps, col_taps, amp_matrix, like_matrix):
    slices, rows, cols = density.shape
    terms = row_taps.shape[0]
    peers = lax.axis_size("cuts")
    fits = (
        peers == 8
        and lax.axis_size("tile") == 4
        and slices == 2 * GROUP
        and terms == 4
        and rows == peers * (LANES // terms - HALO)
        and cols % (2 * LANES) == 0
    )
    run = fast if fits else general
    return run(density, valid, row_taps, col_taps, amp_matrix, like_matrix)


def solution(mesh):
    return jax.shard_map(
        per_device,
        mesh=mesh,
        in_specs=(
            P("cuts", "tile", None),
            P("tile", None),
            P(None, "cuts", None),
            P(None, "cuts", None),
            P(),
            P(),
        ),
        out_specs=(P(None, ("tile", "cuts")), P(None, ("tile", "cuts"))),
        check_vma=False,
    )
```

```python
import functools

import jax
import jax.numpy as jnp
from jax import lax
from jax.experimental import pallas as pl
from jax.experimental.pallas import tpu as pltpu
from jax.sharding import PartitionSpec as P

REACH = 8
TAPS = 2 * REACH + 1
LANES = 128
GROUP = 8
PER = 4
PAIR = 2
CHUNKS = 8
BEFORE_BAND = 2e9
MIB = 1024 * 1024
HALO = 2 * REACH


def params(mib=33):
    return pltpu.CompilerParams(vmem_limit_bytes=mib * MIB)


def hbm(shape, dtype):
    return pltpu.HBM(shape, dtype)


def held(x):
    return pltpu.with_memory_space_constraint(x, pltpu.HBM)


def resident(x):
    return pltpu.with_memory_space_constraint(x, pltpu.VMEM)


def anywhere():
    return pl.BlockSpec(memory_space=pl.ANY)


def cost(flops, moved):
    return pl.CostEstimate(flops=int(flops), bytes_accessed=int(moved), transcendentals=0)


def tap_flip():
    tap = lax.broadcasted_iota(jnp.int32, (TAPS, 2 * LANES), 0)
    lane = lax.broadcasted_iota(jnp.int32, (TAPS, 2 * LANES), 1)
    return (lax.rem(tap + lane, 2 * LANES) == 0).astype(jnp.bfloat16)


def column_band(taps):
    band = pltpu.roll(jnp.broadcast_to(taps, (LANES + HALO, 2 * LANES)), 0, 1, stride=1, stride_axis=0)
    return band[:, :LANES].astype(jnp.bfloat16)


def build_columns(col_taps, col_out):
    terms, slices = len(col_taps), col_taps[0].shape[0]
    for k in range(terms):
        base = jnp.dot(col_taps[k], tap_flip(), preferred_element_type=jnp.float32)
        for s in range(slices):
            col_out[s, : LANES + HALO, k * LANES : (k + 1) * LANES] = column_band(base[s : s + 1])
    for s in range(slices):
        col_out[s, LANES + HALO :, :] = jnp.zeros((LANES - HALO, terms * LANES), jnp.bfloat16)


def build_rows(row_taps, row_out):
    terms, slices = len(row_taps), row_taps[0].shape[0]
    high = LANES // terms
    tap = lax.broadcasted_iota(jnp.int32, (TAPS, LANES), 0)
    lane = lax.broadcasted_iota(jnp.int32, (TAPS, LANES), 1)
    base = jnp.zeros((slices, LANES), jnp.float32)
    for k in range(terms):
        place = (lane == tap + k * high).astype(jnp.bfloat16)
        base = base + jnp.dot(row_taps[k], place, preferred_element_type=jnp.float32)
    sub = lax.broadcasted_iota(jnp.int32, (GROUP, LANES), 0)
    for g in range(slices // GROUP):
        own = base[g * GROUP : (g + 1) * GROUP]
        for pair in range(row_out.shape[1] // (2 * GROUP)):
            shifted = [pltpu.roll(own, 2 * pair + h, 1) for h in range(2)]
            for s in range(GROUP):
                both = jnp.concatenate([jnp.where(sub == s, x, 0.0) for x in shifted], axis=0)
                row_out[
                    g, pair * 2 * GROUP : (pair + 1) * 2 * GROUP, s * LANES : (s + 1) * LANES
                ] = both.astype(jnp.bfloat16)


def listed(taps):
    return [taps[k] for k in range(taps.shape[0])]


def matrix_shapes(terms, slices, rows):
    return (slices, 2 * LANES, terms * LANES), (slices // GROUP, rows * GROUP, GROUP * LANES)


def convolve(field, col, row, tall, rows, read):
    slices, _, wide = col.shape
    terms = wide // LANES
    high, cols = LANES // terms, tall.shape[1]
    if read < high:
        for n in range(tall.shape[0] // high):
            tall[n * high + read : (n + 1) * high] = jnp.zeros((high - read, cols), jnp.bfloat16)
    parts = []
    for g in range(slices // GROUP):
        for j in range(GROUP):
            s = g * GROUP + j
            x = jnp.concatenate([field(s), jnp.zeros((read, LANES), jnp.float32)], axis=1)
            x = pltpu.roll(x, REACH, 1)
            x = jnp.concatenate([x[:, c : c + 2 * LANES] for c in range(0, cols, LANES)], axis=0)
            y = jnp.dot(x.astype(jnp.bfloat16), col[s], preferred_element_type=jnp.float32)
            for c in range(cols // LANES):
                for k in range(terms):
                    at = (j * terms + k) * high
                    tall[at : at + read, c * LANES : (c + 1) * LANES] = y[
                        c * read : (c + 1) * read, k * LANES : (k + 1) * LANES
                    ].astype(jnp.bfloat16)
        z = jnp.dot(row[g, : rows * GROUP], tall[...], preferred_element_type=jnp.float32)
        parts.append(z.reshape(rows, GROUP, cols))
    return jnp.concatenate(parts, axis=1)


def sums_kernel(density, valid, out, first, last, cube, plane, sems):
    slices, rows, cols = cube.shape
    step = rows // CHUNKS

    def copies(i):
        at = pl.ds(pl.multiple_of(i * step, step), step)
        yield pltpu.make_async_copy(density.at[:, at], cube.at[:, at], sems.at[i])
        yield pltpu.make_async_copy(valid.at[at], plane.at[at], sems.at[CHUNKS + i])

    for i in range(CHUNKS):
        for copy in copies(i):
            copy.start()
    out[...] = jnp.zeros_like(out)

    def body(i, _):
        for copy in copies(i):
            copy.wait()
        at = pl.ds(pl.multiple_of(i * step, step), step)
        mask = plane[at] != 0
        for s in range(slices + 1):
            x = cube[s, at].astype(jnp.float32) if s < slices else jnp.ones((step, cols), jnp.float32)
            x = jnp.where(mask, x, 0.0).reshape(step // 8, 8, cols).sum(axis=0)
            x = sum(x[:, c : c + LANES] for c in range(0, cols, LANES))
            out[s : s + 1, :] += jnp.sum(x, axis=0, keepdims=True)
        return 0

    lax.fori_loop(0, CHUNKS, body, 0)
    first[:slices] = cube[:, :REACH]
    first[slices] = plane[:REACH].astype(jnp.bfloat16)
    last[:slices] = cube[:, rows - REACH :]
    last[slices] = plane[rows - REACH :].astype(jnp.bfloat16)


def masked_sums(density, valid):
    slices, rows, cols = density.shape
    edge = pltpu.VMEM((slices + 1, REACH, cols), jnp.bfloat16)
    return pl.pallas_call(
        sums_kernel,
        name="sums",
        in_specs=[anywhere()] * 2,
        out_specs=[pl.BlockSpec(memory_space=pltpu.VMEM)] * 3,
        out_shape=[pltpu.VMEM((slices + 8, LANES), jnp.float32), edge, edge],
        scratch_shapes=[
            pltpu.VMEM(density.shape, jnp.bfloat16),
            pltpu.VMEM(valid.shape, jnp.int32),
            pltpu.SemaphoreType.DMA((2 * CHUNKS,)),
        ],
        compiler_params=params(),
        cost_estimate=cost(1, 1),
    )(held(density), held(valid))


def mean_kernel(*refs):
    sums, (out, token) = refs[:4], refs[-2:]
    slices = out.shape[0]
    token[...] = jnp.zeros_like(token)
    total = sums[0][...] + sums[1][...] + sums[2][...] + sums[3][...]
    total = jnp.sum(total, axis=1, keepdims=True)
    out[...] = jnp.broadcast_to(total[:slices] / total[slices : slices + 1], out.shape)


def means(sums, slices, after):
    vmem = pl.BlockSpec(memory_space=pltpu.VMEM)
    return pl.pallas_call(
        mean_kernel,
        name="means",
        in_specs=[vmem] * len(sums) + [anywhere()],
        out_specs=[vmem] * 2,
        out_shape=[pltpu.VMEM((slices, LANES), jnp.float32), pltpu.VMEM((8, LANES), jnp.float32)],
        compiler_params=params(),
        cost_estimate=cost(1, 1),
    )(*sums, resident(after))


def inner_rows(both, last, high):
    both = both.astype(jnp.float32)
    rows = both.shape[0] - REACH
    chosen = jnp.where(last, both[REACH:], both[:rows])
    if high == rows:
        return chosen
    return jnp.concatenate([chosen, jnp.zeros((high - rows, both.shape[1]), jnp.float32)], axis=0)


def window_copies(b, block, last, density, valid, cube, plane, sems):
    high = plane.shape[1]
    here = pl.ds(pl.multiple_of(jnp.minimum(block, last - 1) * (high // 2), high // 2), high)
    return [
        pltpu.make_async_copy(density.at[:, here], cube.at[b], sems.at[2 * b]),
        pltpu.make_async_copy(valid.at[here], plane.at[b], sems.at[2 * b + 1]),
    ]


def ready_kernel(partner, me, density, valid, row_taps, col_taps, after, col, row, cube, plane, sems):
    last = density.shape[1] * 2 // plane.shape[1] - 1
    copies = window_copies(0, me[0] ^ partner, last, density, valid, cube, plane, sems)
    for copy in copies:
        copy.start()
    build_columns(listed(col_taps), col)
    build_rows(listed(row_taps), row)
    for copy in copies:
        copy.wait()


def make_ready(me, partner, density, valid, row_taps, col_taps, after):
    slices, rows, cols = density.shape
    terms = row_taps.shape[0]
    high = LANES // terms
    vmem = pl.BlockSpec(memory_space=pltpu.VMEM)
    shapes = *matrix_shapes(terms, slices, high - HALO), (1, slices, high, cols)
    return pl.pallas_call(
        functools.partial(ready_kernel, partner),
        name="ready",
        in_specs=[pl.BlockSpec(memory_space=pltpu.SMEM)] + [anywhere()] * 2 + [vmem] * 2 + [anywhere()],
        out_specs=[vmem] * 4,
        out_shape=[pltpu.VMEM(shape, jnp.bfloat16) for shape in shapes] + [pltpu.VMEM((1, high, cols), jnp.int32)],
        scratch_shapes=[pltpu.SemaphoreType.DMA((2,))],
        compiler_params=params(),
        cost_estimate=cost(1, 1),
    )(me, held(density), held(valid), row_taps, col_taps, after)


def inner_kernel(wanted, loaded, end, me, *refs):
    count = len(wanted)
    pieces = [cut for _, cut in wanted]
    blocks = [me[0] ^ k for k, _ in wanted]
    outs = sum(len(cut) for cut in pieces)
    if loaded:
        (cube, plane, col, row, mean), tall = refs[:5], refs[-1]
        outs = list(refs[-1 - outs : -1])
    else:
        (density, valid, col, row, mean), (tall, cube, plane, sems) = refs[:5], refs[-4:]
        outs = list(refs[-4 - outs : -4])
        copies = [window_copies(b, blocks[b], end, density, valid, cube, plane, sems) for b in range(count)]
        for copy in sum(copies, []):
            copy.start()
    high = REACH + HALO if loaded else plane.shape[1]
    for b, cut in enumerate(pieces):
        if not loaded:
            for copy in copies[b]:
                copy.wait()
        last = blocks[b] == end
        mask = inner_rows(plane[b], last, high)
        field = convolve(
            lambda s, b=b, last=last, mask=mask: mask * (inner_rows(cube[b, s], last, high) - mean[s : s + 1, :1]),
            col,
            row,
            tall,
            REACH,
            high,
        ).astype(jnp.bfloat16)
        for _, start, stop in cut:
            outs.pop(0)[...] = field[start:stop]


def filter_inner(me, wanted, density, valid, ready, mean, *after):
    slices, rows, cols = density.shape
    col, row, cube, plane = ready
    high = plane.shape[1]
    count = len(wanted)
    loaded = not after
    vmem = pl.BlockSpec(memory_space=pltpu.VMEM)
    shapes = [(stop - start, slices, cols) for _, cut in wanted for _, start, stop in cut]
    field = [resident(cube), resident(plane)] if loaded else [held(density), held(valid)]
    scratch = [pltpu.VMEM((GROUP * LANES, cols), jnp.bfloat16)]
    if not loaded:
        scratch += [
            pltpu.VMEM((count, slices, high, cols), jnp.bfloat16),
            pltpu.VMEM((count, high, cols), jnp.int32),
            pltpu.SemaphoreType.DMA((2 * count,)),
        ]
    out = pl.pallas_call(
        functools.partial(inner_kernel, wanted, loaded, rows // (high - HALO) - 1),
        name="inner",
        in_specs=[pl.BlockSpec(memory_space=pltpu.SMEM)]
        + [vmem if loaded else anywhere()] * 2
        + [vmem] * 3
        + [anywhere()] * len(after),
        out_specs=[vmem] * len(shapes),
        out_shape=[pltpu.VMEM(shape, jnp.bfloat16) for shape in shapes],
        scratch_shapes=scratch,
        compiler_params=params(),
        cost_estimate=cost(1, 1),
    )(
        me,
        *field,
        resident(col),
        resident(row),
        mean,
        *after,
    )
    out = list(out)
    return [[out.pop(0) for _ in cut] for _, cut in wanted]


def band_kernel(wanted, me, density, valid, above, below, col, row, mean, *refs):
    (mask, tall, done, sems) = refs[-4:]
    pieces = [cut for _, cut in wanted]
    count = sum(len(cut) for cut in pieces)
    outs = refs[-4 - count : -4]
    slices = mean.shape[0]
    rows, cols = valid.shape
    terms = col.shape[2] // LANES
    block = done.shape[1]
    high = block + HALO
    step = pl.program_id(0)
    f32 = jnp.float32

    @pl.when(step == 0)
    def _():
        mask[:REACH] = above[slices].astype(f32)
        mask[REACH : REACH + rows] = valid[...].astype(f32)
        mask[REACH + rows :] = below[slices].astype(f32)

    steps = slices // PER

    @pl.when(step < steps)
    def _():
        for j in range(PER):
            s = step * PER + j
            x = jnp.concatenate([above[s].astype(f32), density[j].astype(f32), below[s].astype(f32)], axis=0)
            x = mask[...] * (x - mean[pl.ds(s, 1), :][:, :1])
            x = jnp.concatenate([x, jnp.zeros((rows + HALO, LANES), f32)], axis=1)
            x = pltpu.roll(x, REACH, 1).astype(jnp.bfloat16)
            x = jnp.concatenate([x[:, c : c + 2 * LANES] for c in range(0, cols, LANES)], axis=0)
            y = jnp.dot(x, col[s], preferred_element_type=f32).astype(jnp.bfloat16)
            for c in range(cols // LANES):
                for k in range(terms):
                    tall[s * terms + k, :, c * LANES : (c + 1) * LANES] = y[
                        c * (rows + HALO) : (c + 1) * (rows + HALO), k * LANES : (k + 1) * LANES
                    ]

    def copies(b):
        at = sum(len(cut) for cut in pieces[:b])
        last = (me[0] ^ wanted[b][0]) == rows // block - 1
        for p, (inner, start, stop) in enumerate(pieces[b]):
            here = jnp.where(last != (inner == 1), block - REACH, 0) + start
            yield pltpu.make_async_copy(done.at[b, pl.ds(here, stop - start)], outs[at + p], sems.at[at + p])

    @pl.when(step >= steps)
    def _():
        for j in range(PAIR):
            b = (step - steps) * PAIR + j
            partner = sum(jnp.where(b == i, k, 0) for i, (k, _) in enumerate(wanted))
            here = pl.ds(pl.multiple_of((me[0] ^ partner) * block, block), high)
            parts = []
            for g in range(slices // GROUP):
                slab = tall[g * GROUP * terms : (g + 1) * GROUP * terms, here, :].reshape(GROUP * LANES, cols)
                z = jnp.dot(row[g], slab, preferred_element_type=f32)
                parts.append(z.reshape(block, GROUP, cols))
            done[b] = jnp.concatenate(parts, axis=1).astype(jnp.bfloat16)

    for n in range(len(pieces) // PAIR):

        @pl.when(step == steps + n)
        def _():
            for b in range(n * PAIR, (n + 1) * PAIR):
                for copy in copies(b):
                    copy.start()

    @pl.when(step == pl.num_programs(0) - 1)
    def _():
        for b in range(len(pieces)):
            for copy in copies(b):
                copy.wait()


def filter_band(me, wanted, density, valid, above, below, ready, mean, *after):
    slices, rows, cols = density.shape
    col, row = ready[:2]
    terms = col.shape[2] // LANES
    block = LANES // terms - HALO
    count = len(wanted)

    def whole(x):
        return pl.BlockSpec(x.shape, lambda i, at: (0,) * x.ndim, pipeline_mode=pl.Buffered(1))

    shapes = [(stop - start, slices, cols) for _, cut in wanted for _, start, stop in cut]
    out = pl.pallas_call(
        functools.partial(band_kernel, wanted),
        name="band",
        grid_spec=pltpu.PrefetchScalarGridSpec(
            num_scalar_prefetch=1,
            grid=(slices // PER + count // PAIR,),
            in_specs=[pl.BlockSpec((PER, rows, cols), lambda i, at: (jnp.minimum(i, slices // PER - 1), 0, 0))]
            + [whole(x) for x in (valid, above, below)]
            + [pl.BlockSpec(memory_space=pltpu.VMEM)] * 2
            + [whole(mean)]
            + [anywhere()] * len(after),
            out_specs=[anywhere()] * len(shapes),
            scratch_shapes=[
                pltpu.VMEM((rows + HALO, cols), jnp.float32),
                pltpu.VMEM((slices * terms, rows + HALO, cols), jnp.bfloat16),
                pltpu.VMEM((count, block, slices, cols), jnp.bfloat16),
                pltpu.SemaphoreType.DMA((len(shapes),)),
            ],
        ),
        out_shape=[hbm(shape, jnp.bfloat16) for shape in shapes],
        compiler_params=params(),
        cost_estimate=cost(1, 1),
    )(
        me,
        held(density),
        held(valid),
        above,
        below,
        resident(col),
        resident(row),
        mean,
        *after,
    )
    out = list(out)
    return [[out.pop(0) for _ in cut] for _, cut in wanted]


def project_kernel(count, me, weights, *refs):
    parts, (amp_out, like_out, token) = refs[:count], refs[-3:]
    zbins = weights.shape[0] // 2
    rows, _, cols = parts[0].shape
    for r in range(rows):
        pencil = jnp.concatenate([x[r] for x in parts], axis=0)
        both = jnp.dot(weights[...], pencil, preferred_element_type=jnp.float32)
        amp = both[:zbins]
        amp_out[:, r * cols : (r + 1) * cols] = amp.astype(jnp.bfloat16)
        like_out[:, r * cols : (r + 1) * cols] = (amp * both[zbins:]).astype(jnp.bfloat16)
    token[...] = jnp.zeros_like(token)


def weights_kernel(peers, me, amp_matrix, like_matrix, out):
    slices = amp_matrix.shape[0] // peers
    for n, matrix in enumerate((amp_matrix, like_matrix)):
        rows = [matrix[pl.ds(pl.multiple_of((me[0] ^ k) * slices, slices), slices)] for k in range(peers)]
        turned = jnp.concatenate(rows, axis=0).astype(jnp.float32).T
        out[n * turned.shape[0] : (n + 1) * turned.shape[0]] = turned.astype(jnp.bfloat16)


def arrange_weights(me, peers, amp_matrix, like_matrix):
    slices, zbins = amp_matrix.shape
    vmem = pl.BlockSpec(memory_space=pltpu.VMEM)
    return pl.pallas_call(
        functools.partial(weights_kernel, peers),
        name="weights",
        in_specs=[pl.BlockSpec(memory_space=pltpu.SMEM), vmem, vmem],
        out_specs=vmem,
        out_shape=pltpu.VMEM((2 * zbins, slices), jnp.bfloat16),
        compiler_params=params(),
        cost_estimate=cost(1, 1),
    )(me, amp_matrix, like_matrix)


def project(me, group, weights, parts, total, earlier):
    inner, start, stop = group
    rows = stop - start
    _, slices, cols = parts[0][0].shape
    peers = len(parts)

    def place(i, me):
        upper = (me[0] == peers - 1) != (inner == 1)
        return 0, i + jnp.where(upper, (total - REACH) // PAIR, 0) + start // PAIR

    zbins = weights.shape[0] // 2
    count = len(parts)
    shape = hbm((zbins, total * cols), jnp.bfloat16)
    return pl.pallas_call(
        functools.partial(project_kernel, count),
        name="project",
        grid_spec=pltpu.PrefetchScalarGridSpec(
            num_scalar_prefetch=1,
            grid=(rows // PAIR,),
            in_specs=[pl.BlockSpec(weights.shape, lambda i, at: (0, 0))]
            + [
                pl.BlockSpec((PAIR, slices, cols), lambda i, at, start=start: (i + start // PAIR, 0, 0))
                for _, start in parts
            ]
            + [anywhere()] * len(earlier),
            out_specs=[pl.BlockSpec((zbins, PAIR * cols), place)] * 2
            + [pl.BlockSpec((8, LANES), lambda i, at: (0, 0))],
        ),
        out_shape=[shape, shape, hbm((8, LANES), jnp.float32)],
        input_output_aliases={2 + count + i: i for i in range(len(earlier))},
        compiler_params=params(),
        cost_estimate=cost(1, 1),
    )(me, weights, *[x for x, _ in parts], *earlier)


def gate_kernel(*refs):
    pass


def gate(x, *earlier, flops=1, space=pltpu.HBM):
    return pl.pallas_call(
        gate_kernel,
        name="gate",
        in_specs=[anywhere()] * (1 + len(earlier)),
        out_specs=anywhere(),
        out_shape=space(x.shape, x.dtype),
        input_output_aliases={0: 0},
        compiler_params=params(),
        cost_estimate=cost(flops, 1),
    )(pltpu.with_memory_space_constraint(x, space), *earlier)


INNER, OUTER = (1, 0, REACH), (0, 0, REACH)
HEAD, TAIL = (0, 0, 6), (0, 6, REACH)
FIRST = (((4, (INNER,)),), ((6, (INNER,)), (5, (INNER,))))
REST = (
    (5, (HEAD, TAIL)),
    (7, (INNER, HEAD, TAIL)),
    (2, (INNER, OUTER)),
    (3, (INNER, OUTER)),
    (4, (HEAD, TAIL)),
    (6, (HEAD, TAIL)),
    (1, (INNER, OUTER)),
    (0, (INNER, OUTER)),
)
ORDER = (
    (4, INNER, None),
    (6, INNER, None),
    (5, INNER, None),
    (7, INNER, 0),
    (2, INNER, 0),
    (4, HEAD, 1),
    (3, INNER, 1),
    (6, HEAD, 2),
    (2, OUTER, 2),
    (5, HEAD, 3),
    (1, INNER, 4),
    (7, HEAD, 5),
    (3, OUTER, 6),
    (1, OUTER, 7),
    (4, TAIL, 9),
    (6, TAIL, 10),
    (5, TAIL, 11),
    (7, TAIL, 12),
)


def fast(density, valid, row_taps, col_taps, amp_matrix, like_matrix):
    slices, rows, cols = density.shape
    peers = lax.axis_size("cuts")
    tiles = lax.axis_size("tile")
    block = rows // peers
    me = lax.axis_index("cuts").astype(jnp.int32).reshape(1)

    def swap(x, k):
        return lax.ppermute(x, "cuts", [(i, i ^ k) for i in range(peers)])

    own, first, last = masked_sums(density, valid)
    sums = [own] + [lax.ppermute(own, "tile", [(i, i ^ k) for i in range(tiles)]) for k in range(1, tiles)]
    ready = make_ready(me, ORDER[0][0], density, valid, row_taps, col_taps, own)
    mean, token = means(sums, slices, ready[0])

    made, arrived = {}, {}

    above = lax.ppermute(last, "tile", [(i, i + 1) for i in range(tiles - 1)])
    below = lax.ppermute(first, "tile", [(i + 1, i) for i in range(tiles - 1)])
    def keep(wanted, got):
        for (k, cut), parts in zip(wanted, got):
            for piece, x in zip(cut, parts):
                made[k, piece] = x

    def send(k, piece, *before):
        x = made[k, piece]
        arrived[k, piece] = swap(gate(x, *before) if before else x, k)

    after = ()
    for wanted in FIRST:
        got = filter_inner(me, wanted, density, valid, ready, mean, *after)
        keep(wanted, got)
        after = (resident(got[0][0]),)
    first_piece = ORDER[0][:2]
    send(*first_piece)
    got = filter_band(
        me, REST, density, valid, above, below, ready, mean, *after, resident(gate(token, arrived[first_piece], flops=BEFORE_BAND, space=pltpu.VMEM))
    )
    keep(REST, got)
    for piece in (INNER, OUTER):
        arrived[0, piece] = made[0, piece]

    weights = arrange_weights(me, peers, amp_matrix, like_matrix)
    result, tokens = [], []

    def finish(group):
        parts = []
        for k in range(peers):
            for piece in (group, INNER, OUTER):
                if (k, piece) in arrived and piece[0] == group[0]:
                    parts.append((arrived[k, piece], group[1] - piece[1]))
                    break
        *result[:], token = project(me, group, weights, parts, block, result)
        tokens.append(token)

    for at, (k, piece, wait) in enumerate(ORDER):
        if (k, piece) in arrived:
            continue
        before = [] if wait is None else [arrived[ORDER[wait][:2]]]
        if at == len(ORDER) - 3:
            finish(INNER)
            before.append(tokens[0])
        send(k, piece, *before)
    finish(HEAD)
    finish(TAIL)
    return tuple(result)


def extended(shard, sides, width):
    for axis, dim in sides:
        size, length = (lax.axis_size(axis), shard.shape[dim])
        up = [(i, (i + 1) % size) for i in range(size - 1)]
        down = [(j, i) for i, j in up]
        last = lax.slice_in_dim(shard, length - width, length, axis=dim)
        initial = lax.slice_in_dim(shard, 0, width, axis=dim)
        before = lax.ppermute(last, axis, up)
        after = lax.ppermute(initial, axis, down)
        shard = jnp.concatenate([before, shard, after], axis=dim)
    return shard


def band_matrix(taps, out_count, in_count):
    offset = lax.broadcasted_iota(jnp.int32, (out_count, in_count), 1) - lax.broadcasted_iota(
        jnp.int32, (out_count, in_count), 0
    )
    positions = lax.broadcasted_iota(jnp.int32, (1, 1, TAPS), 2)
    choose = (offset[:, :, None] == positions).astype(jnp.bfloat16)
    return jnp.einsum("ijt,kst->ksij", choose, taps, preferred_element_type=jnp.float32).astype(jnp.bfloat16)


def filter_field(padded, row_taps, col_taps):
    tall = padded.shape[1]
    cols = padded.shape[2]
    width = 2 * LANES
    row_band = band_matrix(row_taps, tall - HALO, tall)
    rowed = jnp.einsum("ksij,sjc->ksic", row_band, padded, preferred_element_type=jnp.float32).astype(jnp.bfloat16)
    widened = jnp.pad(rowed, ((0, 0), (0, 0), (0, 0), (REACH, REACH)))
    col_band = band_matrix(col_taps, width, width + HALO)
    pieces = []
    for begin in range(0, cols, width):
        segment = widened[:, :, :, begin : begin + width + HALO]
        pieces.append(jnp.einsum("ksrj,ksij->sri", segment, col_band, preferred_element_type=jnp.float32))
    return jnp.concatenate(pieces, axis=2).astype(jnp.bfloat16)


def general(density, valid, row_taps, col_taps, amp_matrix, like_matrix):
    slices, rows, cols = density.shape
    mask = valid.astype(jnp.float32)
    field = density.astype(jnp.float32)
    sums, count = lax.psum((jnp.sum(field * mask[None], axis=(1, 2)), jnp.sum(mask)), "tile")
    masked = (mask[None] * (field - (sums / count)[:, None, None])).astype(jnp.bfloat16)
    filtered = filter_field(extended(masked, (("tile", 1),), REACH), row_taps, col_taps)
    peers = lax.axis_size("cuts")
    share = rows * cols // peers
    pencil = lax.all_to_all(
        filtered.reshape(slices, peers, share), "cuts", split_axis=1, concat_axis=0, tiled=True
    ).reshape(slices * peers, share)
    amp = jnp.dot(amp_matrix.T, pencil, preferred_element_type=jnp.float32)
    like = amp * jnp.dot(like_matrix.T, pencil, preferred_element_type=jnp.float32)
    return amp.astype(jnp.bfloat16), like.astype(jnp.bfloat16)


def per_device(density, valid, row_taps, col_taps, amp_matrix, like_matrix):
    slices, rows, cols = density.shape
    terms = row_taps.shape[0]
    peers = lax.axis_size("cuts")
    fits = (
        peers == 8
        and lax.axis_size("tile") == 4
        and slices == 2 * GROUP
        and terms == 4
        and rows == peers * (LANES // terms - HALO)
        and cols % (2 * LANES) == 0
    )
    run = fast if fits else general
    return run(density, valid, row_taps, col_taps, amp_matrix, like_matrix)


def solution(mesh):
    return jax.shard_map(
        per_device,
        mesh=mesh,
        in_specs=(
            P("cuts", "tile", None),
            P("tile", None),
            P(None, "cuts", None),
            P(None, "cuts", None),
            P(),
            P(),
        ),
        out_specs=(P(None, ("tile", "cuts")), P(None, ("tile", "cuts"))),
        check_vma=False,
    )
```
